32 devices in a mesh: dp: 2 (over y), row: 4 (over x, core), col: 4 (over z).
Axes of the slice: x: 2, y: 2, z: 4, core: 2. Of those that a mesh axis runs over, the one named last changes fastest.
Arguments:
- tokens_in: bfloat16 [16384, 768], P(('dp', 'row', 'col')), may hold values from -6 to 6
- segment_ids: int32 [32, 512], P('dp'), may hold values from 0 to 3, never falling along the last dimension, each value on 1 to 256 neighbouring positions
- attn_gain: float32 [768], replicated, may hold values from 0.5 to 1.5
- attn_shift: float32 [768], replicated, may hold values from -1.25 to 1.25
- mlp_gain: float32 [768], replicated, may hold values from 0.5 to 1.5
- mlp_shift: float32 [768], replicated, may hold values from -1.25 to 1.25
- qkv_weight: bfloat16 [768, 2304], P('row', 'col'), may hold values from -0.21875 to 0.21875
- qkv_bias: float32 [2304], replicated, may hold values from -1.75 to 1.75
- out_weight: bfloat16 [768, 768], P('col', 'row'), may hold values from -0.875 to 0.875
- out_bias: float32 [768], replicated, may hold values from -1.75 to 1.75
- up_weight: bfloat16 [768, 3072], P('row', 'col'), may hold values from -0.21875 to 0.21875
- up_bias: float32 [3072], replicated, may hold values from -1.75 to 1.75
- down_weight: bfloat16 [3072, 768], P('col', 'row'), may hold values from -0.109375 to 0.109375
- down_bias: float32 [768], replicated, may hold values from -1.75 to 1.75
- out_cotangent: bfloat16 [16384, 768], P(('dp', 'row', 'col')), may hold values from -6 to 6
Outputs:
- block_out: bfloat16 [16384, 768], P(('dp', 'row', 'col'))
- in_grad: bfloat16 [16384, 768], P(('dp', 'row', 'col'))
- grad_attn_gain: float32 [768], replicated
- grad_attn_shift: float32 [768], replicated
- grad_mlp_gain: float32 [768], replicated
- grad_mlp_shift: float32 [768], replicated
- grad_qkv_weight: float32 [768, 2304], P('row', 'col')
- grad_qkv_bias: float32 [2304], replicated
- grad_out_weight: float32 [768, 768], P('col', 'row')
- grad_out_bias: float32 [768], replicated
- grad_up_weight: float32 [768, 3072], P('row', 'col')
- grad_up_bias: float32 [3072], replicated
- grad_down_weight: float32 [3072, 768], P('col', 'row')
- grad_down_bias: float32 [768], replicated
The draws below stay inside these ranges and needn't reach their ends.
Inputs may be any that keep to these rules, and one draw needn't show every extreme that they name: `segment_ids`: along each sequence the numbers never fall; each document has 1 to 256 tokens, and some document of each sequence has exactly 256.
All inputs are finite; a program needn't handle non-finite values.
Results may differ from the reference program's by a relative error of at most 0.011.
Values may be sent and summed in bfloat16 or wider, within the bound.
No kernel may reach another device: no remote copies, remote signals or barrier semaphores. Data moves between devices by JAX's collectives and lax.ppermute only.
A program may use at most 384 MiB of HBM per device.

```python
import math
import jax
import jax.numpy as jnp
import numpy as np
from jax import lax

D = 768
H = 12
HD = 64
ROT = 16
FF = 3072
SEQ = 512
SEQS = 32
TOKENS = 16384


def block_scale(own_key, extent, cuts, least, largest):
    def one(axis_at, shards_of):
        heights = jax.random.uniform(jax.random.fold_in(jax.random.fold_in(own_key, 6), axis_at), (shards_of,), jnp.float32, least / len(cuts), largest / len(cuts))
        return jnp.repeat(jnp.exp(heights), extent[axis_at] // shards_of).reshape((-1,) + (1,) * (len(extent) - axis_at - 1))

    loudness = one(*cuts[0])
    for cut in cuts[1:]:
        loudness = loudness * one(*cut)
    return loudness


def profile(number_of, total, limit, lean):
    weights = [(1 << 20) // math.isqrt(standing ** lean) + 1 for standing in range(2, number_of + 1)]
    rest, given = total - limit - (number_of - 1), [1] * (number_of - 1)
    while rest > 0:
        free = [i for i in range(number_of - 1) if given[i] < limit]
        whole, remaining = sum([weights[i] for i in free]), rest
        for i in free:
            extra = min(limit - given[i], max(1, remaining * weights[i] // whole), rest)
            given[i] = given[i] + extra
            rest = rest - extra
    return np.array([limit] + given)


def ragged_sizes(key, count, total, most, lean):
    if count == 2:
        one = jax.random.randint(key, (), max(1, total - most), min(most, total - 1) + 1)
        return jnp.stack([one, total - one])
    sizes = jnp.asarray(profile(count, total, most, lean), jnp.int32)
    couples = (count - 1) // 2
    source_of, receiver = sizes[1:1 + 2 * couples:2], sizes[2:2 + 2 * couples:2]
    slack = jnp.minimum(source_of - 1, most - receiver)
    moved = jax.random.randint(jax.random.fold_in(key, 1), (couples,), 0, 1 << 20) % (slack + 1)
    sizes = sizes.at[1:1 + 2 * couples:2].set(source_of - moved).at[2:2 + 2 * couples:2].set(receiver + moved)
    return sizes[jax.random.permutation(jax.random.fold_in(key, 2), count)]


def centred(own_key, dims, deviation, bound, shards=(), held_as=jnp.bfloat16):
    gain = block_scale(own_key, dims, shards, -0.22, 0.18) if shards else 1.0
    values = jax.random.normal(own_key, dims, jnp.float32) * deviation * gain
    return jnp.minimum(jnp.maximum(values, -bound), bound).astype(held_as)


def setup_inputs(seed: int = 0) -> dict:
    streams_of = jax.random.split(jax.random.key(seed), 16)
    tokens_in = centred(streams_of[0], (TOKENS, D), 1.0, 6.0, ((0, 32),))
    segment_ids = jax.vmap(lambda own: jnp.searchsorted(jnp.cumsum(ragged_sizes(own, 4, SEQ, SEQ // 2, 1)), jnp.arange(SEQ), side="right"))(jax.random.split(streams_of[1], SEQS)).reshape((SEQS, SEQ)).astype(jnp.int32)
    attn_gain = jnp.clip(1.0 + 0.1 * jax.random.normal(streams_of[2], (D,), jnp.float32), 0.5, 1.5)
    attn_shift = centred(streams_of[3], (D,), 0.2, 1.25, (), jnp.float32)
    mlp_gain = jnp.clip(1.0 + 0.1 * jax.random.normal(streams_of[4], (D,), jnp.float32), 0.5, 1.5)
    mlp_shift = centred(streams_of[5], (D,), 0.2, 1.25, (), jnp.float32)
    qkv_weight = centred(streams_of[6], (D, 3 * D), D ** -0.5, 0.21875, ((0, 4), (1, 4)))
    qkv_bias = centred(streams_of[7], (3 * D,), 0.3, 1.75, (), jnp.float32)
    out_weight = centred(streams_of[8], (D, D), (D // 16) ** -0.5, 0.875, ((0, 4), (1, 4)))
    out_bias = centred(streams_of[9], (D,), 0.3, 1.75, (), jnp.float32)
    up_weight = centred(streams_of[10], (D, FF), D ** -0.5, 0.21875, ((0, 4), (1, 4)))
    up_bias = centred(streams_of[11], (FF,), 0.3, 1.75, (), jnp.float32)
    down_weight = centred(streams_of[12], (FF, D), FF ** -0.5, 0.109375, ((0, 4), (1, 4)))
    down_bias = centred(streams_of[13], (D,), 0.3, 1.75, (), jnp.float32)
    out_cotangent = centred(streams_of[14], (TOKENS, D), 1.0, 6.0, ((0, 32),))
    return {"tokens_in": tokens_in, "segment_ids": segment_ids, "attn_gain": attn_gain, "attn_shift": attn_shift, "mlp_gain": mlp_gain, "mlp_shift": mlp_shift, "qkv_weight": qkv_weight, "qkv_bias": qkv_bias, "out_weight": out_weight, "out_bias": out_bias, "up_weight": up_weight, "up_bias": up_bias, "down_weight": down_weight, "down_bias": down_bias, "out_cotangent": out_cotangent}


@jax.custom_vjp
def low(v):
    return lax.optimization_barrier(v.astype(jnp.bfloat16)).astype(jnp.float32)

@jax.custom_vjp
def low_back(v):
    return v

def low_keep(v):
    return (low(v), None)

def low_pass(kept, grad):
    return (grad,)

def back_keep(v):
    return (v, None)

def back_low(kept, grad):
    return (low(grad),)
low.defvjp(low_keep, low_pass)
low_back.defvjp(back_keep, back_low)
EPSILON = 1e-05
ROPE_BASE = 10000.0
HIGHEST = lax.Precision.HIGHEST

def rotary_tables(seg_rows, rot_dims):
    column_ids = lax.broadcasted_iota(jnp.int32, seg_rows.shape, 1)
    previous = jnp.concatenate([seg_rows[:, :1] - 1, seg_rows[:, :-1]], axis=1)
    starts = lax.cummax(jnp.where(seg_rows != previous, column_ids, 0), axis=1)
    places = (column_ids - starts).astype(jnp.float32)
    halves = rot_dims // 2
    frequency = ROPE_BASE ** (-(jnp.arange(halves, dtype=jnp.float32) * (2.0 / rot_dims)))
    angles = places[:, :, None] * frequency
    return (jnp.cos(angles), jnp.sin(angles))

def apply_rotary(vectors, cosine, sine_table, rot_dims):
    halves = rot_dims // 2
    first_half = vectors[..., :halves]
    second_half = vectors[..., halves:rot_dims]
    cos_wide = cosine[:, :, None, :]
    sin_wide = sine_table[:, :, None, :]
    return jnp.concatenate([first_half * cos_wide - second_half * sin_wide, second_half * cos_wide + first_half * sin_wide, vectors[..., rot_dims:]], axis=-1)

def attend_group(qkv_group, seg_group):
    group_count = seg_group.shape[0]
    cosine, sine_table = rotary_tables(seg_group, ROT)
    split_heads = qkv_group.reshape(group_count, SEQ, H, 3, HD)
    queries = low(apply_rotary(split_heads[:, :, :, 0], cosine, sine_table, ROT))
    key_rows = low(apply_rotary(split_heads[:, :, :, 1], cosine, sine_table, ROT))
    value_rows = low(split_heads[:, :, :, 2])
    scores = low_back(jnp.einsum('bqhd,bkhd->bhqk', queries, key_rows, precision=HIGHEST) * (1.0 / math.sqrt(HD)))
    query_ids = lax.broadcasted_iota(jnp.int32, (SEQ, 1), 0)
    key_ids = lax.broadcasted_iota(jnp.int32, (1, SEQ), 1)
    allowed = (key_ids <= query_ids)[None, None] & (seg_group[:, None, :, None] == seg_group[:, None, None, :])
    scores = jnp.where(allowed, scores, -jnp.inf)
    probability = low(jax.nn.softmax(scores, axis=3))
    mixed = jnp.einsum('bhqk,bkhd->bqhd', probability, value_rows, precision=HIGHEST)
    return low_back(low(mixed)).reshape(group_count * SEQ, H * HD)

def attend_all(qkv_proj, segment_ids):
    group_size = math.gcd(SEQS, max(1, 4096 // SEQ))
    group_total = SEQS // group_size
    qkv_groups = qkv_proj.reshape(group_total, group_size, SEQ, 3 * D)
    seg_groups = segment_ids.reshape(group_total, group_size, SEQ)
    step_fn = jax.checkpoint(attend_group)

    def scan_step(carried, packed):
        return (carried, step_fn(packed[0], packed[1]))
    carried, mixed = lax.scan(scan_step, jnp.zeros((), jnp.float32), (qkv_groups, seg_groups))
    return mixed.reshape(SEQS * SEQ, D)

def reference(tokens_in, segment_ids, attn_gain, attn_shift, mlp_gain, mlp_shift, qkv_weight, qkv_bias, out_weight, out_bias, up_weight, up_bias, down_weight, down_bias, out_cotangent):

    def forward(x_float, gain_one, shift_one, gain_two, shift_two, weight_qkv, bias_qkv, weight_out, bias_out, weight_up, bias_up, weight_down, bias_down):
        center = x_float - lax.optimization_barrier(jnp.mean(x_float, axis=1, keepdims=True))
        normed = center * lax.rsqrt(lax.optimization_barrier(jnp.mean(center * center, axis=1, keepdims=True)) + EPSILON)
        norm_attn = low(normed * gain_one + shift_one)
        norm_mlp = low(normed * gain_two + shift_two)
        qkv_proj = low_back(jnp.dot(norm_attn, weight_qkv, precision=HIGHEST) + bias_qkv)
        hidden = low_back(jnp.dot(norm_mlp, weight_up, precision=HIGHEST) + bias_up)
        active = low(jax.nn.gelu(hidden, approximate=False))
        attn_mix = attend_all(qkv_proj, segment_ids)
        branch = jnp.dot(attn_mix, weight_out, precision=HIGHEST) + jnp.dot(active, weight_down, precision=HIGHEST)
        return x_float + branch + bias_out + bias_down
    inputs = (tokens_in, attn_gain, attn_shift, mlp_gain, mlp_shift, qkv_weight, qkv_bias, out_weight, out_bias, up_weight, up_bias, down_weight, down_bias)
    floats = tuple((array.astype(jnp.float32) for array in inputs))
    result, pull = jax.vjp(forward, *floats)
    grads = pull(out_cotangent.astype(jnp.float32))
    return (result.astype(jnp.bfloat16), grads[0].astype(jnp.bfloat16), grads[1], grads[2], grads[3], grads[4], grads[5], grads[6], grads[7], grads[8], grads[9], grads[10], grads[11], grads[12])
```

```python
import functools
import math

import jax
import jax.numpy as jnp
from jax import lax
from jax.experimental import pallas as pl
from jax.experimental.pallas import tpu as pltpu
from jax.sharding import PartitionSpec as P

HD = 64
ROT = 16
QKV = 3 * HD
HEAD = 4 * HD
EPSILON = 1e-05
ROPE_BASE = 10000.0
NEAR = 128
LONGEST = 256
F32 = jnp.float32
BF16 = jnp.bfloat16


def dot_nn(a, b):
    return lax.dot_general(a, b, (((1,), (0,)), ((), ())), preferred_element_type=F32)


def dot_nt(a, b):
    return lax.dot_general(a, b, (((1,), (1,)), ((), ())), preferred_element_type=F32)


def rotary_tables(seg_row):
    length = seg_row.shape[0]
    ids = lax.iota(jnp.int32, length)
    previous = jnp.concatenate([seg_row[:1] - 1, seg_row[:-1]])
    starts = lax.cummax(jnp.where(seg_row != previous, ids, 0))
    places = (ids - starts).astype(F32)
    halves = ROT // 2
    lane = lax.iota(jnp.int32, 2 * HD) % HD
    step = (lane % halves).astype(F32)
    frequency = ROPE_BASE ** (-(step * (2.0 / ROT)))
    angles = places[:, None] * frequency[None, :]
    cosine, sine = jnp.cos(angles), jnp.sin(angles)
    turned = (lane < ROT)[None, :]
    first = (lane < halves)[None, :]
    keep = jnp.where(turned, cosine, 1.0)
    ahead = jnp.where(first, -sine, 0.0)
    behind = jnp.where(turned & ~first, sine, 0.0)
    return keep, ahead, behind


def assemble(me_ref, w_refs, w_scr):
    rows = w_refs[0].shape[1]
    for j, ref in enumerate(w_refs):
        at = pl.multiple_of((me_ref[0] ^ j) * rows, 16)
        w_scr[pl.ds(at, rows), :] = ref[0]


def hand_out(me_ref, g_scr, g_refs):
    rows = g_refs[0].shape[1]
    for j, ref in enumerate(g_refs):
        at = pl.multiple_of((me_ref[0] ^ j) * rows, 16)
        ref[0] = g_scr[pl.ds(at, rows), :]


def attention_kernel(
    na_ref, naT_ref, cot_ref, cotT_ref, w_ref, bias_ref, keep_ref, ahead_ref, behind_ref, segc_ref, segr_ref,
    branch_ref, dna_ref, g_ref, dbias_ref,
    bias_scr, qkv_scr, dattn_scr, dqkv_scr, mix_scr,
):
    length, width = na_ref.shape
    block_cols = w_ref.shape[-1]
    heads = block_cols // HEAD
    step = pl.program_id(0)

    @pl.when(step == 0)
    def _():
        branch_ref[...] = jnp.zeros_like(branch_ref)
        dna_ref[...] = jnp.zeros_like(dna_ref)
        rows = lax.broadcasted_iota(jnp.int32, (length, length), 0)
        cols = lax.broadcasted_iota(jnp.int32, (length, length), 1)
        inside = (cols <= rows) & (segc_ref[...] == segr_ref[...])
        bias_scr[...] = jnp.where(inside, 0.0, -jnp.inf)

    w = w_ref[...].reshape(width, block_cols)
    w_vo = jnp.concatenate([w[:, i * HEAD + 2 * HD : (i + 1) * HEAD] for i in range(heads)], axis=1)
    qkv_scr[...] = dot_nn(na_ref[...], w) + bias_ref[0]
    dattn_scr[...] = dot_nn(cot_ref[...], w_vo).astype(BF16)

    low = lax.broadcasted_iota(jnp.int32, (length, 2 * HD), 1) < HD
    keep, ahead, behind = keep_ref[...], ahead_ref[...], behind_ref[...]
    none = jnp.zeros((length, 2 * HD), BF16)
    blocks = length // NEAR
    for i in range(heads):
        qk = qkv_scr[:, i * HEAD : i * HEAD + 2 * HD]
        qk = qk * keep + pltpu.roll(qk, 2 * HD - ROT // 2, 1) * ahead + pltpu.roll(qk, ROT // 2, 1) * behind
        q32 = jnp.where(low, qk * (1.0 / math.sqrt(HD)), 0.0)
        k32 = jnp.where(low, pltpu.roll(qk, HD, 1), 0.0)
        v32 = jnp.where(low, 0.0, pltpu.roll(qkv_scr[:, i * HEAD + 2 * HD : (i + 1) * HEAD], HD, 1))
        q0 = q32.astype(BF16)
        k0 = k32.astype(BF16)
        v1 = v32.astype(BF16)
        go = dattn_scr[:, i * 2 * HD : (i + 1) * 2 * HD]
        go1 = jnp.where(low, none, go)
        qT = q32.T[:HD].astype(BF16)
        goT = go.astype(F32).T[HD:].astype(BF16)
        dq_parts = []
        mix_parts = []
        dk_sum = [None] * blocks
        dv_sum = [None] * blocks
        for b in range(blocks):
            r0, r1 = b * NEAR, (b + 1) * NEAR
            lo = max(0, r0 - LONGEST)
            s = dot_nt(q0[r0:r1], k0[lo:r1]) + bias_scr[r0:r1, lo:r1]
            e = jnp.exp(s - jnp.max(s, axis=1, keepdims=True))
            p = e * (1.0 / jnp.sum(e, axis=1, keepdims=True))
            p_low = p.astype(BF16)
            mix = dot_nn(p_low, v1[lo:r1])
            mix_parts.append(mix.astype(BF16))
            dp = dot_nt(go1[r0:r1], v1[lo:r1])
            delta = jnp.sum(mix * go1[r0:r1].astype(F32), axis=1, keepdims=True)
            ds = (p * (dp - delta)).astype(BF16)
            dq_parts.append(dot_nn(ds, k0[lo:r1]))
            dkT = dot_nn(qT[:, r0:r1], ds)
            dvT = dot_nn(goT[:, r0:r1], p_low)
            for n in range(lo // NEAR, b + 1):
                at = n * NEAR - lo
                dk_one, dv_one = dkT[:, at : at + NEAR], dvT[:, at : at + NEAR]
                dk_sum[n] = dk_one if dk_sum[n] is None else dk_sum[n] + dk_one
                dv_sum[n] = dv_one if dv_sum[n] is None else dv_sum[n] + dv_one
        dvk = jnp.concatenate(
            [jnp.concatenate([jnp.concatenate(dv_sum, axis=1), jnp.concatenate(dk_sum, axis=1)], axis=0)], axis=0
        ).T
        dqk = jnp.where(low, jnp.concatenate(dq_parts, axis=0) * (1.0 / math.sqrt(HD)), dvk)
        dqk = dqk * keep - pltpu.roll(dqk, 2 * HD - ROT // 2, 1) * ahead - pltpu.roll(dqk, ROT // 2, 1) * behind
        dqkv_scr[:, i * HEAD : i * HEAD + 2 * HD] = dqk.astype(BF16)
        dqkv_scr[:, i * HEAD + 2 * HD : (i + 1) * HEAD] = jnp.where(low, dvk, 0.0).astype(BF16)
        mix_scr[:, i * 2 * HD : (i + 1) * 2 * HD] = jnp.concatenate(mix_parts, axis=0)

    dqkv = dqkv_scr[...]
    mix = mix_scr[...]
    branch_ref[...] += dot_nt(mix, w_vo)
    dna_ref[...] += dot_nt(dqkv, w)
    dbias_ref[0] = jnp.sum(dqkv.astype(F32), axis=0, keepdims=True)
    for i in range(heads):
        g_qk = dot_nn(naT_ref[...], dqkv[:, i * HEAD : i * HEAD + 2 * HD])
        g_vo = dot_nn(naT_ref[...], dqkv[:, i * HEAD + 2 * HD : (i + 1) * HEAD]) + dot_nn(
            cotT_ref[...], mix[:, i * 2 * HD : (i + 1) * 2 * HD]
        )
        both = jnp.concatenate([g_qk, g_vo], axis=1).astype(BF16)
        g_ref[..., i * HEAD : (i + 1) * HEAD] = both.reshape(g_ref.shape[:-1] + (HEAD,))


def attention_part(norm_attn, norm_attn_t, cot, cot_t, w_all, bias, tables, seg_row):
    length, width = norm_attn.shape
    row_size, col_size, rows, block_cols = w_all.shape
    heads = block_cols // HEAD
    whole = lambda *shape: pl.BlockSpec(shape, lambda c: (0,) * len(shape))
    w_spec = pl.BlockSpec((row_size, 1, rows, block_cols), lambda c: (0, c, 0, 0))
    vec_spec = pl.BlockSpec((1, 1, block_cols), lambda c: (c, 0, 0))
    flops = col_size * 2 * length * width * block_cols * 5
    return pl.pallas_call(
        attention_kernel,
        grid=(col_size,),
        in_specs=[
            whole(length, width), whole(width, length), whole(length, width), whole(width, length),
            w_spec, vec_spec,
            whole(length, 2 * HD), whole(length, 2 * HD), whole(length, 2 * HD),
            whole(length, 1), whole(1, length),
        ],
        out_specs=[whole(length, width), whole(length, width), w_spec, vec_spec],
        out_shape=[
            jax.ShapeDtypeStruct((length, width), F32),
            jax.ShapeDtypeStruct((length, width), F32),
            jax.ShapeDtypeStruct(w_all.shape, BF16),
            jax.ShapeDtypeStruct((col_size, 1, block_cols), F32),
        ],
        scratch_shapes=[
            pltpu.VMEM((length, length), F32),
            pltpu.VMEM((length, block_cols), F32),
            pltpu.VMEM((length, heads * 2 * HD), BF16),
            pltpu.VMEM((length, block_cols), BF16),
            pltpu.VMEM((length, heads * 2 * HD), BF16),
        ],
        compiler_params=pltpu.CompilerParams(vmem_limit_bytes=48 * 2**20),
        cost_estimate=pl.CostEstimate(flops=flops, bytes_accessed=20 * 2**20, transcendentals=0),
    )(norm_attn, norm_attn_t, cot, cot_t, w_all, bias, *tables, seg_row[:, None], seg_row[None, :])


def mlp_kernel(pieces, me_ref, nm_ref, nmT_ref, cot_ref, cotT_ref, *rest):
    up_refs, down_refs = rest[:pieces], rest[pieces : 2 * pieces]
    bias_ref, branch_ref, dnm_ref, dbias_ref = rest[2 * pieces : 2 * pieces + 4]
    gu_refs = rest[2 * pieces + 4 : 3 * pieces + 4]
    gd_refs = rest[3 * pieces + 4 : 4 * pieces + 4]
    wu_scr, wd_scr, act_scr, dh_scr, g_scr = rest[4 * pieces + 4 :]
    length, width = nm_ref.shape
    step = pl.program_id(0)
    tile = 256

    @pl.when(step == 0)
    def _():
        branch_ref[...] = jnp.zeros_like(branch_ref)
        dnm_ref[...] = jnp.zeros_like(dnm_ref)

    assemble(me_ref, up_refs, wu_scr)
    assemble(me_ref, down_refs, wd_scr)
    dbias_ref[0] = jnp.zeros_like(dbias_ref[0])

    @pl.loop(0, length // tile)
    def _(t):
        rows = pl.ds(pl.multiple_of(t * tile, tile), tile)
        hidden = dot_nn(nm_ref[rows, :], wu_scr[...]) + bias_ref[0]
        d_act = dot_nn(cot_ref[rows, :], wd_scr[...])
        gate = 0.5 * (1.0 + lax.erf(hidden * (1.0 / math.sqrt(2.0))))
        act = (hidden * gate).astype(BF16)
        slope = gate + hidden * jnp.exp(-0.5 * hidden * hidden) * (1.0 / math.sqrt(2.0 * math.pi))
        dh = (d_act * slope).astype(BF16)
        act_scr[rows, :] = act
        dh_scr[rows, :] = dh
        dbias_ref[0] += jnp.sum(dh.astype(F32), axis=0, keepdims=True)
        branch_ref[rows, :] += dot_nt(act, wd_scr[...])
        dnm_ref[rows, :] += dot_nt(dh, wu_scr[...])

    for left, right, outs in ((nmT_ref, dh_scr, gu_refs), (cotT_ref, act_scr, gd_refs)):

        @pl.loop(0, width // tile)
        def _(t):
            rows = pl.ds(pl.multiple_of(t * tile, tile), tile)
            g_scr[rows, :] = dot_nn(left[rows, :], right[...]).astype(BF16)

        hand_out(me_ref, g_scr, outs)


def mlp_part(me, norm_mlp, norm_mlp_t, cot, cot_t, up_pieces, down_pieces, bias):
    length, width = norm_mlp.shape
    col_size, rows, block_cols = up_pieces[0].shape
    pieces = len(up_pieces)
    whole = lambda *shape: pl.BlockSpec(shape, lambda c: (0,) * len(shape))
    piece_spec = pl.BlockSpec((1, rows, block_cols), lambda c: (c, 0, 0))
    vec_spec = pl.BlockSpec((1, 1, block_cols), lambda c: (c, 0, 0))
    flops = col_size * 2 * length * width * block_cols * 6
    outs = pl.pallas_call(
        functools.partial(mlp_kernel, pieces),
        grid=(col_size,),
        in_specs=[
            pl.BlockSpec(memory_space=pltpu.SMEM),
            whole(length, width), whole(width, length), whole(length, width), whole(width, length),
        ]
        + [piece_spec] * (2 * pieces)
        + [vec_spec],
        out_specs=[whole(length, width), whole(length, width), vec_spec] + [piece_spec] * (2 * pieces),
        out_shape=[
            jax.ShapeDtypeStruct((length, width), F32),
            jax.ShapeDtypeStruct((length, width), F32),
            jax.ShapeDtypeStruct((col_size, 1, block_cols), F32),
        ]
        + [jax.ShapeDtypeStruct((col_size, rows, block_cols), BF16)] * (2 * pieces),
        scratch_shapes=[
            pltpu.VMEM((width, block_cols), BF16),
            pltpu.VMEM((width, block_cols), BF16),
            pltpu.VMEM((length, block_cols), BF16),
            pltpu.VMEM((length, block_cols), BF16),
            pltpu.VMEM((width, block_cols), BF16),
        ],
        compiler_params=pltpu.CompilerParams(vmem_limit_bytes=48 * 2**20),
        cost_estimate=pl.CostEstimate(flops=flops, bytes_accessed=30 * 2**20, transcendentals=0),
    )(me, norm_mlp, norm_mlp_t, cot, cot_t, *up_pieces, *down_pieces, bias)
    return outs[0], outs[1], outs[2], outs[3 : 3 + pieces], outs[3 + pieces :]


def swap(value, bit):
    axis, flip = ("dp", 1) if bit == 1 else ("row", bit // 2)
    size = lax.axis_size(axis)
    return lax.ppermute(value, axis, [(i, i ^ flip) for i in range(size)])


def gather_pieces(own, order):
    pieces = {0: own}
    for bit in order:
        for j in list(pieces):
            pieces[j ^ bit] = swap(pieces[j], bit)
    return [pieces[j] for j in range(len(pieces))]


def scatter_pieces(pieces, order):
    pieces = dict(enumerate(pieces))
    for bit in order:
        for j in [j for j in pieces if j & bit]:
            came = swap(pieces.pop(j), bit)
            kept = pieces[j ^ bit]
            pieces[j ^ bit] = (kept.astype(F32) + came.astype(F32)).astype(BF16)
    return pieces[0]


def sum_other_pairs(value):
    flip = 2
    while flip < lax.axis_size("dp"):
        value = value + lax.ppermute(value, "dp", [(i, i ^ flip) for i in range(lax.axis_size("dp"))])
        flip *= 2
    return value


def on_device(
    tokens_in,
    segment_ids,
    attn_gain,
    attn_shift,
    mlp_gain,
    mlp_shift,
    qkv_weight,
    qkv_bias,
    out_weight,
    out_bias,
    up_weight,
    up_bias,
    down_weight,
    down_bias,
    out_cotangent,
):
    row_size = lax.axis_size("row")
    col_size = lax.axis_size("col")
    length, width = tokens_in.shape
    rows = qkv_weight.shape[0]
    half_rows = rows // 2
    local_heads = qkv_weight.shape[1] // QKV
    block_cols = local_heads * HEAD
    up_cols = up_weight.shape[1]
    row_id = lax.axis_index("row")
    col_id = lax.axis_index("col")
    half = lax.axis_index("dp") % 2
    me = row_id * 2 + half
    row_bits = [2 << i for i in range(row_size.bit_length() - 1)]
    far_bits = row_bits[1:][::-1]

    head_weight = jnp.concatenate(
        [qkv_weight.reshape(rows, local_heads, QKV), out_weight.T.reshape(rows, local_heads, HD)], axis=2
    ).reshape(rows, block_cols)
    w_attn = lax.all_gather(head_weight, ("row", "col"), axis=0, tiled=False)
    w_attn = w_attn.reshape(row_size, col_size, rows, block_cols)
    up_half = lax.dynamic_slice_in_dim(up_weight, half * half_rows, half_rows, axis=0)
    down_half = lax.dynamic_slice_in_dim(down_weight, half * half_rows, half_rows, axis=1).T
    up_own = lax.all_gather(up_half, "col", axis=0, tiled=False)
    down_own = lax.all_gather(down_half, "col", axis=0, tiled=False)
    up_pieces = gather_pieces(up_own, [1] + far_bits + row_bits[:1])
    down_pieces = gather_pieces(down_own, far_bits + [1] + row_bits[:1])

    x_float = tokens_in.astype(F32)
    grad_float = out_cotangent.astype(F32)
    center = x_float - jnp.mean(x_float, axis=1, keepdims=True)
    inv_std = lax.rsqrt(jnp.mean(center * center, axis=1, keepdims=True) + EPSILON)
    normed = center * inv_std
    norm_attn = (normed * attn_gain + attn_shift).astype(BF16)
    norm_mlp = (normed * mlp_gain + mlp_shift).astype(BF16)
    cot_t = out_cotangent.T
    seg_row = lax.dynamic_index_in_dim(segment_ids, row_id * col_size + col_id, axis=0, keepdims=False)
    tables = rotary_tables(seg_row)
    head_bias = jnp.pad(
        qkv_bias.reshape(col_size, local_heads, QKV), ((0, 0), (0, 0), (0, HEAD - QKV))
    ).reshape(col_size, 1, block_cols)

    attn_branch, d_norm_attn, g_attn, d_bias_attn = attention_part(
        norm_attn, norm_attn.T, out_cotangent, cot_t, w_attn, head_bias, tables, seg_row
    )
    g_attn = lax.psum_scatter(
        g_attn.reshape(row_size * col_size * rows, block_cols), ("row", "col"), scatter_dimension=0, tiled=True
    )
    g_attn = lax.psum(g_attn, "dp").astype(F32)

    mlp_branch, d_norm_mlp, d_bias_up, g_up, g_down = mlp_part(
        me.reshape(1).astype(jnp.int32), norm_mlp, norm_mlp.T, out_cotangent, cot_t, up_pieces, down_pieces,
        up_bias.reshape(col_size, 1, up_cols),
    )
    g_up = scatter_pieces(g_up, row_bits[:1] + far_bits + [1])
    g_down = scatter_pieces(g_down, row_bits[:1] + [1] + far_bits)
    g_mlp = lax.psum_scatter(
        jnp.concatenate([g_up, g_down], axis=2).reshape(col_size * half_rows, 2 * up_cols),
        "col", scatter_dimension=0, tiled=True,
    )
    g_mlp = sum_other_pairs(g_mlp.astype(F32)).astype(BF16)
    g_other = swap(g_mlp, 1)
    g_mlp = jnp.where(
        half == 0, jnp.concatenate([g_mlp, g_other], axis=0), jnp.concatenate([g_other, g_mlp], axis=0)
    ).astype(F32)

    block_out = (x_float + (attn_branch + mlp_branch) + out_bias + down_bias).astype(BF16)
    d_normed = d_norm_attn * attn_gain + d_norm_mlp * mlp_gain
    in_grad = (
        grad_float
        + inv_std
        * (
            d_normed
            - jnp.mean(d_normed, axis=1, keepdims=True)
            - normed * jnp.mean(d_normed * normed, axis=1, keepdims=True)
        )
    ).astype(BF16)
    smalls = jnp.concatenate(
        [
            jnp.sum(grad_float, axis=0),
            jnp.sum(d_norm_attn * normed, axis=0),
            jnp.sum(d_norm_attn, axis=0),
            jnp.sum(d_norm_mlp * normed, axis=0),
            jnp.sum(d_norm_mlp, axis=0),
            d_bias_up.reshape(-1),
            d_bias_attn.reshape(col_size * local_heads, HEAD)[:, :QKV].reshape(-1),
        ]
    ).astype(BF16)
    smalls = jnp.sum(
        lax.all_gather(smalls, ("dp", "row", "col"), axis=0, tiled=False).astype(F32), axis=0
    )
    stats = smalls[: 5 * width].reshape(5, width)
    grad_up_bias = smalls[5 * width : 5 * width + up_bias.shape[0]]
    grad_qkv_bias = smalls[5 * width + up_bias.shape[0] :]
    g_heads = g_attn.reshape(rows, local_heads, HEAD)
    return (
        block_out,
        in_grad,
        stats[1],
        stats[2],
        stats[3],
        stats[4],
        g_heads[:, :, :QKV].reshape(rows, local_heads * QKV),
        grad_qkv_bias,
        g_heads[:, :, QKV:].reshape(rows, local_heads * HD).T,
        stats[0],
        g_mlp[:, :up_cols],
        grad_up_bias,
        g_mlp[:, up_cols:].T,
        stats[0],
    )


def solution(mesh):
    return jax.shard_map(
        on_device,
        mesh=mesh,
        in_specs=(
            P(("dp", "row", "col"), None),
            P("dp", None),
            P(),
            P(),
            P(),
            P(),
            P("row", "col"),
            P(),
            P("col", "row"),
            P(),
            P("row", "col"),
            P(),
            P("col", "row"),
            P(),
            P(("dp", "row", "col"), None),
        ),
        out_specs=(
            P(("dp", "row", "col"), None),
            P(("dp", "row", "col"), None),
            P(),
            P(),
            P(),
            P(),
            P("row", "col"),
            P(),
            P("col", "row"),
            P(),
            P("row", "col"),
            P(),
            P("col", "row"),
            P(),
        ),
        check_vma=False,
    )
```

```python
import functools
import math

import jax
import jax.numpy as jnp
from jax import lax
from jax.experimental import pallas as pl
from jax.experimental.pallas import tpu as pltpu
from jax.sharding import PartitionSpec as P

HD = 64
ROT = 16
QKV = 3 * HD
HEAD = 4 * HD
EPSILON = 1e-05
ROPE_BASE = 10000.0
NEAR = 128
LONGEST = 256
F32 = jnp.float32
BF16 = jnp.bfloat16


def dot_nn(a, b):
    return lax.dot_general(a, b, (((1,), (0,)), ((), ())), preferred_element_type=F32)


def dot_nt(a, b):
    return lax.dot_general(a, b, (((1,), (1,)), ((), ())), preferred_element_type=F32)


def piece_order(order):
    firsts = [0]
    for bit in order[::-1]:
        firsts = firsts + [j | bit for j in firsts]
    return firsts


def assemble(me_ref, w_refs, w_scr, at_col):
    _, rows, cols = w_refs[0].shape
    for j, ref in enumerate(w_refs):
        at = pl.multiple_of((me_ref[0] ^ j) * rows, 16)
        w_scr[pl.ds(at, rows), at_col : at_col + cols] = ref[0]


def hand_out(me_ref, g_scr, at_col, keep_ref, send_ref, order, core_bit):
    _, _, rows, cols = keep_ref.shape
    for t, j in enumerate(piece_order(order)):
        for ref, piece in ((keep_ref, j), (send_ref, j | core_bit)):
            at = pl.multiple_of((me_ref[0] ^ piece) * rows, 16)
            ref[t, 0] = g_scr[pl.ds(at, rows), at_col : at_col + cols]


def normalize(x):
    center = x - jnp.mean(x, axis=1, keepdims=True)
    inv_std = lax.rsqrt(jnp.mean(center * center, axis=1, keepdims=True) + EPSILON)
    return center * inv_std, inv_std


def prep_kernel(
    x_ref, cot_ref, ga_ref, sa_ref, gm_ref, sm_ref, segc_ref, segr_ref, freq_ref, _up_in, _down_in,
    na_ref, naT_ref, nm_ref, nmT_ref, cotT_ref, keep_ref, ahead_ref, behind_ref, mask_ref, _up_out, _down_out,
):
    length = x_ref.shape[0]
    tile = 128

    @pl.loop(0, length // tile)
    def _(t):
        rows = pl.ds(pl.multiple_of(t * tile, tile), tile)
        normed, _ = normalize(x_ref[rows, :].astype(F32))
        na_ref[rows, :] = (normed * ga_ref[...] + sa_ref[...]).astype(BF16)
        nm_ref[rows, :] = (normed * gm_ref[...] + sm_ref[...]).astype(BF16)
        same = segc_ref[rows, :] == segr_ref[...]
        cols = lax.broadcasted_iota(jnp.int32, (tile, length), 1)
        ids = lax.broadcasted_iota(jnp.int32, (tile, length), 0) + t * tile
        mask_ref[rows, :] = jnp.where(same & (cols <= ids), 0.0, -jnp.inf)
        starts = jnp.min(jnp.where(same, cols, length).astype(F32), axis=1, keepdims=True)
        places = ids[:, :1].astype(F32) - starts
        angles = places * freq_ref[...]
        lane = lax.broadcasted_iota(jnp.int32, (tile, 2 * HD), 1) % HD
        cosine, sine = jnp.cos(angles), jnp.sin(angles)
        keep_ref[rows, :] = jnp.where(lane < ROT, cosine, 1.0)
        ahead_ref[rows, :] = jnp.where(lane < ROT // 2, -sine, 0.0)
        behind_ref[rows, :] = jnp.where((lane < ROT) & (lane >= ROT // 2), sine, 0.0)

    naT_ref[...] = na_ref[...].T
    nmT_ref[...] = nm_ref[...].T
    cotT_ref[...] = cot_ref[...].T


def full(*shape):
    return pl.BlockSpec(shape, lambda *_: (0,) * len(shape))


ANY = pl.BlockSpec(memory_space=pl.ANY)
SCALAR = pl.BlockSpec(memory_space=pltpu.SMEM)


def cost(us):
    return pl.CostEstimate(flops=int(us * 1.15e9), bytes_accessed=2**20, transcendentals=0)


def shaped(shape, dtype):
    return jax.ShapeDtypeStruct(shape, dtype)


def prep_part(tokens, cot, gains, seg_row, up0, down0):
    length, width = tokens.shape
    halves = ROT // 2
    step = (lax.iota(jnp.int32, 2 * HD) % HD % halves).astype(F32)
    freq = (ROPE_BASE ** (-(step * (2.0 / ROT))))[None, :]
    table = shaped((length, 2 * HD), F32)
    return pl.pallas_call(
        prep_kernel,
        grid=(1,),
        in_specs=[full(length, width)] * 2 + [full(1, width)] * 4
        + [full(length, 1), full(1, length), full(1, 2 * HD), ANY, ANY],
        out_specs=[full(length, width), full(width, length)] * 2 + [full(width, length)]
        + [full(length, 2 * HD)] * 3 + [full(length, length), ANY, ANY],
        out_shape=[shaped((length, width), BF16), shaped((width, length), BF16)] * 2
        + [shaped((width, length), BF16)] + [table] * 3 + [shaped((length, length), F32)]
        + [shaped(up0.shape, BF16), shaped(down0.shape, BF16)],
        input_output_aliases={9: 9, 10: 10},
        compiler_params=pltpu.CompilerParams(vmem_limit_bytes=48 * 2**20),
        cost_estimate=cost(6),
    )(tokens, cot, *gains, seg_row[:, None], seg_row[None, :], freq, up0, down0)


def attention_kernel(orders, core_bit, waits, me_ref, na_ref, naT_ref, cot_ref, cotT_ref, *rest):
    pieces = (len(rest) - 16 - waits) // 2
    left, right = rest[:pieces], rest[pieces : 2 * pieces]
    bias_ref, keep_ref, ahead_ref, behind_ref, mask_ref = rest[2 * pieces : 2 * pieces + 5]
    dqkv_ref, mix_ref, dbias_ref, lk_ref, ls_ref, rk_ref, rs_ref = rest[2 * pieces + 5 + waits : 2 * pieces + 12 + waits]
    w_scr, qkv_scr, dattn_scr, g_scr = rest[2 * pieces + 12 + waits : 2 * pieces + 16 + waits]
    length, width = na_ref.shape
    block_cols = w_scr.shape[1]
    heads = block_cols // HEAD
    assemble(me_ref, left, w_scr, 0)
    assemble(me_ref, right, w_scr, block_cols // 2)

    w_vo = jnp.concatenate([w_scr[:, i * HEAD + 2 * HD : (i + 1) * HEAD] for i in range(heads)], axis=1)
    qkv_scr[...] = dot_nn(na_ref[...], w_scr[...]) + bias_ref[0]
    dattn_scr[...] = dot_nn(cot_ref[...], w_vo).astype(BF16)

    low = lax.broadcasted_iota(jnp.int32, (length, 2 * HD), 1) < HD
    keep, ahead, behind = keep_ref[...], ahead_ref[...], behind_ref[...]
    none = jnp.zeros((length, 2 * HD), BF16)
    blocks = length // NEAR
    for i in range(heads):
        qk = qkv_scr[:, i * HEAD : i * HEAD + 2 * HD]
        qk = qk * keep + pltpu.roll(qk, 2 * HD - ROT // 2, 1) * ahead + pltpu.roll(qk, ROT // 2, 1) * behind
        q32 = jnp.where(low, qk * (1.0 / math.sqrt(HD)), 0.0)
        k32 = jnp.where(low, pltpu.roll(qk, HD, 1), 0.0)
        v32 = jnp.where(low, 0.0, pltpu.roll(qkv_scr[:, i * HEAD + 2 * HD : (i + 1) * HEAD], HD, 1))
        q0 = q32.astype(BF16)
        k0 = k32.astype(BF16)
        v1 = v32.astype(BF16)
        go = dattn_scr[:, i * 2 * HD : (i + 1) * 2 * HD]
        go1 = jnp.where(low, none, go)
        qT = q0.T[:HD]
        goT = go.T[HD:]
        dq_parts = []
        mix_parts = []
        dk_sum = [None] * blocks
        dv_sum = [None] * blocks
        for b in range(blocks):
            r0, r1 = b * NEAR, (b + 1) * NEAR
            lo = max(0, r0 - LONGEST)
            s = dot_nt(q0[r0:r1], k0[lo:r1]) + mask_ref[r0:r1, lo:r1]
            e = jnp.exp(s - jnp.max(s, axis=1, keepdims=True))
            p = e * (1.0 / jnp.sum(e, axis=1, keepdims=True))
            p_low = p.astype(BF16)
            mix = dot_nn(p_low, v1[lo:r1])
            mix_parts.append(mix.astype(BF16))
            dp = dot_nt(go1[r0:r1], v1[lo:r1])
            delta = jnp.sum(mix * go1[r0:r1].astype(F32), axis=1, keepdims=True)
            ds = (p * (dp - delta)).astype(BF16)
            dq_parts.append(dot_nn(ds, k0[lo:r1]))
            dkT = dot_nn(qT[:, r0:r1], ds)
            dvT = dot_nn(goT[:, r0:r1], p_low)
            for n in range(lo // NEAR, b + 1):
                at = n * NEAR - lo
                dk_one, dv_one = dkT[:, at : at + NEAR], dvT[:, at : at + NEAR]
                dk_sum[n] = dk_one if dk_sum[n] is None else dk_sum[n] + dk_one
                dv_sum[n] = dv_one if dv_sum[n] is None else dv_sum[n] + dv_one
        dvk = jnp.concatenate([jnp.concatenate(dv_sum, axis=1), jnp.concatenate(dk_sum, axis=1)], axis=0).T
        dqk = jnp.where(low, jnp.concatenate(dq_parts, axis=0) * (1.0 / math.sqrt(HD)), dvk)
        dqk = dqk * keep - pltpu.roll(dqk, 2 * HD - ROT // 2, 1) * ahead - pltpu.roll(dqk, ROT // 2, 1) * behind
        dqkv_ref[0, :, i * HEAD : i * HEAD + 2 * HD] = dqk.astype(BF16)
        dqkv_ref[0, :, i * HEAD + 2 * HD : (i + 1) * HEAD] = jnp.where(low, dvk, 0.0).astype(BF16)
        mix_ref[0, :, i * 2 * HD : (i + 1) * 2 * HD] = jnp.concatenate(mix_parts, axis=0)

    dqkv = dqkv_ref[0]
    mix = mix_ref[0]
    dbias_ref[0] = jnp.sum(dqkv.astype(F32), axis=0, keepdims=True)
    for i in range(heads):
        g_qk = dot_nn(naT_ref[...], dqkv[:, i * HEAD : i * HEAD + 2 * HD])
        g_vo = dot_nn(naT_ref[...], dqkv[:, i * HEAD + 2 * HD : (i + 1) * HEAD]) + dot_nn(
            cotT_ref[...], mix[:, i * 2 * HD : (i + 1) * 2 * HD]
        )
        g_scr[:, i * HEAD : (i + 1) * HEAD] = jnp.concatenate([g_qk, g_vo], axis=1).astype(BF16)
    hand_out(me_ref, g_scr, 0, lk_ref, ls_ref, orders[0], core_bit)
    hand_out(me_ref, g_scr, block_cols // 2, rk_ref, rs_ref, orders[1], core_bit)


def mlp_kernel(orders, core_bit, waits, me_ref, nm_ref, nmT_ref, cot_ref, cotT_ref, *rest):
    pieces = (len(rest) - 11 - waits) // 2
    left, right = rest[:pieces], rest[pieces : 2 * pieces]
    bias_ref = rest[2 * pieces]
    act_ref, dh_ref, dbias_ref, lk_ref, ls_ref, rk_ref, rs_ref = rest[2 * pieces + 1 + waits : 2 * pieces + 8 + waits]
    wu_scr, wd_scr, g_scr = rest[2 * pieces + 8 + waits : 2 * pieces + 11 + waits]
    length, width = nm_ref.shape
    tile = 256
    assemble(me_ref, left, wu_scr, 0)
    assemble(me_ref, right, wd_scr, 0)
    dbias_ref[0] = jnp.zeros_like(dbias_ref[0])

    @pl.loop(0, length // tile)
    def _(t):
        rows = pl.ds(pl.multiple_of(t * tile, tile), tile)
        hidden = dot_nn(nm_ref[rows, :], wu_scr[...]) + bias_ref[0]
        d_act = dot_nn(cot_ref[rows, :], wd_scr[...])
        gate = 0.5 * (1.0 + lax.erf(hidden * (1.0 / math.sqrt(2.0))))
        act_ref[0, rows, :] = (hidden * gate).astype(BF16)
        slope = gate + hidden * jnp.exp(-0.5 * hidden * hidden) * (1.0 / math.sqrt(2.0 * math.pi))
        dh = (d_act * slope).astype(BF16)
        dh_ref[0, rows, :] = dh
        dbias_ref[0] += jnp.sum(dh.astype(F32), axis=0, keepdims=True)

    sides = ((nmT_ref, dh_ref, lk_ref, ls_ref, orders[0]), (cotT_ref, act_ref, rk_ref, rs_ref, orders[1]))
    for lhs, rhs, keep, send, order in sides:

        @pl.loop(0, width // tile)
        def _(t):
            rows = pl.ds(pl.multiple_of(t * tile, tile), tile)
            g_scr[rows, :] = dot_nn(lhs[rows, :], rhs[0]).astype(BF16)

        hand_out(me_ref, g_scr, 0, keep, send, order, core_bit)


def block_part(kernel, k0, count, orders, core_bit, after, me, norm, norm_t, cot, cot_t, left, right, vectors, mid_cols,
               g_cols, scratch, us):
    length, width = norm.shape
    pieces = len(left)
    rows = left[0].shape[1]
    kept = pieces // 2
    cols = vectors[0].shape[-1]

    def piece_spec(array):
        return pl.BlockSpec((1,) + array.shape[1:], lambda s: (k0 + s, 0, 0))

    g_spec = pl.BlockSpec((kept, 1, rows, g_cols), lambda s: (0, s, 0, 0))
    return pl.pallas_call(
        functools.partial(kernel, orders, core_bit, len(after)),
        grid=(count,),
        in_specs=[SCALAR, full(length, width), full(width, length), full(length, width), full(width, length)]
        + [piece_spec(p) for p in left + right]
        + [pl.BlockSpec((1, 1, cols), lambda s: (k0 + s, 0, 0))]
        + [full(*v.shape) for v in vectors[1:]]
        + [ANY] * len(after),
        out_specs=[pl.BlockSpec((1, length, m), lambda s: (s, 0, 0)) for m in mid_cols]
        + [pl.BlockSpec((1, 1, cols), lambda s: (s, 0, 0))] + [g_spec] * 4,
        out_shape=[shaped((count, length, m), BF16) for m in mid_cols]
        + [shaped((count, 1, cols), F32)] + [shaped((kept, count, rows, g_cols), BF16)] * 4,
        scratch_shapes=scratch,
        compiler_params=pltpu.CompilerParams(vmem_limit_bytes=56 * 2**20),
        cost_estimate=cost(us * count),
    )(me, norm, norm_t, cot, cot_t, *left, *right, *vectors, *after)


def tail_kernel(first, last, pieces, waits, me_ref, *rest):
    attn_left, attn_right = rest[:pieces], rest[pieces : 2 * pieces]
    up, down = rest[2 * pieces : 3 * pieces], rest[3 * pieces : 4 * pieces]
    dqkv_ref, mix_ref, act_ref, dh_ref = rest[4 * pieces : 4 * pieces + 4]
    rest = rest[4 * pieces + 4 :]
    if not first:
        branch_in, dna_in, dnm_in = rest[:3]
        rest = rest[3:]
    if last:
        x_ref, cot_ref, ga_ref, gm_ref, bo_ref, bd_ref = rest[:6]
        rest = rest[6:]
    rest = rest[waits:]
    if last:
        block_ref, grad_ref, stats_ref = rest[:3]
        branch_ref, dna_ref, dnm_ref = rest[3:6]
        rest = rest[6:]
    else:
        branch_ref, dna_ref, dnm_ref = rest[:3]
        rest = rest[3:]
    wa_scr, wv_scr, wu_scr, wd_scr = rest
    length, width = branch_ref.shape
    block_cols = wa_scr.shape[1]
    step = pl.program_id(0)
    tile = 256

    @pl.when(step == 0)
    def _():
        if first:
            branch_ref[...] = jnp.zeros_like(branch_ref)
            dna_ref[...] = jnp.zeros_like(dna_ref)
            dnm_ref[...] = jnp.zeros_like(dnm_ref)
        else:
            branch_ref[...] = branch_in[...]
            dna_ref[...] = dna_in[...]
            dnm_ref[...] = dnm_in[...]

    assemble(me_ref, attn_left, wa_scr, 0)
    assemble(me_ref, attn_right, wa_scr, block_cols // 2)
    assemble(me_ref, up, wu_scr, 0)
    assemble(me_ref, down, wd_scr, 0)
    for i in range(block_cols // HEAD):
        wv_scr[:, i * 2 * HD : (i + 1) * 2 * HD] = wa_scr[:, i * HEAD + 2 * HD : (i + 1) * HEAD]

    @pl.loop(0, length // tile)
    def _(t):
        rows = pl.ds(pl.multiple_of(t * tile, tile), tile)
        branch_ref[rows, :] += dot_nt(mix_ref[0, rows, :], wv_scr[...]) + dot_nt(act_ref[0, rows, :], wd_scr[...])
        dna_ref[rows, :] += dot_nt(dqkv_ref[0, rows, :], wa_scr[...])
        dnm_ref[rows, :] += dot_nt(dh_ref[0, rows, :], wu_scr[...])

    if last:

        @pl.when(step == pl.num_programs(0) - 1)
        def _():
            stats_ref[...] = jnp.zeros_like(stats_ref)
            small = 128

            @pl.loop(0, length // small)
            def _(t):
                rows = pl.ds(pl.multiple_of(t * small, small), small)
                x = x_ref[rows, :].astype(F32)
                cot = cot_ref[rows, :].astype(F32)
                normed, inv_std = normalize(x)
                block_ref[rows, :] = (x + branch_ref[rows, :] + bo_ref[...] + bd_ref[...]).astype(BF16)
                dna, dnm = dna_ref[rows, :], dnm_ref[rows, :]
                d_normed = dna * ga_ref[...] + dnm * gm_ref[...]
                pulled = (
                    d_normed
                    - jnp.mean(d_normed, axis=1, keepdims=True)
                    - normed * jnp.mean(d_normed * normed, axis=1, keepdims=True)
                )
                grad_ref[rows, :] = (cot + inv_std * pulled).astype(BF16)
                for at, term in enumerate((cot, dna * normed, dna, dnm * normed, dnm)):
                    stats_ref[at : at + 1, :] += jnp.sum(term, axis=0, keepdims=True)


def tail_part(k0, count, after, me, weights, mids, sums, finals):
    length = mids[0].shape[1]
    pieces = len(weights[0])
    width = pieces * weights[0][0].shape[1]
    first, last = sums is None, finals is not None
    block_cols = mids[0].shape[2]
    up_cols = mids[2].shape[2]

    def piece_spec(array):
        return pl.BlockSpec((1,) + array.shape[1:], lambda s: (k0 + s, 0, 0))

    total = shaped((length, width), F32)
    out_specs, out_shape = [full(length, width)] * 3, [total] * 3
    scratch = [
        pltpu.VMEM((width, block_cols), BF16), pltpu.VMEM((width, block_cols // 2), BF16),
        pltpu.VMEM((width, up_cols), BF16), pltpu.VMEM((width, up_cols), BF16),
    ]
    if last:
        out_specs = [full(length, width)] * 2 + [full(8, width)]
        out_shape = [shaped((length, width), BF16)] * 2 + [shaped((8, width), F32)]
        scratch = [pltpu.VMEM((length, width), F32)] * 3 + scratch
    extra = ([] if first else list(sums)) + (list(finals) if last else [])
    return pl.pallas_call(
        functools.partial(tail_kernel, first, last, pieces, len(after)),
        grid=(count,),
        in_specs=[SCALAR] + [piece_spec(p) for group in weights for p in group]
        + [pl.BlockSpec((1, length, m.shape[2]), lambda s: (s, 0, 0)) for m in mids]
        + [full(*e.shape) for e in extra] + [ANY] * len(after),
        out_specs=out_specs,
        out_shape=out_shape,
        scratch_shapes=scratch,
        compiler_params=pltpu.CompilerParams(vmem_limit_bytes=56 * 2**20),
        cost_estimate=cost(4 * count),
    )(me, *[p for group in weights for p in group], *mids, *extra, *after)


def swap(value, bit):
    axis, flip = ("dp", 1) if bit == 1 else ("row", bit // 2)
    return flipped(value, axis, flip)


def flipped(value, axis, flip):
    return lax.ppermute(value, axis, [(i, i ^ flip) for i in range(lax.axis_size(axis))])


def shifted(value, by):
    size = lax.axis_size("col")
    return lax.ppermute(value, "col", [(i, (i + by) % size) for i in range(size)])


def gather_pieces(own, order):
    pieces = {0: own}
    for bit in order:
        for j in list(pieces):
            pieces[j ^ bit] = swap(pieces[j], bit)
    return [pieces[j] for j in range(len(pieces))]


def add(a, b):
    return (a.astype(F32) + b.astype(F32)).astype(BF16)


class Reduction:
    def __init__(self, keep, send, order, core_bit):
        self.keep, self.came, self.order = keep, swap(send, core_bit), list(order)
        self.steps = [self.came]
        for bit in self.order:
            half = self.keep.shape[0] // 2
            send = add(self.keep[half:], self.came[half:])
            self.keep = add(self.keep[:half], self.came[:half])
            self.came = swap(send, bit)
            self.steps.append(self.came)
        self.total = add(self.keep[0], self.came[0])


def all_sum(value):
    for axis in ("row", "dp", "col"):
        flip = 1
        while flip < lax.axis_size(axis):
            value = value + flipped(value, axis, flip)
            flip *= 2
    return value


def on_device(
    tokens_in,
    segment_ids,
    attn_gain,
    attn_shift,
    mlp_gain,
    mlp_shift,
    qkv_weight,
    qkv_bias,
    out_weight,
    out_bias,
    up_weight,
    up_bias,
    down_weight,
    down_bias,
    out_cotangent,
):
    row_size = lax.axis_size("row")
    col_size = lax.axis_size("col")
    length, width = tokens_in.shape
    rows = qkv_weight.shape[0]
    half_rows = rows // 2
    local_heads = qkv_weight.shape[1] // QKV
    block_cols = local_heads * HEAD
    up_cols = up_weight.shape[1]
    row_id = lax.axis_index("row")
    col_id = lax.axis_index("col")
    half = lax.axis_index("dp") % 2
    me = (row_id * 2 + half).reshape(1).astype(jnp.int32)
    row_bits = [2 << i for i in range(row_size.bit_length() - 1)]
    core_bit, far_bits = row_bits[0], row_bits[1:][::-1]
    orders = (far_bits + [1], [1] + far_bits)

    head_weight = jnp.concatenate(
        [qkv_weight.reshape(rows, local_heads, QKV), out_weight.T.reshape(rows, local_heads, HD)], axis=2
    ).reshape(rows, block_cols)
    attn_own = lax.dynamic_slice_in_dim(head_weight, half * half_rows, half_rows, axis=0)
    mlp_own = jnp.concatenate(
        [
            lax.dynamic_slice_in_dim(up_weight, half * half_rows, half_rows, axis=0),
            lax.dynamic_slice_in_dim(down_weight, half * half_rows, half_rows, axis=1).T,
        ],
        axis=1,
    )
    attn_all = jnp.stack([attn_own] + [shifted(attn_own, k) for k in range(1, col_size)])
    mlp_all = jnp.stack([mlp_own] + [shifted(mlp_own, k) for k in range(1, col_size)])
    cut = block_cols // 2
    attn_left = gather_pieces(attn_all[:, :, :cut], orders[0] + [core_bit])
    attn_right = gather_pieces(attn_all[:, :, cut:], orders[1] + [core_bit])

    seg_row = lax.dynamic_index_in_dim(segment_ids, row_id * col_size + col_id, axis=0, keepdims=False)
    na, na_t, nm, nm_t, cot_t, keep, ahead, behind, mask, up_own, down_own = prep_part(
        tokens_in, out_cotangent, [v[None, :] for v in (attn_gain, attn_shift, mlp_gain, mlp_shift)], seg_row,
        mlp_all[:, :, :up_cols], mlp_all[:, :, up_cols:],
    )
    up = gather_pieces(up_own, orders[0] + [core_bit])
    down = gather_pieces(down_own, orders[1] + [core_bit])

    blocks_here = (col_id - jnp.arange(col_size)) % col_size
    head_bias = jnp.pad(
        qkv_bias.reshape(col_size, local_heads, QKV), ((0, 0), (0, 0), (0, HEAD - QKV))
    ).reshape(col_size, 1, block_cols)
    head_bias = jnp.take(head_bias, blocks_here, axis=0)
    hidden_bias = jnp.take(up_bias.reshape(col_size, 1, up_cols), blocks_here, axis=0)

    per_call = 2 if col_size % 2 == 0 else 1
    attn_calls, mlp_calls, attn_sums, mlp_sums = [], [], [], []
    last = None
    for k0 in range(0, col_size, per_call):
        after = [] if last is None else [last, up[orders[0][0]], down[orders[1][0]]]
        outs = block_part(
            attention_kernel, k0, per_call, orders, core_bit, after, me, na, na_t, out_cotangent, cot_t,
            attn_left, attn_right, [head_bias, keep, ahead, behind, mask], [block_cols, block_cols // 2], cut,
            [
                pltpu.VMEM((width, block_cols), BF16), pltpu.VMEM((length, block_cols), F32),
                pltpu.VMEM((length, block_cols // 2), BF16), pltpu.VMEM((width, block_cols), BF16),
            ],
            11,
        )
        last = outs[2]
        attn_calls.append(outs[:3])
        attn_sums.append([
            Reduction(outs[3], outs[4], orders[0], core_bit), Reduction(outs[5], outs[6], orders[1], core_bit)
        ])
    for n, k0 in enumerate(range(0, col_size, per_call)):
        after = [last]
        if n == 0:
            after += [r.steps[0] for r in attn_sums[0]]
        else:
            after += [r.steps[0] for r in attn_sums[1]] + [r.steps[1] for r in attn_sums[0]]
        outs = block_part(
            mlp_kernel, k0, per_call, orders, core_bit, after, me, nm, nm_t, out_cotangent, cot_t,
            up, down, [hidden_bias], [up_cols, up_cols], up_cols,
            [
                pltpu.VMEM((width, up_cols), BF16), pltpu.VMEM((width, up_cols), BF16),
                pltpu.VMEM((width, up_cols), BF16),
            ],
            6,
        )
        last = outs[2]
        mlp_calls.append(outs[:3])
        mlp_sums.append([
            Reduction(outs[3], outs[4], orders[0], core_bit), Reduction(outs[5], outs[6], orders[1], core_bit)
        ])

    sums, weights = None, (attn_left, attn_right, up, down)
    for n, k0 in enumerate(range(0, col_size, per_call)):
        finals = None
        after = [last]
        if k0 + per_call == col_size:
            finals = (
                tokens_in, out_cotangent, attn_gain[None, :], mlp_gain[None, :], out_bias[None, :], down_bias[None, :]
            )
            after += [r.steps[0] for r in mlp_sums[-1]]
        mids = list(attn_calls[n][:2]) + list(mlp_calls[n][:2])
        sums = tail_part(k0, per_call, after, me, weights, mids, sums, finals)
    block_out, in_grad, stats = sums

    def settle(parts):
        total = None
        for n, pair in enumerate(parts):
            both = jnp.concatenate([r.total for r in pair], axis=2)
            for i in range(per_call):
                k = n * per_call + i
                term = (both[i] if k == 0 else shifted(both[i], -k)).astype(F32)
                total = term if total is None else total + term
        flip = 2
        while flip < lax.axis_size("dp"):
            total = total + flipped(total, "dp", flip)
            flip *= 2
        mine = total.astype(BF16)
        other = swap(mine, 1)
        first = half == 0
        return jnp.concatenate([jnp.where(first, mine, other), jnp.where(first, other, mine)], axis=0).astype(F32)

    g_heads = settle(attn_sums).reshape(rows, local_heads, HEAD)
    g_mlp = settle(mlp_sums)

    d_bias_up = jnp.take(jnp.concatenate([c[2] for c in mlp_calls]), blocks_here, axis=0)
    d_bias_attn = jnp.take(jnp.concatenate([c[2] for c in attn_calls]), blocks_here, axis=0)
    smalls = jnp.concatenate(
        [
            stats[:5].reshape(-1),
            d_bias_up.reshape(-1),
            d_bias_attn.reshape(col_size * local_heads, HEAD)[:, :QKV].reshape(-1),
        ]
    )
    smalls = all_sum(smalls.reshape(-1, 128)).reshape(-1)
    stats = smalls[: 5 * width].reshape(5, width)
    grad_up_bias = smalls[5 * width : 5 * width + up_bias.shape[0]]
    grad_qkv_bias = smalls[5 * width + up_bias.shape[0] :]
    return (
        block_out,
        in_grad,
        stats[1],
        stats[2],
        stats[3],
        stats[4],
        g_heads[:, :, :QKV].reshape(rows, local_heads * QKV),
        grad_qkv_bias,
        g_heads[:, :, QKV:].reshape(rows, local_heads * HD).T,
        stats[0],
        g_mlp[:, :up_cols],
        grad_up_bias,
        g_mlp[:, up_cols:].T,
        stats[0],
    )


def solution(mesh):
    return jax.shard_map(
        on_device,
        mesh=mesh,
        in_specs=(
            P(("dp", "row", "col"), None),
            P("dp", None),
            P(),
            P(),
            P(),
            P(),
            P("row", "col"),
            P(),
            P("col", "row"),
            P(),
            P("row", "col"),
            P(),
            P("col", "row"),
            P(),
            P(("dp", "row", "col"), None),
        ),
        out_specs=(
            P(("dp", "row", "col"), None),
            P(("dp", "row", "col"), None),
            P(),
            P(),
            P(),
            P(),
            P("row", "col"),
            P(),
            P("col", "row"),
            P(),
            P("row", "col"),
            P(),
            P("col", "row"),
            P(),
        ),
        check_vma=False,
    )
```

```python
import functools
import math

import jax
import jax.numpy as jnp
from jax import lax
from jax.experimental import pallas as pl
from jax.experimental.pallas import tpu as pltpu
from jax.sharding import PartitionSpec as P

HD = 64
ROT = 16
QKV = 3 * HD
HEAD = 4 * HD
EPSILON = 1e-05
ROPE_BASE = 10000.0
NEAR = 128
LONGEST = 256
F32 = jnp.float32
BF16 = jnp.bfloat16


def dot_nn(a, b):
    return lax.dot_general(a, b, (((1,), (0,)), ((), ())), preferred_element_type=F32)


def dot_nt(a, b):
    return lax.dot_general(a, b, (((1,), (1,)), ((), ())), preferred_element_type=F32)


def gathered_order(order, core_bit):
    held = [0]
    for bit in order[:-1]:
        held = held + [j | bit for j in held]
    came = [j | order[-1] for j in held]
    return held, came, [j | core_bit for j in held], [j | core_bit for j in came]


def reduced_order(order):
    kept = [0]
    for bit in order[::-1]:
        kept = kept + [j | bit for j in kept]
    return kept


def assemble(me_ref, w_refs, held, w_scr, at_col):
    for ref, pieces in zip(w_refs, held):
        _, _, rows, cols = ref.shape
        for t, j in enumerate(pieces):
            at = pl.multiple_of((me_ref[0] ^ j) * rows, 16)
            w_scr[pl.ds(at, rows), at_col : at_col + cols] = ref[t, 0]


def hand_out(me_ref, g_scr, at_col, keep_ref, send_ref, first, order, core_bit):
    _, _, rows, cols = keep_ref.shape
    for t, j in enumerate(reduced_order(order)):
        for ref, piece in ((keep_ref, j), (send_ref, j | core_bit)):
            at = pl.multiple_of((me_ref[0] ^ piece) * rows, 16)
            ref[first + t, 0] = g_scr[pl.ds(at, rows), at_col : at_col + cols]


def normalize(x):
    center = x - jnp.mean(x, axis=1, keepdims=True)
    inv_std = lax.rsqrt(jnp.mean(center * center, axis=1, keepdims=True) + EPSILON)
    return center * inv_std, inv_std


def prep_kernel(
    x_ref, cot_ref, ga_ref, sa_ref, gm_ref, sm_ref, segc_ref, segr_ref, freq_ref, _mlp_in, _after,
    na_ref, naT_ref, nm_ref, nmT_ref, cotT_ref, keep_ref, ahead_ref, behind_ref, mask_ref, _mlp_out,
):
    length = x_ref.shape[0]
    tile = 128

    @pl.loop(0, length // tile)
    def _(t):
        rows = pl.ds(pl.multiple_of(t * tile, tile), tile)
        normed, _ = normalize(x_ref[rows, :].astype(F32))
        na_ref[rows, :] = (normed * ga_ref[...] + sa_ref[...]).astype(BF16)
        nm_ref[rows, :] = (normed * gm_ref[...] + sm_ref[...]).astype(BF16)
        same = segc_ref[rows, :] == segr_ref[...]
        cols = lax.broadcasted_iota(jnp.int32, (tile, length), 1)
        ids = lax.broadcasted_iota(jnp.int32, (tile, length), 0) + t * tile
        mask_ref[rows, :] = jnp.where(same & (cols <= ids), 0.0, -jnp.inf)
        starts = jnp.min(jnp.where(same, cols, length).astype(F32), axis=1, keepdims=True)
        places = ids[:, :1].astype(F32) - starts
        angles = places * freq_ref[...]
        lane = lax.broadcasted_iota(jnp.int32, (tile, 2 * HD), 1) % HD
        cosine, sine = jnp.cos(angles), jnp.sin(angles)
        keep_ref[rows, :] = jnp.where(lane < ROT, cosine, 1.0)
        ahead_ref[rows, :] = jnp.where(lane < ROT // 2, -sine, 0.0)
        behind_ref[rows, :] = jnp.where((lane < ROT) & (lane >= ROT // 2), sine, 0.0)

    naT_ref[...] = na_ref[...].T
    nmT_ref[...] = nm_ref[...].T
    cotT_ref[...] = cot_ref[...].T


def full(*shape):
    return pl.BlockSpec(shape, lambda *_: (0,) * len(shape))


ANY = pl.BlockSpec(memory_space=pl.ANY)
SCALAR = pl.BlockSpec(memory_space=pltpu.SMEM)


def cost(us):
    return pl.CostEstimate(flops=int(us * 1.15e9), bytes_accessed=2**20, transcendentals=0)


def shaped(shape, dtype):
    return jax.ShapeDtypeStruct(shape, dtype)


def prep_part(tokens, cot, gains, seg_row, mlp_own, after):
    length, width = tokens.shape
    halves = ROT // 2
    step = (lax.iota(jnp.int32, 2 * HD) % HD % halves).astype(F32)
    freq = (ROPE_BASE ** (-(step * (2.0 / ROT))))[None, :]
    table = shaped((length, 2 * HD), F32)
    return pl.pallas_call(
        prep_kernel,
        grid=(1,),
        in_specs=[full(length, width)] * 2 + [full(1, width)] * 4
        + [full(length, 1), full(1, length), full(1, 2 * HD), ANY, ANY],
        out_specs=[full(length, width), full(width, length)] * 2 + [full(width, length)]
        + [full(length, 2 * HD)] * 3 + [full(length, length), ANY],
        out_shape=[shaped((length, width), BF16), shaped((width, length), BF16)] * 2
        + [shaped((width, length), BF16)] + [table] * 3 + [shaped((length, length), F32)]
        + [shaped(mlp_own.shape, BF16)],
        input_output_aliases={9: 9},
        compiler_params=pltpu.CompilerParams(vmem_limit_bytes=48 * 2**20),
        cost_estimate=cost(6),
    )(tokens, cot, *gains, seg_row[:, None], seg_row[None, :], freq, mlp_own, after)


def attention_kernel(orders, core_bit, waits, me_ref, na_ref, naT_ref, cot_ref, cotT_ref, *rest):
    left, right, rest = rest[:4], rest[4:8], rest[8:]
    bias_ref, keep_ref, ahead_ref, behind_ref, mask_ref = rest[:5]
    dqkv_ref, mix_ref, dbias_ref, gk_ref, gs_ref, w_scr, wv_scr, qkv_scr, dattn_scr, g_scr = rest[5 + waits :]
    length, width = na_ref.shape
    block_cols = w_scr.shape[1]
    heads = block_cols // HEAD
    kept = gk_ref.shape[0] // 2
    tile = 256
    assemble(me_ref, left, gathered_order(orders[0], core_bit), w_scr, 0)
    assemble(me_ref, right, gathered_order(orders[1], core_bit), w_scr, block_cols // 2)
    for i in range(heads):
        wv_scr[:, i * 2 * HD : (i + 1) * 2 * HD] = w_scr[:, i * HEAD + 2 * HD : (i + 1) * HEAD]

    @pl.loop(0, length // tile)
    def _(t):
        rows = pl.ds(pl.multiple_of(t * tile, tile), tile)
        qkv_scr[rows, :] = dot_nn(na_ref[rows, :], w_scr[...]) + bias_ref[0]
        dattn_scr[rows, :] = dot_nn(cot_ref[rows, :], wv_scr[...]).astype(BF16)

    low = lax.broadcasted_iota(jnp.int32, (length, 2 * HD), 1) < HD
    keep, ahead, behind = keep_ref[...], ahead_ref[...], behind_ref[...]
    none = jnp.zeros((length, 2 * HD), BF16)
    spans = [(b * NEAR, (b + 1) * NEAR, max(0, b * NEAR - LONGEST)) for b in range(length // NEAR)]
    for i in range(heads):
        qk = qkv_scr[:, i * HEAD : i * HEAD + 2 * HD]
        qk = qk * keep + pltpu.roll(qk, 2 * HD - ROT // 2, 1) * ahead + pltpu.roll(qk, ROT // 2, 1) * behind
        q0 = jnp.where(low, qk * (1.0 / math.sqrt(HD)), 0.0).astype(BF16)
        k0 = jnp.where(low, pltpu.roll(qk, HD, 1), 0.0).astype(BF16)
        v1 = jnp.where(low, 0.0, pltpu.roll(qkv_scr[:, i * HEAD + 2 * HD : (i + 1) * HEAD], HD, 1)).astype(BF16)
        go = dattn_scr[:, i * 2 * HD : (i + 1) * 2 * HD]
        go1 = jnp.where(low, none, go)
        qT = q0.T[:HD]
        goT = go.T[HD:]
        s = [dot_nt(q0[r0:r1], k0[lo:r1]) + mask_ref[r0:r1, lo:r1] for r0, r1, lo in spans]
        dp = [dot_nt(go1[r0:r1], v1[lo:r1]) for r0, r1, lo in spans]
        peak = [jnp.max(one, axis=1, keepdims=True) for one in s]
        e = [jnp.exp(one - top) for one, top in zip(s, peak)]
        norm = [1.0 / jnp.sum(one, axis=1, keepdims=True) for one in e]
        p = [one * scale for one, scale in zip(e, norm)]
        p_low = [one.astype(BF16) for one in p]
        mix = [dot_nn(one, v1[lo:r1]) for one, (r0, r1, lo) in zip(p_low, spans)]
        delta = [
            jnp.sum(one * go1[r0:r1].astype(F32), axis=1, keepdims=True) for one, (r0, r1, lo) in zip(mix, spans)
        ]
        ds = [(one * (grad - centre)).astype(BF16) for one, grad, centre in zip(p, dp, delta)]
        dq = [dot_nn(one, k0[lo:r1]) for one, (r0, r1, lo) in zip(ds, spans)]
        dkT = [dot_nn(qT[:, r0:r1], one) for one, (r0, r1, lo) in zip(ds, spans)]
        dvT = [dot_nn(goT[:, r0:r1], one) for one, (r0, r1, lo) in zip(p_low, spans)]
        sums = []
        for parts in (dvT, dkT):
            total = [None] * len(spans)
            for part, (r0, r1, lo) in zip(parts, spans):
                for n in range(lo // NEAR, r1 // NEAR):
                    one = part[:, n * NEAR - lo : (n + 1) * NEAR - lo]
                    total[n] = one if total[n] is None else total[n] + one
            sums.append(jnp.concatenate(total, axis=1))
        dvk = jnp.concatenate(sums, axis=0).T
        dqk = jnp.where(low, jnp.concatenate(dq, axis=0) * (1.0 / math.sqrt(HD)), dvk)
        dqk = dqk * keep - pltpu.roll(dqk, 2 * HD - ROT // 2, 1) * ahead - pltpu.roll(dqk, ROT // 2, 1) * behind
        dqkv_ref[0, :, i * HEAD : i * HEAD + 2 * HD] = dqk.astype(BF16)
        dqkv_ref[0, :, i * HEAD + 2 * HD : (i + 1) * HEAD] = jnp.where(low, dvk, 0.0).astype(BF16)
        mix_ref[0, :, i * 2 * HD : (i + 1) * 2 * HD] = jnp.concatenate(mix, axis=0).astype(BF16)

    dbias_ref[0] = jnp.sum(dqkv_ref[0].astype(F32), axis=0, keepdims=True)

    @pl.loop(0, width // tile)
    def _(t):
        rows = pl.ds(pl.multiple_of(t * tile, tile), tile)
        g_in = dot_nn(naT_ref[rows, :], dqkv_ref[0])
        g_out = dot_nn(cotT_ref[rows, :], mix_ref[0])
        for i in range(heads):
            at = i * HEAD
            g_scr[rows, at : at + 2 * HD] = g_in[:, at : at + 2 * HD].astype(BF16)
            g_scr[rows, at + 2 * HD : at + HEAD] = (
                g_in[:, at + 2 * HD : at + HEAD] + g_out[:, i * 2 * HD : (i + 1) * 2 * HD]
            ).astype(BF16)

    hand_out(me_ref, g_scr, 0, gk_ref, gs_ref, 0, orders[0], core_bit)
    hand_out(me_ref, g_scr, block_cols // 2, gk_ref, gs_ref, kept, orders[1], core_bit)


def mlp_kernel(orders, core_bit, waits, me_ref, nm_ref, nmT_ref, cot_ref, cotT_ref, *rest):
    left, right, bias_ref, rest = rest[:4], rest[4:8], rest[8], rest[9 + waits :]
    act_ref, dh_ref, dbias_ref, gk_ref, gs_ref, wu_scr, wd_scr, g_scr = rest
    length, width = nm_ref.shape
    up_cols = wu_scr.shape[1]
    kept = gk_ref.shape[0] // 2
    tile = 256
    assemble(me_ref, left, gathered_order(orders[0], core_bit), wu_scr, 0)
    assemble(me_ref, right, gathered_order(orders[1], core_bit), wd_scr, 0)
    dbias_ref[0] = jnp.zeros_like(dbias_ref[0])

    @pl.loop(0, length // tile)
    def _(t):
        rows = pl.ds(pl.multiple_of(t * tile, tile), tile)
        for n in range(0, up_cols, tile):
            hidden = dot_nn(nm_ref[rows, :], wu_scr[:, n : n + tile]) + bias_ref[0, :, n : n + tile]
            d_act = dot_nn(cot_ref[rows, :], wd_scr[:, n : n + tile])
            gate = 0.5 * (1.0 + lax.erf(hidden * (1.0 / math.sqrt(2.0))))
            act_ref[0, rows, n : n + tile] = (hidden * gate).astype(BF16)
            slope = gate + hidden * jnp.exp(-0.5 * hidden * hidden) * (1.0 / math.sqrt(2.0 * math.pi))
            dh = (d_act * slope).astype(BF16)
            dh_ref[0, rows, n : n + tile] = dh
            dbias_ref[0, :, n : n + tile] += jnp.sum(dh.astype(F32), axis=0, keepdims=True)

    for side, lhs, rhs in ((0, nmT_ref, dh_ref), (1, cotT_ref, act_ref)):

        @pl.loop(0, width // tile)
        def _(t):
            rows = pl.ds(pl.multiple_of(t * tile, tile), tile)
            g_scr[rows, :] = dot_nn(lhs[rows, :], rhs[0]).astype(BF16)

        hand_out(me_ref, g_scr, 0, gk_ref, gs_ref, side * kept, orders[side], core_bit)


def weight_spec(array, block_of):
    count, _, rows, cols = array.shape
    return pl.BlockSpec((count, 1, rows, cols), lambda s: (0, block_of(s), 0, 0))


def block_part(kernel, k0, count, orders, core_bit, after, me, norm, norm_t, cot, cot_t, left, right, vectors, mid_cols,
               g_cols, scratch, us):
    length, width = norm.shape
    rows = left[0].shape[2]
    pieces = width // rows
    cols = vectors[0].shape[-1]
    g_spec = pl.BlockSpec((pieces, 1, rows, g_cols), lambda s: (0, s, 0, 0))
    return pl.pallas_call(
        functools.partial(kernel, orders, core_bit, len(after)),
        grid=(count,),
        in_specs=[SCALAR, full(length, width), full(width, length), full(length, width), full(width, length)]
        + [weight_spec(w, lambda s: k0 + s) for w in left + right]
        + [pl.BlockSpec((1, 1, cols), lambda s: (k0 + s, 0, 0))]
        + [full(*v.shape) for v in vectors[1:]]
        + [ANY] * len(after),
        out_specs=[pl.BlockSpec((1, length, m), lambda s: (s, 0, 0)) for m in mid_cols]
        + [pl.BlockSpec((1, 1, cols), lambda s: (s, 0, 0))] + [g_spec] * 2,
        out_shape=[shaped((count, length, m), BF16) for m in mid_cols]
        + [shaped((count, 1, cols), F32)] + [shaped((pieces, count, rows, g_cols), BF16)] * 2,
        scratch_shapes=scratch,
        compiler_params=pltpu.CompilerParams(vmem_limit_bytes=56 * 2**20),
        cost_estimate=cost(us * count),
    )(me, norm, norm_t, cot, cot_t, *left, *right, *vectors, *after)


def pick(refs, per_call, scr):
    for n, ref in enumerate(refs):

        @pl.when(pl.program_id(0) // per_call == n)
        def _():
            scr[...] = ref[0]


def attention_tail_kernel(orders, core_bit, calls, per_call, waits, me_ref, *rest):
    left, right, rest = rest[:4], rest[4:8], rest[8:]
    dqkv_refs, mix_refs, rest = rest[:calls], rest[calls : 2 * calls], rest[2 * calls + waits :]
    branch_ref, dna_ref, w_scr, wv_scr, dqkv_scr, mix_scr = rest
    block_cols = w_scr.shape[1]

    @pl.when(pl.program_id(0) == 0)
    def _():
        branch_ref[...] = jnp.zeros_like(branch_ref)
        dna_ref[...] = jnp.zeros_like(dna_ref)

    pick(dqkv_refs, per_call, dqkv_scr)
    pick(mix_refs, per_call, mix_scr)
    assemble(me_ref, left, gathered_order(orders[0], core_bit), w_scr, 0)
    assemble(me_ref, right, gathered_order(orders[1], core_bit), w_scr, block_cols // 2)
    for i in range(block_cols // HEAD):
        wv_scr[:, i * 2 * HD : (i + 1) * 2 * HD] = w_scr[:, i * HEAD + 2 * HD : (i + 1) * HEAD]
    tile = 256

    @pl.loop(0, branch_ref.shape[0] // tile)
    def _(t):
        rows = pl.ds(pl.multiple_of(t * tile, tile), tile)
        branch_ref[rows, :] += dot_nt(mix_scr[rows, :], wv_scr[...])
        dna_ref[rows, :] += dot_nt(dqkv_scr[rows, :], w_scr[...])


def mlp_tail_kernel(orders, core_bit, calls, per_call, waits, me_ref, *rest):
    left, right, rest = rest[:4], rest[4:8], rest[8:]
    dh_refs, act_refs, rest = rest[:calls], rest[calls : 2 * calls], rest[2 * calls :]
    branch_in, dna_ref, x_ref, cot_ref, ga_ref, gm_ref, bo_ref, bd_ref = rest[:8]
    block_ref, grad_ref, stats_ref, branch_ref, dnm_ref, wu_scr, wd_scr, dh_scr, act_scr = rest[8 + waits :]
    length = x_ref.shape[0]
    step = pl.program_id(0)

    @pl.when(step == 0)
    def _():
        branch_ref[...] = branch_in[...]
        dnm_ref[...] = jnp.zeros_like(dnm_ref)

    pick(dh_refs, per_call, dh_scr)
    pick(act_refs, per_call, act_scr)
    assemble(me_ref, left, gathered_order(orders[0], core_bit), wu_scr, 0)
    assemble(me_ref, right, gathered_order(orders[1], core_bit), wd_scr, 0)
    tile = 256

    @pl.loop(0, length // tile)
    def _(t):
        rows = pl.ds(pl.multiple_of(t * tile, tile), tile)
        branch_ref[rows, :] += dot_nt(act_scr[rows, :], wd_scr[...])
        dnm_ref[rows, :] += dot_nt(dh_scr[rows, :], wu_scr[...])

    @pl.when(step == pl.num_programs(0) - 1)
    def _():
        stats_ref[...] = jnp.zeros_like(stats_ref)
        small = 128

        @pl.loop(0, length // small)
        def _(t):
            rows = pl.ds(pl.multiple_of(t * small, small), small)
            x = x_ref[rows, :].astype(F32)
            cot = cot_ref[rows, :].astype(F32)
            normed, inv_std = normalize(x)
            block_ref[rows, :] = (x + branch_ref[rows, :] + bo_ref[...] + bd_ref[...]).astype(BF16)
            dna, dnm = dna_ref[rows, :], dnm_ref[rows, :]
            d_normed = dna * ga_ref[...] + dnm * gm_ref[...]
            pulled = (
                d_normed
                - jnp.mean(d_normed, axis=1, keepdims=True)
                - normed * jnp.mean(d_normed * normed, axis=1, keepdims=True)
            )
            grad_ref[rows, :] = (cot + inv_std * pulled).astype(BF16)
            for at, term in enumerate((cot, dna * normed, dna, dnm * normed, dnm)):
                stats_ref[at : at + 1, :] += jnp.sum(term, axis=0, keepdims=True)


def tail_part(kernel, block_of, per_call, orders, core_bit, after, me, left, right, mids, extra, outs, scratch, us):
    steps = left[0].shape[1]
    calls = steps // per_call

    def mid_spec(array, n):
        _, length, cols = array.shape
        return pl.BlockSpec((1, length, cols), lambda s: (jnp.clip(s - n * per_call, 0, per_call - 1), 0, 0))

    kept = [pltpu.VMEM(group[0].shape[1:], BF16) for group in mids]
    return pl.pallas_call(
        functools.partial(kernel, orders, core_bit, calls, per_call, len(after)),
        grid=(steps,),
        in_specs=[SCALAR] + [weight_spec(w, block_of) for w in left + right]
        + [mid_spec(array, n) for group in mids for n, array in enumerate(group)]
        + [full(*e.shape) for e in extra] + [ANY] * len(after),
        out_specs=[full(*o.shape) for o in outs],
        out_shape=outs,
        scratch_shapes=scratch + kept,
        compiler_params=pltpu.CompilerParams(vmem_limit_bytes=56 * 2**20),
        cost_estimate=cost(us),
    )(me, *left, *right, *[array for group in mids for array in group], *extra, *after)


def swap(value, bit):
    axis, flip = ("dp", 1) if bit == 1 else ("row", bit // 2)
    return flipped(value, axis, flip)


def flipped(value, axis, flip):
    return lax.ppermute(value, axis, [(i, i ^ flip) for i in range(lax.axis_size(axis))])


def shifted(value, by):
    size = lax.axis_size("col")
    return lax.ppermute(value, "col", [(i, (i + by) % size) for i in range(size)])


def gather_pieces(own, order, core_bit):
    held, steps = own[None], []
    for bit in order[:-1]:
        came = swap(held, bit)
        steps.append(came)
        held = jnp.concatenate([held, came], axis=0)
    came = swap(held, order[-1])
    steps.append(came)
    return [held, came, swap(held, core_bit), swap(came, core_bit)], steps


def add(a, b):
    return (a.astype(F32) + b.astype(F32)).astype(BF16)


def reduce_pieces(keep, send, orders, core_bit):
    came = swap(send, core_bit)
    steps = [[came]] + [[] for _ in orders[0]]
    size = keep.shape[0] // len(orders)
    totals = []
    for side, order in enumerate(orders):
        held, other = keep[side * size : (side + 1) * size], came[side * size : (side + 1) * size]
        for at, bit in enumerate(order):
            half = held.shape[0] // 2
            moved = swap(add(held[half:], other[half:]), bit)
            held, other = add(held[:half], other[:half]), moved
            steps[at + 1].append(moved)
        totals.append(add(held[0], other[0]))
    return jnp.concatenate(totals, axis=2), steps


def all_sum(value):
    for axis in ("row", "dp", "col"):
        flip = 1
        while flip < lax.axis_size(axis):
            value = value + flipped(value, axis, flip)
            flip *= 2
    return value


def on_device(
    tokens_in,
    segment_ids,
    attn_gain,
    attn_shift,
    mlp_gain,
    mlp_shift,
    qkv_weight,
    qkv_bias,
    out_weight,
    out_bias,
    up_weight,
    up_bias,
    down_weight,
    down_bias,
    out_cotangent,
):
    row_size = lax.axis_size("row")
    col_size = lax.axis_size("col")
    length, width = tokens_in.shape
    rows = qkv_weight.shape[0]
    half_rows = rows // 2
    local_heads = qkv_weight.shape[1] // QKV
    block_cols = local_heads * HEAD
    up_cols = up_weight.shape[1]
    row_id = lax.axis_index("row")
    col_id = lax.axis_index("col")
    half = lax.axis_index("dp") % 2
    me = (row_id * 2 + half).reshape(1).astype(jnp.int32)
    row_bits = [2 << i for i in range(row_size.bit_length() - 1)]
    core_bit, far_bits = row_bits[0], row_bits[1:][::-1]
    orders = (far_bits + [1], [1] + far_bits)

    head_weight = jnp.concatenate(
        [qkv_weight.reshape(rows, local_heads, QKV), out_weight.T.reshape(rows, local_heads, HD)], axis=2
    ).reshape(rows, block_cols)
    attn_own = lax.dynamic_slice_in_dim(head_weight, half * half_rows, half_rows, axis=0)
    mlp_own = jnp.concatenate(
        [
            lax.dynamic_slice_in_dim(up_weight, half * half_rows, half_rows, axis=0),
            lax.dynamic_slice_in_dim(down_weight, half * half_rows, half_rows, axis=1).T,
        ],
        axis=1,
    )
    def gather_col(own):
        return jnp.stack([own] + [shifted(own, k) for k in range(1, col_size)])

    attn_all = gather_col(attn_own)
    cut = block_cols // 2
    attn_left, _ = gather_pieces(attn_all[:, :, :cut], orders[0], core_bit)
    attn_right, _ = gather_pieces(attn_all[:, :, cut:], orders[1], core_bit)

    seg_row = lax.dynamic_index_in_dim(segment_ids, row_id * col_size + col_id, axis=0, keepdims=False)
    na, na_t, nm, nm_t, cot_t, keep, ahead, behind, mask, mlp_own = prep_part(
        tokens_in, out_cotangent, [v[None, :] for v in (attn_gain, attn_shift, mlp_gain, mlp_shift)], seg_row,
        mlp_own, attn_all,
    )
    mlp_all = gather_col(mlp_own)
    up, up_steps = gather_pieces(mlp_all[:, :, :up_cols], orders[0], core_bit)
    down, down_steps = gather_pieces(mlp_all[:, :, up_cols:], orders[1], core_bit)
    mlp_steps = [list(pair) for pair in zip(up_steps, down_steps)]

    blocks_here = (col_id - jnp.arange(col_size)) % col_size
    head_bias = jnp.pad(
        qkv_bias.reshape(col_size, local_heads, QKV), ((0, 0), (0, 0), (0, HEAD - QKV))
    ).reshape(col_size, 1, block_cols)
    head_bias = jnp.take(head_bias, blocks_here, axis=0)
    hidden_bias = jnp.take(up_bias.reshape(col_size, 1, up_cols), blocks_here, axis=0)

    per_call = 2
    calls = col_size // per_call
    starts = [k0 for k0 in range(0, col_size, per_call)][::-1]

    def block_of(s):
        return (calls - 1 - s // per_call) * per_call + s % per_call

    attn_calls, attn_sums, attn_steps = [], [], []
    last = []
    for n, k0 in enumerate(starts):
        after = last + ([mlp_all] if n == 0 else mlp_steps[0] if n == 1 else [])
        *mids, d_bias, g_keep, g_send = block_part(
            attention_kernel, k0, per_call, orders, core_bit, after, me, na, na_t, out_cotangent, cot_t,
            attn_left, attn_right, [head_bias, keep, ahead, behind, mask], [block_cols, cut], cut,
            [
                pltpu.VMEM((width, block_cols), BF16), pltpu.VMEM((width, cut), BF16),
                pltpu.VMEM((length, block_cols), F32), pltpu.VMEM((length, cut), BF16),
                pltpu.VMEM((width, block_cols), BF16),
            ],
            11,
        )
        last = [d_bias]
        attn_calls.append(mids + [d_bias])
        total, steps = reduce_pieces(g_keep, g_send, orders, core_bit)
        attn_sums.append(total)
        attn_steps.append(steps)
    branch, d_norm_attn = tail_part(
        attention_tail_kernel, block_of, per_call, orders, core_bit, last + mlp_steps[-1], me, attn_left, attn_right,
        [[c[0] for c in attn_calls], [c[1] for c in attn_calls]], [], [shaped((length, width), F32)] * 2,
        [pltpu.VMEM((width, block_cols), BF16), pltpu.VMEM((width, cut), BF16)], 9,
    )
    mlp_calls, mlp_sums, mlp_moves = [], [], []
    last = [branch]
    for n, k0 in enumerate(starts):
        after = last + attn_steps[0][min(n, len(orders[0]))]
        *mids, d_bias, g_keep, g_send = block_part(
            mlp_kernel, k0, per_call, orders, core_bit, after, me, nm, nm_t, out_cotangent, cot_t,
            up, down, [hidden_bias], [up_cols, up_cols], up_cols,
            [pltpu.VMEM((width, up_cols), BF16)] * 3,
            6,
        )
        last = [d_bias]
        mlp_calls.append(mids + [d_bias])
        total, steps = reduce_pieces(g_keep, g_send, orders, core_bit)
        mlp_sums.append(total)
        mlp_moves.append(steps)
    block_out, in_grad, stats = tail_part(
        mlp_tail_kernel, block_of, per_call, orders, core_bit, last + mlp_moves[0][0], me, up, down,
        [[c[1] for c in mlp_calls], [c[0] for c in mlp_calls]],
        [
            branch, d_norm_attn, tokens_in, out_cotangent, attn_gain[None, :], mlp_gain[None, :], out_bias[None, :],
            down_bias[None, :],
        ],
        [shaped((length, width), BF16)] * 2 + [shaped((8, width), F32)],
        [pltpu.VMEM((length, width), F32)] * 2 + [pltpu.VMEM((width, up_cols), BF16)] * 2, 13,
    )

    def settle(parts):
        total = None
        for both, k0 in zip(parts, starts):
            for i in range(per_call):
                k = k0 + i
                term = (both[i] if k == 0 else shifted(both[i], -k)).astype(F32)
                total = term if total is None else total + term
        flip = 2
        while flip < lax.axis_size("dp"):
            total = total + flipped(total, "dp", flip)
            flip *= 2
        mine = total.astype(BF16)
        other = swap(mine, 1)
        first = half == 0
        return jnp.concatenate([jnp.where(first, mine, other), jnp.where(first, other, mine)], axis=0).astype(F32)

    g_heads = settle(attn_sums).reshape(rows, local_heads, HEAD)
    g_mlp = settle(mlp_sums)

    d_bias_up = jnp.take(jnp.concatenate([c[2] for c in mlp_calls[::-1]]), blocks_here, axis=0)
    d_bias_attn = jnp.take(jnp.concatenate([c[2] for c in attn_calls[::-1]]), blocks_here, axis=0)
    smalls = jnp.concatenate(
        [
            stats[:5].reshape(-1),
            d_bias_up.reshape(-1),
            d_bias_attn.reshape(col_size * local_heads, HEAD)[:, :QKV].reshape(-1),
        ]
    )
    smalls = all_sum(smalls.reshape(-1, 128)).reshape(-1)
    stats = smalls[: 5 * width].reshape(5, width)
    grad_up_bias = smalls[5 * width : 5 * width + up_bias.shape[0]]
    grad_qkv_bias = smalls[5 * width + up_bias.shape[0] :]
    return (
        block_out,
        in_grad,
        stats[1],
        stats[2],
        stats[3],
        stats[4],
        g_heads[:, :, :QKV].reshape(rows, local_heads * QKV),
        grad_qkv_bias,
        g_heads[:, :, QKV:].reshape(rows, local_heads * HD).T,
        stats[0],
        g_mlp[:, :up_cols],
        grad_up_bias,
        g_mlp[:, up_cols:].T,
        stats[0],
    )


def solution(mesh):
    return jax.shard_map(
        on_device,
        mesh=mesh,
        in_specs=(
            P(("dp", "row", "col"), None),
            P("dp", None),
            P(),
            P(),
            P(),
            P(),
            P("row", "col"),
            P(),
            P("col", "row"),
            P(),
            P("row", "col"),
            P(),
            P("col", "row"),
            P(),
            P(("dp", "row", "col"), None),
        ),
        out_specs=(
            P(("dp", "row", "col"), None),
            P(("dp", "row", "col"), None),
            P(),
            P(),
            P(),
            P(),
            P("row", "col"),
            P(),
            P("col", "row"),
            P(),
            P("row", "col"),
            P(),
            P("col", "row"),
            P(),
        ),
        check_vma=False,
    )
```

```python
import functools
import math

import jax
import jax.numpy as jnp
from jax import lax
from jax.experimental import pallas as pl
from jax.experimental.pallas import tpu as pltpu
from jax.sharding import PartitionSpec as P

HD = 64
ROT = 16
QKV = 3 * HD
HEAD = 4 * HD
EPSILON = 1e-05
ROPE_BASE = 10000.0
NEAR = 128
LONGEST = 256
F32 = jnp.float32
BF16 = jnp.bfloat16


def dot_nn(a, b):
    return lax.dot_general(a, b, (((1,), (0,)), ((), ())), preferred_element_type=F32)


def dot_nt(a, b):
    return lax.dot_general(a, b, (((1,), (1,)), ((), ())), preferred_element_type=F32)


def gathered_order(order, core_bit):
    held = [0]
    for bit in order[:-1]:
        held = held + [j | bit for j in held]
    came = [j | order[-1] for j in held]
    return held, came, [j | core_bit for j in held], [j | core_bit for j in came]


def reduced_order(order):
    kept = [0]
    for bit in order[::-1]:
        kept = kept + [j | bit for j in kept]
    return kept


def assemble(me_ref, w_refs, held, w_scr, at_col):
    for ref, pieces in zip(w_refs, held):
        _, _, rows, cols = ref.shape
        for t, j in enumerate(pieces):
            at = pl.multiple_of((me_ref[0] ^ j) * rows, 16)
            w_scr[pl.ds(at, rows), at_col : at_col + cols] = ref[t, 0]


def hand_out(me_ref, g_scr, at_col, keep_ref, send_ref, first, order, core_bit):
    _, _, rows, cols = keep_ref.shape
    for t, j in enumerate(reduced_order(order)):
        for ref, piece in ((keep_ref, j), (send_ref, j | core_bit)):
            at = pl.multiple_of((me_ref[0] ^ piece) * rows, 16)
            ref[first + t, 0] = g_scr[pl.ds(at, rows), at_col : at_col + cols]


def normalize(x):
    center = x - jnp.mean(x, axis=1, keepdims=True)
    inv_std = lax.rsqrt(jnp.mean(center * center, axis=1, keepdims=True) + EPSILON)
    return center * inv_std, inv_std


def prep_kernel(
    x_ref, cot_ref, ga_ref, sa_ref, gm_ref, sm_ref, segc_ref, segr_ref, freq_ref,
    na_ref, naT_ref, nm_ref, nmT_ref, cotT_ref, keep_ref, ahead_ref, behind_ref, mask_ref,
):
    length = x_ref.shape[0]
    tile = 128

    @pl.loop(0, length // tile)
    def _(t):
        rows = pl.ds(pl.multiple_of(t * tile, tile), tile)
        normed, _ = normalize(x_ref[rows, :].astype(F32))
        na_ref[rows, :] = (normed * ga_ref[...] + sa_ref[...]).astype(BF16)
        nm_ref[rows, :] = (normed * gm_ref[...] + sm_ref[...]).astype(BF16)
        same = segc_ref[rows, :] == segr_ref[...]
        cols = lax.broadcasted_iota(jnp.int32, (tile, length), 1)
        ids = lax.broadcasted_iota(jnp.int32, (tile, length), 0) + t * tile
        mask_ref[rows, :] = jnp.where(same & (cols <= ids), 0.0, -jnp.inf)
        starts = jnp.min(jnp.where(same, cols, length).astype(F32), axis=1, keepdims=True)
        places = ids[:, :1].astype(F32) - starts
        angles = places * freq_ref[...]
        lane = lax.broadcasted_iota(jnp.int32, (tile, 2 * HD), 1) % HD
        cosine, sine = jnp.cos(angles), jnp.sin(angles)
        keep_ref[rows, :] = jnp.where(lane < ROT, cosine, 1.0)
        ahead_ref[rows, :] = jnp.where(lane < ROT // 2, -sine, 0.0)
        behind_ref[rows, :] = jnp.where((lane < ROT) & (lane >= ROT // 2), sine, 0.0)

    naT_ref[...] = na_ref[...].T
    nmT_ref[...] = nm_ref[...].T
    cotT_ref[...] = cot_ref[...].T


def full(*shape):
    return pl.BlockSpec(shape, lambda *_: (0,) * len(shape), pipeline_mode=pl.Buffered(1))


ANY = pl.BlockSpec(memory_space=pl.ANY)
SCALAR = pl.BlockSpec(memory_space=pltpu.SMEM)


def cost(us):
    return pl.CostEstimate(flops=int(us * 1.15e9), bytes_accessed=2**20, transcendentals=0)


def shaped(shape, dtype):
    return jax.ShapeDtypeStruct(shape, dtype)


def prep_part(tokens, cot, gains, seg_row):
    length, width = tokens.shape
    halves = ROT // 2
    step = (lax.iota(jnp.int32, 2 * HD) % HD % halves).astype(F32)
    freq = (ROPE_BASE ** (-(step * (2.0 / ROT))))[None, :]
    table = shaped((length, 2 * HD), F32)
    return pl.pallas_call(
        prep_kernel,
        grid=(1,),
        in_specs=[full(length, width)] * 2 + [full(1, width)] * 4
        + [full(length, 1), full(1, length), full(1, 2 * HD)],
        out_specs=[full(length, width), full(width, length)] * 2 + [full(width, length)]
        + [full(length, 2 * HD)] * 3 + [full(length, length)],
        out_shape=[shaped((length, width), BF16), shaped((width, length), BF16)] * 2
        + [shaped((width, length), BF16)] + [table] * 3 + [shaped((length, length), F32)],
        compiler_params=pltpu.CompilerParams(vmem_limit_bytes=24 * 2**20),
        cost_estimate=cost(6),
    )(tokens, cot, *gains, seg_row[:, None], seg_row[None, :], freq)


def attention_kernel(orders, core_bit, waits, me_ref, na_ref, naT_ref, cot_ref, cotT_ref, *rest):
    left, right, rest = rest[:4], rest[4:8], rest[8:]
    bias_ref, keep_ref, ahead_ref, behind_ref, mask_ref = rest[:5]
    dqkv_ref, mix_ref, dbias_ref, gk_ref, gs_ref, w_scr, wv_scr, qkv_scr, dattn_scr, g_scr = rest[5 + waits :]
    length, width = na_ref.shape
    block_cols = w_scr.shape[1]
    heads = block_cols // HEAD
    kept = gk_ref.shape[0] // 2
    tile = 256
    assemble(me_ref, left, gathered_order(orders[0], core_bit), w_scr, 0)
    assemble(me_ref, right, gathered_order(orders[1], core_bit), w_scr, block_cols // 2)
    for i in range(heads):
        wv_scr[:, i * 2 * HD : (i + 1) * 2 * HD] = w_scr[:, i * HEAD + 2 * HD : (i + 1) * HEAD]

    @pl.loop(0, length // tile)
    def _(t):
        rows = pl.ds(pl.multiple_of(t * tile, tile), tile)
        qkv_scr[rows, :] = dot_nn(na_ref[rows, :], w_scr[...]) + bias_ref[0]
        dattn_scr[rows, :] = dot_nn(cot_ref[rows, :], wv_scr[...]).astype(BF16)

    low = lax.broadcasted_iota(jnp.int32, (length, 2 * HD), 1) < HD
    keep, ahead, behind = keep_ref[...], ahead_ref[...], behind_ref[...]
    none = jnp.zeros((length, 2 * HD), BF16)
    spans = [(b * NEAR, (b + 1) * NEAR, max(0, b * NEAR - LONGEST)) for b in range(length // NEAR)]
    for i in range(heads):
        qk = qkv_scr[:, i * HEAD : i * HEAD + 2 * HD]
        qk = qk * keep + pltpu.roll(qk, 2 * HD - ROT // 2, 1) * ahead + pltpu.roll(qk, ROT // 2, 1) * behind
        q0 = jnp.where(low, qk * (1.0 / math.sqrt(HD)), 0.0).astype(BF16)
        k0 = jnp.where(low, pltpu.roll(qk, HD, 1), 0.0).astype(BF16)
        v1 = jnp.where(low, 0.0, pltpu.roll(qkv_scr[:, i * HEAD + 2 * HD : (i + 1) * HEAD], HD, 1)).astype(BF16)
        go = dattn_scr[:, i * 2 * HD : (i + 1) * 2 * HD]
        go1 = jnp.where(low, none, go)
        qT = q0.T[:HD]
        goT = go.T[HD:]
        s = [dot_nt(q0[r0:r1], k0[lo:r1]) + mask_ref[r0:r1, lo:r1] for r0, r1, lo in spans]
        dp = [dot_nt(go1[r0:r1], v1[lo:r1]) for r0, r1, lo in spans]
        peak = [jnp.max(one, axis=1, keepdims=True) for one in s]
        e = [jnp.exp(one - top) for one, top in zip(s, peak)]
        norm = [1.0 / jnp.sum(one, axis=1, keepdims=True) for one in e]
        p = [one * scale for one, scale in zip(e, norm)]
        p_low = [one.astype(BF16) for one in p]
        mix = [dot_nn(one, v1[lo:r1]) for one, (r0, r1, lo) in zip(p_low, spans)]
        delta = [
            jnp.sum(one * go1[r0:r1].astype(F32), axis=1, keepdims=True) for one, (r0, r1, lo) in zip(mix, spans)
        ]
        ds = [(one * (grad - centre)).astype(BF16) for one, grad, centre in zip(p, dp, delta)]
        dq = [dot_nn(one, k0[lo:r1]) for one, (r0, r1, lo) in zip(ds, spans)]
        dkT = [dot_nn(qT[:, r0:r1], one) for one, (r0, r1, lo) in zip(ds, spans)]
        dvT = [dot_nn(goT[:, r0:r1], one) for one, (r0, r1, lo) in zip(p_low, spans)]
        sums = []
        for parts in (dvT, dkT):
            total = [None] * len(spans)
            for part, (r0, r1, lo) in zip(parts, spans):
                for n in range(lo // NEAR, r1 // NEAR):
                    one = part[:, n * NEAR - lo : (n + 1) * NEAR - lo]
                    total[n] = one if total[n] is None else total[n] + one
            sums.append(jnp.concatenate(total, axis=1))
        dvk = jnp.concatenate(sums, axis=0).T
        dqk = jnp.where(low, jnp.concatenate(dq, axis=0) * (1.0 / math.sqrt(HD)), dvk)
        dqk = dqk * keep - pltpu.roll(dqk, 2 * HD - ROT // 2, 1) * ahead - pltpu.roll(dqk, ROT // 2, 1) * behind
        dqkv_ref[0, :, i * HEAD : i * HEAD + 2 * HD] = dqk.astype(BF16)
        dqkv_ref[0, :, i * HEAD + 2 * HD : (i + 1) * HEAD] = jnp.where(low, dvk, 0.0).astype(BF16)
        mix_ref[0, :, i * 2 * HD : (i + 1) * 2 * HD] = jnp.concatenate(mix, axis=0).astype(BF16)

    dbias_ref[0] = jnp.sum(dqkv_ref[0].astype(F32), axis=0, keepdims=True)

    @pl.loop(0, width // tile)
    def _(t):
        rows = pl.ds(pl.multiple_of(t * tile, tile), tile)
        g_in = dot_nn(naT_ref[rows, :], dqkv_ref[0])
        g_out = dot_nn(cotT_ref[rows, :], mix_ref[0])
        for i in range(heads):
            at = i * HEAD
            g_scr[rows, at : at + 2 * HD] = g_in[:, at : at + 2 * HD].astype(BF16)
            g_scr[rows, at + 2 * HD : at + HEAD] = (
                g_in[:, at + 2 * HD : at + HEAD] + g_out[:, i * 2 * HD : (i + 1) * 2 * HD]
            ).astype(BF16)

    hand_out(me_ref, g_scr, 0, gk_ref, gs_ref, 0, orders[0], core_bit)
    hand_out(me_ref, g_scr, block_cols // 2, gk_ref, gs_ref, kept, orders[1], core_bit)


def mlp_kernel(orders, core_bit, waits, me_ref, nm_ref, nmT_ref, cot_ref, cotT_ref, *rest):
    left, right, bias_ref, rest = rest[:4], rest[4:8], rest[8], rest[9 + waits :]
    act_ref, dh_ref, dbias_ref, gk_ref, gs_ref, wu_scr, wd_scr, g_scr = rest
    length, width = nm_ref.shape
    up_cols = wu_scr.shape[1]
    kept = gk_ref.shape[0] // 2
    tile = 256
    assemble(me_ref, left, gathered_order(orders[0], core_bit), wu_scr, 0)
    assemble(me_ref, right, gathered_order(orders[1], core_bit), wd_scr, 0)
    dbias_ref[0] = jnp.zeros_like(dbias_ref[0])

    @pl.loop(0, length // tile)
    def _(t):
        rows = pl.ds(pl.multiple_of(t * tile, tile), tile)
        for n in range(0, up_cols, tile):
            hidden = dot_nn(nm_ref[rows, :], wu_scr[:, n : n + tile]) + bias_ref[0, :, n : n + tile]
            d_act = dot_nn(cot_ref[rows, :], wd_scr[:, n : n + tile])
            gate = 0.5 * (1.0 + lax.erf(hidden * (1.0 / math.sqrt(2.0))))
            act_ref[0, rows, n : n + tile] = (hidden * gate).astype(BF16)
            slope = gate + hidden * jnp.exp(-0.5 * hidden * hidden) * (1.0 / math.sqrt(2.0 * math.pi))
            dh = (d_act * slope).astype(BF16)
            dh_ref[0, rows, n : n + tile] = dh
            dbias_ref[0, :, n : n + tile] += jnp.sum(dh.astype(F32), axis=0, keepdims=True)

    for side, lhs, rhs in ((0, nmT_ref, dh_ref), (1, cotT_ref, act_ref)):

        @pl.loop(0, width // tile)
        def _(t):
            rows = pl.ds(pl.multiple_of(t * tile, tile), tile)
            g_scr[rows, :] = dot_nn(lhs[rows, :], rhs[0]).astype(BF16)

        hand_out(me_ref, g_scr, 0, gk_ref, gs_ref, side * kept, orders[side], core_bit)


def weight_spec(array, block_of):
    count, _, rows, cols = array.shape
    return pl.BlockSpec((count, 1, rows, cols), lambda s: (0, block_of(s), 0, 0))


def block_part(kernel, k0, count, orders, core_bit, after, me, norm, norm_t, cot, cot_t, left, right, vectors, mid_cols,
               g_cols, scratch, us, into=None):
    length, width = norm.shape
    rows = left[0].shape[2]
    pieces = width // rows
    cols = vectors[0].shape[-1]
    shared = into is not None
    g_blocks = left[0].shape[1] if shared else count
    g_spec = pl.BlockSpec((pieces, 1, rows, g_cols), lambda s: (0, k0 + s if shared else s, 0, 0))
    after = list(after) + list(into or [])
    fixed = 5 + len(left + right) + len(vectors) + len(after)
    return pl.pallas_call(
        functools.partial(kernel, orders, core_bit, len(after)),
        grid=(count,),
        in_specs=[SCALAR, full(length, width), full(width, length), full(length, width), full(width, length)]
        + [weight_spec(w, lambda s: k0 + s) for w in left + right]
        + [pl.BlockSpec((1, 1, cols), lambda s: (k0 + s, 0, 0))]
        + [full(*v.shape) for v in vectors[1:]]
        + [ANY] * len(after),
        out_specs=[pl.BlockSpec((1, length, m), lambda s: (s, 0, 0)) for m in mid_cols]
        + [pl.BlockSpec((1, 1, cols), lambda s: (s, 0, 0))] + [g_spec] * 2,
        out_shape=[shaped((count, length, m), BF16) for m in mid_cols]
        + [shaped((count, 1, cols), F32)] + [shaped((pieces, g_blocks, rows, g_cols), BF16)] * 2,
        input_output_aliases={fixed - 2: len(mid_cols) + 1, fixed - 1: len(mid_cols) + 2} if into else {},
        scratch_shapes=scratch,
        compiler_params=pltpu.CompilerParams(vmem_limit_bytes=30 * 2**20),
        cost_estimate=cost(us * count),
    )(me, norm, norm_t, cot, cot_t, *left, *right, *vectors, *after)


def pick(refs, per_call, scr):
    for n, ref in enumerate(refs):

        @pl.when(pl.program_id(0) // per_call == n)
        def _():
            scr[...] = ref[0]


def attention_tail_kernel(orders, core_bit, calls, per_call, waits, me_ref, *rest):
    left, right, rest = rest[:4], rest[4:8], rest[8:]
    dqkv_refs, mix_refs, rest = rest[:calls], rest[calls : 2 * calls], rest[2 * calls + waits :]
    branch_ref, dna_ref, w_scr, wv_scr, dqkv_scr, mix_scr = rest
    block_cols = w_scr.shape[1]

    @pl.when(pl.program_id(0) == 0)
    def _():
        branch_ref[...] = jnp.zeros_like(branch_ref)
        dna_ref[...] = jnp.zeros_like(dna_ref)

    pick(dqkv_refs, per_call, dqkv_scr)
    pick(mix_refs, per_call, mix_scr)
    assemble(me_ref, left, gathered_order(orders[0], core_bit), w_scr, 0)
    assemble(me_ref, right, gathered_order(orders[1], core_bit), w_scr, block_cols // 2)
    for i in range(block_cols // HEAD):
        wv_scr[:, i * 2 * HD : (i + 1) * 2 * HD] = w_scr[:, i * HEAD + 2 * HD : (i + 1) * HEAD]
    tile = 256

    @pl.loop(0, branch_ref.shape[0] // tile)
    def _(t):
        rows = pl.ds(pl.multiple_of(t * tile, tile), tile)
        branch_ref[rows, :] += dot_nt(mix_scr[rows, :], wv_scr[...])
        dna_ref[rows, :] += dot_nt(dqkv_scr[rows, :], w_scr[...])


def mlp_tail_kernel(orders, core_bit, calls, per_call, waits, me_ref, *rest):
    left, right, rest = rest[:4], rest[4:8], rest[8:]
    dh_refs, act_refs, rest = rest[:calls], rest[calls : 2 * calls], rest[2 * calls :]
    branch_in, dna_ref, x_ref, cot_ref, ga_ref, gm_ref, bo_ref, bd_ref = rest[:8]
    block_ref, grad_ref, stats_ref, branch_ref, dnm_ref, wu_scr, wd_scr, dh_scr, act_scr = rest[8 + waits :]
    length = x_ref.shape[0]
    step = pl.program_id(0)

    @pl.when(step == 0)
    def _():
        branch_ref[...] = branch_in[...]
        dnm_ref[...] = jnp.zeros_like(dnm_ref)

    pick(dh_refs, per_call, dh_scr)
    pick(act_refs, per_call, act_scr)
    assemble(me_ref, left, gathered_order(orders[0], core_bit), wu_scr, 0)
    assemble(me_ref, right, gathered_order(orders[1], core_bit), wd_scr, 0)
    tile = 256

    @pl.loop(0, length // tile)
    def _(t):
        rows = pl.ds(pl.multiple_of(t * tile, tile), tile)
        branch_ref[rows, :] += dot_nt(act_scr[rows, :], wd_scr[...])
        dnm_ref[rows, :] += dot_nt(dh_scr[rows, :], wu_scr[...])

    @pl.when(step == pl.num_programs(0) - 1)
    def _():
        stats_ref[...] = jnp.zeros_like(stats_ref)
        small = 128

        @pl.loop(0, length // small)
        def _(t):
            rows = pl.ds(pl.multiple_of(t * small, small), small)
            x = x_ref[rows, :].astype(F32)
            cot = cot_ref[rows, :].astype(F32)
            normed, inv_std = normalize(x)
            block_ref[rows, :] = (x + branch_ref[rows, :] + bo_ref[...] + bd_ref[...]).astype(BF16)
            dna, dnm = dna_ref[rows, :], dnm_ref[rows, :]
            d_normed = dna * ga_ref[...] + dnm * gm_ref[...]
            pulled = (
                d_normed
                - jnp.mean(d_normed, axis=1, keepdims=True)
                - normed * jnp.mean(d_normed * normed, axis=1, keepdims=True)
            )
            grad_ref[rows, :] = (cot + inv_std * pulled).astype(BF16)
            for at, term in enumerate((cot, dna * normed, dna, dnm * normed, dnm)):
                stats_ref[at : at + 1, :] += jnp.sum(term, axis=0, keepdims=True)


def tail_part(kernel, block_of, per_call, orders, core_bit, after, me, left, right, mids, extra, outs, scratch, us):
    steps = left[0].shape[1]
    calls = steps // per_call

    def mid_spec(array, n):
        _, length, cols = array.shape
        return pl.BlockSpec((1, length, cols), lambda s: (jnp.clip(s - n * per_call, 0, per_call - 1), 0, 0))

    kept = [pltpu.VMEM(group[0].shape[1:], BF16) for group in mids]
    return pl.pallas_call(
        functools.partial(kernel, orders, core_bit, calls, per_call, len(after)),
        grid=(steps,),
        in_specs=[SCALAR] + [weight_spec(w, block_of) for w in left + right]
        + [mid_spec(array, n) for group in mids for n, array in enumerate(group)]
        + [full(*e.shape) for e in extra] + [ANY] * len(after),
        out_specs=[full(*o.shape) for o in outs],
        out_shape=outs,
        scratch_shapes=scratch + kept,
        compiler_params=pltpu.CompilerParams(vmem_limit_bytes=40 * 2**20),
        cost_estimate=cost(us),
    )(me, *left, *right, *[array for group in mids for array in group], *extra, *after)


def fence_kernel(*_):
    pass


def fence(values, after=()):
    count = len(values)
    return pl.pallas_call(
        fence_kernel,
        in_specs=[ANY] * (count + len(after)),
        out_specs=[ANY] * count,
        out_shape=[shaped(value.shape, value.dtype) for value in values],
        input_output_aliases={n: n for n in range(count)},
        cost_estimate=cost(1),
    )(*values, *after)


def swap(value, bit):
    axis, flip = ("dp", 1) if bit == 1 else ("row", bit // 2)
    return flipped(value, axis, flip)


def flipped(value, axis, flip):
    return lax.ppermute(value, axis, [(i, i ^ flip) for i in range(lax.axis_size(axis))])


def shifted(value, by):
    size = lax.axis_size("col")
    return lax.ppermute(value, "col", [(i, (i + by) % size) for i in range(size)])


def gather_pieces(own, order, core_bit):
    held = own[None]
    for bit in order[:-1]:
        held = jnp.concatenate([held, swap(held, bit)], axis=0)
    came = swap(held, order[-1])
    return [held, came, swap(held, core_bit), swap(came, core_bit)]


def add(a, b):
    return (a.astype(F32) + b.astype(F32)).astype(BF16)


class Reduction:
    def __init__(self, keep, send, orders, core_bit):
        self.keep, self.orders, self.core_bit = keep, orders, core_bit
        self.moving, self.held, self.done, self.closed = [send], None, -1, False

    def advance(self):
        if self.done < 0:
            self.moving = [swap(self.moving[0], self.core_bit)]
        else:
            if self.done == 0:
                size = self.keep.shape[0] // len(self.orders)
                cuts = [slice(side * size, (side + 1) * size) for side in range(len(self.orders))]
                self.held, self.moving = [self.keep[c] for c in cuts], [self.moving[0][c] for c in cuts]
            half = self.held[0].shape[0] // 2
            sent = [add(a[half:], b[half:]) for a, b in zip(self.held, self.moving)]
            self.held = [add(a[:half], b[:half]) for a, b in zip(self.held, self.moving)]
            self.moving = [swap(one, order[self.done]) for one, order in zip(sent, self.orders)]
        self.done += 1

    def total(self):
        assert self.done == len(self.orders[0])
        return jnp.concatenate([add(a[0], b[0]) for a, b in zip(self.held, self.moving)], axis=2)


def phase(reductions, values=(), after=()):
    values = list(values)
    reductions = [r for r in reductions if not r.closed]
    out = list(fence(values + [one for r in reductions for one in r.moving], after))
    at = len(values)
    for r in reductions:
        r.moving = out[at : at + len(r.moving)]
        at += len(r.moving)
        if r.done < len(r.orders[0]):
            r.advance()
        else:
            r.closed = True
    return out


def all_sum(value):
    for axis in ("row", "dp", "col"):
        flip = 1
        while flip < lax.axis_size(axis):
            value = value + flipped(value, axis, flip)
            flip *= 2
    return value


def on_device(
    tokens_in,
    segment_ids,
    attn_gain,
    attn_shift,
    mlp_gain,
    mlp_shift,
    qkv_weight,
    qkv_bias,
    out_weight,
    out_bias,
    up_weight,
    up_bias,
    down_weight,
    down_bias,
    out_cotangent,
):
    row_size = lax.axis_size("row")
    col_size = lax.axis_size("col")
    length, width = tokens_in.shape
    rows = qkv_weight.shape[0]
    half_rows = rows // 2
    local_heads = qkv_weight.shape[1] // QKV
    block_cols = local_heads * HEAD
    up_cols = up_weight.shape[1]
    row_id = lax.axis_index("row")
    col_id = lax.axis_index("col")
    half = lax.axis_index("dp") % 2
    me = (row_id * 2 + half).reshape(1).astype(jnp.int32)
    row_bits = [2 << i for i in range(row_size.bit_length() - 1)]
    core_bit, far_bits = row_bits[0], row_bits[1:][::-1]
    orders = (far_bits + [1], [1] + far_bits)

    head_weight = jnp.concatenate(
        [qkv_weight.reshape(rows, local_heads, QKV), out_weight.T.reshape(rows, local_heads, HD)], axis=2
    ).reshape(rows, block_cols)
    attn_own = lax.dynamic_slice_in_dim(head_weight, half * half_rows, half_rows, axis=0)
    mlp_own = jnp.concatenate(
        [
            lax.dynamic_slice_in_dim(up_weight, half * half_rows, half_rows, axis=0),
            lax.dynamic_slice_in_dim(down_weight, half * half_rows, half_rows, axis=1).T,
        ],
        axis=1,
    )
    def gather_col(own):
        return jnp.stack([own] + [shifted(own, k) for k in range(1, col_size)])

    attn_all = gather_col(attn_own)
    cut = block_cols // 2
    attn_left = gather_pieces(attn_all[:, :, :cut], orders[0], core_bit)
    attn_right = gather_pieces(attn_all[:, :, cut:], orders[1], core_bit)

    seg_row = lax.dynamic_index_in_dim(segment_ids, row_id * col_size + col_id, axis=0, keepdims=False)
    na, na_t, nm, nm_t, cot_t, keep, ahead, behind, mask = prep_part(
        tokens_in, out_cotangent, [v[None, :] for v in (attn_gain, attn_shift, mlp_gain, mlp_shift)], seg_row,
    )
    mlp_all = gather_col(fence([mlp_own], [attn_all])[0])
    blocks_here = (col_id - jnp.arange(col_size)) % col_size
    head_bias = jnp.pad(
        qkv_bias.reshape(col_size, local_heads, QKV), ((0, 0), (0, 0), (0, HEAD - QKV))
    ).reshape(col_size, 1, block_cols)
    head_bias = jnp.take(head_bias, blocks_here, axis=0)
    hidden_bias = jnp.take(up_bias.reshape(col_size, 1, up_cols), blocks_here, axis=0)

    per_call = 2
    calls = col_size // per_call
    starts = [k0 for k0 in range(0, col_size, per_call)][::-1]

    def block_of(s):
        return (calls - 1 - s // per_call) * per_call + s % per_call

    def held_until_last(own, order):
        held = own[None]
        for bit in order[:-1]:
            held = jnp.concatenate([held, swap(held, bit)], axis=0)
        return held

    def attention_call(k0, after, into):
        return block_part(
            attention_kernel, k0, per_call, orders, core_bit, after, me, na, na_t, out_cotangent, cot_t,
            attn_left, attn_right, [head_bias, keep, ahead, behind, mask], [block_cols, cut], cut,
            [
                pltpu.VMEM((width, block_cols), BF16), pltpu.VMEM((width, cut), BF16),
                pltpu.VMEM((length, block_cols), F32), pltpu.VMEM((length, cut), BF16),
                pltpu.VMEM((width, block_cols), BF16),
            ],
            11, into,
        )

    def mlp_call(k0, after):
        return block_part(
            mlp_kernel, k0, per_call, orders, core_bit, after, me, nm, nm_t, out_cotangent, cot_t,
            up, down, [hidden_bias], [up_cols, up_cols], up_cols, [pltpu.VMEM((width, up_cols), BF16)] * 3, 6,
        )

    held = [held_until_last(mlp_all[:, :, :up_cols], orders[0]), held_until_last(mlp_all[:, :, up_cols:], orders[1])]
    held = list(fence(held, [w for w in attn_left + attn_right]))
    came = [swap(one, order[-1]) for one, order in zip(held, orders)]
    held_over = [swap(one, core_bit) for one in held]

    attn_calls, into = [], []
    for n, k0 in enumerate(starts):
        outs = attention_call(k0, [held[0]] if n == 0 else [came[0]], into)
        attn_calls.append(outs[:3])
        into = list(outs[3:])
        if n == 0:
            came = list(fence(came, [outs[2]] + held_over))
            came_over = [swap(one, core_bit) for one in came]
    attn_sum = Reduction(into[0], into[1], orders, core_bit)
    up, down = ([held[i], came[i], held_over[i], came_over[i]] for i in range(2))

    token = phase([attn_sum], [], came_over)
    mlp_calls, mlp_sums = [], []
    for k0 in starts:
        *mids, g_keep, g_send = mlp_call(k0, token[:1])
        mlp_calls.append(mids)
        mlp_sums.append(Reduction(g_keep, g_send, orders, core_bit))
        token = phase([attn_sum] + mlp_sums, [], [mids[2]])

    branch, d_norm_attn = tail_part(
        attention_tail_kernel, block_of, per_call, orders, core_bit, token[:1], me, attn_left, attn_right,
        [[c[0] for c in attn_calls], [c[1] for c in attn_calls]], [], [shaped((length, width), F32)] * 2,
        [pltpu.VMEM((width, block_cols), BF16), pltpu.VMEM((width, cut), BF16)], 9,
    )
    token = phase([attn_sum] + mlp_sums, [], [branch])
    block_out, in_grad, stats = tail_part(
        mlp_tail_kernel, block_of, per_call, orders, core_bit, token[:1], me, up, down,
        [[c[1] for c in mlp_calls], [c[0] for c in mlp_calls]],
        [
            branch, d_norm_attn, tokens_in, out_cotangent, attn_gain[None, :], mlp_gain[None, :], out_bias[None, :],
            down_bias[None, :],
        ],
        [shaped((length, width), BF16)] * 2 + [shaped((8, width), F32)],
        [pltpu.VMEM((length, width), F32)] * 2 + [pltpu.VMEM((width, up_cols), BF16)] * 2, 13,
    )
    stats = phase([attn_sum] + mlp_sums, [stats])[0]
    while any(r.done < len(orders[0]) for r in mlp_sums):
        for r in mlp_sums:
            if r.done < len(orders[0]):
                r.advance()

    def settle(parts):
        total = None
        for k, part in parts:
            term = (part if k == 0 else shifted(part, -k)).astype(F32)
            total = term if total is None else total + term
        flip = 2
        while flip < lax.axis_size("dp"):
            total = total + flipped(total, "dp", flip)
            flip *= 2
        mine = total.astype(BF16)
        other = swap(mine, 1)
        first = half == 0
        return jnp.concatenate([jnp.where(first, mine, other), jnp.where(first, other, mine)], axis=0).astype(F32)

    attn_sum = attn_sum.total()
    g_heads = settle([(k, attn_sum[k]) for k in range(col_size)]).reshape(rows, local_heads, HEAD)
    mlp_totals = [r.total() for r in mlp_sums]
    g_mlp = settle([(k0 + i, one[i]) for k0, one in zip(starts, mlp_totals) for i in range(per_call)])

    d_bias_up = jnp.take(jnp.concatenate([c[2] for c in mlp_calls[::-1]]), blocks_here, axis=0)
    d_bias_attn = jnp.take(jnp.concatenate([c[2] for c in attn_calls[::-1]]), blocks_here, axis=0)
    smalls = jnp.concatenate(
        [
            stats[:5].reshape(-1),
            d_bias_up.reshape(-1),
            d_bias_attn.reshape(col_size * local_heads, HEAD)[:, :QKV].reshape(-1),
        ]
    )
    smalls = all_sum(smalls.reshape(-1, 128)).reshape(-1)
    stats = smalls[: 5 * width].reshape(5, width)
    grad_up_bias = smalls[5 * width : 5 * width + up_bias.shape[0]]
    grad_qkv_bias = smalls[5 * width + up_bias.shape[0] :]
    return (
        block_out,
        in_grad,
        stats[1],
        stats[2],
        stats[3],
        stats[4],
        g_heads[:, :, :QKV].reshape(rows, local_heads * QKV),
        grad_qkv_bias,
        g_heads[:, :, QKV:].reshape(rows, local_heads * HD).T,
        stats[0],
        g_mlp[:, :up_cols],
        grad_up_bias,
        g_mlp[:, up_cols:].T,
        stats[0],
    )


def solution(mesh):
    return jax.shard_map(
        on_device,
        mesh=mesh,
        in_specs=(
            P(("dp", "row", "col"), None),
            P("dp", None),
            P(),
            P(),
            P(),
            P(),
            P("row", "col"),
            P(),
            P("col", "row"),
            P(),
            P("row", "col"),
            P(),
            P("col", "row"),
            P(),
            P(("dp", "row", "col"), None),
        ),
        out_specs=(
            P(("dp", "row", "col"), None),
            P(("dp", "row", "col"), None),
            P(),
            P(),
            P(),
            P(),
            P("row", "col"),
            P(),
            P("col", "row"),
            P(),
            P("row", "col"),
            P(),
            P("col", "row"),
            P(),
        ),
        check_vma=False,
    )
```

```python
import functools
import math

import jax
import jax.numpy as jnp
from jax import lax
from jax.experimental import pallas as pl
from jax.experimental.pallas import tpu as pltpu
from jax.sharding import PartitionSpec as P

HD = 64
ROT = 16
QKV = 3 * HD
HEAD = 4 * HD
EPSILON = 1e-05
ROPE_BASE = 10000.0
NEAR = 128
LONGEST = 256
F32 = jnp.float32
BF16 = jnp.bfloat16


def dot_nn(a, b):
    return lax.dot_general(a, b, (((1,), (0,)), ((), ())), preferred_element_type=F32)


def dot_nt(a, b):
    return lax.dot_general(a, b, (((1,), (1,)), ((), ())), preferred_element_type=F32)


def gathered_order(order, core_bit):
    held = [0]
    for bit in order[:-1]:
        held = held + [j | bit for j in held]
    came = [j | order[-1] for j in held]
    return held, came, [j | core_bit for j in held], [j | core_bit for j in came]


def reduced_order(order):
    kept = [0]
    for bit in order[::-1]:
        kept = kept + [j | bit for j in kept]
    return kept


def assemble(me_ref, w_refs, held, w_scr, at_col):
    for ref, pieces in zip(w_refs, held):
        _, _, rows, cols = ref.shape
        for t, j in enumerate(pieces):
            at = pl.multiple_of((me_ref[0] ^ j) * rows, 16)
            w_scr[pl.ds(at, rows), at_col : at_col + cols] = ref[t, 0]


def hand_out(me_ref, g_scr, at_col, keep_ref, send_ref, first, order, core_bit):
    _, _, rows, cols = keep_ref.shape
    for t, j in enumerate(reduced_order(order)):
        for ref, piece in ((keep_ref, j), (send_ref, j | core_bit)):
            at = pl.multiple_of((me_ref[0] ^ piece) * rows, 16)
            ref[first + t, 0] = g_scr[pl.ds(at, rows), at_col : at_col + cols]


def normalize(x):
    center = x - jnp.mean(x, axis=1, keepdims=True)
    inv_std = lax.rsqrt(jnp.mean(center * center, axis=1, keepdims=True) + EPSILON)
    return center * inv_std, inv_std


def prep_kernel(
    x_ref, cot_ref, ga_ref, sa_ref, gm_ref, sm_ref, segc_ref, segr_ref, freq_ref,
    na_ref, naT_ref, nm_ref, nmT_ref, cotT_ref, keep_ref, ahead_ref, behind_ref, mask_ref,
):
    length = x_ref.shape[0]
    tile = 128

    @pl.loop(0, length // tile)
    def _(t):
        rows = pl.ds(pl.multiple_of(t * tile, tile), tile)
        normed, _ = normalize(x_ref[rows, :].astype(F32))
        na_ref[rows, :] = (normed * ga_ref[...] + sa_ref[...]).astype(BF16)
        nm_ref[rows, :] = (normed * gm_ref[...] + sm_ref[...]).astype(BF16)
        same = segc_ref[rows, :] == segr_ref[...]
        cols = lax.broadcasted_iota(jnp.int32, (tile, length), 1)
        ids = lax.broadcasted_iota(jnp.int32, (tile, length), 0) + t * tile
        mask_ref[rows, :] = jnp.where(same & (cols <= ids), 0.0, -jnp.inf)
        starts = jnp.min(jnp.where(same, cols, length).astype(F32), axis=1, keepdims=True)
        places = ids[:, :1].astype(F32) - starts
        angles = places * freq_ref[...]
        lane = lax.broadcasted_iota(jnp.int32, (tile, 2 * HD), 1) % HD
        cosine, sine = jnp.cos(angles), jnp.sin(angles)
        keep_ref[rows, :] = jnp.where(lane < ROT, cosine, 1.0)
        ahead_ref[rows, :] = jnp.where(lane < ROT // 2, -sine, 0.0)
        behind_ref[rows, :] = jnp.where((lane < ROT) & (lane >= ROT // 2), sine, 0.0)

    naT_ref[...] = na_ref[...].T
    nmT_ref[...] = nm_ref[...].T
    cotT_ref[...] = cot_ref[...].T


def full(*shape):
    return pl.BlockSpec(shape, lambda *_: (0,) * len(shape), pipeline_mode=pl.Buffered(1))


ANY = pl.BlockSpec(memory_space=pl.ANY)
SCALAR = pl.BlockSpec(memory_space=pltpu.SMEM)


def cost(us):
    return pl.CostEstimate(flops=int(us * 1.15e9), bytes_accessed=2**20, transcendentals=0)


def shaped(shape, dtype):
    return jax.ShapeDtypeStruct(shape, dtype)


def prep_part(tokens, cot, gains, seg_row):
    length, width = tokens.shape
    halves = ROT // 2
    step = (lax.iota(jnp.int32, 2 * HD) % HD % halves).astype(F32)
    freq = (ROPE_BASE ** (-(step * (2.0 / ROT))))[None, :]
    table = shaped((length, 2 * HD), F32)
    return pl.pallas_call(
        prep_kernel,
        grid=(1,),
        in_specs=[full(length, width)] * 2 + [full(1, width)] * 4
        + [full(length, 1), full(1, length), full(1, 2 * HD)],
        out_specs=[full(length, width), full(width, length)] * 2 + [full(width, length)]
        + [full(length, 2 * HD)] * 3 + [full(length, length)],
        out_shape=[shaped((length, width), BF16), shaped((width, length), BF16)] * 2
        + [shaped((width, length), BF16)] + [table] * 3 + [shaped((length, length), F32)],
        compiler_params=pltpu.CompilerParams(vmem_limit_bytes=60 * 2**20),
        cost_estimate=cost(6),
    )(tokens, cot, *gains, seg_row[:, None], seg_row[None, :], freq)


def attention_kernel(orders, core_bit, waits, me_ref, na_ref, naT_ref, cot_ref, cotT_ref, *rest):
    left, right, rest = rest[:4], rest[4:8], rest[8:]
    bias_ref, keep_ref, ahead_ref, behind_ref, mask_ref = rest[:5]
    dqkv_ref, mix_ref, dbias_ref, gk_ref, gs_ref, w_scr, wv_scr, qkv_scr, dattn_scr, g_scr = rest[5 + waits :]
    length, width = na_ref.shape
    block_cols = w_scr.shape[1]
    heads = block_cols // HEAD
    kept = gk_ref.shape[0] // 2
    tile = 256
    assemble(me_ref, left, gathered_order(orders[0], core_bit), w_scr, 0)
    assemble(me_ref, right, gathered_order(orders[1], core_bit), w_scr, block_cols // 2)
    for i in range(heads):
        wv_scr[:, i * 2 * HD : (i + 1) * 2 * HD] = w_scr[:, i * HEAD + 2 * HD : (i + 1) * HEAD]

    @pl.loop(0, length // tile)
    def _(t):
        rows = pl.ds(pl.multiple_of(t * tile, tile), tile)
        qkv_scr[rows, :] = dot_nn(na_ref[rows, :], w_scr[...]) + bias_ref[0]
        dattn_scr[rows, :] = dot_nn(cot_ref[rows, :], wv_scr[...]).astype(BF16)

    low = lax.broadcasted_iota(jnp.int32, (length, 2 * HD), 1) < HD
    keep, ahead, behind = keep_ref[...], ahead_ref[...], behind_ref[...]
    none = jnp.zeros((length, 2 * HD), BF16)
    spans = [(b * NEAR, (b + 1) * NEAR, max(0, b * NEAR - LONGEST)) for b in range(length // NEAR)]
    for i in range(heads):
        qk = qkv_scr[:, i * HEAD : i * HEAD + 2 * HD]
        qk = qk * keep + pltpu.roll(qk, 2 * HD - ROT // 2, 1) * ahead + pltpu.roll(qk, ROT // 2, 1) * behind
        q0 = jnp.where(low, qk * (1.0 / math.sqrt(HD)), 0.0).astype(BF16)
        k0 = jnp.where(low, pltpu.roll(qk, HD, 1), 0.0).astype(BF16)
        v1 = jnp.where(low, 0.0, pltpu.roll(qkv_scr[:, i * HEAD + 2 * HD : (i + 1) * HEAD], HD, 1)).astype(BF16)
        go = dattn_scr[:, i * 2 * HD : (i + 1) * 2 * HD]
        go1 = jnp.where(low, none, go)
        qT = q0.T[:HD]
        goT = go.T[HD:]
        s = [dot_nt(q0[r0:r1], k0[lo:r1]) + mask_ref[r0:r1, lo:r1] for r0, r1, lo in spans]
        dp = [dot_nt(go1[r0:r1], v1[lo:r1]) for r0, r1, lo in spans]
        peak = [jnp.max(one, axis=1, keepdims=True) for one in s]
        e = [jnp.exp(one - top) for one, top in zip(s, peak)]
        norm = [1.0 / jnp.sum(one, axis=1, keepdims=True) for one in e]
        p = [one * scale for one, scale in zip(e, norm)]
        p_low = [one.astype(BF16) for one in p]
        mix = [dot_nn(one, v1[lo:r1]) for one, (r0, r1, lo) in zip(p_low, spans)]
        delta = [
            jnp.sum(one * go1[r0:r1].astype(F32), axis=1, keepdims=True) for one, (r0, r1, lo) in zip(mix, spans)
        ]
        ds = [(one * (grad - centre)).astype(BF16) for one, grad, centre in zip(p, dp, delta)]
        dq = [dot_nn(one, k0[lo:r1]) for one, (r0, r1, lo) in zip(ds, spans)]
        dkT = [dot_nn(qT[:, r0:r1], one) for one, (r0, r1, lo) in zip(ds, spans)]
        dvT = [dot_nn(goT[:, r0:r1], one) for one, (r0, r1, lo) in zip(p_low, spans)]
        sums = []
        for parts in (dvT, dkT):
            total = [None] * len(spans)
            for part, (r0, r1, lo) in zip(parts, spans):
                for n in range(lo // NEAR, r1 // NEAR):
                    one = part[:, n * NEAR - lo : (n + 1) * NEAR - lo]
                    total[n] = one if total[n] is None else total[n] + one
            sums.append(jnp.concatenate(total, axis=1))
        dvk = jnp.concatenate(sums, axis=0).T
        dqk = jnp.where(low, jnp.concatenate(dq, axis=0) * (1.0 / math.sqrt(HD)), dvk)
        dqk = dqk * keep - pltpu.roll(dqk, 2 * HD - ROT // 2, 1) * ahead - pltpu.roll(dqk, ROT // 2, 1) * behind
        dqkv_ref[0, :, i * HEAD : i * HEAD + 2 * HD] = dqk.astype(BF16)
        dqkv_ref[0, :, i * HEAD + 2 * HD : (i + 1) * HEAD] = jnp.where(low, dvk, 0.0).astype(BF16)
        mix_ref[0, :, i * 2 * HD : (i + 1) * 2 * HD] = jnp.concatenate(mix, axis=0).astype(BF16)

    dbias_ref[0] = jnp.sum(dqkv_ref[0].astype(F32), axis=0, keepdims=True)

    @pl.loop(0, width // tile)
    def _(t):
        rows = pl.ds(pl.multiple_of(t * tile, tile), tile)
        g_in = dot_nn(naT_ref[rows, :], dqkv_ref[0])
        g_out = dot_nn(cotT_ref[rows, :], mix_ref[0])
        for i in range(heads):
            at = i * HEAD
            g_scr[rows, at : at + 2 * HD] = g_in[:, at : at + 2 * HD].astype(BF16)
            g_scr[rows, at + 2 * HD : at + HEAD] = (
                g_in[:, at + 2 * HD : at + HEAD] + g_out[:, i * 2 * HD : (i + 1) * 2 * HD]
            ).astype(BF16)

    hand_out(me_ref, g_scr, 0, gk_ref, gs_ref, 0, orders[0], core_bit)
    hand_out(me_ref, g_scr, block_cols // 2, gk_ref, gs_ref, kept, orders[1], core_bit)


def mlp_kernel(orders, core_bit, waits, me_ref, nm_ref, nmT_ref, cot_ref, cotT_ref, *rest):
    left, right, bias_ref, rest = rest[:4], rest[4:8], rest[8], rest[9 + waits :]
    act_ref, dh_ref, dbias_ref, gk_ref, gs_ref, wu_scr, wd_scr, g_scr = rest
    length, width = nm_ref.shape
    up_cols = wu_scr.shape[1]
    kept = gk_ref.shape[0] // 2
    tile = 256
    assemble(me_ref, left, gathered_order(orders[0], core_bit), wu_scr, 0)
    assemble(me_ref, right, gathered_order(orders[1], core_bit), wd_scr, 0)
    dbias_ref[0] = jnp.zeros_like(dbias_ref[0])

    @pl.loop(0, length // tile)
    def _(t):
        rows = pl.ds(pl.multiple_of(t * tile, tile), tile)
        for n in range(0, up_cols, tile):
            hidden = dot_nn(nm_ref[rows, :], wu_scr[:, n : n + tile]) + bias_ref[0, :, n : n + tile]
            d_act = dot_nn(cot_ref[rows, :], wd_scr[:, n : n + tile])
            gate = 0.5 * (1.0 + lax.erf(hidden * (1.0 / math.sqrt(2.0))))
            act_ref[0, rows, n : n + tile] = (hidden * gate).astype(BF16)
            slope = gate + hidden * jnp.exp(-0.5 * hidden * hidden) * (1.0 / math.sqrt(2.0 * math.pi))
            dh = (d_act * slope).astype(BF16)
            dh_ref[0, rows, n : n + tile] = dh
            dbias_ref[0, :, n : n + tile] += jnp.sum(dh.astype(F32), axis=0, keepdims=True)

    for side, lhs, rhs in ((0, nmT_ref, dh_ref), (1, cotT_ref, act_ref)):

        @pl.loop(0, width // tile)
        def _(t):
            rows = pl.ds(pl.multiple_of(t * tile, tile), tile)
            g_scr[rows, :] = dot_nn(lhs[rows, :], rhs[0]).astype(BF16)

        hand_out(me_ref, g_scr, 0, gk_ref, gs_ref, side * kept, orders[side], core_bit)


def weight_spec(array, block_of):
    count, _, rows, cols = array.shape
    return pl.BlockSpec((count, 1, rows, cols), lambda s: (0, block_of(s), 0, 0))


def block_part(kernel, k0, count, orders, core_bit, after, me, norm, norm_t, cot, cot_t, left, right, vectors, mid_cols,
               g_cols, scratch, us, into=None):
    length, width = norm.shape
    rows = left[0].shape[2]
    pieces = width // rows
    cols = vectors[0].shape[-1]
    shared = into is not None
    g_blocks = left[0].shape[1] if shared else count
    g_spec = pl.BlockSpec((pieces, 1, rows, g_cols), lambda s: (0, k0 + s if shared else s, 0, 0))
    after = list(after) + list(into or [])
    fixed = 5 + len(left + right) + len(vectors) + len(after)
    return pl.pallas_call(
        functools.partial(kernel, orders, core_bit, len(after)),
        grid=(count,),
        in_specs=[SCALAR, full(length, width), full(width, length), full(length, width), full(width, length)]
        + [weight_spec(w, lambda s: k0 + s) for w in left + right]
        + [pl.BlockSpec((1, 1, cols), lambda s: (k0 + s, 0, 0))]
        + [full(*v.shape) for v in vectors[1:]]
        + [ANY] * len(after),
        out_specs=[pl.BlockSpec((1, length, m), lambda s: (s, 0, 0)) for m in mid_cols]
        + [pl.BlockSpec((1, 1, cols), lambda s: (s, 0, 0))] + [g_spec] * 2,
        out_shape=[shaped((count, length, m), BF16) for m in mid_cols]
        + [shaped((count, 1, cols), F32)] + [shaped((pieces, g_blocks, rows, g_cols), BF16)] * 2,
        input_output_aliases={fixed - 2: len(mid_cols) + 1, fixed - 1: len(mid_cols) + 2} if into else {},
        scratch_shapes=scratch,
        compiler_params=pltpu.CompilerParams(vmem_limit_bytes=60 * 2**20),
        cost_estimate=cost(us * count),
    )(me, norm, norm_t, cot, cot_t, *left, *right, *vectors, *after)


def pick(refs, per_call, scr):
    for n, ref in enumerate(refs):

        @pl.when(pl.program_id(0) // per_call == n)
        def _():
            scr[...] = ref[0]


def attention_tail_kernel(orders, core_bit, calls, per_call, waits, me_ref, *rest):
    left, right, rest = rest[:4], rest[4:8], rest[8:]
    dqkv_refs, mix_refs, rest = rest[:calls], rest[calls : 2 * calls], rest[2 * calls + waits :]
    branch_ref, dna_ref, w_scr, wv_scr, dqkv_scr, mix_scr = rest
    block_cols = w_scr.shape[1]

    @pl.when(pl.program_id(0) == 0)
    def _():
        branch_ref[...] = jnp.zeros_like(branch_ref)
        dna_ref[...] = jnp.zeros_like(dna_ref)

    pick(dqkv_refs, per_call, dqkv_scr)
    pick(mix_refs, per_call, mix_scr)
    assemble(me_ref, left, gathered_order(orders[0], core_bit), w_scr, 0)
    assemble(me_ref, right, gathered_order(orders[1], core_bit), w_scr, block_cols // 2)
    for i in range(block_cols // HEAD):
        wv_scr[:, i * 2 * HD : (i + 1) * 2 * HD] = w_scr[:, i * HEAD + 2 * HD : (i + 1) * HEAD]
    tile = 256

    @pl.loop(0, branch_ref.shape[0] // tile)
    def _(t):
        rows = pl.ds(pl.multiple_of(t * tile, tile), tile)
        branch_ref[rows, :] += dot_nt(mix_scr[rows, :], wv_scr[...])
        dna_ref[rows, :] += dot_nt(dqkv_scr[rows, :], w_scr[...])


def mlp_tail_kernel(orders, core_bit, last, waits, me_ref, *rest):
    left, right, dh_ref, act_ref, rest = rest[:4], rest[4:8], rest[8], rest[9], rest[10:]
    if last:
        branch_in, dnm_in, dna_ref, x_ref, cot_ref, ga_ref, gm_ref, bo_ref, bd_ref = rest[:9]
        block_ref, grad_ref, stats_ref, branch_ref, dnm_ref, wu_scr, wd_scr = rest[9 + waits :]
    else:
        branch_in = rest[0]
        branch_ref, dnm_ref, wu_scr, wd_scr = rest[1 + waits :]
    length = branch_ref.shape[0]
    step = pl.program_id(0)

    @pl.when(step == 0)
    def _():
        branch_ref[...] = branch_in[...]
        dnm_ref[...] = dnm_in[...] if last else jnp.zeros_like(dnm_ref)

    assemble(me_ref, left, gathered_order(orders[0], core_bit), wu_scr, 0)
    assemble(me_ref, right, gathered_order(orders[1], core_bit), wd_scr, 0)
    tile = 256

    @pl.loop(0, length // tile)
    def _(t):
        rows = pl.ds(pl.multiple_of(t * tile, tile), tile)
        branch_ref[rows, :] += dot_nt(act_ref[0, rows, :], wd_scr[...])
        dnm_ref[rows, :] += dot_nt(dh_ref[0, rows, :], wu_scr[...])

    if not last:
        return

    @pl.when(step == pl.num_programs(0) - 1)
    def _():
        stats_ref[...] = jnp.zeros_like(stats_ref)
        small = 128

        @pl.loop(0, length // small)
        def _(t):
            rows = pl.ds(pl.multiple_of(t * small, small), small)
            x = x_ref[rows, :].astype(F32)
            cot = cot_ref[rows, :].astype(F32)
            normed, inv_std = normalize(x)
            block_ref[rows, :] = (x + branch_ref[rows, :] + bo_ref[...] + bd_ref[...]).astype(BF16)
            dna, dnm = dna_ref[rows, :], dnm_ref[rows, :]
            d_normed = dna * ga_ref[...] + dnm * gm_ref[...]
            pulled = (
                d_normed
                - jnp.mean(d_normed, axis=1, keepdims=True)
                - normed * jnp.mean(d_normed * normed, axis=1, keepdims=True)
            )
            grad_ref[rows, :] = (cot + inv_std * pulled).astype(BF16)
            for at, term in enumerate((cot, dna * normed, dna, dnm * normed, dnm)):
                stats_ref[at : at + 1, :] += jnp.sum(term, axis=0, keepdims=True)


def attention_tail_part(block_of, per_call, orders, core_bit, after, me, left, right, mids, outs, scratch, us):
    steps = left[0].shape[1]
    calls = steps // per_call

    def mid_spec(array, n):
        _, length, cols = array.shape
        return pl.BlockSpec((1, length, cols), lambda s: (jnp.clip(s - n * per_call, 0, per_call - 1), 0, 0))

    kept = [pltpu.VMEM(group[0].shape[1:], BF16) for group in mids]
    return pl.pallas_call(
        functools.partial(attention_tail_kernel, orders, core_bit, calls, per_call, len(after)),
        grid=(steps,),
        in_specs=[SCALAR] + [weight_spec(w, block_of) for w in left + right]
        + [mid_spec(array, n) for group in mids for n, array in enumerate(group)] + [ANY] * len(after),
        out_specs=[full(*o.shape) for o in outs],
        out_shape=outs,
        scratch_shapes=scratch + kept,
        compiler_params=pltpu.CompilerParams(vmem_limit_bytes=60 * 2**20),
        cost_estimate=cost(us),
    )(me, *left, *right, *[array for group in mids for array in group], *after)


def mlp_tail_part(k0, last, orders, core_bit, after, me, left, right, dh, act, extra, outs, scratch, us):
    count, length, cols = dh.shape
    mid_spec = pl.BlockSpec((1, length, cols), lambda s: (s, 0, 0))
    return pl.pallas_call(
        functools.partial(mlp_tail_kernel, orders, core_bit, last, len(after)),
        grid=(count,),
        in_specs=[SCALAR] + [weight_spec(w, lambda s: k0 + s) for w in left + right] + [mid_spec] * 2
        + [full(*e.shape) for e in extra] + [ANY] * len(after),
        out_specs=[full(*o.shape) for o in outs],
        out_shape=outs,
        scratch_shapes=scratch,
        compiler_params=pltpu.CompilerParams(vmem_limit_bytes=60 * 2**20),
        cost_estimate=cost(us),
    )(me, *left, *right, dh, act, *extra, *after)


def fence_kernel(*_):
    pass


def fence(values, after=()):
    count = len(values)
    return pl.pallas_call(
        fence_kernel,
        in_specs=[ANY] * (count + len(after)),
        out_specs=[ANY] * count,
        out_shape=[shaped(value.shape, value.dtype) for value in values],
        input_output_aliases={n: n for n in range(count)},
        cost_estimate=cost(1),
    )(*values, *after)


def swap(value, bit):
    axis, flip = ("dp", 1) if bit == 1 else ("row", bit // 2)
    return flipped(value, axis, flip)


def flipped(value, axis, flip):
    return lax.ppermute(value, axis, [(i, i ^ flip) for i in range(lax.axis_size(axis))])


def shifted(value, by):
    size = lax.axis_size("col")
    return lax.ppermute(value, "col", [(i, (i + by) % size) for i in range(size)])


def gather_pieces(own, order, core_bit):
    held = own[None]
    for bit in order[:-1]:
        held = jnp.concatenate([held, swap(held, bit)], axis=0)
    came = swap(held, order[-1])
    return [held, came, swap(held, core_bit), swap(came, core_bit)]


def add(a, b):
    return (a.astype(F32) + b.astype(F32)).astype(BF16)


class Reduction:
    def __init__(self, keep, send, orders, core_bit):
        self.keep, self.orders, self.core_bit = keep, orders, core_bit
        self.moving, self.held, self.done, self.closed = [send], None, -1, False

    def advance(self):
        if self.done < 0:
            self.moving = [swap(self.moving[0], self.core_bit)]
        else:
            if self.done == 0:
                size = self.keep.shape[0] // len(self.orders)
                cuts = [slice(side * size, (side + 1) * size) for side in range(len(self.orders))]
                self.held, self.moving = [self.keep[c] for c in cuts], [self.moving[0][c] for c in cuts]
            half = self.held[0].shape[0] // 2
            sent = [add(a[half:], b[half:]) for a, b in zip(self.held, self.moving)]
            self.held = [add(a[:half], b[:half]) for a, b in zip(self.held, self.moving)]
            self.moving = [swap(one, order[self.done]) for one, order in zip(sent, self.orders)]
        self.done += 1

    def total(self):
        assert self.done == len(self.orders[0])
        return jnp.concatenate([add(a[0], b[0]) for a, b in zip(self.held, self.moving)], axis=2)


def phase(reductions, values=(), after=()):
    values = list(values)
    reductions = [r for r in reductions if not r.closed]
    out = list(fence(values + [one for r in reductions for one in r.moving], after))
    at = len(values)
    for r in reductions:
        r.moving = out[at : at + len(r.moving)]
        at += len(r.moving)
        if r.done < len(r.orders[0]):
            r.advance()
        else:
            r.closed = True
    return out


def all_sum(value):
    for axis in ("row", "dp", "col"):
        flip = 1
        while flip < lax.axis_size(axis):
            value = value + flipped(value, axis, flip)
            flip *= 2
    return value


def on_device(
    tokens_in,
    segment_ids,
    attn_gain,
    attn_shift,
    mlp_gain,
    mlp_shift,
    qkv_weight,
    qkv_bias,
    out_weight,
    out_bias,
    up_weight,
    up_bias,
    down_weight,
    down_bias,
    out_cotangent,
):
    row_size = lax.axis_size("row")
    col_size = lax.axis_size("col")
    length, width = tokens_in.shape
    rows = qkv_weight.shape[0]
    half_rows = rows // 2
    local_heads = qkv_weight.shape[1] // QKV
    block_cols = local_heads * HEAD
    up_cols = up_weight.shape[1]
    row_id = lax.axis_index("row")
    col_id = lax.axis_index("col")
    half = lax.axis_index("dp") % 2
    me = (row_id * 2 + half).reshape(1).astype(jnp.int32)
    row_bits = [2 << i for i in range(row_size.bit_length() - 1)]
    core_bit, far_bits = row_bits[0], row_bits[1:][::-1]
    orders = (far_bits + [1], [1] + far_bits)

    head_weight = jnp.concatenate(
        [qkv_weight.reshape(rows, local_heads, QKV), out_weight.T.reshape(rows, local_heads, HD)], axis=2
    ).reshape(rows, block_cols)
    attn_own = lax.dynamic_slice_in_dim(head_weight, half * half_rows, half_rows, axis=0)
    mlp_own = jnp.concatenate(
        [
            lax.dynamic_slice_in_dim(up_weight, half * half_rows, half_rows, axis=0),
            lax.dynamic_slice_in_dim(down_weight, half * half_rows, half_rows, axis=1).T,
        ],
        axis=1,
    )
    cut = block_cols // 2
    attn_all = jnp.stack([attn_own] + [shifted(attn_own, k) for k in range(1, col_size)])

    seg_row = lax.dynamic_index_in_dim(segment_ids, row_id * col_size + col_id, axis=0, keepdims=False)
    na, na_t, nm, nm_t, cot_t, keep, ahead, behind, mask = prep_part(
        tokens_in, out_cotangent, [v[None, :] for v in (attn_gain, attn_shift, mlp_gain, mlp_shift)], seg_row,
    )
    mlp_own = fence([mlp_own], [attn_all])[0]
    attn_held = [attn_all[None, :, :, :cut], attn_all[None, :, :, cut:]]
    mlp_parts = [shifted(mlp_own, k) for k in range(1, col_size)]
    for at in range(len(orders[0]) - 1):
        came = [swap(one, order[at]) for one, order in zip(attn_held, orders)]
        came = fence(came, [na])
        attn_held = [jnp.concatenate(pair, axis=0) for pair in zip(attn_held, came)]
    came = [swap(one, order[-1]) for one, order in zip(attn_held, orders)]
    over = [swap(one, core_bit) for one in attn_held]
    came = fence(came + mlp_parts, over)
    came, mlp_parts = came[:2], came[2:]
    came_over = [swap(one, core_bit) for one in came]
    attn_left, attn_right = ([attn_held[i], came[i], over[i], came_over[i]] for i in range(2))
    mlp_all = jnp.stack([mlp_own] + list(mlp_parts))
    mlp_held = [mlp_all[None, :, :, :up_cols], mlp_all[None, :, :, up_cols:]]
    for at in range(len(orders[0]) - 1):
        came = [swap(one, order[at]) for one, order in zip(mlp_held, orders)]
        came = fence(came, came_over)
        mlp_held = [jnp.concatenate(pair, axis=0) for pair in zip(mlp_held, came)]

    blocks_here = (col_id - jnp.arange(col_size)) % col_size
    head_bias = jnp.pad(
        qkv_bias.reshape(col_size, local_heads, QKV), ((0, 0), (0, 0), (0, HEAD - QKV))
    ).reshape(col_size, 1, block_cols)
    head_bias = jnp.take(head_bias, blocks_here, axis=0)
    hidden_bias = jnp.take(up_bias.reshape(col_size, 1, up_cols), blocks_here, axis=0)

    per_call = 2
    calls = col_size // per_call
    starts = [k0 for k0 in range(0, col_size, per_call)][::-1]

    def block_of(s):
        return (calls - 1 - s // per_call) * per_call + s % per_call

    def attention_call(k0, after, into):
        return block_part(
            attention_kernel, k0, per_call, orders, core_bit, after, me, na, na_t, out_cotangent, cot_t,
            attn_left, attn_right, [head_bias, keep, ahead, behind, mask], [block_cols, cut], cut,
            [
                pltpu.VMEM((width, block_cols), BF16), pltpu.VMEM((width, cut), BF16),
                pltpu.VMEM((length, block_cols), F32), pltpu.VMEM((length, cut), BF16),
                pltpu.VMEM((width, block_cols), BF16),
            ],
            11, into,
        )

    def mlp_call(k0, after):
        return block_part(
            mlp_kernel, k0, per_call, orders, core_bit, after, me, nm, nm_t, out_cotangent, cot_t,
            up, down, [hidden_bias], [up_cols, up_cols], up_cols, [pltpu.VMEM((width, up_cols), BF16)] * 3, 6,
        )

    came = [swap(one, order[-1]) for one, order in zip(mlp_held, orders)]
    held_over = [swap(one, core_bit) for one in mlp_held]

    attn_calls, into = [], []
    for n, k0 in enumerate(starts):
        outs = attention_call(k0, [mlp_held[0]] if n == 0 else [came[0]], into)
        attn_calls.append(outs[:3])
        into = list(outs[3:])
        if n == 0:
            came = list(fence(came, [outs[2]] + held_over))
            came_over = [swap(one, core_bit) for one in came]
    attn_sum = Reduction(into[0], into[1], orders, core_bit)
    up, down = ([mlp_held[i], came[i], held_over[i], came_over[i]] for i in range(2))

    token = phase([attn_sum], [], came_over)
    mlp_calls, mlp_sums = [], []
    for k0 in starts:
        *mids, g_keep, g_send = mlp_call(k0, token[:1])
        mlp_calls.append(mids)
        mlp_sums.append(Reduction(g_keep, g_send, orders, core_bit))
        token = phase([attn_sum] + mlp_sums, [], [mids[2]])

    branch, d_norm_attn = attention_tail_part(
        block_of, per_call, orders, core_bit, token[:1], me, attn_left, attn_right,
        [[c[0] for c in attn_calls], [c[1] for c in attn_calls]], [shaped((length, width), F32)] * 2,
        [pltpu.VMEM((width, block_cols), BF16), pltpu.VMEM((width, cut), BF16)], 9,
    )
    token = phase([attn_sum] + mlp_sums, [], [branch])
    for n, k0 in enumerate(starts):
        last = n == len(starts) - 1
        extra = [branch]
        outs = [shaped((length, width), F32)] * 2
        scratch = [pltpu.VMEM((width, up_cols), BF16)] * 2
        if n > 0:
            extra.append(d_norm_mlp)
        if last:
            extra += [
                d_norm_attn, tokens_in, out_cotangent, attn_gain[None, :], mlp_gain[None, :], out_bias[None, :],
                down_bias[None, :],
            ]
            scratch = [pltpu.VMEM((length, width), F32)] * 2 + scratch
            outs = [shaped((length, width), BF16)] * 2 + [shaped((8, width), F32)]
        result = mlp_tail_part(
            k0, last, orders, core_bit, token[:1], me, up, down, mlp_calls[n][1], mlp_calls[n][0], extra, outs, scratch, 9
        )
        if last:
            block_out, in_grad, stats = result
            stats = phase([attn_sum] + mlp_sums, [stats])[0]
        else:
            branch, d_norm_mlp = result
            token = phase([attn_sum] + mlp_sums, [], [branch])

    attn_total = attn_sum.total()
    total = None
    for k0, one in zip(starts, [r.total() for r in mlp_sums]):
        for i in range(per_call):
            part = jnp.concatenate([attn_total[k0 + i], one[i]], axis=1)
            term = (part if k0 + i == 0 else shifted(part, -(k0 + i))).astype(F32)
            total = term if total is None else total + term
    flip = 2
    while flip < lax.axis_size("dp"):
        total = total + flipped(total, "dp", flip)
        flip *= 2
    mine = total.astype(BF16)
    other = swap(mine, 1)
    first = half == 0
    grads = jnp.concatenate([jnp.where(first, mine, other), jnp.where(first, other, mine)], axis=0).astype(F32)
    g_heads = grads[:, :block_cols].reshape(rows, local_heads, HEAD)
    g_mlp = grads[:, block_cols:]

    d_bias_up = jnp.take(jnp.concatenate([c[2] for c in mlp_calls[::-1]]), blocks_here, axis=0)
    d_bias_attn = jnp.take(jnp.concatenate([c[2] for c in attn_calls[::-1]]), blocks_here, axis=0)
    smalls = jnp.concatenate(
        [
            stats[:5].reshape(-1),
            d_bias_up.reshape(-1),
            d_bias_attn.reshape(col_size * local_heads, HEAD)[:, :QKV].reshape(-1),
        ]
    )
    smalls = all_sum(smalls.reshape(-1, 128)).reshape(-1)
    stats = smalls[: 5 * width].reshape(5, width)
    grad_up_bias = smalls[5 * width : 5 * width + up_bias.shape[0]]
    grad_qkv_bias = smalls[5 * width + up_bias.shape[0] :]
    return (
        block_out,
        in_grad,
        stats[1],
        stats[2],
        stats[3],
        stats[4],
        g_heads[:, :, :QKV].reshape(rows, local_heads * QKV),
        grad_qkv_bias,
        g_heads[:, :, QKV:].reshape(rows, local_heads * HD).T,
        stats[0],
        g_mlp[:, :up_cols],
        grad_up_bias,
        g_mlp[:, up_cols:].T,
        stats[0],
    )


def solution(mesh):
    return jax.shard_map(
        on_device,
        mesh=mesh,
        in_specs=(
            P(("dp", "row", "col"), None),
            P("dp", None),
            P(),
            P(),
            P(),
            P(),
            P("row", "col"),
            P(),
            P("col", "row"),
            P(),
            P("row", "col"),
            P(),
            P("col", "row"),
            P(),
            P(("dp", "row", "col"), None),
        ),
        out_specs=(
            P(("dp", "row", "col"), None),
            P(("dp", "row", "col"), None),
            P(),
            P(),
            P(),
            P(),
            P("row", "col"),
            P(),
            P("col", "row"),
            P(),
            P("row", "col"),
            P(),
            P("col", "row"),
            P(),
        ),
        check_vma=False,
    )
```

```python
import functools
import math

import jax
import jax.numpy as jnp
from jax import lax
from jax.experimental import pallas as pl
from jax.experimental.pallas import tpu as pltpu
from jax.sharding import PartitionSpec as P

HD = 64
ROT = 16
QKV = 3 * HD
HEAD = 4 * HD
EPSILON = 1e-05
ROPE_BASE = 10000.0
NEAR = 256
LONGEST = 256
F32 = jnp.float32
BF16 = jnp.bfloat16


def dot_nn(a, b):
    return lax.dot_general(a, b, (((1,), (0,)), ((), ())), preferred_element_type=F32)


def dot_nt(a, b):
    return lax.dot_general(a, b, (((1,), (1,)), ((), ())), preferred_element_type=F32)


def gathered_order(order, core_bit):
    held = [0]
    for bit in order[:-1]:
        held = held + [j | bit for j in held]
    came = [j | order[-1] for j in held]
    return held, came, [j | core_bit for j in held], [j | core_bit for j in came]


def reduced_order(order):
    kept = [0]
    for bit in order[::-1]:
        kept = kept + [j | bit for j in kept]
    return kept


def assemble(me_ref, w_refs, held, w_scr, at_col):
    for ref, pieces in zip(w_refs, held):
        _, _, rows, cols = ref.shape
        for t, j in enumerate(pieces):
            at = pl.multiple_of((me_ref[0] ^ j) * rows, 16)
            w_scr[pl.ds(at, rows), at_col : at_col + cols] = ref[t, 0]


def hand_out(me_ref, g_scr, at_col, keep_ref, send_ref, first, order, core_bit):
    _, slots, rows, cols = keep_ref.shape
    for t, j in enumerate(reduced_order(order)):
        for ref, piece in ((keep_ref, j), (send_ref, j | core_bit)):
            at = pl.multiple_of((me_ref[0] ^ piece) * rows, 16)
            for slot in range(slots):
                left = at_col + slot * cols
                ref[first + t, slot] = g_scr[pl.ds(at, rows), left : left + cols]


def normalize(x):
    center = x - jnp.mean(x, axis=1, keepdims=True)
    inv_std = lax.rsqrt(jnp.mean(center * center, axis=1, keepdims=True) + EPSILON)
    return center * inv_std, inv_std


def prep_kernel(
    x_ref, cot_ref, ga_ref, sa_ref, gm_ref, sm_ref, segc_ref, segr_ref, freq_ref,
    na_ref, naT_ref, nm_ref, nmT_ref, cotT_ref, keep_ref, ahead_ref, behind_ref, mask_ref,
):
    length = x_ref.shape[0]
    tile = 128

    @pl.loop(0, length // tile)
    def _(t):
        rows = pl.ds(pl.multiple_of(t * tile, tile), tile)
        normed, _ = normalize(x_ref[rows, :].astype(F32))
        na_ref[rows, :] = (normed * ga_ref[...] + sa_ref[...]).astype(BF16)
        nm_ref[rows, :] = (normed * gm_ref[...] + sm_ref[...]).astype(BF16)
        same = segc_ref[rows, :] == segr_ref[...]
        cols = lax.broadcasted_iota(jnp.int32, (tile, length), 1)
        ids = lax.broadcasted_iota(jnp.int32, (tile, length), 0) + t * tile
        mask_ref[rows, :] = jnp.where(same & (cols <= ids), 0.0, -jnp.inf)
        starts = jnp.min(jnp.where(same, cols, length).astype(F32), axis=1, keepdims=True)
        places = ids[:, :1].astype(F32) - starts
        angles = places * freq_ref[...]
        lane = lax.broadcasted_iota(jnp.int32, (tile, 2 * HD), 1) % HD
        cosine, sine = jnp.cos(angles), jnp.sin(angles)
        keep_ref[rows, :] = jnp.where(lane < ROT, cosine, 1.0)
        ahead_ref[rows, :] = jnp.where(lane < ROT // 2, -sine, 0.0)
        behind_ref[rows, :] = jnp.where((lane < ROT) & (lane >= ROT // 2), sine, 0.0)

    naT_ref[...] = na_ref[...].T
    nmT_ref[...] = nm_ref[...].T
    cotT_ref[...] = cot_ref[...].T


def full(*shape):
    return pl.BlockSpec(shape, lambda *_: (0,) * len(shape), pipeline_mode=pl.Buffered(1))


ANY = pl.BlockSpec(memory_space=pl.ANY)
SCALAR = pl.BlockSpec(memory_space=pltpu.SMEM)


def cost(us):
    return pl.CostEstimate(flops=int(us * 1.15e9), bytes_accessed=2**20, transcendentals=0)


def shaped(shape, dtype):
    return jax.ShapeDtypeStruct(shape, dtype)


def prep_part(tokens, cot, gains, seg_row):
    length, width = tokens.shape
    halves = ROT // 2
    step = (lax.iota(jnp.int32, 2 * HD) % HD % halves).astype(F32)
    freq = (ROPE_BASE ** (-(step * (2.0 / ROT))))[None, :]
    table = shaped((length, 2 * HD), F32)
    return pl.pallas_call(
        prep_kernel,
        grid=(1,),
        in_specs=[full(length, width)] * 2 + [full(1, width)] * 4
        + [full(length, 1), full(1, length), full(1, 2 * HD)],
        out_specs=[full(length, width), full(width, length)] * 2 + [full(width, length)]
        + [full(length, 2 * HD)] * 3 + [full(length, length)],
        out_shape=[shaped((length, width), BF16), shaped((width, length), BF16)] * 2
        + [shaped((width, length), BF16)] + [table] * 3 + [shaped((length, length), F32)],
        compiler_params=pltpu.CompilerParams(vmem_limit_bytes=60 * 2**20),
        cost_estimate=cost(6),
    )(tokens, cot, *gains, seg_row[:, None], seg_row[None, :], freq)


def attention_kernel(orders, core_bit, waits, me_ref, na_ref, naT_ref, cot_ref, cotT_ref, *rest):
    left, right, rest = rest[:4], rest[4:8], rest[8:]
    bias_ref, keep_ref, ahead_ref, behind_ref, mask_ref = rest[:5]
    dqkv_ref, mix_ref, dbias_ref, gk_ref, gs_ref, w_scr, wv_scr, qkv_scr, dattn_scr, g_scr = rest[5 + waits :]
    length, width = na_ref.shape
    block_cols = w_scr.shape[1]
    heads = block_cols // HEAD
    kept = gk_ref.shape[0] // 2
    tile = 256
    assemble(me_ref, left, gathered_order(orders[0], core_bit), w_scr, 0)
    assemble(me_ref, right, gathered_order(orders[1], core_bit), w_scr, block_cols // 2)
    for i in range(heads):
        wv_scr[:, i * 2 * HD : (i + 1) * 2 * HD] = w_scr[:, i * HEAD + 2 * HD : (i + 1) * HEAD]

    @pl.loop(0, length // tile)
    def _(t):
        rows = pl.ds(pl.multiple_of(t * tile, tile), tile)
        qkv_scr[rows, :] = dot_nn(na_ref[rows, :], w_scr[...]) + bias_ref[0]
        dattn_scr[rows, :] = dot_nn(cot_ref[rows, :], wv_scr[...]).astype(BF16)

    low = lax.broadcasted_iota(jnp.int32, (length, 2 * HD), 1) < HD
    keep, ahead, behind = keep_ref[...], ahead_ref[...], behind_ref[...]
    none = jnp.zeros((length, 2 * HD), BF16)
    spans = [(b * NEAR, (b + 1) * NEAR, max(0, b * NEAR - LONGEST)) for b in range(length // NEAR)]
    for i in range(heads):
        qk = qkv_scr[:, i * HEAD : i * HEAD + 2 * HD]
        qk = qk * keep + pltpu.roll(qk, 2 * HD - ROT // 2, 1) * ahead + pltpu.roll(qk, ROT // 2, 1) * behind
        q0 = jnp.where(low, qk * (1.0 / math.sqrt(HD)), 0.0).astype(BF16)
        k0 = jnp.where(low, pltpu.roll(qk, HD, 1), 0.0).astype(BF16)
        v1 = jnp.where(low, 0.0, pltpu.roll(qkv_scr[:, i * HEAD + 2 * HD : (i + 1) * HEAD], HD, 1)).astype(BF16)
        go = dattn_scr[:, i * 2 * HD : (i + 1) * 2 * HD]
        go1 = jnp.where(low, none, go)
        qT = q0.T[:HD]
        goT = go.T[HD:]
        s = [dot_nt(q0[r0:r1], k0[lo:r1]) + mask_ref[r0:r1, lo:r1] for r0, r1, lo in spans]
        dp = [dot_nt(go1[r0:r1], v1[lo:r1]) for r0, r1, lo in spans]
        peak = [jnp.max(one, axis=1, keepdims=True) for one in s]
        e = [jnp.exp(one - top) for one, top in zip(s, peak)]
        norm = [1.0 / jnp.sum(one, axis=1, keepdims=True) for one in e]
        p = [one * scale for one, scale in zip(e, norm)]
        p_low = [one.astype(BF16) for one in p]
        mix = [dot_nn(one, v1[lo:r1]) for one, (r0, r1, lo) in zip(p_low, spans)]
        delta = [
            jnp.sum(one * go1[r0:r1].astype(F32), axis=1, keepdims=True) for one, (r0, r1, lo) in zip(mix, spans)
        ]
        ds = [(one * (grad - centre)).astype(BF16) for one, grad, centre in zip(p, dp, delta)]
        dq = [dot_nn(one, k0[lo:r1]) for one, (r0, r1, lo) in zip(ds, spans)]
        dkT = [dot_nn(qT[:, r0:r1], one) for one, (r0, r1, lo) in zip(ds, spans)]
        dvT = [dot_nn(goT[:, r0:r1], one) for one, (r0, r1, lo) in zip(p_low, spans)]
        sums = []
        for parts in (dvT, dkT):
            total = [None] * len(spans)
            for part, (r0, r1, lo) in zip(parts, spans):
                for n in range(lo // NEAR, r1 // NEAR):
                    one = part[:, n * NEAR - lo : (n + 1) * NEAR - lo]
                    total[n] = one if total[n] is None else total[n] + one
            sums.append(jnp.concatenate(total, axis=1))
        dvk = jnp.concatenate(sums, axis=0).T
        dqk = jnp.where(low, jnp.concatenate(dq, axis=0) * (1.0 / math.sqrt(HD)), dvk)
        dqk = dqk * keep - pltpu.roll(dqk, 2 * HD - ROT // 2, 1) * ahead - pltpu.roll(dqk, ROT // 2, 1) * behind
        dqkv_ref[0, :, i * HEAD : i * HEAD + 2 * HD] = dqk.astype(BF16)
        dqkv_ref[0, :, i * HEAD + 2 * HD : (i + 1) * HEAD] = jnp.where(low, dvk, 0.0).astype(BF16)
        mix_ref[0, :, i * 2 * HD : (i + 1) * 2 * HD] = jnp.concatenate(mix, axis=0).astype(BF16)

    dbias_ref[0] = jnp.sum(dqkv_ref[0].astype(F32), axis=0, keepdims=True)

    @pl.loop(0, width // tile)
    def _(t):
        rows = pl.ds(pl.multiple_of(t * tile, tile), tile)
        g_in = dot_nn(naT_ref[rows, :], dqkv_ref[0])
        g_out = dot_nn(cotT_ref[rows, :], mix_ref[0])
        for i in range(heads):
            at = i * HEAD
            g_scr[rows, at : at + 2 * HD] = g_in[:, at : at + 2 * HD].astype(BF16)
            g_scr[rows, at + 2 * HD : at + HEAD] = (
                g_in[:, at + 2 * HD : at + HEAD] + g_out[:, i * 2 * HD : (i + 1) * 2 * HD]
            ).astype(BF16)

    hand_out(me_ref, g_scr, 0, gk_ref, gs_ref, 0, orders[0], core_bit)
    hand_out(me_ref, g_scr, block_cols // 2, gk_ref, gs_ref, kept, orders[1], core_bit)


def mlp_kernel(orders, core_bit, waits, me_ref, nm_ref, nmT_ref, cot_ref, cotT_ref, *rest):
    left, right, bias_ref, rest = rest[:4], rest[4:8], rest[8], rest[9 + waits :]
    act_ref, dh_ref, dbias_ref, gk_ref, gs_ref, wu_scr, wd_scr, g_scr = rest
    length, width = nm_ref.shape
    up_cols = wu_scr.shape[1]
    kept = gk_ref.shape[0] // 2
    tile = 256
    assemble(me_ref, left, gathered_order(orders[0], core_bit), wu_scr, 0)
    assemble(me_ref, right, gathered_order(orders[1], core_bit), wd_scr, 0)
    dbias_ref[0] = jnp.zeros_like(dbias_ref[0])

    @pl.loop(0, length // tile)
    def _(t):
        rows = pl.ds(pl.multiple_of(t * tile, tile), tile)
        for n in range(0, up_cols, tile):
            hidden = dot_nn(nm_ref[rows, :], wu_scr[:, n : n + tile]) + bias_ref[0, :, n : n + tile]
            d_act = dot_nn(cot_ref[rows, :], wd_scr[:, n : n + tile])
            gate = 0.5 * (1.0 + lax.erf(hidden * (1.0 / math.sqrt(2.0))))
            act_ref[0, rows, n : n + tile] = (hidden * gate).astype(BF16)
            slope = gate + hidden * jnp.exp(-0.5 * hidden * hidden) * (1.0 / math.sqrt(2.0 * math.pi))
            dh = (d_act * slope).astype(BF16)
            dh_ref[0, rows, n : n + tile] = dh
            dbias_ref[0, :, n : n + tile] += jnp.sum(dh.astype(F32), axis=0, keepdims=True)

    for side, lhs, rhs in ((0, nmT_ref, dh_ref), (1, cotT_ref, act_ref)):

        @pl.loop(0, width // tile)
        def _(t):
            rows = pl.ds(pl.multiple_of(t * tile, tile), tile)
            g_scr[rows, :] = dot_nn(lhs[rows, :], rhs[0]).astype(BF16)

        hand_out(me_ref, g_scr, 0, gk_ref, gs_ref, side * kept, orders[side], core_bit)


def weight_spec(array, block_of):
    count, _, rows, cols = array.shape
    return pl.BlockSpec((count, 1, rows, cols), lambda s: (0, block_of(s), 0, 0))


def block_part(kernel, w0, k0, count, slots, slot0, into, orders, core_bit, after, me, norm, norm_t, cot, cot_t,
               left, right, vectors, mid_cols, g_cols, scratch, us):
    length, width = norm.shape
    rows = left[0].shape[2]
    pieces = width // rows
    cols = vectors[0].shape[-1]
    per_step, total_slots = slots
    g_spec = pl.BlockSpec((pieces, per_step, rows, g_cols), lambda s: (0, slot0 + s, 0, 0))
    after = list(after) + list(into)
    fixed = 5 + len(left + right) + len(vectors) + len(after)
    return pl.pallas_call(
        functools.partial(kernel, orders, core_bit, len(after)),
        grid=(count,),
        in_specs=[SCALAR, full(length, width), full(width, length), full(length, width), full(width, length)]
        + [weight_spec(w, lambda s: w0 + s) for w in left + right]
        + [pl.BlockSpec((1, 1, cols), lambda s: (k0 + s, 0, 0))]
        + [full(*v.shape) for v in vectors[1:]]
        + [ANY] * len(after),
        out_specs=[pl.BlockSpec((1, length, m), lambda s: (s, 0, 0)) for m in mid_cols]
        + [pl.BlockSpec((1, 1, cols), lambda s: (s, 0, 0))] + [g_spec] * 2,
        out_shape=[shaped((count, length, m), BF16) for m in mid_cols]
        + [shaped((count, 1, cols), F32)] + [shaped((pieces, total_slots, rows, g_cols), BF16)] * 2,
        input_output_aliases={fixed - 2: len(mid_cols) + 1, fixed - 1: len(mid_cols) + 2} if into else {},
        scratch_shapes=scratch,
        compiler_params=pltpu.CompilerParams(vmem_limit_bytes=60 * 2**20),
        cost_estimate=cost(us * count),
    )(me, norm, norm_t, cot, cot_t, *left, *right, *vectors, *after)


def pick(refs, begins, scr):
    step = pl.program_id(0)
    for ref, begin, end in zip(refs, begins, begins[1:]):

        @pl.when((step >= begin) & (step < end))
        def _():
            scr[...] = ref[0]


def attention_tail_kernel(orders, core_bit, begins, waits, me_ref, *rest):
    left, right, rest = rest[:4], rest[4:8], rest[8:]
    calls = len(begins) - 1
    dqkv_refs, mix_refs, rest = rest[:calls], rest[calls : 2 * calls], rest[2 * calls :]
    sums_in, rest = rest[: len(rest) - waits - 6], rest[len(rest) - 6 :]
    branch_ref, dna_ref, w_scr, wv_scr, dqkv_scr, mix_scr = rest
    block_cols = w_scr.shape[1]

    @pl.when(pl.program_id(0) == 0)
    def _():
        branch_ref[...] = sums_in[0][...]
        dna_ref[...] = sums_in[1][...] if len(sums_in) > 1 else jnp.zeros_like(dna_ref)

    pick(dqkv_refs, begins, dqkv_scr)
    pick(mix_refs, begins, mix_scr)
    assemble(me_ref, left, gathered_order(orders[0], core_bit), w_scr, 0)
    assemble(me_ref, right, gathered_order(orders[1], core_bit), w_scr, block_cols // 2)
    for i in range(block_cols // HEAD):
        wv_scr[:, i * 2 * HD : (i + 1) * 2 * HD] = w_scr[:, i * HEAD + 2 * HD : (i + 1) * HEAD]
    tile = 256

    @pl.loop(0, branch_ref.shape[0] // tile)
    def _(t):
        rows = pl.ds(pl.multiple_of(t * tile, tile), tile)
        branch_ref[rows, :] += dot_nt(mix_scr[rows, :], wv_scr[...])
        dna_ref[rows, :] += dot_nt(dqkv_scr[rows, :], w_scr[...])


def mlp_tail_kernel(orders, core_bit, sums, small_ks, waits, me_ref, *rest):
    left, right, dh_ref, act_ref, rest = rest[:4], rest[4:8], rest[8], rest[9], rest[10:]
    sums_in, rest = rest[:sums], rest[sums:]
    last = small_ks is not None
    if last:
        dna_ref, x_ref, cot_ref, ga_ref, gm_ref, bo_ref, bd_ref = rest[:7]
        small_refs = rest[7 : 7 + len(small_ks)]
        block_ref, grad_ref, stats_ref, branch_ref, dnm_ref, wu_scr, wd_scr = rest[7 + len(small_ks) + waits :]
    else:
        branch_ref, dnm_ref, wu_scr, wd_scr = rest[waits:]
    length = branch_ref.shape[0]
    step = pl.program_id(0)

    @pl.when(step == 0)
    def _():
        branch_ref[...] = sums_in[0][...] if sums else jnp.zeros_like(branch_ref)
        dnm_ref[...] = sums_in[1][...] if sums else jnp.zeros_like(dnm_ref)

    assemble(me_ref, left, gathered_order(orders[0], core_bit), wu_scr, 0)
    assemble(me_ref, right, gathered_order(orders[1], core_bit), wd_scr, 0)
    tile = 256

    @pl.loop(0, length // tile)
    def _(t):
        rows = pl.ds(pl.multiple_of(t * tile, tile), tile)
        branch_ref[rows, :] += dot_nt(act_ref[0, rows, :], wd_scr[...])
        dnm_ref[rows, :] += dot_nt(dh_ref[0, rows, :], wu_scr[...])

    if not last:
        return

    @pl.when(step == pl.num_programs(0) - 1)
    def _():
        stats_ref[...] = jnp.zeros_like(stats_ref)
        small = 128

        @pl.loop(0, length // small)
        def _(t):
            rows = pl.ds(pl.multiple_of(t * small, small), small)
            x = x_ref[rows, :].astype(F32)
            cot = cot_ref[rows, :].astype(F32)
            normed, inv_std = normalize(x)
            block_ref[rows, :] = (x + branch_ref[rows, :] + bo_ref[...] + bd_ref[...]).astype(BF16)
            dna, dnm = dna_ref[rows, :], dnm_ref[rows, :]
            d_normed = dna * ga_ref[...] + dnm * gm_ref[...]
            pulled = (
                d_normed
                - jnp.mean(d_normed, axis=1, keepdims=True)
                - normed * jnp.mean(d_normed * normed, axis=1, keepdims=True)
            )
            grad_ref[rows, :] = (cot + inv_std * pulled).astype(BF16)
            for at, term in enumerate((cot, dna * normed, dna, dnm * normed, dnm)):
                stats_ref[at : at + 1, :] += jnp.sum(term, axis=0, keepdims=True)

        for ref, (first, k0, blocks) in zip(small_refs, small_ks):
            for i in range(ref.shape[0]):
                block = lax.rem(me_ref[1] + (blocks - k0 - i), blocks)
                stats_ref[pl.ds(first + block, 1), :] = ref[i]


def attention_tail_part(begins, orders, core_bit, after, me, left, right, mids, sums, us):
    steps = left[0].shape[1]
    pieces = 2 * sum(w.shape[0] for w in left) // 2
    width = pieces * left[0].shape[2]
    length = sums[0].shape[0]

    def mid_spec(array, n):
        begin, end = begins[n], begins[n + 1]
        return pl.BlockSpec(
            (1,) + array.shape[1:], lambda s: (jnp.clip(s - begin, 0, end - begin - 1), 0, 0)
        )

    block_cols, half_cols = mids[0][0].shape[2], mids[1][0].shape[2]
    outs = [shaped((length, width), F32)] * 2
    return pl.pallas_call(
        functools.partial(attention_tail_kernel, orders, core_bit, begins, len(after)),
        grid=(steps,),
        in_specs=[SCALAR] + [weight_spec(w, lambda s: s) for w in left + right]
        + [mid_spec(array, n) for group in mids for n, array in enumerate(group)]
        + [full(*e.shape) for e in sums] + [ANY] * len(after),
        out_specs=[full(*o.shape) for o in outs],
        out_shape=outs,
        scratch_shapes=[pltpu.VMEM((width, block_cols), BF16), pltpu.VMEM((width, half_cols), BF16)]
        + [pltpu.VMEM(group[0].shape[1:], BF16) for group in mids],
        compiler_params=pltpu.CompilerParams(vmem_limit_bytes=60 * 2**20),
        cost_estimate=cost(us),
    )(me, *left, *right, *[array for group in mids for array in group], *sums, *after)


def mlp_tail_part(w0, orders, core_bit, after, me, left, right, act, dh, sums, finals, smalls, us):
    count, length, cols = dh.shape
    width = sum(w.shape[0] for w in left) * left[0].shape[2]
    mid_spec = pl.BlockSpec((1, length, cols), lambda s: (s, 0, 0))
    total = shaped((length, width), F32)
    scratch = [pltpu.VMEM((width, cols), BF16)] * 2
    outs, small_ks = [total] * 2, None
    if finals:
        small_ks, arrays = smalls
        blocks = small_ks[0][2]
        outs = [shaped((length, width), BF16)] * 2 + [shaped((-(-(5 + 2 * blocks) // 8) * 8, width), F32)]
        scratch = [pltpu.VMEM((length, width), F32)] * 2 + scratch
        finals = list(finals) + list(arrays)
    extra = list(sums) + list(finals)
    return pl.pallas_call(
        functools.partial(mlp_tail_kernel, orders, core_bit, len(sums), small_ks, len(after)),
        grid=(count,),
        in_specs=[SCALAR] + [weight_spec(w, lambda s: w0 + s) for w in left + right] + [mid_spec] * 2
        + [full(*e.shape) for e in extra] + [ANY] * len(after),
        out_specs=[full(*o.shape) for o in outs],
        out_shape=outs,
        scratch_shapes=scratch,
        compiler_params=pltpu.CompilerParams(vmem_limit_bytes=60 * 2**20),
        cost_estimate=cost(us),
    )(me, *left, *right, dh, act, *extra, *after)


def fence_kernel(*_):
    pass


def fence(values, after=()):
    count = len(values)
    return pl.pallas_call(
        fence_kernel,
        in_specs=[ANY] * (count + len(after)),
        out_specs=[ANY] * count,
        out_shape=[shaped(value.shape, value.dtype) for value in values],
        input_output_aliases={n: n for n in range(count)},
        cost_estimate=cost(1),
    )(*values, *after)


def swap(value, bit):
    axis, flip = ("dp", 1) if bit == 1 else ("row", bit // 2)
    return flipped(value, axis, flip)


def flipped(value, axis, flip):
    return lax.ppermute(value, axis, [(i, i ^ flip) for i in range(lax.axis_size(axis))])


def shifted(value, by):
    size = lax.axis_size("col")
    return lax.ppermute(value, "col", [(i, (i + by) % size) for i in range(size)])


class Gather:
    def __init__(self, blocks, orders, core_bit):
        cut = blocks.shape[2] // 2
        self.orders, self.core_bit, self.done = orders, core_bit, 0
        self.block = blocks[0]
        self.held = [blocks[None, :, :, :cut], blocks[None, :, :, cut:]]

    def advance(self):
        if self.done > 0:
            self.held = [jnp.concatenate(pair, axis=0) for pair in zip(self.held, self.moving)]
        self.moving = [swap(one, order[self.done]) for one, order in zip(self.held, self.orders)]
        self.done += 1

    def cross(self):
        self.over = [swap(one, self.core_bit) for one in self.held + self.moving]

    def sides(self):
        return ([self.held[i], self.moving[i], self.over[i], self.over[i + 2]] for i in range(2))


def add(a, b):
    return (a.astype(F32) + b.astype(F32)).astype(BF16)


class Reduction:
    def __init__(self, keep, send, orders, core_bit):
        self.keep, self.orders, self.core_bit = keep, orders, core_bit
        self.moving, self.held, self.done = [send], None, -1

    def advance(self):
        if self.done < 0:
            self.moving = [swap(self.moving[0], self.core_bit)]
        else:
            if self.done == 0:
                size = self.keep.shape[0] // len(self.orders)
                cuts = [slice(side * size, (side + 1) * size) for side in range(len(self.orders))]
                self.held, self.moving = [self.keep[c] for c in cuts], [self.moving[0][c] for c in cuts]
            half = self.held[0].shape[0] // 2
            sent = [add(a[half:], b[half:]) for a, b in zip(self.held, self.moving)]
            self.held = [add(a[:half], b[:half]) for a, b in zip(self.held, self.moving)]
            self.moving = [swap(one, order[self.done]) for one, order in zip(sent, self.orders)]
        self.done += 1

    def total(self):
        assert self.done == len(self.orders[0])
        return jnp.concatenate([add(a[0], b[0]) for a, b in zip(self.held, self.moving)], axis=2)


def phase(users, values=(), after=()):
    values = list(values)
    out = list(fence(values + [one for user in users for one in user.moving], after))
    at = len(values)
    for user in users:
        user.moving = out[at : at + len(user.moving)]
        at += len(user.moving)
    return out


def sum_over(value, axes):
    for axis in axes:
        flip = 1
        while flip < lax.axis_size(axis):
            value = value + flipped(value, axis, flip)
            flip *= 2
    return value


def on_device(
    tokens_in,
    segment_ids,
    attn_gain,
    attn_shift,
    mlp_gain,
    mlp_shift,
    qkv_weight,
    qkv_bias,
    out_weight,
    out_bias,
    up_weight,
    up_bias,
    down_weight,
    down_bias,
    out_cotangent,
):
    row_size = lax.axis_size("row")
    col_size = lax.axis_size("col")
    length, width = tokens_in.shape
    rows = qkv_weight.shape[0]
    half_rows = rows // 2
    local_heads = qkv_weight.shape[1] // QKV
    block_cols = local_heads * HEAD
    up_cols = up_weight.shape[1]
    row_id = lax.axis_index("row")
    col_id = lax.axis_index("col")
    half = lax.axis_index("dp") % 2
    me = jnp.stack([row_id * 2 + half, col_id]).astype(jnp.int32)
    row_bits = [2 << i for i in range(row_size.bit_length() - 1)]
    core_bit, far_bits = row_bits[0], row_bits[1:][::-1]
    orders = (far_bits + [1], [1] + far_bits)

    head_weight = jnp.concatenate(
        [qkv_weight.reshape(rows, local_heads, QKV), out_weight.T.reshape(rows, local_heads, HD)], axis=2
    ).reshape(rows, block_cols)
    attn_own = lax.dynamic_slice_in_dim(head_weight, half * half_rows, half_rows, axis=0)
    mlp_own = jnp.concatenate(
        [
            lax.dynamic_slice_in_dim(up_weight, half * half_rows, half_rows, axis=0),
            lax.dynamic_slice_in_dim(down_weight, half * half_rows, half_rows, axis=1).T,
        ],
        axis=1,
    )
    cut = block_cols // 2

    seg_row = lax.dynamic_index_in_dim(segment_ids, row_id * col_size + col_id, axis=0, keepdims=False)
    na, na_t, nm, nm_t, cot_t, keep, ahead, behind, mask = prep_part(
        tokens_in, out_cotangent, [v[None, :] for v in (attn_gain, attn_shift, mlp_gain, mlp_shift)], seg_row,
    )
    blocks_here = (col_id - jnp.arange(col_size)) % col_size
    head_bias = jnp.pad(
        qkv_bias.reshape(col_size, local_heads, QKV), ((0, 0), (0, 0), (0, HEAD - QKV))
    ).reshape(col_size, 1, block_cols)
    head_bias = jnp.take(head_bias, blocks_here, axis=0)
    hidden_bias = jnp.take(up_bias.reshape(col_size, 1, up_cols), blocks_here, axis=0)

    others = range(1, col_size)
    far = len(orders[0])
    attn_own, mlp_own = Gather(attn_own[None], orders, core_bit), Gather(mlp_own[None], orders, core_bit)
    attn_blocks = [shifted(attn_own.block, k) for k in others]
    for _ in range(far):
        attn_own.advance()
        mlp_own.advance()
        first = attn_own.done == 1
        phase([attn_own, mlp_own], [], [na] if first else [])
    attn_own.cross()
    mlp_own.cross()
    gathered = fence(attn_blocks, attn_own.over)
    attn_rest = Gather(jnp.stack(gathered), orders, core_bit)
    mlp_block = fence([mlp_own.block], gathered[:1])[0]
    mlp_blocks = [shifted(mlp_block, k) for k in others]
    attn_rest.advance()

    def attention_call(weights, w0, k0, count, slots, slot0, into, after):
        return block_part(
            attention_kernel, w0, k0, count, slots, slot0, into, orders, core_bit, after, me, na, na_t, out_cotangent,
            cot_t, *weights.sides(), [head_bias, keep, ahead, behind, mask], [block_cols, cut], cut,
            [
                pltpu.VMEM((width, block_cols), BF16), pltpu.VMEM((width, cut), BF16),
                pltpu.VMEM((length, block_cols), F32), pltpu.VMEM((length, cut), BF16),
                pltpu.VMEM((width, block_cols), BF16),
            ],
            10,
        )

    def mlp_call(weights, w0, k0, count, slots, slot0, into, after):
        return block_part(
            mlp_kernel, w0, k0, count, slots, slot0, into, orders, core_bit, after, me, nm, nm_t, out_cotangent, cot_t,
            *weights.sides(), [hidden_bias], [up_cols, up_cols], cut, [pltpu.VMEM((width, up_cols), BF16)] * 3, 6,
        )

    per_mlp = up_cols // cut
    own_slots = per_mlp + 1
    rest = col_size - 1
    a0 = attention_call(attn_own, 0, 0, 1, (1, own_slots), per_mlp, [], [gathered[0]])
    token = phase([attn_rest], [], [a0[2]])
    while attn_rest.done < far:
        attn_rest.advance()
        if attn_rest.done < far:
            token = phase([attn_rest])
    m0 = mlp_call(mlp_own, 0, 0, 1, (per_mlp, own_slots), 0, a0[3:], token[:1])
    own_sum = Reduction(m0[3], m0[4], orders, core_bit)
    mlp_blocks = phase([attn_rest], mlp_blocks, [m0[2]])[:rest]
    attn_rest.cross()
    mlp_rest = Gather(jnp.stack(mlp_blocks), orders, core_bit)
    mlp_rest.advance()
    own_sum.advance()
    branch, d_norm_mlp = mlp_tail_part(
        0, orders, core_bit, mlp_blocks[:1], me, *mlp_own.sides(), m0[0], m0[1], [], [], None, 4
    )
    token = fence([branch], attn_rest.over)
    branch = token[0]
    a1 = attention_call(attn_rest, 0, 1, 1, (1, rest), 0, [], token)
    token = phase([mlp_rest, own_sum], [], [a1[2]])
    while mlp_rest.done < far:
        mlp_rest.advance()
        if mlp_rest.done < far:
            token = phase([mlp_rest])
    own_sum.advance()
    a2 = attention_call(attn_rest, 1, 2, rest - 1, (1, rest), 1, a1[3:], token[:1])
    attn_sum = Reduction(a2[3], a2[4], orders, core_bit)
    token = phase([mlp_rest, own_sum, attn_sum])
    mlp_rest.cross()
    attn_sum.advance()
    branch, d_norm_attn = attention_tail_part(
        [0, 1], orders, core_bit, token[:1], me, *attn_own.sides(), [[a0[0]], [a0[1]]], [branch], 4
    )
    token = phase([attn_sum], [branch], mlp_rest.over)
    branch = token[0]
    while own_sum.done < far:
        own_sum.advance()
        if own_sum.done < far:
            phase([own_sum])
    attn_sum.advance()
    m2 = mlp_call(mlp_rest, 1, 2, rest - 1, (per_mlp, per_mlp * (rest - 1)), 0, [], token[:1])
    far_sum = Reduction(m2[3], m2[4], orders, core_bit)
    token = phase([own_sum, attn_sum, far_sum])
    while attn_sum.done < far:
        attn_sum.advance()
        if attn_sum.done < far:
            phase([attn_sum])
    far_sum.advance()
    m1 = mlp_call(mlp_rest, 0, 1, 1, (per_mlp, per_mlp), 0, [], token[:1])
    near_sum = Reduction(m1[3], m1[4], orders, core_bit)
    token = phase([attn_sum, far_sum, near_sum])
    attn_total = attn_sum.total()
    far_sum.advance()
    near_sum.advance()
    attn_moves = [shifted(attn_total[k - 1], -k) for k in others if k > 1]
    branch, d_norm_attn = attention_tail_part(
        [0, 1, rest], orders, core_bit, token[:1], me, *attn_rest.sides(), [[a1[0], a2[0]], [a1[1], a2[1]]],
        [branch, d_norm_attn], 9,
    )
    token = phase([far_sum, near_sum], attn_moves, [branch])
    attn_moves = token[: rest - 1]
    while far_sum.done < far:
        far_sum.advance()
        if far_sum.done < far:
            phase([far_sum])
    near_sum.advance()
    attn_moves.append(shifted(attn_total[0], -1))
    branch, d_norm_mlp = mlp_tail_part(
        1, orders, core_bit, token[:1], me, *mlp_rest.sides(), m2[0], m2[1], [branch, d_norm_mlp], [], None, 8
    )
    token = phase([far_sum, near_sum], attn_moves[-1:], [branch])
    attn_moves[-1] = token[0]
    far_total = far_sum.total()
    mlp_moves = [shifted(far_total[(k - 2) * per_mlp : (k - 1) * per_mlp], -k) for k in others if k > 1]
    while near_sum.done < far:
        near_sum.advance()
        if near_sum.done < far:
            phase([near_sum])
    up_row, head_row = 5, 5 + col_size
    small_ks = ((up_row, 0, col_size), (up_row, 1, col_size), (up_row, 2, col_size),
                (head_row, 0, col_size), (head_row, 1, col_size), (head_row, 2, col_size))
    block_out, in_grad, smalls = mlp_tail_part(
        0, orders, core_bit, token[:1], me, *mlp_rest.sides(), m1[0], m1[1], [branch, d_norm_mlp],
        [
            d_norm_attn, tokens_in, out_cotangent, attn_gain[None, :], mlp_gain[None, :], out_bias[None, :],
            down_bias[None, :],
        ],
        (small_ks, [m0[2], m1[2], m2[2], a0[2], a1[2], a2[2]]), 9,
    )
    token = phase([near_sum], [smalls] + mlp_moves)
    smalls, mlp_moves = token[0], token[1:rest]
    mlp_moves.append(shifted(near_sum.total(), -1))
    smalls = sum_over(smalls, ("row", "dp"))
    smalls, mlp_moves[-1] = fence([smalls, mlp_moves[-1]])

    own_total = own_sum.total()
    mlp_sum = own_total[:per_mlp].astype(F32) + sum(move.astype(F32) for move in mlp_moves)
    attn_sum = own_total[per_mlp].astype(F32) + sum(move.astype(F32) for move in attn_moves)
    total = jnp.concatenate([mlp_sum, attn_sum[None]], axis=0)
    flip = 2
    while flip < lax.axis_size("dp"):
        total = total + flipped(total, "dp", flip)
        flip *= 2
    mine = total.astype(BF16)
    other = swap(mine, 1)
    first = half == 0
    grads = jnp.concatenate([jnp.where(first, mine, other), jnp.where(first, other, mine)], axis=1).astype(F32)
    g_up = jnp.concatenate([grads[i, :, :cut] for i in range(per_mlp)], axis=1)
    g_down = jnp.concatenate([grads[i, :, cut:] for i in range(per_mlp)], axis=1)
    g_heads = grads[per_mlp].reshape(rows, local_heads, HEAD)
    smalls = sum_over(smalls, ("col",))
    return (
        block_out,
        in_grad,
        smalls[1],
        smalls[2],
        smalls[3],
        smalls[4],
        g_heads[:, :, :QKV].reshape(rows, local_heads * QKV),
        smalls[head_row : head_row + col_size].reshape(col_size * local_heads, HEAD)[:, :QKV].reshape(-1),
        g_heads[:, :, QKV:].reshape(rows, local_heads * HD).T,
        smalls[0],
        g_up,
        smalls[up_row : up_row + col_size].reshape(-1),
        g_down.T,
        smalls[0],
    )


def solution(mesh):
    return jax.shard_map(
        on_device,
        mesh=mesh,
        in_specs=(
            P(("dp", "row", "col"), None),
            P("dp", None),
            P(),
            P(),
            P(),
            P(),
            P("row", "col"),
            P(),
            P("col", "row"),
            P(),
            P("row", "col"),
            P(),
            P("col", "row"),
            P(),
            P(("dp", "row", "col"), None),
        ),
        out_specs=(
            P(("dp", "row", "col"), None),
            P(("dp", "row", "col"), None),
            P(),
            P(),
            P(),
            P(),
            P("row", "col"),
            P(),
            P("col", "row"),
            P(),
            P("row", "col"),
            P(),
            P("col", "row"),
            P(),
        ),
        check_vma=False,
    )
```

```python
import functools
import math

import jax
import jax.numpy as jnp
from jax import lax
from jax.experimental import pallas as pl
from jax.experimental.pallas import tpu as pltpu
from jax.sharding import PartitionSpec as P

HD = 64
ROT = 16
QKV = 3 * HD
HEAD = 4 * HD
EPSILON = 1e-05
ROPE_BASE = 10000.0
NEAR = 128
LONGEST = 256
F32 = jnp.float32
BF16 = jnp.bfloat16


def dot_nn(a, b):
    return lax.dot_general(a, b, (((1,), (0,)), ((), ())), preferred_element_type=F32)


def dot_nt(a, b):
    return lax.dot_general(a, b, (((1,), (1,)), ((), ())), preferred_element_type=F32)


def gathered_order(order, core_bit):
    held = [0]
    for bit in order[:-1]:
        held = held + [j | bit for j in held]
    came = [j | order[-1] for j in held]
    return held, came, [j | core_bit for j in held], [j | core_bit for j in came]


def reduced_order(order):
    kept = [0]
    for bit in order[::-1]:
        kept = kept + [j | bit for j in kept]
    return kept


def assemble(me_ref, w_refs, held, w_scr, at_col):
    for ref, pieces in zip(w_refs, held):
        _, _, rows, cols = ref.shape
        for t, j in enumerate(pieces):
            at = pl.multiple_of((me_ref[0] ^ j) * rows, 16)
            w_scr[pl.ds(at, rows), at_col : at_col + cols] = ref[t, 0]


def hand_out(me_ref, g_scr, at_col, keep_ref, send_ref, first, order, core_bit):
    _, slots, rows, cols = keep_ref.shape
    for t, j in enumerate(reduced_order(order)):
        for ref, piece in ((keep_ref, j), (send_ref, j | core_bit)):
            at = pl.multiple_of((me_ref[0] ^ piece) * rows, 16)
            for slot in range(slots):
                left = at_col + slot * cols
                ref[first + t, slot] = g_scr[pl.ds(at, rows), left : left + cols]


def normalize(x):
    center = x - jnp.mean(x, axis=1, keepdims=True)
    inv_std = lax.rsqrt(jnp.mean(center * center, axis=1, keepdims=True) + EPSILON)
    return center * inv_std, inv_std


def prep_kernel(
    x_ref, cot_ref, ga_ref, sa_ref, gm_ref, sm_ref, segc_ref, segr_ref, freq_ref,
    na_ref, naT_ref, nm_ref, nmT_ref, cotT_ref, keep_ref, ahead_ref, behind_ref, mask_ref,
):
    length = x_ref.shape[0]
    tile = 128

    @pl.loop(0, length // tile)
    def _(t):
        rows = pl.ds(pl.multiple_of(t * tile, tile), tile)
        normed, _ = normalize(x_ref[rows, :].astype(F32))
        na_ref[rows, :] = (normed * ga_ref[...] + sa_ref[...]).astype(BF16)
        nm_ref[rows, :] = (normed * gm_ref[...] + sm_ref[...]).astype(BF16)
        same = segc_ref[rows, :] == segr_ref[...]
        cols = lax.broadcasted_iota(jnp.int32, (tile, length), 1)
        ids = lax.broadcasted_iota(jnp.int32, (tile, length), 0) + t * tile
        mask_ref[rows, :] = jnp.where(same & (cols <= ids), 0.0, -jnp.inf)
        starts = jnp.min(jnp.where(same, cols, length).astype(F32), axis=1, keepdims=True)
        places = ids[:, :1].astype(F32) - starts
        angles = places * freq_ref[...]
        lane = lax.broadcasted_iota(jnp.int32, (tile, 2 * HD), 1) % HD
        cosine, sine = jnp.cos(angles), jnp.sin(angles)
        keep_ref[rows, :] = jnp.where(lane < ROT, cosine, 1.0)
        ahead_ref[rows, :] = jnp.where(lane < ROT // 2, -sine, 0.0)
        behind_ref[rows, :] = jnp.where((lane < ROT) & (lane >= ROT // 2), sine, 0.0)

    naT_ref[...] = na_ref[...].T
    nmT_ref[...] = nm_ref[...].T
    cotT_ref[...] = cot_ref[...].T


def full(*shape):
    return pl.BlockSpec(shape, lambda *_: (0,) * len(shape), pipeline_mode=pl.Buffered(1))


ANY = pl.BlockSpec(memory_space=pl.ANY)
SCALAR = pl.BlockSpec(memory_space=pltpu.SMEM)


def cost(us):
    return pl.CostEstimate(flops=int(us * 1.15e9), bytes_accessed=2**20, transcendentals=0)


def shaped(shape, dtype):
    return jax.ShapeDtypeStruct(shape, dtype)


def prep_part(tokens, cot, gains, seg_row):
    length, width = tokens.shape
    halves = ROT // 2
    step = (lax.iota(jnp.int32, 2 * HD) % HD % halves).astype(F32)
    freq = (ROPE_BASE ** (-(step * (2.0 / ROT))))[None, :]
    table = shaped((length, 2 * HD), F32)
    return pl.pallas_call(
        prep_kernel,
        grid=(1,),
        in_specs=[full(length, width)] * 2 + [full(1, width)] * 4
        + [full(length, 1), full(1, length), full(1, 2 * HD)],
        out_specs=[full(length, width), full(width, length)] * 2 + [full(width, length)]
        + [full(length, 2 * HD)] * 3 + [full(length, length)],
        out_shape=[shaped((length, width), BF16), shaped((width, length), BF16)] * 2
        + [shaped((width, length), BF16)] + [table] * 3 + [shaped((length, length), F32)],
        compiler_params=pltpu.CompilerParams(vmem_limit_bytes=60 * 2**20),
        cost_estimate=cost(6),
    )(tokens, cot, *gains, seg_row[:, None], seg_row[None, :], freq)


def attention_kernel(orders, core_bit, waits, me_ref, na_ref, naT_ref, cot_ref, cotT_ref, *rest):
    left, right, rest = rest[:4], rest[4:8], rest[8:]
    bias_ref, keep_ref, ahead_ref, behind_ref, mask_ref = rest[:5]
    dqkv_ref, mix_ref, dbias_ref, gk_ref, gs_ref, w_scr, wv_scr, qkv_scr, dattn_scr, g_scr = rest[5 + waits :]
    length, width = na_ref.shape
    block_cols = w_scr.shape[1]
    heads = block_cols // HEAD
    kept = gk_ref.shape[0] // 2
    tile = 256
    assemble(me_ref, left, gathered_order(orders[0], core_bit), w_scr, 0)
    assemble(me_ref, right, gathered_order(orders[1], core_bit), w_scr, block_cols // 2)
    for i in range(heads):
        wv_scr[:, i * 2 * HD : (i + 1) * 2 * HD] = w_scr[:, i * HEAD + 2 * HD : (i + 1) * HEAD]

    @pl.loop(0, length // tile)
    def _(t):
        rows = pl.ds(pl.multiple_of(t * tile, tile), tile)
        qkv_scr[rows, :] = dot_nn(na_ref[rows, :], w_scr[...]) + bias_ref[0]
        dattn_scr[rows, :] = dot_nn(cot_ref[rows, :], wv_scr[...]).astype(BF16)

    low = lax.broadcasted_iota(jnp.int32, (length, 2 * HD), 1) < HD
    keep, ahead, behind = keep_ref[...], ahead_ref[...], behind_ref[...]
    none = jnp.zeros((length, 2 * HD), BF16)
    spans = [(b * NEAR, (b + 1) * NEAR, max(0, b * NEAR - LONGEST)) for b in range(length // NEAR)]
    q0, k0, v1, go1, qT, goT = [], [], [], [], [], []
    for i in range(heads):
        qk = qkv_scr[:, i * HEAD : i * HEAD + 2 * HD]
        qk = qk * keep + pltpu.roll(qk, 2 * HD - ROT // 2, 1) * ahead + pltpu.roll(qk, ROT // 2, 1) * behind
        q0.append(jnp.where(low, qk * (1.0 / math.sqrt(HD)), 0.0).astype(BF16))
        k0.append(jnp.where(low, pltpu.roll(qk, HD, 1), 0.0).astype(BF16))
        value = pltpu.roll(qkv_scr[:, i * HEAD + 2 * HD : (i + 1) * HEAD], HD, 1)
        v1.append(jnp.where(low, 0.0, value).astype(BF16))
        go = dattn_scr[:, i * 2 * HD : (i + 1) * 2 * HD]
        go1.append(jnp.where(low, none, go))
        qT.append(q0[i].T[:HD])
        goT.append(go.T[HD:])
    parts = [(i, r0, r1, lo) for i in range(heads) for r0, r1, lo in spans]
    s = [dot_nt(q0[i][r0:r1], k0[i][lo:r1]) + mask_ref[r0:r1, lo:r1] for i, r0, r1, lo in parts]
    dp = [dot_nt(go1[i][r0:r1], v1[i][lo:r1]) for i, r0, r1, lo in parts]
    peak = [jnp.max(one, axis=1, keepdims=True) for one in s]
    e = [jnp.exp(one - top) for one, top in zip(s, peak)]
    norm = [1.0 / jnp.sum(one, axis=1, keepdims=True) for one in e]
    p = [one * scale for one, scale in zip(e, norm)]
    p_low = [one.astype(BF16) for one in p]
    mix = [dot_nn(one, v1[i][lo:r1]) for one, (i, r0, r1, lo) in zip(p_low, parts)]
    delta = [
        jnp.sum(one * go1[i][r0:r1].astype(F32), axis=1, keepdims=True) for one, (i, r0, r1, lo) in zip(mix, parts)
    ]
    ds = [(one * (grad - centre)).astype(BF16) for one, grad, centre in zip(p, dp, delta)]
    dq = [dot_nn(one, k0[i][lo:r1]) for one, (i, r0, r1, lo) in zip(ds, parts)]
    dkT = [dot_nn(qT[i][:, r0:r1], one) for one, (i, r0, r1, lo) in zip(ds, parts)]
    dvT = [dot_nn(goT[i][:, r0:r1], one) for one, (i, r0, r1, lo) in zip(p_low, parts)]
    for i in range(heads):
        mine = slice(i * len(spans), (i + 1) * len(spans))
        sums = []
        for group in (dvT[mine], dkT[mine]):
            total = [None] * len(spans)
            for part, (r0, r1, lo) in zip(group, spans):
                for n in range(lo // NEAR, r1 // NEAR):
                    one = part[:, n * NEAR - lo : (n + 1) * NEAR - lo]
                    total[n] = one if total[n] is None else total[n] + one
            sums.append(jnp.concatenate(total, axis=1))
        dvk = jnp.concatenate(sums, axis=0).T
        dqk = jnp.where(low, jnp.concatenate(dq[mine], axis=0) * (1.0 / math.sqrt(HD)), dvk)
        dqk = dqk * keep - pltpu.roll(dqk, 2 * HD - ROT // 2, 1) * ahead - pltpu.roll(dqk, ROT // 2, 1) * behind
        dqkv_ref[0, :, i * HEAD : i * HEAD + 2 * HD] = dqk.astype(BF16)
        dqkv_ref[0, :, i * HEAD + 2 * HD : (i + 1) * HEAD] = jnp.where(low, dvk, 0.0).astype(BF16)
        mix_ref[0, :, i * 2 * HD : (i + 1) * 2 * HD] = jnp.concatenate(mix[mine], axis=0).astype(BF16)

    dbias_ref[0] = jnp.sum(dqkv_ref[0].astype(F32), axis=0, keepdims=True)

    @pl.loop(0, width // tile)
    def _(t):
        rows = pl.ds(pl.multiple_of(t * tile, tile), tile)
        g_in = dot_nn(naT_ref[rows, :], dqkv_ref[0])
        g_out = dot_nn(cotT_ref[rows, :], mix_ref[0])
        for i in range(heads):
            at = i * HEAD
            g_scr[rows, at : at + 2 * HD] = g_in[:, at : at + 2 * HD].astype(BF16)
            g_scr[rows, at + 2 * HD : at + HEAD] = (
                g_in[:, at + 2 * HD : at + HEAD] + g_out[:, i * 2 * HD : (i + 1) * 2 * HD]
            ).astype(BF16)

    hand_out(me_ref, g_scr, 0, gk_ref, gs_ref, 0, orders[0], core_bit)
    hand_out(me_ref, g_scr, block_cols // 2, gk_ref, gs_ref, kept, orders[1], core_bit)


def mlp_kernel(orders, core_bit, waits, me_ref, nm_ref, nmT_ref, cot_ref, cotT_ref, *rest):
    left, right, bias_ref, rest = rest[:4], rest[4:8], rest[8], rest[9 + waits :]
    act_ref, dh_ref, dbias_ref, gk_ref, gs_ref, wu_scr, wd_scr, g_scr = rest
    length, width = nm_ref.shape
    up_cols = wu_scr.shape[1]
    kept = gk_ref.shape[0] // 2
    tile = 256
    assemble(me_ref, left, gathered_order(orders[0], core_bit), wu_scr, 0)
    assemble(me_ref, right, gathered_order(orders[1], core_bit), wd_scr, 0)
    dbias_ref[0] = jnp.zeros_like(dbias_ref[0])

    @pl.loop(0, length // tile)
    def _(t):
        rows = pl.ds(pl.multiple_of(t * tile, tile), tile)
        for n in range(0, up_cols, tile):
            hidden = dot_nn(nm_ref[rows, :], wu_scr[:, n : n + tile]) + bias_ref[0, :, n : n + tile]
            d_act = dot_nn(cot_ref[rows, :], wd_scr[:, n : n + tile])
            gate = 0.5 * (1.0 + lax.erf(hidden * (1.0 / math.sqrt(2.0))))
            act_ref[0, rows, n : n + tile] = (hidden * gate).astype(BF16)
            slope = gate + hidden * jnp.exp(-0.5 * hidden * hidden) * (1.0 / math.sqrt(2.0 * math.pi))
            dh = (d_act * slope).astype(BF16)
            dh_ref[0, rows, n : n + tile] = dh
            dbias_ref[0, :, n : n + tile] += jnp.sum(dh.astype(F32), axis=0, keepdims=True)

    for side, lhs, rhs in ((0, nmT_ref, dh_ref), (1, cotT_ref, act_ref)):

        @pl.loop(0, width // tile)
        def _(t):
            rows = pl.ds(pl.multiple_of(t * tile, tile), tile)
            g_scr[rows, :] = dot_nn(lhs[rows, :], rhs[0]).astype(BF16)

        hand_out(me_ref, g_scr, 0, gk_ref, gs_ref, side * kept, orders[side], core_bit)


def weight_spec(array, block_of):
    count, _, rows, cols = array.shape
    return pl.BlockSpec((count, 1, rows, cols), lambda s: (0, block_of(s), 0, 0))


def block_part(kernel, w0, k0, count, slots, slot0, into, orders, core_bit, after, me, norm, norm_t, cot, cot_t,
               left, right, vectors, mid_cols, g_cols, scratch, us):
    length, width = norm.shape
    rows = left[0].shape[2]
    pieces = width // rows
    cols = vectors[0].shape[-1]
    per_step, total_slots = slots
    g_spec = pl.BlockSpec((pieces, per_step, rows, g_cols), lambda s: (0, slot0 + s, 0, 0))
    after = list(after) + list(into)
    fixed = 5 + len(left + right) + len(vectors) + len(after)
    return pl.pallas_call(
        functools.partial(kernel, orders, core_bit, len(after)),
        grid=(count,),
        in_specs=[SCALAR, full(length, width), full(width, length), full(length, width), full(width, length)]
        + [weight_spec(w, lambda s: w0 + s) for w in left + right]
        + [pl.BlockSpec((1, 1, cols), lambda s: (k0 + s, 0, 0))]
        + [full(*v.shape) for v in vectors[1:]]
        + [ANY] * len(after),
        out_specs=[pl.BlockSpec((1, length, m), lambda s: (s, 0, 0)) for m in mid_cols]
        + [pl.BlockSpec((1, 1, cols), lambda s: (s, 0, 0))] + [g_spec] * 2,
        out_shape=[shaped((count, length, m), BF16) for m in mid_cols]
        + [shaped((count, 1, cols), F32)] + [shaped((pieces, total_slots, rows, g_cols), BF16)] * 2,
        input_output_aliases={fixed - 2: len(mid_cols) + 1, fixed - 1: len(mid_cols) + 2} if into else {},
        scratch_shapes=scratch,
        compiler_params=pltpu.CompilerParams(vmem_limit_bytes=60 * 2**20),
        cost_estimate=cost(us * count),
    )(me, norm, norm_t, cot, cot_t, *left, *right, *vectors, *after)


def pick(refs, begins, scr):
    step = pl.program_id(0)
    for ref, begin, end in zip(refs, begins, begins[1:]):

        @pl.when((step >= begin) & (step < end))
        def _():
            scr[...] = ref[0]


def attention_tail_kernel(orders, core_bit, begins, waits, me_ref, *rest):
    left, right, rest = rest[:4], rest[4:8], rest[8:]
    calls = len(begins) - 1
    dqkv_refs, mix_refs, rest = rest[:calls], rest[calls : 2 * calls], rest[2 * calls :]
    sums_in, rest = rest[: len(rest) - waits - 6], rest[len(rest) - 6 :]
    branch_ref, dna_ref, w_scr, wv_scr, dqkv_scr, mix_scr = rest
    block_cols = w_scr.shape[1]

    @pl.when(pl.program_id(0) == 0)
    def _():
        branch_ref[...] = sums_in[0][...] if sums_in else jnp.zeros_like(branch_ref)
        dna_ref[...] = sums_in[1][...] if len(sums_in) > 1 else jnp.zeros_like(dna_ref)

    pick(dqkv_refs, begins, dqkv_scr)
    pick(mix_refs, begins, mix_scr)
    assemble(me_ref, left, gathered_order(orders[0], core_bit), w_scr, 0)
    assemble(me_ref, right, gathered_order(orders[1], core_bit), w_scr, block_cols // 2)
    for i in range(block_cols // HEAD):
        wv_scr[:, i * 2 * HD : (i + 1) * 2 * HD] = w_scr[:, i * HEAD + 2 * HD : (i + 1) * HEAD]
    tile = 256

    @pl.loop(0, branch_ref.shape[0] // tile)
    def _(t):
        rows = pl.ds(pl.multiple_of(t * tile, tile), tile)
        branch_ref[rows, :] += dot_nt(mix_scr[rows, :], wv_scr[...])
        dna_ref[rows, :] += dot_nt(dqkv_scr[rows, :], w_scr[...])


def mlp_tail_kernel(orders, core_bit, sums, small_ks, waits, me_ref, *rest):
    left, right, dh_ref, act_ref, rest = rest[:4], rest[4:8], rest[8], rest[9], rest[10:]
    sums_in, rest = rest[:sums], rest[sums:]
    last = small_ks is not None
    if last:
        dna_ref, x_ref, cot_ref, ga_ref, gm_ref, bo_ref, bd_ref = rest[:7]
        small_refs = rest[7 : 7 + len(small_ks)]
        block_ref, grad_ref, stats_ref, branch_ref, dnm_ref, wu_scr, wd_scr = rest[7 + len(small_ks) + waits :]
    else:
        branch_ref, dnm_ref, wu_scr, wd_scr = rest[waits:]
    length = branch_ref.shape[0]
    step = pl.program_id(0)

    @pl.when(step == 0)
    def _():
        branch_ref[...] = sums_in[0][...] if sums else jnp.zeros_like(branch_ref)
        dnm_ref[...] = sums_in[1][...] if sums > 1 else jnp.zeros_like(dnm_ref)

    assemble(me_ref, left, gathered_order(orders[0], core_bit), wu_scr, 0)
    assemble(me_ref, right, gathered_order(orders[1], core_bit), wd_scr, 0)
    tile = 256

    @pl.loop(0, length // tile)
    def _(t):
        rows = pl.ds(pl.multiple_of(t * tile, tile), tile)
        branch_ref[rows, :] += dot_nt(act_ref[0, rows, :], wd_scr[...])
        dnm_ref[rows, :] += dot_nt(dh_ref[0, rows, :], wu_scr[...])

    if not last:
        return

    @pl.when(step == pl.num_programs(0) - 1)
    def _():
        stats_ref[...] = jnp.zeros_like(stats_ref)
        small = 128

        @pl.loop(0, length // small)
        def _(t):
            rows = pl.ds(pl.multiple_of(t * small, small), small)
            x = x_ref[rows, :].astype(F32)
            cot = cot_ref[rows, :].astype(F32)
            normed, inv_std = normalize(x)
            block_ref[rows, :] = (x + branch_ref[rows, :] + bo_ref[...] + bd_ref[...]).astype(BF16)
            dna, dnm = dna_ref[rows, :], dnm_ref[rows, :]
            d_normed = dna * ga_ref[...] + dnm * gm_ref[...]
            pulled = (
                d_normed
                - jnp.mean(d_normed, axis=1, keepdims=True)
                - normed * jnp.mean(d_normed * normed, axis=1, keepdims=True)
            )
            grad_ref[rows, :] = (cot + inv_std * pulled).astype(BF16)
            for at, term in enumerate((cot, dna * normed, dna, dnm * normed, dnm)):
                stats_ref[at : at + 1, :] += jnp.sum(term, axis=0, keepdims=True)

        for ref, (first, k0, blocks) in zip(small_refs, small_ks):
            for i in range(ref.shape[0]):
                block = lax.rem(me_ref[1] + (blocks - k0 - i), blocks)
                stats_ref[pl.ds(first + block, 1), :] = ref[i]


def attention_tail_part(begins, starts, orders, core_bit, after, me, left, right, mids, sums, us):
    steps = left[0].shape[1]
    pieces = 2 * sum(w.shape[0] for w in left) // 2
    width = pieces * left[0].shape[2]
    length = mids[0][0].shape[1]

    def mid_spec(array, n):
        begin, end = begins[n], begins[n + 1]
        return pl.BlockSpec(
            (1,) + array.shape[1:], lambda s: (jnp.clip(s - begin, 0, end - begin - 1), 0, 0)
        )

    def block_of(step):
        block = step
        for begin, start in zip(begins, starts):
            block = jnp.where(step >= begin, start + step - begin, block)
        return block

    block_cols, half_cols = mids[0][0].shape[2], mids[1][0].shape[2]
    outs = [shaped((length, width), F32)] * 2
    return pl.pallas_call(
        functools.partial(attention_tail_kernel, orders, core_bit, begins, len(after)),
        grid=(steps,),
        in_specs=[SCALAR] + [weight_spec(w, lambda s: block_of(s)) for w in left + right]
        + [mid_spec(array, n) for group in mids for n, array in enumerate(group)]
        + [full(*e.shape) for e in sums] + [ANY] * len(after),
        out_specs=[full(*o.shape) for o in outs],
        out_shape=outs,
        scratch_shapes=[pltpu.VMEM((width, block_cols), BF16), pltpu.VMEM((width, half_cols), BF16)]
        + [pltpu.VMEM(group[0].shape[1:], BF16) for group in mids],
        compiler_params=pltpu.CompilerParams(vmem_limit_bytes=60 * 2**20),
        cost_estimate=cost(us),
    )(me, *left, *right, *[array for group in mids for array in group], *sums, *after)


def mlp_tail_part(w0, orders, core_bit, after, me, left, right, act, dh, sums, finals, smalls, us):
    count, length, cols = dh.shape
    width = sum(w.shape[0] for w in left) * left[0].shape[2]
    mid_spec = pl.BlockSpec((1, length, cols), lambda s: (s, 0, 0))
    total = shaped((length, width), F32)
    scratch = [pltpu.VMEM((width, cols), BF16)] * 2
    outs, small_ks = [total] * 2, None
    if finals:
        small_ks, arrays = smalls
        blocks = small_ks[0][2]
        outs = [shaped((length, width), BF16)] * 2 + [shaped((-(-(5 + 2 * blocks) // 8) * 8, width), F32)]
        scratch = [pltpu.VMEM((length, width), F32)] * 2 + scratch
        finals = list(finals) + list(arrays)
    extra = list(sums) + list(finals)
    return pl.pallas_call(
        functools.partial(mlp_tail_kernel, orders, core_bit, len(sums), small_ks, len(after)),
        grid=(count,),
        in_specs=[SCALAR] + [weight_spec(w, lambda s: w0 + s) for w in left + right] + [mid_spec] * 2
        + [full(*e.shape) for e in extra] + [ANY] * len(after),
        out_specs=[full(*o.shape) for o in outs],
        out_shape=outs,
        scratch_shapes=scratch,
        compiler_params=pltpu.CompilerParams(vmem_limit_bytes=60 * 2**20),
        cost_estimate=cost(us),
    )(me, *left, *right, dh, act, *extra, *after)


def fence_kernel(*_):
    pass


def fence(values, after=()):
    count = len(values)
    return pl.pallas_call(
        fence_kernel,
        in_specs=[ANY] * (count + len(after)),
        out_specs=[ANY] * count,
        out_shape=[shaped(value.shape, value.dtype) for value in values],
        input_output_aliases={n: n for n in range(count)},
        cost_estimate=cost(1),
    )(*values, *after)


def swap(value, bit):
    axis, flip = ("dp", 1) if bit == 1 else ("row", bit // 2)
    return flipped(value, axis, flip)


def flipped(value, axis, flip):
    return lax.ppermute(value, axis, [(i, i ^ flip) for i in range(lax.axis_size(axis))])


def shifted(value, by):
    size = lax.axis_size("col")
    return lax.ppermute(value, "col", [(i, (i + by) % size) for i in range(size)])


class Gather:
    def __init__(self, blocks, orders, core_bit):
        cut = blocks.shape[2] // 2
        self.orders, self.core_bit, self.done = orders, core_bit, 0
        self.block = blocks[0]
        self.held = [blocks[None, :, :, :cut], blocks[None, :, :, cut:]]

    def advance(self):
        if self.done > 0:
            self.held = [jnp.concatenate(pair, axis=0) for pair in zip(self.held, self.moving)]
        self.moving = [swap(one, order[self.done]) for one, order in zip(self.held, self.orders)]
        self.done += 1

    def cross(self):
        self.over = [swap(one, self.core_bit) for one in self.held + self.moving]

    def sides(self):
        return ([self.held[i], self.moving[i], self.over[i], self.over[i + 2]] for i in range(2))


class Reduction:
    def __init__(self, keep, send, orders, core_bit):
        self.keep, self.orders, self.came = keep, orders, swap(send, core_bit)
        self.later = [[] for _ in orders]
        self.done = 0

    def half(self):
        return self.keep.shape[0] // len(self.orders) >> (self.done + 1)


def merge_kernel(layout, ins, first_out, *refs):
    outs = refs[first_out : first_out + len(layout)]
    at = 0
    for group, out in zip(layout, outs):
        column = 0
        for terms in group:
            total = refs[at][...].astype(F32)
            for ref in refs[at + 1 : at + terms]:
                total = total + ref[...].astype(F32)
            at += terms
            cols = total.shape[-1]
            out[..., column : column + cols] = total.astype(BF16)
            column += cols
    assert at == ins


def merge(reductions, after, values=()):
    specs, arrays, layout, shapes, plans = [], [], [], [], []

    def block(array, count, index):
        shape = (count,) + array.shape[1:]
        return pl.BlockSpec(shape, lambda s: (index,) + (0,) * (len(shape) - 1), pipeline_mode=pl.Buffered(1))

    for r in reductions:
        half = r.half()
        count = max(half, 1)
        size = r.keep.shape[0] // len(r.orders)
        groups = []
        for side in range(len(r.orders)):
            terms = [(one, (side * size + half) // count) for one in (r.keep, r.came)]
            terms += [(one, half // count) for one in r.later[side]]
            for one, index in terms:
                specs.append(block(one, count, index))
                arrays.append(one)
            groups.append(len(terms))
        _, slots, rows, cols = r.keep.shape
        if half:
            layout += [(terms,) for terms in groups]
            shapes += [(half, slots, rows, cols)] * len(groups)
        else:
            layout.append(tuple(groups))
            shapes.append((1, slots, rows, cols * len(groups)))
        plans.append((r, half))
    out = list(pl.pallas_call(
        functools.partial(merge_kernel, layout, len(arrays), len(arrays) + len(values) + len(after)),
        grid=(1,),
        in_specs=specs + [ANY] * (len(values) + len(after)),
        out_specs=[full(*shape) for shape in shapes] + [ANY] * len(values),
        out_shape=[shaped(shape, BF16) for shape in shapes] + [shaped(v.shape, v.dtype) for v in values],
        input_output_aliases={len(arrays) + n: len(shapes) + n for n in range(len(values))},
        compiler_params=pltpu.CompilerParams(vmem_limit_bytes=60 * 2**20),
        cost_estimate=cost(3),
    )(*arrays, *values, *after))
    token, finished = out[0], []
    passed = out[len(shapes) :]
    for r, half in plans:
        if half:
            for side, order in enumerate(r.orders):
                r.later[side].append(swap(out.pop(0), order[r.done]))
            r.done += 1
        else:
            finished.append(out.pop(0)[0])
    return finished, [token], passed


def phase(users, values=(), after=()):
    values = list(values)
    out = list(fence(values + [one for user in users for one in user.moving], after))
    at = len(values)
    for user in users:
        user.moving = out[at : at + len(user.moving)]
        at += len(user.moving)
    return out


def sum_over(value, axes):
    for axis in axes:
        flip = 1
        while flip < lax.axis_size(axis):
            value = value + flipped(value, axis, flip)
            flip *= 2
    return value


def on_device(
    tokens_in,
    segment_ids,
    attn_gain,
    attn_shift,
    mlp_gain,
    mlp_shift,
    qkv_weight,
    qkv_bias,
    out_weight,
    out_bias,
    up_weight,
    up_bias,
    down_weight,
    down_bias,
    out_cotangent,
):
    row_size = lax.axis_size("row")
    col_size = lax.axis_size("col")
    length, width = tokens_in.shape
    rows = qkv_weight.shape[0]
    half_rows = rows // 2
    local_heads = qkv_weight.shape[1] // QKV
    block_cols = local_heads * HEAD
    up_cols = up_weight.shape[1]
    row_id = lax.axis_index("row")
    col_id = lax.axis_index("col")
    half = lax.axis_index("dp") % 2
    me = jnp.stack([row_id * 2 + half, col_id]).astype(jnp.int32)
    row_bits = [2 << i for i in range(row_size.bit_length() - 1)]
    core_bit, far_bits = row_bits[0], row_bits[1:][::-1]
    orders = (far_bits + [1], [1] + far_bits)

    head_weight = jnp.concatenate(
        [qkv_weight.reshape(rows, local_heads, QKV), out_weight.T.reshape(rows, local_heads, HD)], axis=2
    ).reshape(rows, block_cols)
    attn_own = lax.dynamic_slice_in_dim(head_weight, half * half_rows, half_rows, axis=0)
    mlp_own = jnp.concatenate(
        [
            lax.dynamic_slice_in_dim(up_weight, half * half_rows, half_rows, axis=0),
            lax.dynamic_slice_in_dim(down_weight, half * half_rows, half_rows, axis=1).T,
        ],
        axis=1,
    )
    cut = block_cols // 2

    seg_row = lax.dynamic_index_in_dim(segment_ids, row_id * col_size + col_id, axis=0, keepdims=False)
    na, na_t, nm, nm_t, cot_t, keep, ahead, behind, mask = prep_part(
        tokens_in, out_cotangent, [v[None, :] for v in (attn_gain, attn_shift, mlp_gain, mlp_shift)], seg_row,
    )
    blocks_here = (col_id - jnp.arange(col_size)) % col_size
    head_bias = jnp.pad(
        qkv_bias.reshape(col_size, local_heads, QKV), ((0, 0), (0, 0), (0, HEAD - QKV))
    ).reshape(col_size, 1, block_cols)
    head_bias = jnp.take(head_bias, blocks_here, axis=0)
    hidden_bias = jnp.take(up_bias.reshape(col_size, 1, up_cols), blocks_here, axis=0)

    far = len(orders[0])

    def gather_col(own):
        return [own] + [shifted(own, k) for k in range(1, col_size)]

    attn = Gather(jnp.stack(gather_col(attn_own)), orders, core_bit)
    mlp_blocks = gather_col(fence([mlp_own], [attn.held[0]])[0])
    for _ in range(far):
        attn.advance()
        phase([attn], [], [na] if attn.done == 1 else [])
    mlp_blocks = fence(mlp_blocks, attn.moving)
    attn.cross()
    mlp = Gather(jnp.stack(mlp_blocks), orders, core_bit)
    mlp.advance()

    def attention_call(weights, w0, k0, count, slots, slot0, into, after):
        return block_part(
            attention_kernel, w0, k0, count, slots, slot0, into, orders, core_bit, after, me, na, na_t, out_cotangent,
            cot_t, *weights.sides(), [head_bias, keep, ahead, behind, mask], [block_cols, cut], cut,
            [
                pltpu.VMEM((width, block_cols), BF16), pltpu.VMEM((width, cut), BF16),
                pltpu.VMEM((length, block_cols), F32), pltpu.VMEM((length, cut), BF16),
                pltpu.VMEM((width, block_cols), BF16),
            ],
            10,
        )

    def mlp_call(weights, w0, k0, count, slots, slot0, into, after):
        return block_part(
            mlp_kernel, w0, k0, count, slots, slot0, into, orders, core_bit, after, me, nm, nm_t, out_cotangent, cot_t,
            *weights.sides(), [hidden_bias], [up_cols, up_cols], cut, [pltpu.VMEM((width, up_cols), BF16)] * 3, 6,
        )

    per_mlp = up_cols // cut
    per_call = 2
    starts = list(range(0, col_size, per_call))[::-1]
    attn_calls, into, token = [], [], []
    for k0 in starts:
        outs = attention_call(attn, k0, k0, per_call, (1, col_size), k0 // 1, into, token)
        attn_calls.append(outs)
        into = list(outs[3:])
        sent = into[1:] if k0 == starts[-1] else []
        token = phase([mlp], sent, [outs[2]])
        sent, token = token[: len(sent)], token[-1:]
        if mlp.done < far:
            mlp.advance()
            while mlp.done < far and k0 == starts[-1]:
                phase([mlp])
                mlp.advance()
    while mlp.done < far:
        mlp.advance()
        token = phase([mlp])[:1]
    mlp.cross()
    attn_sum = Reduction(into[0], sent[0], orders, core_bit)

    mlp_calls, mlp_sums = [], []
    for k0 in starts:
        outs = mlp_call(mlp, k0, k0, per_call, (per_mlp, per_mlp * per_call), 0, [], token)
        mlp_calls.append(outs)
        _, token, sent = merge([attn_sum] + mlp_sums, [outs[2]], [outs[4]])
        mlp_sums.append(Reduction(outs[3], sent[0], orders, core_bit))
    begins = list(range(0, col_size + 1, per_call))
    branch, d_norm_attn = attention_tail_part(
        begins, starts, orders, core_bit, token, me, *attn.sides(), [[c[0] for c in attn_calls], [c[1] for c in attn_calls]],
        [], 11,
    )
    totals = {}

    def go_on(after):
        open_ones = [r for r in [attn_sum] + mlp_sums if id(r) not in totals]
        ending = [r for r in open_ones if not r.half()]
        finished, token, _ = merge(open_ones, after)
        for r, total in zip(ending, finished):
            totals[id(r)] = total
        return token

    moves = {}

    def send_home(k, parts):
        part = jnp.concatenate(parts, axis=1)
        moves[k] = part if k == 0 else shifted(part, -k)

    small_ks = tuple((5, k0, col_size) for k0 in starts) + tuple((5 + col_size, k0, col_size) for k0 in starts)
    small_parts = [c[2] for c in mlp_calls] + [c[2] for c in attn_calls]
    token = go_on([branch])
    d_norm_mlp = None
    for n, k0 in enumerate(starts):
        last = n == len(starts) - 1
        sums = [branch] if n == 0 else [branch, d_norm_mlp]
        finals = [
            d_norm_attn, tokens_in, out_cotangent, attn_gain[None, :], mlp_gain[None, :], out_bias[None, :],
            down_bias[None, :],
        ]
        result = mlp_tail_part(
            k0, orders, core_bit, token, me, *mlp.sides(), mlp_calls[n][0], mlp_calls[n][1], sums,
            finals if last else [], (small_ks, small_parts) if last else None, 9,
        )
        token = go_on(result[2:] if last else result[:1])
        if last:
            block_out, in_grad, smalls = result
        else:
            branch, d_norm_mlp = result
        for at, k1 in enumerate(starts):
            if id(mlp_sums[at]) in totals and id(attn_sum) in totals and k1 not in moves:
                attn_total, mlp_total = totals[id(attn_sum)], totals[id(mlp_sums[at])]
                for i in range(per_call):
                    send_home(k1 + i, [attn_total[k1 + i]] + [mlp_total[i * per_mlp + j] for j in range(per_mlp)])
    while len(moves) < col_size:
        token = go_on(token)
        for at, k1 in enumerate(starts):
            if id(mlp_sums[at]) in totals and k1 not in moves:
                attn_total, mlp_total = totals[id(attn_sum)], totals[id(mlp_sums[at])]
                for i in range(per_call):
                    send_home(k1 + i, [attn_total[k1 + i]] + [mlp_total[i * per_mlp + j] for j in range(per_mlp)])
    head_row, up_row = 5 + col_size, 5
    smalls = sum_over(smalls, ("row", "dp"))
    smalls, *came = fence([smalls] + [moves[k] for k in range(1, col_size)])

    total = sum((move.astype(F32) for move in came), moves[0].astype(F32))
    flip = 2
    while flip < lax.axis_size("dp"):
        total = total + flipped(total, "dp", flip)
        flip *= 2
    mine = total.astype(BF16)
    other = swap(mine, 1)
    first = half == 0
    grads = jnp.concatenate([jnp.where(first, mine, other), jnp.where(first, other, mine)], axis=0).astype(F32)
    g_heads = grads[:, :block_cols].reshape(rows, local_heads, HEAD)
    sides = grads[:, block_cols:].reshape(rows, per_mlp, 2, cut)
    g_up = sides[:, :, 0].reshape(rows, up_cols)
    g_down = sides[:, :, 1].reshape(rows, up_cols)
    smalls = sum_over(smalls, ("col",))
    return (
        block_out,
        in_grad,
        smalls[1],
        smalls[2],
        smalls[3],
        smalls[4],
        g_heads[:, :, :QKV].reshape(rows, local_heads * QKV),
        smalls[head_row : head_row + col_size].reshape(col_size * local_heads, HEAD)[:, :QKV].reshape(-1),
        g_heads[:, :, QKV:].reshape(rows, local_heads * HD).T,
        smalls[0],
        g_up,
        smalls[up_row : up_row + col_size].reshape(-1),
        g_down.T,
        smalls[0],
    )


def solution(mesh):
    return jax.shard_map(
        on_device,
        mesh=mesh,
        in_specs=(
            P(("dp", "row", "col"), None),
            P("dp", None),
            P(),
            P(),
            P(),
            P(),
            P("row", "col"),
            P(),
            P("col", "row"),
            P(),
            P("row", "col"),
            P(),
            P("col", "row"),
            P(),
            P(("dp", "row", "col"), None),
        ),
        out_specs=(
            P(("dp", "row", "col"), None),
            P(("dp", "row", "col"), None),
            P(),
            P(),
            P(),
            P(),
            P("row", "col"),
            P(),
            P("col", "row"),
            P(),
            P("row", "col"),
            P(),
            P("col", "row"),
            P(),
        ),
        check_vma=False,
    )
```

```python
import functools
import math

import jax
import jax.numpy as jnp
from jax import lax
from jax.experimental import pallas as pl
from jax.experimental.pallas import tpu as pltpu
from jax.sharding import PartitionSpec as P

HD = 64
ROT = 16
QKV = 3 * HD
HEAD = 4 * HD
EPSILON = 1e-05
ROPE_BASE = 10000.0
NEAR = 128
LONGEST = 256
F32 = jnp.float32
BF16 = jnp.bfloat16


def dot_nn(a, b):
    return lax.dot_general(a, b, (((1,), (0,)), ((), ())), preferred_element_type=F32)


def dot_nt(a, b):
    return lax.dot_general(a, b, (((1,), (1,)), ((), ())), preferred_element_type=F32)


def gathered_order(order, core_bit):
    held = [0]
    for bit in order[:-1]:
        held = held + [j | bit for j in held]
    came = [j | order[-1] for j in held]
    return held, came, [j | core_bit for j in held], [j | core_bit for j in came]


def reduced_order(order):
    kept = [0]
    for bit in order[::-1]:
        kept = kept + [j | bit for j in kept]
    return kept


def assemble(me_ref, w_refs, held, w_scr, at_col):
    for ref, pieces in zip(w_refs, held):
        _, _, rows, cols = ref.shape
        for t, j in enumerate(pieces):
            at = pl.multiple_of((me_ref[0] ^ j) * rows, 16)
            w_scr[pl.ds(at, rows), at_col : at_col + cols] = ref[t, 0]


def hand_out(me_ref, g_scr, at_col, keep_ref, send_ref, first, order, core_bit):
    _, slots, rows, cols = keep_ref.shape
    for t, j in enumerate(reduced_order(order)):
        for ref, piece in ((keep_ref, j), (send_ref, j | core_bit)):
            at = pl.multiple_of((me_ref[0] ^ piece) * rows, 16)
            for slot in range(slots):
                left = at_col + slot * cols
                ref[first + t, slot] = g_scr[pl.ds(at, rows), left : left + cols]


def normalize(x):
    center = x - jnp.mean(x, axis=1, keepdims=True)
    inv_std = lax.rsqrt(jnp.mean(center * center, axis=1, keepdims=True) + EPSILON)
    return center * inv_std, inv_std


def prep_kernel(
    x_ref, cot_ref, ga_ref, sa_ref, gm_ref, sm_ref, segc_ref, segr_ref, freq_ref,
    na_ref, naT_ref, nm_ref, nmT_ref, cotT_ref, keep_ref, ahead_ref, behind_ref, mask_ref,
):
    length = x_ref.shape[0]
    tile = 128

    @pl.loop(0, length // tile)
    def _(t):
        rows = pl.ds(pl.multiple_of(t * tile, tile), tile)
        normed, _ = normalize(x_ref[rows, :].astype(F32))
        na_ref[rows, :] = (normed * ga_ref[...] + sa_ref[...]).astype(BF16)
        nm_ref[rows, :] = (normed * gm_ref[...] + sm_ref[...]).astype(BF16)
        same = segc_ref[rows, :] == segr_ref[...]
        cols = lax.broadcasted_iota(jnp.int32, (tile, length), 1)
        ids = lax.broadcasted_iota(jnp.int32, (tile, length), 0) + t * tile
        mask_ref[rows, :] = jnp.where(same & (cols <= ids), 0.0, -jnp.inf)
        starts = jnp.min(jnp.where(same, cols, length).astype(F32), axis=1, keepdims=True)
        places = ids[:, :1].astype(F32) - starts
        angles = places * freq_ref[...]
        lane = lax.broadcasted_iota(jnp.int32, (tile, 2 * HD), 1) % HD
        cosine, sine = jnp.cos(angles), jnp.sin(angles)
        keep_ref[rows, :] = jnp.where(lane < ROT, cosine, 1.0)
        ahead_ref[rows, :] = jnp.where(lane < ROT // 2, -sine, 0.0)
        behind_ref[rows, :] = jnp.where((lane < ROT) & (lane >= ROT // 2), sine, 0.0)

    naT_ref[...] = na_ref[...].T
    nmT_ref[...] = nm_ref[...].T
    cotT_ref[...] = cot_ref[...].T


def full(*shape):
    return pl.BlockSpec(shape, lambda *_: (0,) * len(shape), pipeline_mode=pl.Buffered(1))


ANY = pl.BlockSpec(memory_space=pl.ANY)
SCALAR = pl.BlockSpec(memory_space=pltpu.SMEM)


def cost(us):
    return pl.CostEstimate(flops=int(us * 1.15e9), bytes_accessed=2**20, transcendentals=0)


def shaped(shape, dtype):
    return jax.ShapeDtypeStruct(shape, dtype)


def prep_part(tokens, cot, gains, seg_row):
    length, width = tokens.shape
    halves = ROT // 2
    step = (lax.iota(jnp.int32, 2 * HD) % HD % halves).astype(F32)
    freq = (ROPE_BASE ** (-(step * (2.0 / ROT))))[None, :]
    table = shaped((length, 2 * HD), F32)
    return pl.pallas_call(
        prep_kernel,
        grid=(1,),
        in_specs=[full(length, width)] * 2 + [full(1, width)] * 4
        + [full(length, 1), full(1, length), full(1, 2 * HD)],
        out_specs=[full(length, width), full(width, length)] * 2 + [full(width, length)]
        + [full(length, 2 * HD)] * 3 + [full(length, length)],
        out_shape=[shaped((length, width), BF16), shaped((width, length), BF16)] * 2
        + [shaped((width, length), BF16)] + [table] * 3 + [shaped((length, length), F32)],
        compiler_params=pltpu.CompilerParams(vmem_limit_bytes=60 * 2**20),
        cost_estimate=cost(6),
    )(tokens, cot, *gains, seg_row[:, None], seg_row[None, :], freq)


def attention_kernel(orders, core_bit, waits, me_ref, na_ref, naT_ref, cot_ref, cotT_ref, *rest):
    left, right, rest = rest[:4], rest[4:8], rest[8:]
    bias_ref, keep_ref, ahead_ref, behind_ref, mask_ref = rest[:5]
    dqkv_ref, mix_ref, dbias_ref, gk_ref, gs_ref, w_scr, wv_scr, qkv_scr, dattn_scr, g_scr = rest[5 + waits :]
    length, width = na_ref.shape
    block_cols = w_scr.shape[1]
    heads = block_cols // HEAD
    kept = gk_ref.shape[0] // 2
    tile = 256
    assemble(me_ref, left, gathered_order(orders[0], core_bit), w_scr, 0)
    assemble(me_ref, right, gathered_order(orders[1], core_bit), w_scr, block_cols // 2)
    for i in range(heads):
        wv_scr[:, i * 2 * HD : (i + 1) * 2 * HD] = w_scr[:, i * HEAD + 2 * HD : (i + 1) * HEAD]

    for t in range(length // tile):
        rows = slice(t * tile, (t + 1) * tile)
        qkv_scr[rows, :] = dot_nn(na_ref[rows, :], w_scr[...]) + bias_ref[0]
        dattn_scr[rows, :] = dot_nn(cot_ref[rows, :], wv_scr[...]).astype(BF16)

    low = lax.broadcasted_iota(jnp.int32, (length, 2 * HD), 1) < HD
    keep, ahead, behind = keep_ref[...], ahead_ref[...], behind_ref[...]
    none = jnp.zeros((length, 2 * HD), BF16)
    spans = [(b * NEAR, (b + 1) * NEAR, max(0, b * NEAR - LONGEST)) for b in range(length // NEAR)]
    q0, k0, v1, go1, qT, goT = [], [], [], [], [], []
    for i in range(heads):
        qk = qkv_scr[:, i * HEAD : i * HEAD + 2 * HD]
        qk = qk * keep + pltpu.roll(qk, 2 * HD - ROT // 2, 1) * ahead + pltpu.roll(qk, ROT // 2, 1) * behind
        q0.append(jnp.where(low, qk * (1.0 / math.sqrt(HD)), 0.0).astype(BF16))
        k0.append(jnp.where(low, pltpu.roll(qk, HD, 1), 0.0).astype(BF16))
        value = pltpu.roll(qkv_scr[:, i * HEAD + 2 * HD : (i + 1) * HEAD], HD, 1)
        v1.append(jnp.where(low, 0.0, value).astype(BF16))
        go = dattn_scr[:, i * 2 * HD : (i + 1) * 2 * HD]
        go1.append(jnp.where(low, none, go))
        qT.append(q0[i].T[:HD])
        goT.append(go.T[HD:])
    parts = [(i, r0, r1, lo) for i in range(heads) for r0, r1, lo in spans]
    s = [dot_nt(q0[i][r0:r1], k0[i][lo:r1]) + mask_ref[r0:r1, lo:r1] for i, r0, r1, lo in parts]
    dp = [dot_nt(go1[i][r0:r1], v1[i][lo:r1]) for i, r0, r1, lo in parts]
    peak = [jnp.max(one, axis=1, keepdims=True) for one in s]
    e = [jnp.exp(one - top) for one, top in zip(s, peak)]
    norm = [1.0 / jnp.sum(one, axis=1, keepdims=True) for one in e]
    p = [one * scale for one, scale in zip(e, norm)]
    p_low = [one.astype(BF16) for one in p]
    mix = [dot_nn(one, v1[i][lo:r1]) for one, (i, r0, r1, lo) in zip(p_low, parts)]
    delta = [
        jnp.sum(one * go1[i][r0:r1].astype(F32), axis=1, keepdims=True) for one, (i, r0, r1, lo) in zip(mix, parts)
    ]
    ds = [(one * (grad - centre)).astype(BF16) for one, grad, centre in zip(p, dp, delta)]
    dq = [dot_nn(one, k0[i][lo:r1]) for one, (i, r0, r1, lo) in zip(ds, parts)]
    dkT = [dot_nn(qT[i][:, r0:r1], one) for one, (i, r0, r1, lo) in zip(ds, parts)]
    dvT = [dot_nn(goT[i][:, r0:r1], one) for one, (i, r0, r1, lo) in zip(p_low, parts)]
    for i in range(heads):
        mine = slice(i * len(spans), (i + 1) * len(spans))
        sums = []
        for group in (dvT[mine], dkT[mine]):
            total = [None] * len(spans)
            for part, (r0, r1, lo) in zip(group, spans):
                for n in range(lo // NEAR, r1 // NEAR):
                    one = part[:, n * NEAR - lo : (n + 1) * NEAR - lo]
                    total[n] = one if total[n] is None else total[n] + one
            sums.append(jnp.concatenate(total, axis=1))
        dvk = jnp.concatenate(sums, axis=0).T
        dqk = jnp.where(low, jnp.concatenate(dq[mine], axis=0) * (1.0 / math.sqrt(HD)), dvk)
        dqk = dqk * keep - pltpu.roll(dqk, 2 * HD - ROT // 2, 1) * ahead - pltpu.roll(dqk, ROT // 2, 1) * behind
        dqkv_ref[0, :, i * HEAD : i * HEAD + 2 * HD] = dqk.astype(BF16)
        dqkv_ref[0, :, i * HEAD + 2 * HD : (i + 1) * HEAD] = jnp.where(low, dvk, 0.0).astype(BF16)
        mix_ref[0, :, i * 2 * HD : (i + 1) * 2 * HD] = jnp.concatenate(mix[mine], axis=0).astype(BF16)

    dbias_ref[0] = jnp.sum(dqkv_ref[0].astype(F32), axis=0, keepdims=True)

    for t in range(width // tile):
        rows = slice(t * tile, (t + 1) * tile)
        g_in = dot_nn(naT_ref[rows, :], dqkv_ref[0])
        g_out = dot_nn(cotT_ref[rows, :], mix_ref[0])
        for i in range(heads):
            at = i * HEAD
            g_scr[rows, at : at + 2 * HD] = g_in[:, at : at + 2 * HD].astype(BF16)
            g_scr[rows, at + 2 * HD : at + HEAD] = (
                g_in[:, at + 2 * HD : at + HEAD] + g_out[:, i * 2 * HD : (i + 1) * 2 * HD]
            ).astype(BF16)

    hand_out(me_ref, g_scr, 0, gk_ref, gs_ref, 0, orders[0], core_bit)
    hand_out(me_ref, g_scr, block_cols // 2, gk_ref, gs_ref, kept, orders[1], core_bit)


def mlp_kernel(orders, core_bit, waits, me_ref, nm_ref, nmT_ref, cot_ref, cotT_ref, *rest):
    left, right, bias_ref, rest = rest[:4], rest[4:8], rest[8], rest[9 + waits :]
    act_ref, dh_ref, dbias_ref, gk_ref, gs_ref, wu_scr, wd_scr, g_scr = rest
    length, width = nm_ref.shape
    up_cols = wu_scr.shape[1]
    kept = gk_ref.shape[0] // 2
    tile = 256
    assemble(me_ref, left, gathered_order(orders[0], core_bit), wu_scr, 0)
    assemble(me_ref, right, gathered_order(orders[1], core_bit), wd_scr, 0)
    dbias_ref[0] = jnp.zeros_like(dbias_ref[0])

    for t in range(length // tile):
        rows = slice(t * tile, (t + 1) * tile)
        for n in range(0, up_cols, tile):
            hidden = dot_nn(nm_ref[rows, :], wu_scr[:, n : n + tile]) + bias_ref[0, :, n : n + tile]
            d_act = dot_nn(cot_ref[rows, :], wd_scr[:, n : n + tile])
            gate = 0.5 * (1.0 + lax.erf(hidden * (1.0 / math.sqrt(2.0))))
            act_ref[0, rows, n : n + tile] = (hidden * gate).astype(BF16)
            slope = gate + hidden * jnp.exp(-0.5 * hidden * hidden) * (1.0 / math.sqrt(2.0 * math.pi))
            dh = (d_act * slope).astype(BF16)
            dh_ref[0, rows, n : n + tile] = dh
            dbias_ref[0, :, n : n + tile] += jnp.sum(dh.astype(F32), axis=0, keepdims=True)

    for side, lhs, rhs in ((0, nmT_ref, dh_ref), (1, cotT_ref, act_ref)):

        for t in range(width // tile):
            rows = slice(t * tile, (t + 1) * tile)
            g_scr[rows, :] = dot_nn(lhs[rows, :], rhs[0]).astype(BF16)

        hand_out(me_ref, g_scr, 0, gk_ref, gs_ref, side * kept, orders[side], core_bit)


def weight_spec(array, block_of):
    count, _, rows, cols = array.shape
    return pl.BlockSpec((count, 1, rows, cols), lambda s: (0, block_of(s), 0, 0))


def block_part(kernel, w0, k0, count, slots, slot0, into, orders, core_bit, after, me, norm, norm_t, cot, cot_t,
               left, right, vectors, mid_cols, g_cols, scratch, us):
    length, width = norm.shape
    rows = left[0].shape[2]
    pieces = width // rows
    cols = vectors[0].shape[-1]
    per_step, total_slots = slots
    g_spec = pl.BlockSpec((pieces, per_step, rows, g_cols), lambda s: (0, slot0 + s, 0, 0))
    after = list(after) + list(into)
    fixed = 5 + len(left + right) + len(vectors) + len(after)
    return pl.pallas_call(
        functools.partial(kernel, orders, core_bit, len(after)),
        grid=(count,),
        in_specs=[SCALAR, full(length, width), full(width, length), full(length, width), full(width, length)]
        + [weight_spec(w, lambda s: w0 + s) for w in left + right]
        + [pl.BlockSpec((1, 1, cols), lambda s: (k0 + s, 0, 0))]
        + [full(*v.shape) for v in vectors[1:]]
        + [ANY] * len(after),
        out_specs=[pl.BlockSpec((1, length, m), lambda s: (s, 0, 0)) for m in mid_cols]
        + [pl.BlockSpec((1, 1, cols), lambda s: (s, 0, 0))] + [g_spec] * 2,
        out_shape=[shaped((count, length, m), BF16) for m in mid_cols]
        + [shaped((count, 1, cols), F32)] + [shaped((pieces, total_slots, rows, g_cols), BF16)] * 2,
        input_output_aliases={fixed - 2: len(mid_cols) + 1, fixed - 1: len(mid_cols) + 2} if into else {},
        scratch_shapes=scratch,
        compiler_params=pltpu.CompilerParams(vmem_limit_bytes=60 * 2**20),
        cost_estimate=cost(us * count),
    )(me, norm, norm_t, cot, cot_t, *left, *right, *vectors, *after)


def pick(refs, begins, scr):
    step = pl.program_id(0)
    for ref, begin, end in zip(refs, begins, begins[1:]):

        @pl.when((step >= begin) & (step < end))
        def _():
            scr[...] = ref[0]


def attention_tail_kernel(orders, core_bit, begins, waits, me_ref, *rest):
    left, right, rest = rest[:4], rest[4:8], rest[8:]
    calls = len(begins) - 1
    dqkv_refs, mix_refs, rest = rest[:calls], rest[calls : 2 * calls], rest[2 * calls :]
    sums_in, rest = rest[: len(rest) - waits - 6], rest[len(rest) - 6 :]
    branch_ref, dna_ref, w_scr, wv_scr, dqkv_scr, mix_scr = rest
    block_cols = w_scr.shape[1]

    @pl.when(pl.program_id(0) == 0)
    def _():
        branch_ref[...] = sums_in[0][...] if sums_in else jnp.zeros_like(branch_ref)
        dna_ref[...] = sums_in[1][...] if len(sums_in) > 1 else jnp.zeros_like(dna_ref)

    pick(dqkv_refs, begins, dqkv_scr)
    pick(mix_refs, begins, mix_scr)
    assemble(me_ref, left, gathered_order(orders[0], core_bit), w_scr, 0)
    assemble(me_ref, right, gathered_order(orders[1], core_bit), w_scr, block_cols // 2)
    for i in range(block_cols // HEAD):
        wv_scr[:, i * 2 * HD : (i + 1) * 2 * HD] = w_scr[:, i * HEAD + 2 * HD : (i + 1) * HEAD]
    tile = 256

    for t in range(branch_ref.shape[0] // tile):
        rows = slice(t * tile, (t + 1) * tile)
        branch_ref[rows, :] += dot_nt(mix_scr[rows, :], wv_scr[...])
        dna_ref[rows, :] += dot_nt(dqkv_scr[rows, :], w_scr[...])


def mlp_tail_kernel(orders, core_bit, sums, small_ks, waits, me_ref, *rest):
    left, right, dh_ref, act_ref, rest = rest[:4], rest[4:8], rest[8], rest[9], rest[10:]
    sums_in, rest = rest[:sums], rest[sums:]
    last = small_ks is not None
    if last:
        dna_ref, x_ref, cot_ref, ga_ref, gm_ref, bo_ref, bd_ref = rest[:7]
        small_refs = rest[7 : 7 + len(small_ks)]
        block_ref, grad_ref, stats_ref, branch_ref, dnm_ref, wu_scr, wd_scr = rest[7 + len(small_ks) + waits :]
    else:
        branch_ref, dnm_ref, wu_scr, wd_scr = rest[waits:]
    length = branch_ref.shape[0]
    step = pl.program_id(0)

    @pl.when(step == 0)
    def _():
        branch_ref[...] = sums_in[0][...] if sums else jnp.zeros_like(branch_ref)
        dnm_ref[...] = sums_in[1][...] if sums > 1 else jnp.zeros_like(dnm_ref)

    assemble(me_ref, left, gathered_order(orders[0], core_bit), wu_scr, 0)
    assemble(me_ref, right, gathered_order(orders[1], core_bit), wd_scr, 0)
    tile = 256

    for t in range(length // tile):
        rows = slice(t * tile, (t + 1) * tile)
        branch_ref[rows, :] += dot_nt(act_ref[0, rows, :], wd_scr[...])
        dnm_ref[rows, :] += dot_nt(dh_ref[0, rows, :], wu_scr[...])

    if not last:
        return

    @pl.when(step == pl.num_programs(0) - 1)
    def _():
        stats_ref[...] = jnp.zeros_like(stats_ref)
        small = 128

        @pl.loop(0, length // small)
        def _(t):
            rows = pl.ds(pl.multiple_of(t * small, small), small)
            x = x_ref[rows, :].astype(F32)
            cot = cot_ref[rows, :].astype(F32)
            normed, inv_std = normalize(x)
            block_ref[rows, :] = (x + branch_ref[rows, :] + bo_ref[...] + bd_ref[...]).astype(BF16)
            dna, dnm = dna_ref[rows, :], dnm_ref[rows, :]
            d_normed = dna * ga_ref[...] + dnm * gm_ref[...]
            pulled = (
                d_normed
                - jnp.mean(d_normed, axis=1, keepdims=True)
                - normed * jnp.mean(d_normed * normed, axis=1, keepdims=True)
            )
            grad_ref[rows, :] = (cot + inv_std * pulled).astype(BF16)
            for at, term in enumerate((cot, dna * normed, dna, dnm * normed, dnm)):
                stats_ref[at : at + 1, :] += jnp.sum(term, axis=0, keepdims=True)

        for ref, (first, k0, blocks) in zip(small_refs, small_ks):
            for i in range(ref.shape[0]):
                block = lax.rem(me_ref[1] + (blocks - k0 - i), blocks)
                stats_ref[pl.ds(first + block, 1), :] = ref[i]


def attention_tail_part(begins, starts, orders, core_bit, after, me, left, right, mids, sums, us):
    steps = left[0].shape[1]
    pieces = 2 * sum(w.shape[0] for w in left) // 2
    width = pieces * left[0].shape[2]
    length = mids[0][0].shape[1]

    def mid_spec(array, n):
        begin, end = begins[n], begins[n + 1]
        return pl.BlockSpec(
            (1,) + array.shape[1:], lambda s: (jnp.clip(s - begin, 0, end - begin - 1), 0, 0)
        )

    def block_of(step):
        block = step
        for begin, start in zip(begins, starts):
            block = jnp.where(step >= begin, start + step - begin, block)
        return block

    block_cols, half_cols = mids[0][0].shape[2], mids[1][0].shape[2]
    outs = [shaped((length, width), F32)] * 2
    return pl.pallas_call(
        functools.partial(attention_tail_kernel, orders, core_bit, begins, len(after)),
        grid=(steps,),
        in_specs=[SCALAR] + [weight_spec(w, lambda s: block_of(s)) for w in left + right]
        + [mid_spec(array, n) for group in mids for n, array in enumerate(group)]
        + [full(*e.shape) for e in sums] + [ANY] * len(after),
        out_specs=[full(*o.shape) for o in outs],
        out_shape=outs,
        scratch_shapes=[pltpu.VMEM((width, block_cols), BF16), pltpu.VMEM((width, half_cols), BF16)]
        + [pltpu.VMEM(group[0].shape[1:], BF16) for group in mids],
        compiler_params=pltpu.CompilerParams(vmem_limit_bytes=60 * 2**20),
        cost_estimate=cost(us),
    )(me, *left, *right, *[array for group in mids for array in group], *sums, *after)


def mlp_tail_part(w0, orders, core_bit, after, me, left, right, act, dh, sums, finals, smalls, us):
    count, length, cols = dh.shape
    width = sum(w.shape[0] for w in left) * left[0].shape[2]
    mid_spec = pl.BlockSpec((1, length, cols), lambda s: (s, 0, 0))
    total = shaped((length, width), F32)
    scratch = [pltpu.VMEM((width, cols), BF16)] * 2
    outs, small_ks = [total] * 2, None
    if finals:
        small_ks, arrays = smalls
        blocks = small_ks[0][2]
        outs = [shaped((length, width), BF16)] * 2 + [shaped((-(-(5 + 2 * blocks) // 8) * 8, width), F32)]
        scratch = [pltpu.VMEM((length, width), F32)] * 2 + scratch
        finals = list(finals) + list(arrays)
    extra = list(sums) + list(finals)
    return pl.pallas_call(
        functools.partial(mlp_tail_kernel, orders, core_bit, len(sums), small_ks, len(after)),
        grid=(count,),
        in_specs=[SCALAR] + [weight_spec(w, lambda s: w0 + s) for w in left + right] + [mid_spec] * 2
        + [full(*e.shape) for e in extra] + [ANY] * len(after),
        out_specs=[full(*o.shape) for o in outs],
        out_shape=outs,
        scratch_shapes=scratch,
        compiler_params=pltpu.CompilerParams(vmem_limit_bytes=60 * 2**20),
        cost_estimate=cost(us),
    )(me, *left, *right, dh, act, *extra, *after)


def fence_kernel(*_):
    pass


def fence(values, after=()):
    count = len(values)
    return pl.pallas_call(
        fence_kernel,
        in_specs=[ANY] * (count + len(after)),
        out_specs=[ANY] * count,
        out_shape=[shaped(value.shape, value.dtype) for value in values],
        input_output_aliases={n: n for n in range(count)},
        cost_estimate=cost(1),
    )(*values, *after)


def swap(value, bit):
    axis, flip = ("dp", 1) if bit == 1 else ("row", bit // 2)
    return flipped(value, axis, flip)


def flipped(value, axis, flip):
    return lax.ppermute(value, axis, [(i, i ^ flip) for i in range(lax.axis_size(axis))])


def shifted(value, by):
    size = lax.axis_size("col")
    return lax.ppermute(value, "col", [(i, (i + by) % size) for i in range(size)])


class Gather:
    def __init__(self, blocks, orders, core_bit):
        cut = blocks.shape[2] // 2
        self.orders, self.core_bit, self.done = orders, core_bit, 0
        self.block = blocks[0]
        self.held = [blocks[None, :, :, :cut], blocks[None, :, :, cut:]]

    def advance(self):
        if self.done > 0:
            self.held = [jnp.concatenate(pair, axis=0) for pair in zip(self.held, self.moving)]
        self.moving = [swap(one, order[self.done]) for one, order in zip(self.held, self.orders)]
        self.done += 1

    def cross(self):
        self.over = [swap(one, self.core_bit) for one in self.held + self.moving]

    def sides(self):
        return ([self.held[i], self.moving[i], self.over[i], self.over[i + 2]] for i in range(2))


class Reduction:
    def __init__(self, keep, send, orders, core_bit):
        self.keep, self.orders, self.came = keep, orders, swap(send, core_bit)
        self.later = [[] for _ in orders]
        self.done = 0

    def half(self):
        return self.keep.shape[0] // len(self.orders) >> (self.done + 1)


def merge_kernel(layout, ins, first_out, *refs):
    outs = refs[first_out : first_out + len(layout)]
    at = 0
    for group, out in zip(layout, outs):
        column = 0
        for terms in group:
            total = refs[at][...].astype(F32)
            for ref in refs[at + 1 : at + terms]:
                total = total + ref[...].astype(F32)
            at += terms
            cols = total.shape[-1]
            out[..., column : column + cols] = total.astype(BF16)
            column += cols
    assert at == ins


def merge(reductions, after, values=()):
    specs, arrays, layout, shapes, plans = [], [], [], [], []

    def block(array, count, index):
        shape = (count,) + array.shape[1:]
        return pl.BlockSpec(shape, lambda s: (index,) + (0,) * (len(shape) - 1), pipeline_mode=pl.Buffered(1))

    for r in reductions:
        half = r.half()
        count = max(half, 1)
        size = r.keep.shape[0] // len(r.orders)
        groups = []
        for side in range(len(r.orders)):
            terms = [(one, (side * size + half) // count) for one in (r.keep, r.came)]
            terms += [(one, half // count) for one in r.later[side]]
            for one, index in terms:
                specs.append(block(one, count, index))
                arrays.append(one)
            groups.append(len(terms))
        _, slots, rows, cols = r.keep.shape
        if half:
            layout += [(terms,) for terms in groups]
            shapes += [(half, slots, rows, cols)] * len(groups)
        else:
            layout.append(tuple(groups))
            shapes.append((1, slots, rows, cols * len(groups)))
        plans.append((r, half))
    out = list(pl.pallas_call(
        functools.partial(merge_kernel, layout, len(arrays), len(arrays) + len(values) + len(after)),
        grid=(1,),
        in_specs=specs + [ANY] * (len(values) + len(after)),
        out_specs=[full(*shape) for shape in shapes] + [ANY] * len(values),
        out_shape=[shaped(shape, BF16) for shape in shapes] + [shaped(v.shape, v.dtype) for v in values],
        input_output_aliases={len(arrays) + n: len(shapes) + n for n in range(len(values))},
        compiler_params=pltpu.CompilerParams(vmem_limit_bytes=60 * 2**20),
        cost_estimate=cost(3),
    )(*arrays, *values, *after))
    token, finished = out[0], []
    passed = out[len(shapes) :]
    for r, half in plans:
        if half:
            for side, order in enumerate(r.orders):
                r.later[side].append(swap(out.pop(0), order[r.done]))
            r.done += 1
        else:
            finished.append(out.pop(0)[0])
    return finished, [token], passed


def phase(users, values=(), after=()):
    values = list(values)
    out = list(fence(values + [one for user in users for one in user.moving], after))
    at = len(values)
    for user in users:
        user.moving = out[at : at + len(user.moving)]
        at += len(user.moving)
    return out


def sum_over(value, axes):
    for axis in axes:
        flip = 1
        while flip < lax.axis_size(axis):
            value = value + flipped(value, axis, flip)
            flip *= 2
    return value


def on_device(
    tokens_in,
    segment_ids,
    attn_gain,
    attn_shift,
    mlp_gain,
    mlp_shift,
    qkv_weight,
    qkv_bias,
    out_weight,
    out_bias,
    up_weight,
    up_bias,
    down_weight,
    down_bias,
    out_cotangent,
):
    row_size = lax.axis_size("row")
    col_size = lax.axis_size("col")
    length, width = tokens_in.shape
    rows = qkv_weight.shape[0]
    half_rows = rows // 2
    local_heads = qkv_weight.shape[1] // QKV
    block_cols = local_heads * HEAD
    up_cols = up_weight.shape[1]
    row_id = lax.axis_index("row")
    col_id = lax.axis_index("col")
    half = lax.axis_index("dp") % 2
    me = jnp.stack([row_id * 2 + half, col_id]).astype(jnp.int32)
    row_bits = [2 << i for i in range(row_size.bit_length() - 1)]
    core_bit, far_bits = row_bits[0], row_bits[1:][::-1]
    orders = (far_bits + [1], [1] + far_bits)

    head_weight = jnp.concatenate(
        [qkv_weight.reshape(rows, local_heads, QKV), out_weight.T.reshape(rows, local_heads, HD)], axis=2
    ).reshape(rows, block_cols)
    attn_own = lax.dynamic_slice_in_dim(head_weight, half * half_rows, half_rows, axis=0)
    mlp_own = jnp.concatenate(
        [
            lax.dynamic_slice_in_dim(up_weight, half * half_rows, half_rows, axis=0),
            lax.dynamic_slice_in_dim(down_weight, half * half_rows, half_rows, axis=1).T,
        ],
        axis=1,
    )
    cut = block_cols // 2

    seg_row = lax.dynamic_index_in_dim(segment_ids, row_id * col_size + col_id, axis=0, keepdims=False)
    na, na_t, nm, nm_t, cot_t, keep, ahead, behind, mask = prep_part(
        tokens_in, out_cotangent, [v[None, :] for v in (attn_gain, attn_shift, mlp_gain, mlp_shift)], seg_row,
    )
    blocks_here = (col_id - jnp.arange(col_size)) % col_size
    head_bias = jnp.pad(
        qkv_bias.reshape(col_size, local_heads, QKV), ((0, 0), (0, 0), (0, HEAD - QKV))
    ).reshape(col_size, 1, block_cols)
    head_bias = jnp.take(head_bias, blocks_here, axis=0)
    hidden_bias = jnp.take(up_bias.reshape(col_size, 1, up_cols), blocks_here, axis=0)

    far = len(orders[0])

    def gather_col(own):
        return [own] + [shifted(own, k) for k in range(1, col_size)]

    attn = Gather(jnp.stack(gather_col(attn_own)), orders, core_bit)
    mlp_blocks = gather_col(fence([mlp_own], [attn.held[0]])[0])
    for _ in range(far):
        attn.advance()
        phase([attn], [], [na, mlp_blocks[1]] if attn.done == 1 else mlp_blocks[2:])
    mlp_blocks = fence(mlp_blocks, attn.moving)
    attn.cross()
    mlp = Gather(jnp.stack(mlp_blocks), orders, core_bit)
    mlp.advance()

    def attention_call(weights, w0, k0, count, slots, slot0, into, after):
        return block_part(
            attention_kernel, w0, k0, count, slots, slot0, into, orders, core_bit, after, me, na, na_t, out_cotangent,
            cot_t, *weights.sides(), [head_bias, keep, ahead, behind, mask], [block_cols, cut], cut,
            [
                pltpu.VMEM((width, block_cols), BF16), pltpu.VMEM((width, cut), BF16),
                pltpu.VMEM((length, block_cols), F32), pltpu.VMEM((length, cut), BF16),
                pltpu.VMEM((width, block_cols), BF16),
            ],
            10,
        )

    def mlp_call(weights, w0, k0, count, slots, slot0, into, after):
        return block_part(
            mlp_kernel, w0, k0, count, slots, slot0, into, orders, core_bit, after, me, nm, nm_t, out_cotangent, cot_t,
            *weights.sides(), [hidden_bias], [up_cols, up_cols], cut, [pltpu.VMEM((width, up_cols), BF16)] * 3, 6,
        )

    per_mlp = up_cols // cut
    per_call = 2
    starts = list(range(0, col_size, per_call))[::-1]
    attn_calls, into, token = [], [], []
    for k0 in starts:
        outs = attention_call(attn, k0, k0, per_call, (1, col_size), k0 // 1, into, token)
        attn_calls.append(outs)
        into = list(outs[3:])
        sent = into[1:] if k0 == starts[-1] else []
        token = phase([mlp], sent, [outs[2]])
        sent, token = token[: len(sent)], token[-1:]
        if mlp.done < far:
            mlp.advance()
            while mlp.done < far and k0 == starts[-1]:
                phase([mlp])
                mlp.advance()
    while mlp.done < far:
        mlp.advance()
        token = phase([mlp])[:1]
    mlp.cross()
    attn_sum = Reduction(into[0], sent[0], orders, core_bit)

    totals = {}

    def go_on(reductions, after, values=()):
        reductions = [r for r in reductions if id(r) not in totals]
        ending = [r for r in reductions if not r.half()]
        finished, token, passed = merge(reductions, after, values)
        totals.update(zip((id(r) for r in ending), finished))
        return token, passed

    token, _ = go_on([attn_sum], mlp.over[2:])
    mlp_calls, mlp_sums = [], []
    for n, k0 in enumerate(starts):
        outs = mlp_call(mlp, k0, k0, per_call, (per_mlp, per_mlp * per_call), 0, [], token)
        mlp_calls.append(outs)
        token, sent = go_on([attn_sum] + mlp_sums, [outs[2]], [outs[4]])
        mlp_sums.append(Reduction(outs[3], sent[0], orders, core_bit))
    while id(attn_sum) not in totals:
        token, _ = go_on([attn_sum], token)
    attn_total = totals[id(attn_sum)]
    attn_moves = {0: attn_total[0]}
    for k in range(2, col_size):
        attn_moves[k] = shifted(attn_total[k], -k)
    begins = list(range(0, col_size + 1, per_call))
    branch, d_norm_attn = attention_tail_part(
        begins, starts, orders, core_bit, token, me, *attn.sides(), [[c[0] for c in attn_calls], [c[1] for c in attn_calls]],
        [], 11,
    )
    token, passed = go_on(mlp_sums, [branch], [attn_moves[k] for k in range(2, col_size)])
    attn_moves.update(zip(range(2, col_size), passed))
    attn_moves[1] = shifted(attn_total[1], -1)

    def settle(parts):
        total = sum((part.astype(F32) for part in parts[1:]), parts[0].astype(F32))
        flip = 2
        while flip < lax.axis_size("dp"):
            total = total + flipped(total, "dp", flip)
            flip *= 2
        mine = total.astype(BF16)
        return mine, swap(mine, 1)

    def whole_block(mine, other):
        first = half == 0
        return jnp.concatenate([jnp.where(first, mine, other), jnp.where(first, other, mine)], axis=0).astype(F32)

    small_ks = tuple((5, k0, col_size) for k0 in starts) + tuple((5 + col_size, k0, col_size) for k0 in starts)
    small_parts = [c[2] for c in mlp_calls] + [c[2] for c in attn_calls]
    mlp_moves = {}
    d_norm_mlp = None
    for n, k0 in enumerate(starts):
        last = n == len(starts) - 1
        sums = [branch] if n == 0 else [branch, d_norm_mlp]
        finals = [
            d_norm_attn, tokens_in, out_cotangent, attn_gain[None, :], mlp_gain[None, :], out_bias[None, :],
            down_bias[None, :],
        ]
        result = mlp_tail_part(
            k0, orders, core_bit, token, me, *mlp.sides(), mlp_calls[n][0], mlp_calls[n][1], sums,
            finals if last else [], (small_ks, small_parts) if last else None, 9,
        )
        if n == 0:
            token, passed = go_on(mlp_sums, result[:1], [attn_moves[1]])
            attn_moves[1] = passed[0]
            attn_mine, attn_other = settle([attn_moves[k] for k in range(col_size)])
        else:
            token, passed = go_on(mlp_sums, result[:1], result[2:])
        if last:
            block_out, in_grad, _ = result
            smalls = passed[0]
        else:
            branch, d_norm_mlp = result
        while last and any(id(r) not in totals for r in mlp_sums):
            token, _ = go_on(mlp_sums, token)
        for k1, r in zip(starts, mlp_sums):
            if id(r) in totals and k1 not in mlp_moves:
                for i in range(per_call):
                    slots = [totals[id(r)][i * per_mlp + j] for j in range(per_mlp)]
                    part = jnp.concatenate([s[:, :cut] for s in slots] + [s[:, cut:] for s in slots], axis=1)
                    mlp_moves[k1 + i] = part if k1 + i == 0 else shifted(part, -(k1 + i))
    head_row, up_row = 5 + col_size, 5
    smalls = sum_over(smalls, ("row", "dp"))
    smalls, *came = fence([smalls] + [mlp_moves[k] for k in range(1, col_size)])
    mlp_mine, mlp_other = settle([mlp_moves[0]] + came)
    g_heads = whole_block(attn_mine, attn_other).reshape(rows, local_heads, HEAD)
    g_mlp = whole_block(mlp_mine, mlp_other)
    g_up, g_down = g_mlp[:, :up_cols], g_mlp[:, up_cols:]
    smalls = sum_over(smalls, ("col",))
    return (
        block_out,
        in_grad,
        smalls[1],
        smalls[2],
        smalls[3],
        smalls[4],
        g_heads[:, :, :QKV].reshape(rows, local_heads * QKV),
        smalls[head_row : head_row + col_size].reshape(col_size * local_heads, HEAD)[:, :QKV].reshape(-1),
        g_heads[:, :, QKV:].reshape(rows, local_heads * HD).T,
        smalls[0],
        g_up,
        smalls[up_row : up_row + col_size].reshape(-1),
        g_down.T,
        smalls[0],
    )


def solution(mesh):
    return jax.shard_map(
        on_device,
        mesh=mesh,
        in_specs=(
            P(("dp", "row", "col"), None),
            P("dp", None),
            P(),
            P(),
            P(),
            P(),
            P("row", "col"),
            P(),
            P("col", "row"),
            P(),
            P("row", "col"),
            P(),
            P("col", "row"),
            P(),
            P(("dp", "row", "col"), None),
        ),
        out_specs=(
            P(("dp", "row", "col"), None),
            P(("dp", "row", "col"), None),
            P(),
            P(),
            P(),
            P(),
            P("row", "col"),
            P(),
            P("col", "row"),
            P(),
            P("row", "col"),
            P(),
            P("col", "row"),
            P(),
        ),
        check_vma=False,
    )
```

```python
import functools
import math

import jax
import jax.numpy as jnp
from jax import lax
from jax.experimental import pallas as pl
from jax.experimental.pallas import tpu as pltpu
from jax.sharding import PartitionSpec as P

HD = 64
ROT = 16
QKV = 3 * HD
HEAD = 4 * HD
EPSILON = 1e-05
ROPE_BASE = 10000.0
NEAR = 128
LONGEST = 256
F32 = jnp.float32
BF16 = jnp.bfloat16


def dot_nn(a, b):
    return lax.dot_general(a, b, (((1,), (0,)), ((), ())), preferred_element_type=F32)


def dot_nt(a, b):
    return lax.dot_general(a, b, (((1,), (1,)), ((), ())), preferred_element_type=F32)


def gathered_order(order, core_bit):
    held = [0]
    for bit in order[:-1]:
        held = held + [j | bit for j in held]
    came = [j | order[-1] for j in held]
    return held, came, [j | core_bit for j in held], [j | core_bit for j in came]


def reduced_order(order):
    kept = [0]
    for bit in order[::-1]:
        kept = kept + [j | bit for j in kept]
    return kept


def assemble(me_ref, w_refs, held, w_scr, at_col):
    for ref, pieces in zip(w_refs, held):
        _, _, rows, cols = ref.shape
        for t, j in enumerate(pieces):
            at = pl.multiple_of((me_ref[0] ^ j) * rows, 16)
            w_scr[pl.ds(at, rows), at_col : at_col + cols] = ref[t, 0]


def hand_out(me_ref, g_scr, at_col, keep_ref, send_ref, first, order, core_bit):
    _, slots, rows, cols = keep_ref.shape
    for t, j in enumerate(reduced_order(order)):
        for ref, piece in ((keep_ref, j), (send_ref, j | core_bit)):
            at = pl.multiple_of((me_ref[0] ^ piece) * rows, 16)
            for slot in range(slots):
                left = at_col + slot * cols
                ref[first + t, slot] = g_scr[pl.ds(at, rows), left : left + cols]


def normalize(x):
    center = x - jnp.mean(x, axis=1, keepdims=True)
    inv_std = lax.rsqrt(jnp.mean(center * center, axis=1, keepdims=True) + EPSILON)
    return center * inv_std, inv_std


def prep_kernel(
    x_ref, cot_ref, ga_ref, sa_ref, gm_ref, sm_ref, segc_ref, segr_ref, freq_ref,
    na_ref, naT_ref, nm_ref, nmT_ref, cotT_ref, keep_ref, ahead_ref, behind_ref, mask_ref,
):
    length = x_ref.shape[0]
    tile = 128

    @pl.loop(0, length // tile)
    def _(t):
        rows = pl.ds(pl.multiple_of(t * tile, tile), tile)
        normed, _ = normalize(x_ref[rows, :].astype(F32))
        na_ref[rows, :] = (normed * ga_ref[...] + sa_ref[...]).astype(BF16)
        nm_ref[rows, :] = (normed * gm_ref[...] + sm_ref[...]).astype(BF16)
        same = segc_ref[rows, :] == segr_ref[...]
        cols = lax.broadcasted_iota(jnp.int32, (tile, length), 1)
        ids = lax.broadcasted_iota(jnp.int32, (tile, length), 0) + t * tile
        mask_ref[rows, :] = jnp.where(same & (cols <= ids), 0.0, -jnp.inf)
        starts = jnp.min(jnp.where(same, cols, length).astype(F32), axis=1, keepdims=True)
        places = ids[:, :1].astype(F32) - starts
        angles = places * freq_ref[...]
        lane = lax.broadcasted_iota(jnp.int32, (tile, 2 * HD), 1) % HD
        cosine, sine = jnp.cos(angles), jnp.sin(angles)
        keep_ref[rows, :] = jnp.where(lane < ROT, cosine, 1.0)
        ahead_ref[rows, :] = jnp.where(lane < ROT // 2, -sine, 0.0)
        behind_ref[rows, :] = jnp.where((lane < ROT) & (lane >= ROT // 2), sine, 0.0)

    naT_ref[...] = na_ref[...].T
    nmT_ref[...] = nm_ref[...].T
    cotT_ref[...] = cot_ref[...].T


def full(*shape):
    return pl.BlockSpec(shape, lambda *_: (0,) * len(shape), pipeline_mode=pl.Buffered(1))


ANY = pl.BlockSpec(memory_space=pl.ANY)
SCALAR = pl.BlockSpec(memory_space=pltpu.SMEM)


def cost(us):
    return pl.CostEstimate(flops=int(us * 1.15e9), bytes_accessed=2**20, transcendentals=0)


def shaped(shape, dtype):
    return jax.ShapeDtypeStruct(shape, dtype)


def prep_part(tokens, cot, gains, seg_row):
    length, width = tokens.shape
    halves = ROT // 2
    step = (lax.iota(jnp.int32, 2 * HD) % HD % halves).astype(F32)
    freq = (ROPE_BASE ** (-(step * (2.0 / ROT))))[None, :]
    table = shaped((length, 2 * HD), F32)
    return pl.pallas_call(
        prep_kernel,
        grid=(1,),
        in_specs=[full(length, width)] * 2 + [full(1, width)] * 4
        + [full(length, 1), full(1, length), full(1, 2 * HD)],
        out_specs=[full(length, width), full(width, length)] * 2 + [full(width, length)]
        + [full(length, 2 * HD)] * 3 + [full(length, length)],
        out_shape=[shaped((length, width), BF16), shaped((width, length), BF16)] * 2
        + [shaped((width, length), BF16)] + [table] * 3 + [shaped((length, length), F32)],
        compiler_params=pltpu.CompilerParams(vmem_limit_bytes=60 * 2**20),
        cost_estimate=cost(6),
    )(tokens, cot, *gains, seg_row[:, None], seg_row[None, :], freq)


def attention_kernel(orders, core_bit, waits, me_ref, na_ref, naT_ref, cot_ref, cotT_ref, *rest):
    left, right, rest = rest[:4], rest[4:8], rest[8:]
    bias_ref, keep_ref, ahead_ref, behind_ref, mask_ref = rest[:5]
    dqkv_ref, mix_ref, dbias_ref, gk_ref, gs_ref, w_scr, wv_scr, qkv_scr, dattn_scr, g_scr = rest[5 + waits :]
    length, width = na_ref.shape
    block_cols = w_scr.shape[1]
    heads = block_cols // HEAD
    kept = gk_ref.shape[0] // 2
    tile = 256
    assemble(me_ref, left, gathered_order(orders[0], core_bit), w_scr, 0)
    assemble(me_ref, right, gathered_order(orders[1], core_bit), w_scr, block_cols // 2)
    for i in range(heads):
        wv_scr[:, i * 2 * HD : (i + 1) * 2 * HD] = w_scr[:, i * HEAD + 2 * HD : (i + 1) * HEAD]

    for t in range(length // tile):
        rows = slice(t * tile, (t + 1) * tile)
        qkv_scr[rows, :] = dot_nn(na_ref[rows, :], w_scr[...]) + bias_ref[0]
        dattn_scr[rows, :] = dot_nn(cot_ref[rows, :], wv_scr[...]).astype(BF16)

    low = lax.broadcasted_iota(jnp.int32, (length, 2 * HD), 1) < HD
    keep, ahead, behind = keep_ref[...], ahead_ref[...], behind_ref[...]
    none = jnp.zeros((length, 2 * HD), BF16)
    spans = [(b * NEAR, (b + 1) * NEAR, max(0, b * NEAR - LONGEST)) for b in range(length // NEAR)]
    q0, k0, v1, go1, qT, goT = [], [], [], [], [], []
    for i in range(heads):
        qk = qkv_scr[:, i * HEAD : i * HEAD + 2 * HD]
        qk = qk * keep + pltpu.roll(qk, 2 * HD - ROT // 2, 1) * ahead + pltpu.roll(qk, ROT // 2, 1) * behind
        q0.append(jnp.where(low, qk * (1.0 / math.sqrt(HD)), 0.0).astype(BF16))
        k0.append(jnp.where(low, pltpu.roll(qk, HD, 1), 0.0).astype(BF16))
        value = pltpu.roll(qkv_scr[:, i * HEAD + 2 * HD : (i + 1) * HEAD], HD, 1)
        v1.append(jnp.where(low, 0.0, value).astype(BF16))
        go = dattn_scr[:, i * 2 * HD : (i + 1) * 2 * HD]
        go1.append(jnp.where(low, none, go))
        qT.append(q0[i].T[:HD])
        goT.append(go.T[HD:])
    parts = [(i, r0, r1, lo) for i in range(heads) for r0, r1, lo in spans]
    s = [dot_nt(q0[i][r0:r1], k0[i][lo:r1]) + mask_ref[r0:r1, lo:r1] for i, r0, r1, lo in parts]
    dp = [dot_nt(go1[i][r0:r1], v1[i][lo:r1]) for i, r0, r1, lo in parts]
    peak = [jnp.max(one, axis=1, keepdims=True) for one in s]
    e = [jnp.exp(one - top) for one, top in zip(s, peak)]
    norm = [1.0 / jnp.sum(one, axis=1, keepdims=True) for one in e]
    p = [one * scale for one, scale in zip(e, norm)]
    p_low = [one.astype(BF16) for one in p]
    mix = [dot_nn(one, v1[i][lo:r1]) for one, (i, r0, r1, lo) in zip(p_low, parts)]
    delta = [
        jnp.sum(one * go1[i][r0:r1].astype(F32), axis=1, keepdims=True) for one, (i, r0, r1, lo) in zip(mix, parts)
    ]
    ds = [(one * (grad - centre)).astype(BF16) for one, grad, centre in zip(p, dp, delta)]
    dq = [dot_nn(one, k0[i][lo:r1]) for one, (i, r0, r1, lo) in zip(ds, parts)]
    dkT = [dot_nn(qT[i][:, r0:r1], one) for one, (i, r0, r1, lo) in zip(ds, parts)]
    dvT = [dot_nn(goT[i][:, r0:r1], one) for one, (i, r0, r1, lo) in zip(p_low, parts)]
    for i in range(heads):
        mine = slice(i * len(spans), (i + 1) * len(spans))
        sums = []
        for group in (dvT[mine], dkT[mine]):
            total = [None] * len(spans)
            for part, (r0, r1, lo) in zip(group, spans):
                for n in range(lo // NEAR, r1 // NEAR):
                    one = part[:, n * NEAR - lo : (n + 1) * NEAR - lo]
                    total[n] = one if total[n] is None else total[n] + one
            sums.append(jnp.concatenate(total, axis=1))
        dvk = jnp.concatenate(sums, axis=0).T
        dqk = jnp.where(low, jnp.concatenate(dq[mine], axis=0) * (1.0 / math.sqrt(HD)), dvk)
        dqk = dqk * keep - pltpu.roll(dqk, 2 * HD - ROT // 2, 1) * ahead - pltpu.roll(dqk, ROT // 2, 1) * behind
        dqkv_ref[0, :, i * HEAD : i * HEAD + 2 * HD] = dqk.astype(BF16)
        dqkv_ref[0, :, i * HEAD + 2 * HD : (i + 1) * HEAD] = jnp.where(low, dvk, 0.0).astype(BF16)
        mix_ref[0, :, i * 2 * HD : (i + 1) * 2 * HD] = jnp.concatenate(mix[mine], axis=0).astype(BF16)

    dbias_ref[0] = jnp.sum(dqkv_ref[0].astype(F32), axis=0, keepdims=True)

    for t in range(width // tile):
        rows = slice(t * tile, (t + 1) * tile)
        g_in = dot_nn(naT_ref[rows, :], dqkv_ref[0])
        g_out = dot_nn(cotT_ref[rows, :], mix_ref[0])
        for i in range(heads):
            at = i * HEAD
            g_scr[rows, at : at + 2 * HD] = g_in[:, at : at + 2 * HD].astype(BF16)
            g_scr[rows, at + 2 * HD : at + HEAD] = (
                g_in[:, at + 2 * HD : at + HEAD] + g_out[:, i * 2 * HD : (i + 1) * 2 * HD]
            ).astype(BF16)

    hand_out(me_ref, g_scr, 0, gk_ref, gs_ref, 0, orders[0], core_bit)
    hand_out(me_ref, g_scr, block_cols // 2, gk_ref, gs_ref, kept, orders[1], core_bit)


def mlp_kernel(orders, core_bit, waits, me_ref, nm_ref, nmT_ref, cot_ref, cotT_ref, *rest):
    left, right, bias_ref, rest = rest[:4], rest[4:8], rest[8], rest[9 + waits :]
    act_ref, dh_ref, dbias_ref, gk_ref, gs_ref, wu_scr, wd_scr, g_scr = rest
    length, width = nm_ref.shape
    up_cols = wu_scr.shape[1]
    kept = gk_ref.shape[0] // 2
    tile = 256
    assemble(me_ref, left, gathered_order(orders[0], core_bit), wu_scr, 0)
    assemble(me_ref, right, gathered_order(orders[1], core_bit), wd_scr, 0)
    dbias_ref[0] = jnp.zeros_like(dbias_ref[0])

    for t in range(length // tile):
        rows = slice(t * tile, (t + 1) * tile)
        for n in range(0, up_cols, tile):
            hidden = dot_nn(nm_ref[rows, :], wu_scr[:, n : n + tile]) + bias_ref[0, :, n : n + tile]
            d_act = dot_nn(cot_ref[rows, :], wd_scr[:, n : n + tile])
            gate = 0.5 * (1.0 + lax.erf(hidden * (1.0 / math.sqrt(2.0))))
            act_ref[0, rows, n : n + tile] = (hidden * gate).astype(BF16)
            slope = gate + hidden * jnp.exp(-0.5 * hidden * hidden) * (1.0 / math.sqrt(2.0 * math.pi))
            dh = (d_act * slope).astype(BF16)
            dh_ref[0, rows, n : n + tile] = dh
            dbias_ref[0, :, n : n + tile] += jnp.sum(dh.astype(F32), axis=0, keepdims=True)

    for side, lhs, rhs in ((0, nmT_ref, dh_ref), (1, cotT_ref, act_ref)):

        for t in range(width // tile):
            rows = slice(t * tile, (t + 1) * tile)
            g_scr[rows, :] = dot_nn(lhs[rows, :], rhs[0]).astype(BF16)

        hand_out(me_ref, g_scr, 0, gk_ref, gs_ref, side * kept, orders[side], core_bit)


def weight_spec(array, block_of):
    count, _, rows, cols = array.shape
    return pl.BlockSpec((count, 1, rows, cols), lambda s: (0, block_of(s), 0, 0))


def block_part(kernel, w0, k0, count, slots, slot0, into, orders, core_bit, after, me, norm, norm_t, cot, cot_t,
               left, right, vectors, mid_cols, g_cols, scratch, us):
    length, width = norm.shape
    rows = left[0].shape[2]
    pieces = width // rows
    cols = vectors[0].shape[-1]
    per_step, total_slots = slots
    g_spec = pl.BlockSpec((pieces, per_step, rows, g_cols), lambda s: (0, slot0 + s, 0, 0))
    after = list(after) + list(into)
    fixed = 5 + len(left + right) + len(vectors) + len(after)
    return pl.pallas_call(
        functools.partial(kernel, orders, core_bit, len(after)),
        grid=(count,),
        in_specs=[SCALAR, full(length, width), full(width, length), full(length, width), full(width, length)]
        + [weight_spec(w, lambda s: w0 + s) for w in left + right]
        + [pl.BlockSpec((1, 1, cols), lambda s: (k0 + s, 0, 0))]
        + [full(*v.shape) for v in vectors[1:]]
        + [ANY] * len(after),
        out_specs=[pl.BlockSpec((1, length, m), lambda s: (s, 0, 0)) for m in mid_cols]
        + [pl.BlockSpec((1, 1, cols), lambda s: (s, 0, 0))] + [g_spec] * 2,
        out_shape=[shaped((count, length, m), BF16) for m in mid_cols]
        + [shaped((count, 1, cols), F32)] + [shaped((pieces, total_slots, rows, g_cols), BF16)] * 2,
        input_output_aliases={fixed - 2: len(mid_cols) + 1, fixed - 1: len(mid_cols) + 2} if into else {},
        scratch_shapes=scratch,
        compiler_params=pltpu.CompilerParams(vmem_limit_bytes=60 * 2**20),
        cost_estimate=cost(us * count),
    )(me, norm, norm_t, cot, cot_t, *left, *right, *vectors, *after)


def pick(refs, begins, scr):
    step = pl.program_id(0)
    for ref, begin, end in zip(refs, begins, begins[1:]):

        @pl.when((step >= begin) & (step < end))
        def _():
            scr[...] = ref[0]


def attention_tail_kernel(orders, core_bit, begins, waits, me_ref, *rest):
    left, right, rest = rest[:4], rest[4:8], rest[8:]
    calls = len(begins) - 1
    dqkv_refs, mix_refs, rest = rest[:calls], rest[calls : 2 * calls], rest[2 * calls :]
    sums_in, rest = rest[: len(rest) - waits - 6], rest[len(rest) - 6 :]
    branch_ref, dna_ref, w_scr, wv_scr, dqkv_scr, mix_scr = rest
    block_cols = w_scr.shape[1]

    @pl.when(pl.program_id(0) == 0)
    def _():
        branch_ref[...] = sums_in[0][...] if sums_in else jnp.zeros_like(branch_ref)
        dna_ref[...] = sums_in[1][...] if len(sums_in) > 1 else jnp.zeros_like(dna_ref)

    pick(dqkv_refs, begins, dqkv_scr)
    pick(mix_refs, begins, mix_scr)
    assemble(me_ref, left, gathered_order(orders[0], core_bit), w_scr, 0)
    assemble(me_ref, right, gathered_order(orders[1], core_bit), w_scr, block_cols // 2)
    for i in range(block_cols // HEAD):
        wv_scr[:, i * 2 * HD : (i + 1) * 2 * HD] = w_scr[:, i * HEAD + 2 * HD : (i + 1) * HEAD]
    tile = 256

    for t in range(branch_ref.shape[0] // tile):
        rows = slice(t * tile, (t + 1) * tile)
        branch_ref[rows, :] += dot_nt(mix_scr[rows, :], wv_scr[...])
        dna_ref[rows, :] += dot_nt(dqkv_scr[rows, :], w_scr[...])


def mlp_tail_kernel(orders, core_bit, sums, small_ks, waits, me_ref, *rest):
    left, right, dh_ref, act_ref, rest = rest[:4], rest[4:8], rest[8], rest[9], rest[10:]
    sums_in, rest = rest[:sums], rest[sums:]
    last = small_ks is not None
    if last:
        dna_ref, x_ref, cot_ref, ga_ref, gm_ref, bo_ref, bd_ref = rest[:7]
        small_refs = rest[7 : 7 + len(small_ks)]
        block_ref, grad_ref, stats_ref, branch_ref, dnm_ref, wu_scr, wd_scr = rest[7 + len(small_ks) + waits :]
    else:
        branch_ref, dnm_ref, wu_scr, wd_scr = rest[waits:]
    length = branch_ref.shape[0]
    step = pl.program_id(0)

    @pl.when(step == 0)
    def _():
        branch_ref[...] = sums_in[0][...] if sums else jnp.zeros_like(branch_ref)
        dnm_ref[...] = sums_in[1][...] if sums > 1 else jnp.zeros_like(dnm_ref)

    assemble(me_ref, left, gathered_order(orders[0], core_bit), wu_scr, 0)
    assemble(me_ref, right, gathered_order(orders[1], core_bit), wd_scr, 0)
    tile = 256

    for t in range(length // tile):
        rows = slice(t * tile, (t + 1) * tile)
        branch_ref[rows, :] += dot_nt(act_ref[0, rows, :], wd_scr[...])
        dnm_ref[rows, :] += dot_nt(dh_ref[0, rows, :], wu_scr[...])

    if not last:
        return

    @pl.when(step == pl.num_programs(0) - 1)
    def _():
        stats_ref[...] = jnp.zeros_like(stats_ref)
        small = 128

        @pl.loop(0, length // small)
        def _(t):
            rows = pl.ds(pl.multiple_of(t * small, small), small)
            x = x_ref[rows, :].astype(F32)
            cot = cot_ref[rows, :].astype(F32)
            normed, inv_std = normalize(x)
            block_ref[rows, :] = (x + branch_ref[rows, :] + bo_ref[...] + bd_ref[...]).astype(BF16)
            dna, dnm = dna_ref[rows, :], dnm_ref[rows, :]
            d_normed = dna * ga_ref[...] + dnm * gm_ref[...]
            pulled = (
                d_normed
                - jnp.mean(d_normed, axis=1, keepdims=True)
                - normed * jnp.mean(d_normed * normed, axis=1, keepdims=True)
            )
            grad_ref[rows, :] = (cot + inv_std * pulled).astype(BF16)
            for at, term in enumerate((cot, dna * normed, dna, dnm * normed, dnm)):
                stats_ref[at : at + 1, :] += jnp.sum(term, axis=0, keepdims=True)

        for ref, (first, k0, blocks) in zip(small_refs, small_ks):
            for i in range(ref.shape[0]):
                block = lax.rem(me_ref[1] + (blocks - k0 - i), blocks)
                stats_ref[pl.ds(first + block, 1), :] = ref[i]


def attention_tail_part(begins, starts, orders, core_bit, after, me, left, right, mids, sums, us):
    steps = left[0].shape[1]
    pieces = 2 * sum(w.shape[0] for w in left) // 2
    width = pieces * left[0].shape[2]
    length = mids[0][0].shape[1]

    def mid_spec(array, n):
        begin, end = begins[n], begins[n + 1]
        return pl.BlockSpec(
            (1,) + array.shape[1:], lambda s: (jnp.clip(s - begin, 0, end - begin - 1), 0, 0)
        )

    def block_of(step):
        block = step
        for begin, start in zip(begins, starts):
            block = jnp.where(step >= begin, start + step - begin, block)
        return block

    block_cols, half_cols = mids[0][0].shape[2], mids[1][0].shape[2]
    outs = [shaped((length, width), F32)] * 2
    return pl.pallas_call(
        functools.partial(attention_tail_kernel, orders, core_bit, begins, len(after)),
        grid=(steps,),
        in_specs=[SCALAR] + [weight_spec(w, lambda s: block_of(s)) for w in left + right]
        + [mid_spec(array, n) for group in mids for n, array in enumerate(group)]
        + [full(*e.shape) for e in sums] + [ANY] * len(after),
        out_specs=[full(*o.shape) for o in outs],
        out_shape=outs,
        scratch_shapes=[pltpu.VMEM((width, block_cols), BF16), pltpu.VMEM((width, half_cols), BF16)]
        + [pltpu.VMEM(group[0].shape[1:], BF16) for group in mids],
        compiler_params=pltpu.CompilerParams(vmem_limit_bytes=60 * 2**20),
        cost_estimate=cost(us),
    )(me, *left, *right, *[array for group in mids for array in group], *sums, *after)


def mlp_tail_part(w0, orders, core_bit, after, me, left, right, act, dh, sums, finals, smalls, us):
    count, length, cols = dh.shape
    width = sum(w.shape[0] for w in left) * left[0].shape[2]
    mid_spec = pl.BlockSpec((1, length, cols), lambda s: (s, 0, 0))
    total = shaped((length, width), F32)
    scratch = [pltpu.VMEM((width, cols), BF16)] * 2
    outs, small_ks = [total] * 2, None
    if finals:
        small_ks, arrays = smalls
        blocks = small_ks[0][2]
        outs = [shaped((length, width), BF16)] * 2 + [shaped((-(-(5 + 2 * blocks) // 8) * 8, width), F32)]
        scratch = [pltpu.VMEM((length, width), F32)] * 2 + scratch
        finals = list(finals) + list(arrays)
    extra = list(sums) + list(finals)
    return pl.pallas_call(
        functools.partial(mlp_tail_kernel, orders, core_bit, len(sums), small_ks, len(after)),
        grid=(count,),
        in_specs=[SCALAR] + [weight_spec(w, lambda s: w0 + s) for w in left + right] + [mid_spec] * 2
        + [full(*e.shape) for e in extra] + [ANY] * len(after),
        out_specs=[full(*o.shape) for o in outs],
        out_shape=outs,
        scratch_shapes=scratch,
        compiler_params=pltpu.CompilerParams(vmem_limit_bytes=60 * 2**20),
        cost_estimate=cost(us),
    )(me, *left, *right, dh, act, *extra, *after)


def fence_kernel(*_):
    pass


def fence(values, after=()):
    count = len(values)
    return pl.pallas_call(
        fence_kernel,
        in_specs=[ANY] * (count + len(after)),
        out_specs=[ANY] * count,
        out_shape=[shaped(value.shape, value.dtype) for value in values],
        input_output_aliases={n: n for n in range(count)},
        cost_estimate=cost(1),
    )(*values, *after)


def swap(value, bit):
    axis, flip = ("dp", 1) if bit == 1 else ("row", bit // 2)
    return flipped(value, axis, flip)


def flipped(value, axis, flip):
    return lax.ppermute(value, axis, [(i, i ^ flip) for i in range(lax.axis_size(axis))])


def shifted(value, by):
    size = lax.axis_size("col")
    return lax.ppermute(value, "col", [(i, (i + by) % size) for i in range(size)])


class Gather:
    def __init__(self, blocks, orders, core_bit):
        cut = blocks.shape[2] // 2
        self.orders, self.core_bit, self.done = orders, core_bit, 0
        self.block = blocks[0]
        self.held = [blocks[None, :, :, :cut], blocks[None, :, :, cut:]]

    def advance(self):
        if self.done > 0:
            self.held = [jnp.concatenate(pair, axis=0) for pair in zip(self.held, self.moving)]
        self.moving = [swap(one, order[self.done]) for one, order in zip(self.held, self.orders)]
        self.done += 1

    def cross_held(self):
        self.over = [swap(one, self.core_bit) for one in self.held]

    def cross_moving(self):
        self.over += [swap(one, self.core_bit) for one in self.moving]

    def sides(self):
        return ([self.held[i], self.moving[i], self.over[i], self.over[i + 2]] for i in range(2))


class Reduction:
    def __init__(self, keep, send, orders, core_bit):
        self.keep, self.orders, self.came = keep, orders, swap(send, core_bit)
        self.later = [[] for _ in orders]
        self.done = 0

    def half(self):
        return self.keep.shape[0] // len(self.orders) >> (self.done + 1)


def merge_kernel(layout, ins, first_out, *refs):
    outs = refs[first_out : first_out + len(layout)]
    at = 0
    for group, out in zip(layout, outs):
        column = 0
        for terms in group:
            total = refs[at][...].astype(F32)
            for ref in refs[at + 1 : at + terms]:
                total = total + ref[...].astype(F32)
            at += terms
            cols = total.shape[-1]
            out[..., column : column + cols] = total.astype(BF16)
            column += cols
    assert at == ins


def merge(reductions, after, values=()):
    specs, arrays, layout, shapes, plans = [], [], [], [], []

    def block(array, count, index):
        shape = (count,) + array.shape[1:]
        return pl.BlockSpec(shape, lambda s: (index,) + (0,) * (len(shape) - 1), pipeline_mode=pl.Buffered(1))

    for r in reductions:
        half = r.half()
        count = max(half, 1)
        size = r.keep.shape[0] // len(r.orders)
        groups = []
        for side in range(len(r.orders)):
            terms = [(one, (side * size + half) // count) for one in (r.keep, r.came)]
            terms += [(one, half // count) for one in r.later[side]]
            for one, index in terms:
                specs.append(block(one, count, index))
                arrays.append(one)
            groups.append(len(terms))
        _, slots, rows, cols = r.keep.shape
        if half:
            layout += [(terms,) for terms in groups]
            shapes += [(half, slots, rows, cols)] * len(groups)
        else:
            layout.append(tuple(groups))
            shapes.append((1, slots, rows, cols * len(groups)))
        plans.append((r, half))
    out = list(pl.pallas_call(
        functools.partial(merge_kernel, layout, len(arrays), len(arrays) + len(values) + len(after)),
        grid=(1,),
        in_specs=specs + [ANY] * (len(values) + len(after)),
        out_specs=[full(*shape) for shape in shapes] + [ANY] * len(values),
        out_shape=[shaped(shape, BF16) for shape in shapes] + [shaped(v.shape, v.dtype) for v in values],
        input_output_aliases={len(arrays) + n: len(shapes) + n for n in range(len(values))},
        compiler_params=pltpu.CompilerParams(vmem_limit_bytes=60 * 2**20),
        cost_estimate=cost(3),
    )(*arrays, *values, *after))
    token, finished = out[0], []
    passed = out[len(shapes) :]
    for r, half in plans:
        if half:
            for side, order in enumerate(r.orders):
                r.later[side].append(swap(out.pop(0), order[r.done]))
            r.done += 1
        else:
            finished.append(out.pop(0)[0])
    return finished, [token], passed


def phase(users, values=(), after=()):
    values = list(values)
    out = list(fence(values + [one for user in users for one in user.moving], after))
    at = len(values)
    for user in users:
        user.moving = out[at : at + len(user.moving)]
        at += len(user.moving)
    return out


def sum_over(value, axes):
    for axis in axes:
        flip = 1
        while flip < lax.axis_size(axis):
            value = value + flipped(value, axis, flip)
            flip *= 2
    return value


def on_device(
    tokens_in,
    segment_ids,
    attn_gain,
    attn_shift,
    mlp_gain,
    mlp_shift,
    qkv_weight,
    qkv_bias,
    out_weight,
    out_bias,
    up_weight,
    up_bias,
    down_weight,
    down_bias,
    out_cotangent,
):
    row_size = lax.axis_size("row")
    col_size = lax.axis_size("col")
    length, width = tokens_in.shape
    rows = qkv_weight.shape[0]
    half_rows = rows // 2
    local_heads = qkv_weight.shape[1] // QKV
    block_cols = local_heads * HEAD
    up_cols = up_weight.shape[1]
    row_id = lax.axis_index("row")
    col_id = lax.axis_index("col")
    half = lax.axis_index("dp") % 2
    me = jnp.stack([row_id * 2 + half, col_id]).astype(jnp.int32)
    row_bits = [2 << i for i in range(row_size.bit_length() - 1)]
    core_bit, far_bits = row_bits[0], row_bits[1:][::-1]
    orders = (far_bits + [1], [1] + far_bits)

    head_weight = jnp.concatenate(
        [qkv_weight.reshape(rows, local_heads, QKV), out_weight.T.reshape(rows, local_heads, HD)], axis=2
    ).reshape(rows, block_cols)
    attn_own = lax.dynamic_slice_in_dim(head_weight, half * half_rows, half_rows, axis=0)
    mlp_own = jnp.concatenate(
        [
            lax.dynamic_slice_in_dim(up_weight, half * half_rows, half_rows, axis=0),
            lax.dynamic_slice_in_dim(down_weight, half * half_rows, half_rows, axis=1).T,
        ],
        axis=1,
    )
    cut = block_cols // 2

    seg_row = lax.dynamic_index_in_dim(segment_ids, row_id * col_size + col_id, axis=0, keepdims=False)
    na, na_t, nm, nm_t, cot_t, keep, ahead, behind, mask = prep_part(
        tokens_in, out_cotangent, [v[None, :] for v in (attn_gain, attn_shift, mlp_gain, mlp_shift)], seg_row,
    )
    blocks_here = (col_id - jnp.arange(col_size)) % col_size
    head_bias = jnp.pad(
        qkv_bias.reshape(col_size, local_heads, QKV), ((0, 0), (0, 0), (0, HEAD - QKV))
    ).reshape(col_size, 1, block_cols)
    head_bias = jnp.take(head_bias, blocks_here, axis=0)
    hidden_bias = jnp.take(up_bias.reshape(col_size, 1, up_cols), blocks_here, axis=0)

    far = len(orders[0])

    def gather_col(own):
        return [own] + [shifted(own, k) for k in range(1, col_size)]

    attn = Gather(jnp.stack(gather_col(attn_own)), orders, core_bit)
    mlp_blocks = gather_col(fence([mlp_own], [attn.held[0]])[0])
    for _ in range(far):
        attn.advance()
        phase([attn], [], [na, mlp_blocks[1], mlp_blocks[-1]] if attn.done == 1 else mlp_blocks[2:-1])
    mlp_blocks = fence(mlp_blocks, attn.moving)
    attn.cross_held()
    attn.cross_moving()
    per_call = 2
    starts = list(range(0, col_size, per_call))[::-1]
    mlp = [Gather(jnp.stack(mlp_blocks[k0 : k0 + per_call]), orders, core_bit) for k0 in starts]
    for one in mlp:
        one.advance()

    def attention_call(weights, w0, k0, count, slots, slot0, into, after):
        return block_part(
            attention_kernel, w0, k0, count, slots, slot0, into, orders, core_bit, after, me, na, na_t, out_cotangent,
            cot_t, *weights.sides(), [head_bias, keep, ahead, behind, mask], [block_cols, cut], cut,
            [
                pltpu.VMEM((width, block_cols), BF16), pltpu.VMEM((width, cut), BF16),
                pltpu.VMEM((length, block_cols), F32), pltpu.VMEM((length, cut), BF16),
                pltpu.VMEM((width, block_cols), BF16),
            ],
            10,
        )

    def mlp_call(weights, w0, k0, count, slots, slot0, into, after):
        return block_part(
            mlp_kernel, w0, k0, count, slots, slot0, into, orders, core_bit, after, me, nm, nm_t, out_cotangent, cot_t,
            *weights.sides(), [hidden_bias], [up_cols, up_cols], cut, [pltpu.VMEM((width, up_cols), BF16)] * 3, 6,
        )

    per_mlp = up_cols // cut
    attn_calls, into, token = [], [], []
    for n, k0 in enumerate(starts):
        if n == 1:
            while mlp[0].done < far:
                phase([one for one in mlp if one.done < far], [], token)
                mlp[0].advance()
                if mlp[1].done < far - 1:
                    mlp[1].advance()
            mlp[0].cross_held()
            token = mlp[0].held[:1]
        outs = attention_call(attn, k0, k0, per_call, (1, col_size), k0, into, token)
        attn_calls.append(outs)
        into = list(outs[3:])
        token = [outs[2]]
    sent = phase([mlp[0]], into[1:], token + mlp[0].over)
    mlp[1].advance()
    mlp[0].cross_moving()
    token = sent[-1:]
    attn_sum = Reduction(into[0], sent[0], orders, core_bit)
    begins = list(range(0, col_size + 1, per_call))
    branch, d_norm_attn = attention_tail_part(
        begins, starts, orders, core_bit, token, me, *attn.sides(), [[c[0] for c in attn_calls], [c[1] for c in attn_calls]],
        [], 11,
    )
    totals = {}

    def go_on(reductions, after, values=()):
        reductions = [r for r in reductions if id(r) not in totals]
        ending = [r for r in reductions if not r.half()]
        finished, token, passed = merge(reductions, after, values)
        totals.update(zip((id(r) for r in ending), finished))
        return token, passed

    phase(mlp[1:], [], [branch] + mlp[0].over)
    token, _ = go_on([attn_sum], [branch, mlp[1].moving[0]])
    mlp[1].cross_held()
    mlp[1].cross_moving()
    mlp_calls, mlp_sums = [], []
    for n, k0 in enumerate(starts):
        outs = mlp_call(mlp[n], 0, k0, per_call, (per_mlp, per_mlp * per_call), 0, [], token)
        mlp_calls.append(outs)
        token, sent = go_on([attn_sum] + mlp_sums, [outs[2]] + (mlp[1].over if n == 0 else []), [outs[4]])
        mlp_sums.append(Reduction(outs[3], sent[0], orders, core_bit))
    while id(attn_sum) not in totals:
        token, _ = go_on([attn_sum], token)
    attn_total = totals[id(attn_sum)]
    attn_moves = {0: attn_total[0]}
    for k in range(2, col_size):
        attn_moves[k] = shifted(attn_total[k], -k)
    def settle(parts):
        total = sum((part.astype(F32) for part in parts[1:]), parts[0].astype(F32))
        flip = 2
        while flip < lax.axis_size("dp"):
            total = total + flipped(total, "dp", flip)
            flip *= 2
        mine = total.astype(BF16)
        return mine, swap(mine, 1)

    def whole_block(mine, other):
        first = half == 0
        return jnp.concatenate([jnp.where(first, mine, other), jnp.where(first, other, mine)], axis=0).astype(F32)

    small_ks = tuple((5, k0, col_size) for k0 in starts) + tuple((5 + col_size, k0, col_size) for k0 in starts)
    small_parts = [c[2] for c in mlp_calls] + [c[2] for c in attn_calls]
    mlp_moves = {}
    d_norm_mlp = None
    for n, k0 in enumerate(starts):
        last = n == len(starts) - 1
        sums = [branch] if n == 0 else [branch, d_norm_mlp]
        finals = [
            d_norm_attn, tokens_in, out_cotangent, attn_gain[None, :], mlp_gain[None, :], out_bias[None, :],
            down_bias[None, :],
        ]
        result = mlp_tail_part(
            0, orders, core_bit, token, me, *mlp[n].sides(), mlp_calls[n][0], mlp_calls[n][1], sums,
            finals if last else [], (small_ks, small_parts) if last else None, 9,
        )
        if n == 0:
            token, passed = go_on(mlp_sums, result[:1], [attn_moves[k] for k in range(2, col_size)])
            attn_moves.update(zip(range(2, col_size), passed))
            attn_moves[1] = shifted(attn_total[1], -1)
        else:
            token, passed = go_on(mlp_sums, result[:1], list(result[2:]) + [attn_moves[1]])
            attn_moves[1] = passed[-1]
            attn_mine, attn_other = settle([attn_moves[k] for k in range(col_size)])
        if last:
            block_out, in_grad, _ = result
            smalls = passed[0]
        else:
            branch, d_norm_mlp = result
        while last and len(mlp_moves) < col_size:
            for k1, r in zip(starts, mlp_sums):
                if id(r) in totals and k1 not in mlp_moves:
                    for i in range(per_call):
                        slots = [totals[id(r)][i * per_mlp + j] for j in range(per_mlp)]
                        part = jnp.concatenate([s[:, :cut] for s in slots] + [s[:, cut:] for s in slots], axis=1)
                        mlp_moves[k1 + i] = part if k1 + i == 0 else shifted(part, -(k1 + i))
            if len(mlp_moves) < col_size:
                token, _ = go_on(mlp_sums, token)
    head_row, up_row = 5 + col_size, 5
    smalls = sum_over(smalls, ("row", "dp"))
    smalls, *came = fence([smalls] + [mlp_moves[k] for k in range(1, col_size)])
    mlp_mine, mlp_other = settle([mlp_moves[0]] + came)
    g_heads = whole_block(attn_mine, attn_other).reshape(rows, local_heads, HEAD)
    g_mlp = whole_block(mlp_mine, mlp_other)
    g_up, g_down = g_mlp[:, :up_cols], g_mlp[:, up_cols:]
    smalls = sum_over(smalls, ("col",))
    return (
        block_out,
        in_grad,
        smalls[1],
        smalls[2],
        smalls[3],
        smalls[4],
        g_heads[:, :, :QKV].reshape(rows, local_heads * QKV),
        smalls[head_row : head_row + col_size].reshape(col_size * local_heads, HEAD)[:, :QKV].reshape(-1),
        g_heads[:, :, QKV:].reshape(rows, local_heads * HD).T,
        smalls[0],
        g_up,
        smalls[up_row : up_row + col_size].reshape(-1),
        g_down.T,
        smalls[0],
    )


def solution(mesh):
    return jax.shard_map(
        on_device,
        mesh=mesh,
        in_specs=(
            P(("dp", "row", "col"), None),
            P("dp", None),
            P(),
            P(),
            P(),
            P(),
            P("row", "col"),
            P(),
            P("col", "row"),
            P(),
            P("row", "col"),
            P(),
            P("col", "row"),
            P(),
            P(("dp", "row", "col"), None),
        ),
        out_specs=(
            P(("dp", "row", "col"), None),
            P(("dp", "row", "col"), None),
            P(),
            P(),
            P(),
            P(),
            P("row", "col"),
            P(),
            P("col", "row"),
            P(),
            P("row", "col"),
            P(),
            P("col", "row"),
            P(),
        ),
        check_vma=False,
    )
```

```python
import functools
import math

import jax
import jax.numpy as jnp
from jax import lax
from jax.experimental import pallas as pl
from jax.experimental.pallas import tpu as pltpu
from jax.sharding import PartitionSpec as P

HD = 64
ROT = 16
QKV = 3 * HD
HEAD = 4 * HD
EPSILON = 1e-05
ROPE_BASE = 10000.0
NEAR = 128
LONGEST = 256
F32 = jnp.float32
BF16 = jnp.bfloat16


def dot_nn(a, b):
    return lax.dot_general(a, b, (((1,), (0,)), ((), ())), preferred_element_type=F32)


def dot_nt(a, b):
    return lax.dot_general(a, b, (((1,), (1,)), ((), ())), preferred_element_type=F32)


def gathered_order(order, core_bit):
    held = [0]
    for bit in order[:-1]:
        held = held + [j | bit for j in held]
    came = [j | order[-1] for j in held]
    return held, came, [j | core_bit for j in held], [j | core_bit for j in came]


def reduced_order(order):
    kept = [0]
    for bit in order[::-1]:
        kept = kept + [j | bit for j in kept]
    return kept


def assemble(me_ref, w_refs, held, w_scr, at_col):
    for ref, pieces in zip(w_refs, held):
        _, _, rows, cols = ref.shape
        for t, j in enumerate(pieces):
            at = pl.multiple_of((me_ref[0] ^ j) * rows, 16)
            w_scr[pl.ds(at, rows), at_col : at_col + cols] = ref[t, 0]


def hand_out(me_ref, g_scr, at_col, keep_ref, send_ref, first, order, core_bit):
    _, slots, rows, cols = keep_ref.shape
    for t, j in enumerate(reduced_order(order)):
        for ref, piece in ((keep_ref, j), (send_ref, j | core_bit)):
            at = pl.multiple_of((me_ref[0] ^ piece) * rows, 16)
            for slot in range(slots):
                left = at_col + slot * cols
                ref[first + t, slot] = g_scr[pl.ds(at, rows), left : left + cols]


def normalize(x):
    center = x - jnp.mean(x, axis=1, keepdims=True)
    inv_std = lax.rsqrt(jnp.mean(center * center, axis=1, keepdims=True) + EPSILON)
    return center * inv_std, inv_std


def prep_kernel(
    x_ref, cot_ref, ga_ref, sa_ref, gm_ref, sm_ref, segc_ref, segr_ref, freq_ref,
    na_ref, naT_ref, nm_ref, nmT_ref, cotT_ref, keep_ref, ahead_ref, behind_ref, mask_ref,
):
    length = x_ref.shape[0]
    tile = 128

    @pl.loop(0, length // tile)
    def _(t):
        rows = pl.ds(pl.multiple_of(t * tile, tile), tile)
        normed, _ = normalize(x_ref[rows, :].astype(F32))
        na_ref[rows, :] = (normed * ga_ref[...] + sa_ref[...]).astype(BF16)
        nm_ref[rows, :] = (normed * gm_ref[...] + sm_ref[...]).astype(BF16)
        same = segc_ref[rows, :] == segr_ref[...]
        cols = lax.broadcasted_iota(jnp.int32, (tile, length), 1)
        ids = lax.broadcasted_iota(jnp.int32, (tile, length), 0) + t * tile
        mask_ref[rows, :] = jnp.where(same & (cols <= ids), 0.0, -jnp.inf)
        starts = jnp.min(jnp.where(same, cols, length).astype(F32), axis=1, keepdims=True)
        places = ids[:, :1].astype(F32) - starts
        angles = places * freq_ref[...]
        lane = lax.broadcasted_iota(jnp.int32, (tile, 2 * HD), 1) % HD
        cosine, sine = jnp.cos(angles), jnp.sin(angles)
        keep_ref[rows, :] = jnp.where(lane < ROT, cosine, 1.0)
        ahead_ref[rows, :] = jnp.where(lane < ROT // 2, -sine, 0.0)
        behind_ref[rows, :] = jnp.where((lane < ROT) & (lane >= ROT // 2), sine, 0.0)

    naT_ref[...] = na_ref[...].T
    nmT_ref[...] = nm_ref[...].T
    cotT_ref[...] = cot_ref[...].T


def full(*shape):
    return pl.BlockSpec(shape, lambda *_: (0,) * len(shape), pipeline_mode=pl.Buffered(1))


ANY = pl.BlockSpec(memory_space=pl.ANY)
SCALAR = pl.BlockSpec(memory_space=pltpu.SMEM)


def cost(us):
    return pl.CostEstimate(flops=int(us * 1.15e9), bytes_accessed=2**20, transcendentals=0)


def shaped(shape, dtype):
    return jax.ShapeDtypeStruct(shape, dtype)


def prep_part(tokens, cot, gains, seg_row):
    length, width = tokens.shape
    halves = ROT // 2
    step = (lax.iota(jnp.int32, 2 * HD) % HD % halves).astype(F32)
    freq = (ROPE_BASE ** (-(step * (2.0 / ROT))))[None, :]
    table = shaped((length, 2 * HD), F32)
    return pl.pallas_call(
        prep_kernel,
        grid=(1,),
        in_specs=[full(length, width)] * 2 + [full(1, width)] * 4
        + [full(length, 1), full(1, length), full(1, 2 * HD)],
        out_specs=[full(length, width), full(width, length)] * 2 + [full(width, length)]
        + [full(length, 2 * HD)] * 3 + [full(length, length)],
        out_shape=[shaped((length, width), BF16), shaped((width, length), BF16)] * 2
        + [shaped((width, length), BF16)] + [table] * 3 + [shaped((length, length), F32)],
        compiler_params=pltpu.CompilerParams(vmem_limit_bytes=60 * 2**20),
        cost_estimate=cost(6),
    )(tokens, cot, *gains, seg_row[:, None], seg_row[None, :], freq)


def attention_kernel(orders, core_bit, waits, me_ref, na_ref, naT_ref, cot_ref, cotT_ref, *rest):
    left, right, rest = rest[:4], rest[4:8], rest[8:]
    bias_ref, keep_ref, ahead_ref, behind_ref, mask_ref = rest[:5]
    dqkv_ref, mix_ref, dbias_ref, gk_ref, gs_ref, w_scr, wv_scr, qkv_scr, dattn_scr, g_scr = rest[5 + waits :]
    length, width = na_ref.shape
    block_cols = w_scr.shape[1]
    heads = block_cols // HEAD
    kept = gk_ref.shape[0] // 2
    tile = 256
    assemble(me_ref, left, gathered_order(orders[0], core_bit), w_scr, 0)
    assemble(me_ref, right, gathered_order(orders[1], core_bit), w_scr, block_cols // 2)
    for i in range(heads):
        wv_scr[:, i * 2 * HD : (i + 1) * 2 * HD] = w_scr[:, i * HEAD + 2 * HD : (i + 1) * HEAD]

    for t in range(length // tile):
        rows = slice(t * tile, (t + 1) * tile)
        qkv_scr[rows, :] = dot_nn(na_ref[rows, :], w_scr[...]) + bias_ref[0]
        dattn_scr[rows, :] = dot_nn(cot_ref[rows, :], wv_scr[...]).astype(BF16)

    low = lax.broadcasted_iota(jnp.int32, (length, 2 * HD), 1) < HD
    keep, ahead, behind = keep_ref[...], ahead_ref[...], behind_ref[...]
    none = jnp.zeros((length, 2 * HD), BF16)
    spans = [(b * NEAR, (b + 1) * NEAR, max(0, b * NEAR - LONGEST)) for b in range(length // NEAR)]
    q0, k0, v1, go1, qT, goT = [], [], [], [], [], []
    for i in range(heads):
        qk = qkv_scr[:, i * HEAD : i * HEAD + 2 * HD]
        qk = qk * keep + pltpu.roll(qk, 2 * HD - ROT // 2, 1) * ahead + pltpu.roll(qk, ROT // 2, 1) * behind
        q0.append(jnp.where(low, qk * (1.0 / math.sqrt(HD)), 0.0).astype(BF16))
        k0.append(jnp.where(low, pltpu.roll(qk, HD, 1), 0.0).astype(BF16))
        value = pltpu.roll(qkv_scr[:, i * HEAD + 2 * HD : (i + 1) * HEAD], HD, 1)
        v1.append(jnp.where(low, 0.0, value).astype(BF16))
        go = dattn_scr[:, i * 2 * HD : (i + 1) * 2 * HD]
        go1.append(jnp.where(low, none, go))
        qT.append(q0[i].T[:HD])
        goT.append(go.T[HD:])
    parts = [(i, r0, r1, lo) for i in range(heads) for r0, r1, lo in spans]
    s = [dot_nt(q0[i][r0:r1], k0[i][lo:r1]) + mask_ref[r0:r1, lo:r1] for i, r0, r1, lo in parts]
    dp = [dot_nt(go1[i][r0:r1], v1[i][lo:r1]) for i, r0, r1, lo in parts]
    peak = [jnp.max(one, axis=1, keepdims=True) for one in s]
    e = [jnp.exp(one - top) for one, top in zip(s, peak)]
    norm = [1.0 / jnp.sum(one, axis=1, keepdims=True) for one in e]
    p = [one * scale for one, scale in zip(e, norm)]
    p_low = [one.astype(BF16) for one in p]
    mix = [dot_nn(one, v1[i][lo:r1]) for one, (i, r0, r1, lo) in zip(p_low, parts)]
    delta = [
        jnp.sum(one * go1[i][r0:r1].astype(F32), axis=1, keepdims=True) for one, (i, r0, r1, lo) in zip(mix, parts)
    ]
    ds = [(one * (grad - centre)).astype(BF16) for one, grad, centre in zip(p, dp, delta)]
    dq = [dot_nn(one, k0[i][lo:r1]) for one, (i, r0, r1, lo) in zip(ds, parts)]
    dkT = [dot_nn(qT[i][:, r0:r1], one) for one, (i, r0, r1, lo) in zip(ds, parts)]
    dvT = [dot_nn(goT[i][:, r0:r1], one) for one, (i, r0, r1, lo) in zip(p_low, parts)]
    for i in range(heads):
        mine = slice(i * len(spans), (i + 1) * len(spans))
        sums = []
        for group in (dvT[mine], dkT[mine]):
            total = [None] * len(spans)
            for part, (r0, r1, lo) in zip(group, spans):
                for n in range(lo // NEAR, r1 // NEAR):
                    one = part[:, n * NEAR - lo : (n + 1) * NEAR - lo]
                    total[n] = one if total[n] is None else total[n] + one
            sums.append(jnp.concatenate(total, axis=1))
        dvk = jnp.concatenate(sums, axis=0).T
        dqk = jnp.where(low, jnp.concatenate(dq[mine], axis=0) * (1.0 / math.sqrt(HD)), dvk)
        dqk = dqk * keep - pltpu.roll(dqk, 2 * HD - ROT // 2, 1) * ahead - pltpu.roll(dqk, ROT // 2, 1) * behind
        dqkv_ref[0, :, i * HEAD : i * HEAD + 2 * HD] = dqk.astype(BF16)
        dqkv_ref[0, :, i * HEAD + 2 * HD : (i + 1) * HEAD] = jnp.where(low, dvk, 0.0).astype(BF16)
        mix_ref[0, :, i * 2 * HD : (i + 1) * 2 * HD] = jnp.concatenate(mix[mine], axis=0).astype(BF16)

    dbias_ref[0] = jnp.sum(dqkv_ref[0].astype(F32), axis=0, keepdims=True)

    for t in range(width // tile):
        rows = slice(t * tile, (t + 1) * tile)
        g_in = dot_nn(naT_ref[rows, :], dqkv_ref[0])
        g_out = dot_nn(cotT_ref[rows, :], mix_ref[0])
        for i in range(heads):
            at = i * HEAD
            g_scr[rows, at : at + 2 * HD] = g_in[:, at : at + 2 * HD].astype(BF16)
            g_scr[rows, at + 2 * HD : at + HEAD] = (
                g_in[:, at + 2 * HD : at + HEAD] + g_out[:, i * 2 * HD : (i + 1) * 2 * HD]
            ).astype(BF16)

    hand_out(me_ref, g_scr, 0, gk_ref, gs_ref, 0, orders[0], core_bit)
    hand_out(me_ref, g_scr, block_cols // 2, gk_ref, gs_ref, kept, orders[1], core_bit)


def mlp_kernel(orders, core_bit, waits, me_ref, nm_ref, nmT_ref, cot_ref, cotT_ref, *rest):
    left, right, bias_ref, rest = rest[:4], rest[4:8], rest[8], rest[9 + waits :]
    act_ref, dh_ref, dbias_ref, gk_ref, gs_ref, wu_scr, wd_scr, g_scr = rest
    length, width = nm_ref.shape
    up_cols = wu_scr.shape[1]
    kept = gk_ref.shape[0] // 2
    tile = 256
    assemble(me_ref, left, gathered_order(orders[0], core_bit), wu_scr, 0)
    assemble(me_ref, right, gathered_order(orders[1], core_bit), wd_scr, 0)
    dbias_ref[0] = jnp.zeros_like(dbias_ref[0])

    for t in range(length // tile):
        rows = slice(t * tile, (t + 1) * tile)
        for n in range(0, up_cols, tile):
            hidden = dot_nn(nm_ref[rows, :], wu_scr[:, n : n + tile]) + bias_ref[0, :, n : n + tile]
            d_act = dot_nn(cot_ref[rows, :], wd_scr[:, n : n + tile])
            gate = 0.5 * (1.0 + lax.erf(hidden * (1.0 / math.sqrt(2.0))))
            act_ref[0, rows, n : n + tile] = (hidden * gate).astype(BF16)
            slope = gate + hidden * jnp.exp(-0.5 * hidden * hidden) * (1.0 / math.sqrt(2.0 * math.pi))
            dh = (d_act * slope).astype(BF16)
            dh_ref[0, rows, n : n + tile] = dh
            dbias_ref[0, :, n : n + tile] += jnp.sum(dh.astype(F32), axis=0, keepdims=True)

    for side, lhs, rhs in ((0, nmT_ref, dh_ref), (1, cotT_ref, act_ref)):

        for t in range(width // tile):
            rows = slice(t * tile, (t + 1) * tile)
            g_scr[rows, :] = dot_nn(lhs[rows, :], rhs[0]).astype(BF16)

        hand_out(me_ref, g_scr, 0, gk_ref, gs_ref, side * kept, orders[side], core_bit)


def weight_spec(array, block_of):
    count, _, rows, cols = array.shape
    return pl.BlockSpec((count, 1, rows, cols), lambda s: (0, block_of(s), 0, 0))


def block_part(kernel, w0, k0, count, slots, slot0, into, orders, core_bit, after, me, norm, norm_t, cot, cot_t,
               left, right, vectors, mid_cols, g_cols, scratch, us):
    length, width = norm.shape
    rows = left[0].shape[2]
    pieces = width // rows
    cols = vectors[0].shape[-1]
    per_step, total_slots = slots
    g_spec = pl.BlockSpec((pieces, per_step, rows, g_cols), lambda s: (0, slot0 + s, 0, 0))
    after = list(after) + list(into)
    fixed = 5 + len(left + right) + len(vectors) + len(after)
    return pl.pallas_call(
        functools.partial(kernel, orders, core_bit, len(after)),
        grid=(count,),
        in_specs=[SCALAR, full(length, width), full(width, length), full(length, width), full(width, length)]
        + [weight_spec(w, lambda s: w0 + s) for w in left + right]
        + [pl.BlockSpec((1, 1, cols), lambda s: (k0 + s, 0, 0))]
        + [full(*v.shape) for v in vectors[1:]]
        + [ANY] * len(after),
        out_specs=[pl.BlockSpec((1, length, m), lambda s: (s, 0, 0)) for m in mid_cols]
        + [pl.BlockSpec((1, 1, cols), lambda s: (s, 0, 0))] + [g_spec] * 2,
        out_shape=[shaped((count, length, m), BF16) for m in mid_cols]
        + [shaped((count, 1, cols), F32)] + [shaped((pieces, total_slots, rows, g_cols), BF16)] * 2,
        input_output_aliases={fixed - 2: len(mid_cols) + 1, fixed - 1: len(mid_cols) + 2} if into else {},
        scratch_shapes=scratch,
        compiler_params=pltpu.CompilerParams(vmem_limit_bytes=60 * 2**20),
        cost_estimate=cost(us * count),
    )(me, norm, norm_t, cot, cot_t, *left, *right, *vectors, *after)


def pick(refs, begins, scr):
    step = pl.program_id(0)
    for ref, begin, end in zip(refs, begins, begins[1:]):

        @pl.when((step >= begin) & (step < end))
        def _():
            scr[...] = ref[0]


def attention_tail_kernel(orders, core_bit, begins, waits, me_ref, *rest):
    left, right, rest = rest[:4], rest[4:8], rest[8:]
    calls = len(begins) - 1
    dqkv_refs, mix_refs, rest = rest[:calls], rest[calls : 2 * calls], rest[2 * calls :]
    sums_in, rest = rest[: len(rest) - waits - 6], rest[len(rest) - 6 :]
    branch_ref, dna_ref, w_scr, wv_scr, dqkv_scr, mix_scr = rest
    block_cols = w_scr.shape[1]

    @pl.when(pl.program_id(0) == 0)
    def _():
        branch_ref[...] = sums_in[0][...] if sums_in else jnp.zeros_like(branch_ref)
        dna_ref[...] = sums_in[1][...] if len(sums_in) > 1 else jnp.zeros_like(dna_ref)

    pick(dqkv_refs, begins, dqkv_scr)
    pick(mix_refs, begins, mix_scr)
    assemble(me_ref, left, gathered_order(orders[0], core_bit), w_scr, 0)
    assemble(me_ref, right, gathered_order(orders[1], core_bit), w_scr, block_cols // 2)
    for i in range(block_cols // HEAD):
        wv_scr[:, i * 2 * HD : (i + 1) * 2 * HD] = w_scr[:, i * HEAD + 2 * HD : (i + 1) * HEAD]
    tile = 256

    for t in range(branch_ref.shape[0] // tile):
        rows = slice(t * tile, (t + 1) * tile)
        branch_ref[rows, :] += dot_nt(mix_scr[rows, :], wv_scr[...])
        dna_ref[rows, :] += dot_nt(dqkv_scr[rows, :], w_scr[...])


def mlp_tail_kernel(orders, core_bit, sums, small_ks, waits, me_ref, *rest):
    left, right, dh_ref, act_ref, rest = rest[:4], rest[4:8], rest[8], rest[9], rest[10:]
    sums_in, rest = rest[:sums], rest[sums:]
    last = small_ks is not None
    if last:
        dna_ref, x_ref, cot_ref, ga_ref, gm_ref, bo_ref, bd_ref = rest[:7]
        small_refs = rest[7 : 7 + len(small_ks)]
        block_ref, grad_ref, stats_ref, branch_ref, dnm_ref, wu_scr, wd_scr = rest[7 + len(small_ks) + waits :]
    else:
        branch_ref, dnm_ref, wu_scr, wd_scr = rest[waits:]
    length = branch_ref.shape[0]
    step = pl.program_id(0)

    @pl.when(step == 0)
    def _():
        branch_ref[...] = sums_in[0][...] if sums else jnp.zeros_like(branch_ref)
        dnm_ref[...] = sums_in[1][...] if sums > 1 else jnp.zeros_like(dnm_ref)

    assemble(me_ref, left, gathered_order(orders[0], core_bit), wu_scr, 0)
    assemble(me_ref, right, gathered_order(orders[1], core_bit), wd_scr, 0)
    tile = 256

    for t in range(length // tile):
        rows = slice(t * tile, (t + 1) * tile)
        branch_ref[rows, :] += dot_nt(act_ref[0, rows, :], wd_scr[...])
        dnm_ref[rows, :] += dot_nt(dh_ref[0, rows, :], wu_scr[...])

    if not last:
        return

    @pl.when(step == pl.num_programs(0) - 1)
    def _():
        stats_ref[...] = jnp.zeros_like(stats_ref)
        small = 128

        @pl.loop(0, length // small)
        def _(t):
            rows = pl.ds(pl.multiple_of(t * small, small), small)
            x = x_ref[rows, :].astype(F32)
            cot = cot_ref[rows, :].astype(F32)
            normed, inv_std = normalize(x)
            block_ref[rows, :] = (x + branch_ref[rows, :] + bo_ref[...] + bd_ref[...]).astype(BF16)
            dna, dnm = dna_ref[rows, :], dnm_ref[rows, :]
            d_normed = dna * ga_ref[...] + dnm * gm_ref[...]
            pulled = (
                d_normed
                - jnp.mean(d_normed, axis=1, keepdims=True)
                - normed * jnp.mean(d_normed * normed, axis=1, keepdims=True)
            )
            grad_ref[rows, :] = (cot + inv_std * pulled).astype(BF16)
            for at, term in enumerate((cot, dna * normed, dna, dnm * normed, dnm)):
                stats_ref[at : at + 1, :] += jnp.sum(term, axis=0, keepdims=True)

        for ref, (first, k0, blocks) in zip(small_refs, small_ks):
            for i in range(ref.shape[0]):
                block = lax.rem(me_ref[1] + (blocks - k0 - i), blocks)
                stats_ref[pl.ds(first + block, 1), :] = ref[i]


def attention_tail_part(begins, starts, orders, core_bit, after, me, left, right, mids, sums, us):
    steps = left[0].shape[1]
    pieces = 2 * sum(w.shape[0] for w in left) // 2
    width = pieces * left[0].shape[2]
    length = mids[0][0].shape[1]

    def mid_spec(array, n):
        begin, end = begins[n], begins[n + 1]
        return pl.BlockSpec(
            (1,) + array.shape[1:], lambda s: (jnp.clip(s - begin, 0, end - begin - 1), 0, 0)
        )

    def block_of(step):
        block = step
        for begin, start in zip(begins, starts):
            block = jnp.where(step >= begin, start + step - begin, block)
        return block

    block_cols, half_cols = mids[0][0].shape[2], mids[1][0].shape[2]
    outs = [shaped((length, width), F32)] * 2
    return pl.pallas_call(
        functools.partial(attention_tail_kernel, orders, core_bit, begins, len(after)),
        grid=(steps,),
        in_specs=[SCALAR] + [weight_spec(w, lambda s: block_of(s)) for w in left + right]
        + [mid_spec(array, n) for group in mids for n, array in enumerate(group)]
        + [full(*e.shape) for e in sums] + [ANY] * len(after),
        out_specs=[full(*o.shape) for o in outs],
        out_shape=outs,
        scratch_shapes=[pltpu.VMEM((width, block_cols), BF16), pltpu.VMEM((width, half_cols), BF16)]
        + [pltpu.VMEM(group[0].shape[1:], BF16) for group in mids],
        compiler_params=pltpu.CompilerParams(vmem_limit_bytes=60 * 2**20),
        cost_estimate=cost(us),
    )(me, *left, *right, *[array for group in mids for array in group], *sums, *after)


def mlp_tail_part(w0, orders, core_bit, after, me, left, right, act, dh, sums, finals, smalls, us):
    count, length, cols = dh.shape
    width = sum(w.shape[0] for w in left) * left[0].shape[2]
    mid_spec = pl.BlockSpec((1, length, cols), lambda s: (s, 0, 0))
    total = shaped((length, width), F32)
    scratch = [pltpu.VMEM((width, cols), BF16)] * 2
    outs, small_ks = [total] * 2, None
    if finals:
        small_ks, arrays = smalls
        blocks = small_ks[0][2]
        outs = [shaped((length, width), BF16)] * 2 + [shaped((-(-(5 + 2 * blocks) // 8) * 8, width), F32)]
        scratch = [pltpu.VMEM((length, width), F32)] * 2 + scratch
        finals = list(finals) + list(arrays)
    extra = list(sums) + list(finals)
    return pl.pallas_call(
        functools.partial(mlp_tail_kernel, orders, core_bit, len(sums), small_ks, len(after)),
        grid=(count,),
        in_specs=[SCALAR] + [weight_spec(w, lambda s: w0 + s) for w in left + right] + [mid_spec] * 2
        + [full(*e.shape) for e in extra] + [ANY] * len(after),
        out_specs=[full(*o.shape) for o in outs],
        out_shape=outs,
        scratch_shapes=scratch,
        compiler_params=pltpu.CompilerParams(vmem_limit_bytes=60 * 2**20),
        cost_estimate=cost(us),
    )(me, *left, *right, dh, act, *extra, *after)


def fence_kernel(*_):
    pass


def fence(values, after=()):
    count = len(values)
    return pl.pallas_call(
        fence_kernel,
        in_specs=[ANY] * (count + len(after)),
        out_specs=[ANY] * count,
        out_shape=[shaped(value.shape, value.dtype) for value in values],
        input_output_aliases={n: n for n in range(count)},
        cost_estimate=cost(1),
    )(*values, *after)


def swap(value, bit):
    axis, flip = ("dp", 1) if bit == 1 else ("row", bit // 2)
    return flipped(value, axis, flip)


def flipped(value, axis, flip):
    return lax.ppermute(value, axis, [(i, i ^ flip) for i in range(lax.axis_size(axis))])


def shifted(value, by):
    size = lax.axis_size("col")
    return lax.ppermute(value, "col", [(i, (i + by) % size) for i in range(size)])


class Gather:
    def __init__(self, blocks, orders, core_bit):
        cut = blocks.shape[2] // 2
        self.orders, self.core_bit, self.done = orders, core_bit, 0
        self.block = blocks[0]
        self.held = [blocks[None, :, :, :cut], blocks[None, :, :, cut:]]

    def advance(self):
        if self.done > 0:
            self.held = [jnp.concatenate(pair, axis=0) for pair in zip(self.held, self.moving)]
        self.moving = [swap(one, order[self.done]) for one, order in zip(self.held, self.orders)]
        self.done += 1

    def cross_held(self):
        self.over = [swap(one, self.core_bit) for one in self.held]

    def cross_moving(self):
        self.over += [swap(one, self.core_bit) for one in self.moving]

    def sides(self):
        return ([self.held[i], self.moving[i], self.over[i], self.over[i + 2]] for i in range(2))


class Reduction:
    def __init__(self, keep, send, orders, core_bit):
        self.keep, self.orders, self.came = keep, orders, swap(send, core_bit)
        self.later = [[] for _ in orders]
        self.done = 0

    def half(self):
        return self.keep.shape[0] // len(self.orders) >> (self.done + 1)


def merge_kernel(layout, ins, first_out, *refs):
    outs = refs[first_out : first_out + len(layout)]
    at = 0
    for group, out in zip(layout, outs):
        column = 0
        for terms in group:
            total = refs[at][...].astype(F32)
            for ref in refs[at + 1 : at + terms]:
                total = total + ref[...].astype(F32)
            at += terms
            cols = total.shape[-1]
            out[..., column : column + cols] = total.astype(BF16)
            column += cols
    assert at == ins


def merge(reductions, after, values=()):
    specs, arrays, layout, shapes, plans = [], [], [], [], []

    def block(array, count, index):
        return pl.BlockSpec((count, 1) + array.shape[2:], lambda s: (index, s, 0, 0))

    for r in reductions:
        half = r.half()
        count = max(half, 1)
        size = r.keep.shape[0] // len(r.orders)
        groups = []
        for side in range(len(r.orders)):
            terms = [(one, (side * size + half) // count) for one in (r.keep, r.came)]
            terms += [(one, half // count) for one in r.later[side]]
            for one, index in terms:
                specs.append(block(one, count, index))
                arrays.append(one)
            groups.append(len(terms))
        _, slots, rows, cols = r.keep.shape
        if half:
            layout += [(terms,) for terms in groups]
            shapes += [(half, slots, rows, cols)] * len(groups)
        else:
            layout.append(tuple(groups))
            shapes.append((1, slots, rows, cols * len(groups)))
        plans.append((r, half))
    out = list(pl.pallas_call(
        functools.partial(merge_kernel, layout, len(arrays), len(arrays) + len(values) + len(after)),
        grid=(shapes[0][1],),
        in_specs=specs + [ANY] * (len(values) + len(after)),
        out_specs=[pl.BlockSpec((shape[0], 1) + shape[2:], lambda s: (0, s, 0, 0)) for shape in shapes]
        + [ANY] * len(values),
        out_shape=[shaped(shape, BF16) for shape in shapes] + [shaped(v.shape, v.dtype) for v in values],
        input_output_aliases={len(arrays) + n: len(shapes) + n for n in range(len(values))},
        compiler_params=pltpu.CompilerParams(vmem_limit_bytes=60 * 2**20),
        cost_estimate=cost(3),
    )(*arrays, *values, *after))
    token, finished = out[0], []
    passed = out[len(shapes) :]
    for r, half in plans:
        if half:
            for side, order in enumerate(r.orders):
                r.later[side].append(swap(out.pop(0), order[r.done]))
            r.done += 1
        else:
            finished.append(out.pop(0)[0])
    return finished, [token], passed


def phase(users, values=(), after=()):
    values = list(values)
    out = list(fence(values + [one for user in users for one in user.moving], after))
    at = len(values)
    for user in users:
        user.moving = out[at : at + len(user.moving)]
        at += len(user.moving)
    return out


def sum_over(value, axes):
    for axis in axes:
        flip = 1
        while flip < lax.axis_size(axis):
            value = value + flipped(value, axis, flip)
            flip *= 2
    return value


def on_device(
    tokens_in,
    segment_ids,
    attn_gain,
    attn_shift,
    mlp_gain,
    mlp_shift,
    qkv_weight,
    qkv_bias,
    out_weight,
    out_bias,
    up_weight,
    up_bias,
    down_weight,
    down_bias,
    out_cotangent,
):
    row_size = lax.axis_size("row")
    col_size = lax.axis_size("col")
    length, width = tokens_in.shape
    rows = qkv_weight.shape[0]
    half_rows = rows // 2
    local_heads = qkv_weight.shape[1] // QKV
    block_cols = local_heads * HEAD
    up_cols = up_weight.shape[1]
    row_id = lax.axis_index("row")
    col_id = lax.axis_index("col")
    half = lax.axis_index("dp") % 2
    me = jnp.stack([row_id * 2 + half, col_id]).astype(jnp.int32)
    row_bits = [2 << i for i in range(row_size.bit_length() - 1)]
    core_bit, far_bits = row_bits[0], row_bits[1:][::-1]
    orders = (far_bits + [1], [1] + far_bits)

    head_weight = jnp.concatenate(
        [qkv_weight.reshape(rows, local_heads, QKV), out_weight.T.reshape(rows, local_heads, HD)], axis=2
    ).reshape(rows, block_cols)
    attn_own = lax.dynamic_slice_in_dim(head_weight, half * half_rows, half_rows, axis=0)
    mlp_own = jnp.concatenate(
        [
            lax.dynamic_slice_in_dim(up_weight, half * half_rows, half_rows, axis=0),
            lax.dynamic_slice_in_dim(down_weight, half * half_rows, half_rows, axis=1).T,
        ],
        axis=1,
    )
    cut = block_cols // 2

    seg_row = lax.dynamic_index_in_dim(segment_ids, row_id * col_size + col_id, axis=0, keepdims=False)
    na, na_t, nm, nm_t, cot_t, keep, ahead, behind, mask = prep_part(
        tokens_in, out_cotangent, [v[None, :] for v in (attn_gain, attn_shift, mlp_gain, mlp_shift)], seg_row,
    )
    blocks_here = (col_id - jnp.arange(col_size)) % col_size
    head_bias = jnp.pad(
        qkv_bias.reshape(col_size, local_heads, QKV), ((0, 0), (0, 0), (0, HEAD - QKV))
    ).reshape(col_size, 1, block_cols)
    head_bias = jnp.take(head_bias, blocks_here, axis=0)
    hidden_bias = jnp.take(up_bias.reshape(col_size, 1, up_cols), blocks_here, axis=0)

    far = len(orders[0])

    def gather_col(own):
        return [own] + [shifted(own, k) for k in range(1, col_size)]

    attn = Gather(jnp.stack(gather_col(attn_own)), orders, core_bit)
    mlp_blocks = gather_col(fence([mlp_own], [attn.held[0]])[0])
    for _ in range(far):
        attn.advance()
        phase([attn], [], [na, mlp_blocks[2]] if attn.done == 1 else [mlp_blocks[1]] + mlp_blocks[3:])
    mlp_blocks = fence(mlp_blocks, attn.moving)
    attn.cross_held()
    attn.cross_moving()
    per_call = 2
    starts = list(range(0, col_size, per_call))[::-1]
    mlp = [Gather(jnp.stack(mlp_blocks[k0 : k0 + per_call]), orders, core_bit) for k0 in starts]
    for one in mlp:
        one.advance()

    def attention_call(weights, w0, k0, count, slots, slot0, into, after):
        return block_part(
            attention_kernel, w0, k0, count, slots, slot0, into, orders, core_bit, after, me, na, na_t, out_cotangent,
            cot_t, *weights.sides(), [head_bias, keep, ahead, behind, mask], [block_cols, cut], cut,
            [
                pltpu.VMEM((width, block_cols), BF16), pltpu.VMEM((width, cut), BF16),
                pltpu.VMEM((length, block_cols), F32), pltpu.VMEM((length, cut), BF16),
                pltpu.VMEM((width, block_cols), BF16),
            ],
            10,
        )

    def mlp_call(weights, w0, k0, count, slots, slot0, into, after):
        return block_part(
            mlp_kernel, w0, k0, count, slots, slot0, into, orders, core_bit, after, me, nm, nm_t, out_cotangent, cot_t,
            *weights.sides(), [hidden_bias], [up_cols, up_cols], cut, [pltpu.VMEM((width, up_cols), BF16)] * 3, 6,
        )

    per_mlp = up_cols // cut
    attn_calls, into, token = [], [], []
    for n, k0 in enumerate(starts):
        if n == 1:
            while mlp[0].done < far:
                phase([one for one in mlp if one.done < far], [], token)
                mlp[0].advance()
                if mlp[1].done < far - 1:
                    mlp[1].advance()
            mlp[0].cross_held()
            token = mlp[0].held[:1]
        outs = attention_call(attn, k0, k0, per_call, (1, col_size), k0, into, token)
        attn_calls.append(outs)
        into = list(outs[3:])
        token = [outs[2]]
    sent = phase([mlp[0]], into[1:], token + mlp[0].over)
    mlp[1].advance()
    mlp[0].cross_moving()
    token = sent[-1:]
    attn_sum = Reduction(into[0], sent[0], orders, core_bit)
    begins = list(range(0, col_size + 1, per_call))
    branch, d_norm_attn = attention_tail_part(
        begins, starts, orders, core_bit, token, me, *attn.sides(), [[c[0] for c in attn_calls], [c[1] for c in attn_calls]],
        [], 11,
    )
    totals = {}

    def go_on(reductions, after, values=()):
        reductions = [r for r in reductions if id(r) not in totals]
        ending = [r for r in reductions if not r.half()]
        finished, token, passed = merge(reductions, after, values)
        totals.update(zip((id(r) for r in ending), finished))
        return token, passed

    mlp[1].held = phase(mlp[1:], mlp[1].held, [branch] + mlp[0].over)[:2]
    token, _ = go_on([attn_sum], [branch, mlp[1].moving[0]])
    mlp[1].cross_held()
    mlp[1].cross_moving()
    mlp_calls, mlp_sums = [], []
    for n, k0 in enumerate(starts):
        outs = mlp_call(mlp[n], 0, k0, per_call, (per_mlp, per_mlp * per_call), 0, [], token)
        mlp_calls.append(outs)
        token, sent = go_on([attn_sum] + mlp_sums, [outs[2]] + (mlp[1].over if n == 0 else []), [outs[4]])
        mlp_sums.append(Reduction(outs[3], sent[0], orders, core_bit))
    while id(attn_sum) not in totals:
        token, _ = go_on([attn_sum], token)
    attn_total = totals[id(attn_sum)]
    attn_moves = {0: attn_total[0]}
    for k in range(2, col_size):
        attn_moves[k] = shifted(attn_total[k], -k)
    def settle(parts):
        total = sum((part.astype(F32) for part in parts[1:]), parts[0].astype(F32))
        flip = 2
        while flip < lax.axis_size("dp"):
            total = total + flipped(total, "dp", flip)
            flip *= 2
        mine = total.astype(BF16)
        return mine, swap(mine, 1)

    def whole_block(mine, other):
        first = half == 0
        return jnp.concatenate([jnp.where(first, mine, other), jnp.where(first, other, mine)], axis=0).astype(F32)

    small_ks = tuple((5, k0, col_size) for k0 in starts) + tuple((5 + col_size, k0, col_size) for k0 in starts)
    small_parts = [c[2] for c in mlp_calls] + [c[2] for c in attn_calls]
    mlp_moves = {}
    d_norm_mlp = None
    for n, k0 in enumerate(starts):
        last = n == len(starts) - 1
        sums = [branch] if n == 0 else [branch, d_norm_mlp]
        finals = [
            d_norm_attn, tokens_in, out_cotangent, attn_gain[None, :], mlp_gain[None, :], out_bias[None, :],
            down_bias[None, :],
        ]
        result = mlp_tail_part(
            0, orders, core_bit, token, me, *mlp[n].sides(), mlp_calls[n][0], mlp_calls[n][1], sums,
            finals if last else [], (small_ks, small_parts) if last else None, 9,
        )
        if n == 0:
            token, passed = go_on(mlp_sums, result[:1], [attn_moves[k] for k in range(2, col_size)])
            attn_moves.update(zip(range(2, col_size), passed))
            attn_moves[1] = shifted(attn_total[1], -1)
        else:
            token, passed = go_on(mlp_sums, result[:1], list(result[2:]) + [attn_moves[1]])
            attn_moves[1] = passed[-1]
            attn_mine, attn_other = settle([attn_moves[k] for k in range(col_size)])
        if last:
            block_out, in_grad, _ = result
            smalls = passed[0]
        else:
            branch, d_norm_mlp = result
        while last and len(mlp_moves) < col_size:
            for k1, r in zip(starts, mlp_sums):
                if id(r) in totals and k1 not in mlp_moves:
                    for i in range(per_call):
                        slots = [totals[id(r)][i * per_mlp + j] for j in range(per_mlp)]
                        part = jnp.concatenate([s[:, :cut] for s in slots] + [s[:, cut:] for s in slots], axis=1)
                        mlp_moves[k1 + i] = part if k1 + i == 0 else shifted(part, -(k1 + i))
            if len(mlp_moves) < col_size:
                token, _ = go_on(mlp_sums, token)
    head_row, up_row = 5 + col_size, 5
    smalls = sum_over(smalls, ("row", "dp", "col"))
    smalls, *came = fence([smalls] + [mlp_moves[k] for k in range(1, col_size)])
    mlp_mine, mlp_other = settle([mlp_moves[0]] + came)
    g_heads = whole_block(attn_mine, attn_other).reshape(rows, local_heads, HEAD)
    g_mlp = whole_block(mlp_mine, mlp_other)
    g_up, g_down = g_mlp[:, :up_cols], g_mlp[:, up_cols:]
    return (
        block_out,
        in_grad,
        smalls[1],
        smalls[2],
        smalls[3],
        smalls[4],
        g_heads[:, :, :QKV].reshape(rows, local_heads * QKV),
        smalls[head_row : head_row + col_size].reshape(col_size * local_heads, HEAD)[:, :QKV].reshape(-1),
        g_heads[:, :, QKV:].reshape(rows, local_heads * HD).T,
        smalls[0],
        g_up,
        smalls[up_row : up_row + col_size].reshape(-1),
        g_down.T,
        smalls[0],
    )


def solution(mesh):
    return jax.shard_map(
        on_device,
        mesh=mesh,
        in_specs=(
            P(("dp", "row", "col"), None),
            P("dp", None),
            P(),
            P(),
            P(),
            P(),
            P("row", "col"),
            P(),
            P("col", "row"),
            P(),
            P("row", "col"),
            P(),
            P("col", "row"),
            P(),
            P(("dp", "row", "col"), None),
        ),
        out_specs=(
            P(("dp", "row", "col"), None),
            P(("dp", "row", "col"), None),
            P(),
            P(),
            P(),
            P(),
            P("row", "col"),
            P(),
            P("col", "row"),
            P(),
            P("row", "col"),
            P(),
            P("col", "row"),
            P(),
        ),
        check_vma=False,
    )
```

```python
import copy
import functools
import math

import jax
import jax.numpy as jnp
from jax import lax
from jax.experimental import pallas as pl
from jax.experimental.pallas import tpu as pltpu
from jax.sharding import PartitionSpec as P

HD = 64
ROT = 16
QKV = 3 * HD
HEAD = 4 * HD
EPSILON = 1e-05
ROPE_BASE = 10000.0
NEAR = 128
LONGEST = 256
F32 = jnp.float32
BF16 = jnp.bfloat16


def dot_nn(a, b):
    return lax.dot_general(a, b, (((1,), (0,)), ((), ())), preferred_element_type=F32)


def dot_nt(a, b):
    return lax.dot_general(a, b, (((1,), (1,)), ((), ())), preferred_element_type=F32)


def gathered_order(order, core_bit):
    held = [0]
    for bit in order[:-1]:
        held = held + [j | bit for j in held]
    came = [j | order[-1] for j in held]
    return held, came, [j | core_bit for j in held], [j | core_bit for j in came]


def reduced_order(order):
    kept = [0]
    for bit in order[::-1]:
        kept = kept + [j | bit for j in kept]
    return kept


def assemble(me_ref, w_refs, held, w_scr, at_col):
    for ref, pieces in zip(w_refs, held):
        _, _, rows, cols = ref.shape
        for t, j in enumerate(pieces):
            at = pl.multiple_of((me_ref[0] ^ j) * rows, 16)
            w_scr[pl.ds(at, rows), at_col : at_col + cols] = ref[t, 0]


def hand_out(me_ref, g_scr, at_col, keep_ref, send_ref, first, order, core_bit):
    _, slots, rows, cols = keep_ref.shape
    for t, j in enumerate(reduced_order(order)):
        for ref, piece in ((keep_ref, j), (send_ref, j | core_bit)):
            at = pl.multiple_of((me_ref[0] ^ piece) * rows, 16)
            for slot in range(slots):
                left = at_col + slot * cols
                ref[first + t, slot] = g_scr[pl.ds(at, rows), left : left + cols]


def normalize(x):
    center = x - jnp.mean(x, axis=1, keepdims=True)
    inv_std = lax.rsqrt(jnp.mean(center * center, axis=1, keepdims=True) + EPSILON)
    return center * inv_std, inv_std


def prep_kernel(
    x_ref, cot_ref, ga_ref, sa_ref, gm_ref, sm_ref, segc_ref, segr_ref, freq_ref,
    na_ref, naT_ref, nm_ref, nmT_ref, cotT_ref, keep_ref, ahead_ref, behind_ref, mask_ref,
):
    length = x_ref.shape[0]
    tile = 128

    @pl.loop(0, length // tile)
    def _(t):
        rows = pl.ds(pl.multiple_of(t * tile, tile), tile)
        normed, _ = normalize(x_ref[rows, :].astype(F32))
        na_ref[rows, :] = (normed * ga_ref[...] + sa_ref[...]).astype(BF16)
        nm_ref[rows, :] = (normed * gm_ref[...] + sm_ref[...]).astype(BF16)
        same = segc_ref[rows, :] == segr_ref[...]
        cols = lax.broadcasted_iota(jnp.int32, (tile, length), 1)
        ids = lax.broadcasted_iota(jnp.int32, (tile, length), 0) + t * tile
        mask_ref[rows, :] = jnp.where(same & (cols <= ids), 0.0, -jnp.inf)
        starts = jnp.min(jnp.where(same, cols, length).astype(F32), axis=1, keepdims=True)
        places = ids[:, :1].astype(F32) - starts
        angles = places * freq_ref[...]
        lane = lax.broadcasted_iota(jnp.int32, (tile, 2 * HD), 1) % HD
        cosine, sine = jnp.cos(angles), jnp.sin(angles)
        keep_ref[rows, :] = jnp.where(lane < ROT, cosine, 1.0)
        ahead_ref[rows, :] = jnp.where(lane < ROT // 2, -sine, 0.0)
        behind_ref[rows, :] = jnp.where((lane < ROT) & (lane >= ROT // 2), sine, 0.0)

    naT_ref[...] = na_ref[...].T
    nmT_ref[...] = nm_ref[...].T
    cotT_ref[...] = cot_ref[...].T


def full(*shape):
    return pl.BlockSpec(shape, lambda *_: (0,) * len(shape), pipeline_mode=pl.Buffered(1))


ANY = pl.BlockSpec(memory_space=pl.ANY)
SCALAR = pl.BlockSpec(memory_space=pltpu.SMEM)


def cost(us):
    return pl.CostEstimate(flops=int(us * 1.15e9), bytes_accessed=2**20, transcendentals=0)


def shaped(shape, dtype):
    return jax.ShapeDtypeStruct(shape, dtype)


def prep_part(tokens, cot, gains, seg_row):
    length, width = tokens.shape
    halves = ROT // 2
    step = (lax.iota(jnp.int32, 2 * HD) % HD % halves).astype(F32)
    freq = (ROPE_BASE ** (-(step * (2.0 / ROT))))[None, :]
    table = shaped((length, 2 * HD), F32)
    return pl.pallas_call(
        prep_kernel,
        grid=(1,),
        in_specs=[full(length, width)] * 2 + [full(1, width)] * 4
        + [full(length, 1), full(1, length), full(1, 2 * HD)],
        out_specs=[full(length, width), full(width, length)] * 2 + [full(width, length)]
        + [full(length, 2 * HD)] * 3 + [full(length, length)],
        out_shape=[shaped((length, width), BF16), shaped((width, length), BF16)] * 2
        + [shaped((width, length), BF16)] + [table] * 3 + [shaped((length, length), F32)],
        compiler_params=pltpu.CompilerParams(vmem_limit_bytes=60 * 2**20),
        cost_estimate=cost(6),
    )(tokens, cot, *gains, seg_row[:, None], seg_row[None, :], freq)


def attention_kernel(orders, core_bit, waits, me_ref, na_ref, naT_ref, cot_ref, cotT_ref, *rest):
    left, right, rest = rest[:4], rest[4:8], rest[8:]
    bias_ref, keep_ref, ahead_ref, behind_ref, mask_ref = rest[:5]
    dqkv_ref, mix_ref, dbias_ref, gk_ref, gs_ref, w_scr, wv_scr, qkv_scr, dattn_scr, g_scr = rest[5 + waits :]
    length, width = na_ref.shape
    block_cols = w_scr.shape[1]
    heads = block_cols // HEAD
    kept = gk_ref.shape[0] // 2
    tile = 256
    assemble(me_ref, left, gathered_order(orders[0], core_bit), w_scr, 0)
    assemble(me_ref, right, gathered_order(orders[1], core_bit), w_scr, block_cols // 2)
    for i in range(heads):
        wv_scr[:, i * 2 * HD : (i + 1) * 2 * HD] = w_scr[:, i * HEAD + 2 * HD : (i + 1) * HEAD]

    for t in range(length // tile):
        rows = slice(t * tile, (t + 1) * tile)
        qkv_scr[rows, :] = dot_nn(na_ref[rows, :], w_scr[...]) + bias_ref[0]
        dattn_scr[rows, :] = dot_nn(cot_ref[rows, :], wv_scr[...]).astype(BF16)

    low = lax.broadcasted_iota(jnp.int32, (length, 2 * HD), 1) < HD
    keep, ahead, behind = keep_ref[...], ahead_ref[...], behind_ref[...]
    none = jnp.zeros((length, 2 * HD), BF16)
    spans = [(b * NEAR, (b + 1) * NEAR, max(0, b * NEAR - LONGEST)) for b in range(length // NEAR)]
    q0, k0, v1, go1, qT, goT = [], [], [], [], [], []
    for i in range(heads):
        qk = qkv_scr[:, i * HEAD : i * HEAD + 2 * HD]
        qk = qk * keep + pltpu.roll(qk, 2 * HD - ROT // 2, 1) * ahead + pltpu.roll(qk, ROT // 2, 1) * behind
        q0.append(jnp.where(low, qk * (1.0 / math.sqrt(HD)), 0.0).astype(BF16))
        k0.append(jnp.where(low, pltpu.roll(qk, HD, 1), 0.0).astype(BF16))
        value = pltpu.roll(qkv_scr[:, i * HEAD + 2 * HD : (i + 1) * HEAD], HD, 1)
        v1.append(jnp.where(low, 0.0, value).astype(BF16))
        go = dattn_scr[:, i * 2 * HD : (i + 1) * 2 * HD]
        go1.append(jnp.where(low, none, go))
        qT.append(q0[i].T[:HD])
        goT.append(go.T[HD:])
    parts = [(i, r0, r1, lo) for i in range(heads) for r0, r1, lo in spans]
    s = [dot_nt(q0[i][r0:r1], k0[i][lo:r1]) + mask_ref[r0:r1, lo:r1] for i, r0, r1, lo in parts]
    dp = [dot_nt(go1[i][r0:r1], v1[i][lo:r1]) for i, r0, r1, lo in parts]
    peak = [jnp.max(one, axis=1, keepdims=True) for one in s]
    e = [jnp.exp(one - top) for one, top in zip(s, peak)]
    norm = [1.0 / jnp.sum(one, axis=1, keepdims=True) for one in e]
    p = [one * scale for one, scale in zip(e, norm)]
    p_low = [one.astype(BF16) for one in p]
    mix = [dot_nn(one, v1[i][lo:r1]) for one, (i, r0, r1, lo) in zip(p_low, parts)]
    delta = [
        jnp.sum(one * go1[i][r0:r1].astype(F32), axis=1, keepdims=True) for one, (i, r0, r1, lo) in zip(mix, parts)
    ]
    ds = [(one * (grad - centre)).astype(BF16) for one, grad, centre in zip(p, dp, delta)]
    dq = [dot_nn(one, k0[i][lo:r1]) for one, (i, r0, r1, lo) in zip(ds, parts)]
    dkT = [dot_nn(qT[i][:, r0:r1], one) for one, (i, r0, r1, lo) in zip(ds, parts)]
    dvT = [dot_nn(goT[i][:, r0:r1], one) for one, (i, r0, r1, lo) in zip(p_low, parts)]
    for i in range(heads):
        mine = slice(i * len(spans), (i + 1) * len(spans))
        sums = []
        for group in (dvT[mine], dkT[mine]):
            total = [None] * len(spans)
            for part, (r0, r1, lo) in zip(group, spans):
                for n in range(lo // NEAR, r1 // NEAR):
                    one = part[:, n * NEAR - lo : (n + 1) * NEAR - lo]
                    total[n] = one if total[n] is None else total[n] + one
            sums.append(jnp.concatenate(total, axis=1))
        dvk = jnp.concatenate(sums, axis=0).T
        dqk = jnp.where(low, jnp.concatenate(dq[mine], axis=0) * (1.0 / math.sqrt(HD)), dvk)
        dqk = dqk * keep - pltpu.roll(dqk, 2 * HD - ROT // 2, 1) * ahead - pltpu.roll(dqk, ROT // 2, 1) * behind
        dqkv_ref[0, :, i * HEAD : i * HEAD + 2 * HD] = dqk.astype(BF16)
        dqkv_ref[0, :, i * HEAD + 2 * HD : (i + 1) * HEAD] = jnp.where(low, dvk, 0.0).astype(BF16)
        mix_ref[0, :, i * 2 * HD : (i + 1) * 2 * HD] = jnp.concatenate(mix[mine], axis=0).astype(BF16)

    dbias_ref[0] = jnp.sum(dqkv_ref[0].astype(F32), axis=0, keepdims=True)

    for t in range(width // tile):
        rows = slice(t * tile, (t + 1) * tile)
        g_in = dot_nn(naT_ref[rows, :], dqkv_ref[0])
        g_out = dot_nn(cotT_ref[rows, :], mix_ref[0])
        for i in range(heads):
            at = i * HEAD
            g_scr[rows, at : at + 2 * HD] = g_in[:, at : at + 2 * HD].astype(BF16)
            g_scr[rows, at + 2 * HD : at + HEAD] = (
                g_in[:, at + 2 * HD : at + HEAD] + g_out[:, i * 2 * HD : (i + 1) * 2 * HD]
            ).astype(BF16)

    hand_out(me_ref, g_scr, 0, gk_ref, gs_ref, 0, orders[0], core_bit)
    hand_out(me_ref, g_scr, block_cols // 2, gk_ref, gs_ref, kept, orders[1], core_bit)


def mlp_kernel(orders, core_bit, waits, me_ref, nm_ref, nmT_ref, cot_ref, cotT_ref, *rest):
    left, right, bias_ref, rest = rest[:4], rest[4:8], rest[8], rest[9 + waits :]
    act_ref, dh_ref, dbias_ref, gk_ref, gs_ref, wu_scr, wd_scr, g_scr = rest
    length, width = nm_ref.shape
    up_cols = wu_scr.shape[1]
    kept = gk_ref.shape[0] // 2
    tile = 256
    assemble(me_ref, left, gathered_order(orders[0], core_bit), wu_scr, 0)
    assemble(me_ref, right, gathered_order(orders[1], core_bit), wd_scr, 0)
    dbias_ref[0] = jnp.zeros_like(dbias_ref[0])

    for t in range(length // tile):
        rows = slice(t * tile, (t + 1) * tile)
        for n in range(0, up_cols, tile):
            hidden = dot_nn(nm_ref[rows, :], wu_scr[:, n : n + tile]) + bias_ref[0, :, n : n + tile]
            d_act = dot_nn(cot_ref[rows, :], wd_scr[:, n : n + tile])
            gate = 0.5 * (1.0 + lax.erf(hidden * (1.0 / math.sqrt(2.0))))
            act_ref[0, rows, n : n + tile] = (hidden * gate).astype(BF16)
            slope = gate + hidden * jnp.exp(-0.5 * hidden * hidden) * (1.0 / math.sqrt(2.0 * math.pi))
            dh = (d_act * slope).astype(BF16)
            dh_ref[0, rows, n : n + tile] = dh
            dbias_ref[0, :, n : n + tile] += jnp.sum(dh.astype(F32), axis=0, keepdims=True)

    for side, lhs, rhs in ((0, nmT_ref, dh_ref), (1, cotT_ref, act_ref)):

        for t in range(width // tile):
            rows = slice(t * tile, (t + 1) * tile)
            g_scr[rows, :] = dot_nn(lhs[rows, :], rhs[0]).astype(BF16)

        hand_out(me_ref, g_scr, 0, gk_ref, gs_ref, side * kept, orders[side], core_bit)


def weight_spec(array, block_of):
    count, _, rows, cols = array.shape
    return pl.BlockSpec((count, 1, rows, cols), lambda s: (0, block_of(s), 0, 0))


def block_part(kernel, w0, k0, count, slots, slot0, into, orders, core_bit, after, me, norm, norm_t, cot, cot_t,
               left, right, vectors, mid_cols, g_cols, scratch, us):
    length, width = norm.shape
    rows = left[0].shape[2]
    pieces = width // rows
    cols = vectors[0].shape[-1]
    per_step, total_slots = slots
    g_spec = pl.BlockSpec((pieces, per_step, rows, g_cols), lambda s: (0, slot0 + s, 0, 0))
    after = list(after) + list(into)
    fixed = 5 + len(left + right) + len(vectors) + len(after)
    return pl.pallas_call(
        functools.partial(kernel, orders, core_bit, len(after)),
        grid=(count,),
        in_specs=[SCALAR, full(length, width), full(width, length), full(length, width), full(width, length)]
        + [weight_spec(w, lambda s: w0 + s) for w in left + right]
        + [pl.BlockSpec((1, 1, cols), lambda s: (k0 + s, 0, 0))]
        + [full(*v.shape) for v in vectors[1:]]
        + [ANY] * len(after),
        out_specs=[pl.BlockSpec((1, length, m), lambda s: (s, 0, 0)) for m in mid_cols]
        + [pl.BlockSpec((1, 1, cols), lambda s: (s, 0, 0))] + [g_spec] * 2,
        out_shape=[shaped((count, length, m), BF16) for m in mid_cols]
        + [shaped((count, 1, cols), F32)] + [shaped((pieces, total_slots, rows, g_cols), BF16)] * 2,
        input_output_aliases={fixed - 2: len(mid_cols) + 1, fixed - 1: len(mid_cols) + 2} if into else {},
        scratch_shapes=scratch,
        compiler_params=pltpu.CompilerParams(vmem_limit_bytes=60 * 2**20),
        cost_estimate=cost(us * count),
    )(me, norm, norm_t, cot, cot_t, *left, *right, *vectors, *after)


def pick(refs, begins, scr):
    step = pl.program_id(0)
    for ref, begin, end in zip(refs, begins, begins[1:]):

        @pl.when((step >= begin) & (step < end))
        def _():
            scr[...] = ref[0]


def attention_tail_kernel(orders, core_bit, begins, waits, me_ref, *rest):
    left, right, rest = rest[:4], rest[4:8], rest[8:]
    calls = len(begins) - 1
    dqkv_refs, mix_refs, rest = rest[:calls], rest[calls : 2 * calls], rest[2 * calls :]
    sums_in, rest = rest[: len(rest) - waits - 6], rest[len(rest) - 6 :]
    branch_ref, dna_ref, w_scr, wv_scr, dqkv_scr, mix_scr = rest
    block_cols = w_scr.shape[1]

    @pl.when(pl.program_id(0) == 0)
    def _():
        branch_ref[...] = sums_in[0][...] if sums_in else jnp.zeros_like(branch_ref)
        dna_ref[...] = sums_in[1][...] if len(sums_in) > 1 else jnp.zeros_like(dna_ref)

    pick(dqkv_refs, begins, dqkv_scr)
    pick(mix_refs, begins, mix_scr)
    assemble(me_ref, left, gathered_order(orders[0], core_bit), w_scr, 0)
    assemble(me_ref, right, gathered_order(orders[1], core_bit), w_scr, block_cols // 2)
    for i in range(block_cols // HEAD):
        wv_scr[:, i * 2 * HD : (i + 1) * 2 * HD] = w_scr[:, i * HEAD + 2 * HD : (i + 1) * HEAD]
    tile = 256

    for t in range(branch_ref.shape[0] // tile):
        rows = slice(t * tile, (t + 1) * tile)
        branch_ref[rows, :] += dot_nt(mix_scr[rows, :], wv_scr[...])
        dna_ref[rows, :] += dot_nt(dqkv_scr[rows, :], w_scr[...])


def mlp_tail_kernel(orders, core_bit, sums, small_ks, waits, me_ref, *rest):
    left, right, dh_ref, act_ref, rest = rest[:4], rest[4:8], rest[8], rest[9], rest[10:]
    sums_in, rest = rest[:sums], rest[sums:]
    last = small_ks is not None
    if last:
        dna_ref, x_ref, cot_ref, ga_ref, gm_ref, bo_ref, bd_ref = rest[:7]
        small_refs = rest[7 : 7 + len(small_ks)]
        block_ref, grad_ref, stats_ref, branch_ref, dnm_ref, wu_scr, wd_scr = rest[7 + len(small_ks) + waits :]
    else:
        branch_ref, dnm_ref, wu_scr, wd_scr = rest[waits:]
    length = branch_ref.shape[0]
    step = pl.program_id(0)

    @pl.when(step == 0)
    def _():
        branch_ref[...] = sums_in[0][...] if sums else jnp.zeros_like(branch_ref)
        dnm_ref[...] = sums_in[1][...] if sums > 1 else jnp.zeros_like(dnm_ref)

    assemble(me_ref, left, gathered_order(orders[0], core_bit), wu_scr, 0)
    assemble(me_ref, right, gathered_order(orders[1], core_bit), wd_scr, 0)
    tile = 256

    for t in range(length // tile):
        rows = slice(t * tile, (t + 1) * tile)
        branch_ref[rows, :] += dot_nt(act_ref[0, rows, :], wd_scr[...])
        dnm_ref[rows, :] += dot_nt(dh_ref[0, rows, :], wu_scr[...])

    if not last:
        return

    @pl.when(step == pl.num_programs(0) - 1)
    def _():
        stats_ref[...] = jnp.zeros_like(stats_ref)
        small = 128

        @pl.loop(0, length // small)
        def _(t):
            rows = pl.ds(pl.multiple_of(t * small, small), small)
            x = x_ref[rows, :].astype(F32)
            cot = cot_ref[rows, :].astype(F32)
            normed, inv_std = normalize(x)
            block_ref[rows, :] = (x + branch_ref[rows, :] + bo_ref[...] + bd_ref[...]).astype(BF16)
            dna, dnm = dna_ref[rows, :], dnm_ref[rows, :]
            d_normed = dna * ga_ref[...] + dnm * gm_ref[...]
            pulled = (
                d_normed
                - jnp.mean(d_normed, axis=1, keepdims=True)
                - normed * jnp.mean(d_normed * normed, axis=1, keepdims=True)
            )
            grad_ref[rows, :] = (cot + inv_std * pulled).astype(BF16)
            for at, term in enumerate((cot, dna * normed, dna, dnm * normed, dnm)):
                stats_ref[at : at + 1, :] += jnp.sum(term, axis=0, keepdims=True)

        for ref, (first, k0, blocks) in zip(small_refs, small_ks):
            for i in range(ref.shape[0]):
                block = lax.rem(me_ref[1] + (blocks - k0 - i), blocks)
                stats_ref[pl.ds(first + block, 1), :] = ref[i]


def attention_tail_part(begins, starts, orders, core_bit, after, me, left, right, mids, sums, us):
    steps = left[0].shape[1]
    pieces = 2 * sum(w.shape[0] for w in left) // 2
    width = pieces * left[0].shape[2]
    length = mids[0][0].shape[1]

    def mid_spec(array, n):
        begin, end = begins[n], begins[n + 1]
        return pl.BlockSpec(
            (1,) + array.shape[1:], lambda s: (jnp.clip(s - begin, 0, end - begin - 1), 0, 0)
        )

    def block_of(step):
        block = step
        for begin, start in zip(begins, starts):
            block = jnp.where(step >= begin, start + step - begin, block)
        return block

    block_cols, half_cols = mids[0][0].shape[2], mids[1][0].shape[2]
    outs = [shaped((length, width), F32)] * 2
    return pl.pallas_call(
        functools.partial(attention_tail_kernel, orders, core_bit, begins, len(after)),
        grid=(steps,),
        in_specs=[SCALAR] + [weight_spec(w, lambda s: block_of(s)) for w in left + right]
        + [mid_spec(array, n) for group in mids for n, array in enumerate(group)]
        + [full(*e.shape) for e in sums] + [ANY] * len(after),
        out_specs=[full(*o.shape) for o in outs],
        out_shape=outs,
        scratch_shapes=[pltpu.VMEM((width, block_cols), BF16), pltpu.VMEM((width, half_cols), BF16)]
        + [pltpu.VMEM(group[0].shape[1:], BF16) for group in mids],
        compiler_params=pltpu.CompilerParams(vmem_limit_bytes=60 * 2**20),
        cost_estimate=cost(us),
    )(me, *left, *right, *[array for group in mids for array in group], *sums, *after)


def mlp_tail_part(w0, orders, core_bit, after, me, left, right, act, dh, sums, finals, smalls, us):
    count, length, cols = dh.shape
    width = sum(w.shape[0] for w in left) * left[0].shape[2]
    mid_spec = pl.BlockSpec((1, length, cols), lambda s: (s, 0, 0))
    total = shaped((length, width), F32)
    scratch = [pltpu.VMEM((width, cols), BF16)] * 2
    outs, small_ks = [total] * 2, None
    if finals:
        small_ks, arrays = smalls
        blocks = small_ks[0][2]
        outs = [shaped((length, width), BF16)] * 2 + [shaped((-(-(5 + 2 * blocks) // 8) * 8, width), F32)]
        scratch = [pltpu.VMEM((length, width), F32)] * 2 + scratch
        finals = list(finals) + list(arrays)
    extra = list(sums) + list(finals)
    return pl.pallas_call(
        functools.partial(mlp_tail_kernel, orders, core_bit, len(sums), small_ks, len(after)),
        grid=(count,),
        in_specs=[SCALAR] + [weight_spec(w, lambda s: w0 + s) for w in left + right] + [mid_spec] * 2
        + [full(*e.shape) for e in extra] + [ANY] * len(after),
        out_specs=[full(*o.shape) for o in outs],
        out_shape=outs,
        scratch_shapes=scratch,
        compiler_params=pltpu.CompilerParams(vmem_limit_bytes=60 * 2**20),
        cost_estimate=cost(us),
    )(me, *left, *right, dh, act, *extra, *after)


def fence_kernel(*_):
    pass


def fence(values, after=()):
    count = len(values)
    return pl.pallas_call(
        fence_kernel,
        in_specs=[ANY] * (count + len(after)),
        out_specs=[ANY] * count,
        out_shape=[shaped(value.shape, value.dtype) for value in values],
        input_output_aliases={n: n for n in range(count)},
        cost_estimate=cost(1),
    )(*values, *after)


def swap(value, bit):
    axis, flip = ("dp", 1) if bit == 1 else ("row", bit // 2)
    return flipped(value, axis, flip)


def flipped(value, axis, flip):
    return lax.ppermute(value, axis, [(i, i ^ flip) for i in range(lax.axis_size(axis))])


def shifted(value, by):
    size = lax.axis_size("col")
    return lax.ppermute(value, "col", [(i, (i + by) % size) for i in range(size)])


class Gather:
    def __init__(self, blocks, orders, core_bit):
        cut = blocks.shape[2] // 2
        self.orders, self.core_bit, self.done = orders, core_bit, 0
        self.block = blocks[0]
        self.held = [blocks[None, :, :, :cut], blocks[None, :, :, cut:]]

    def advance(self):
        if self.done > 0:
            self.held = [jnp.concatenate(pair, axis=0) for pair in zip(self.held, self.moving)]
        self.moving = [swap(one, order[self.done]) for one, order in zip(self.held, self.orders)]
        self.done += 1

    def part(self, blocks):
        one = copy.copy(self)
        one.held = [array[:, blocks] for array in self.held]
        one.moving = [array[:, blocks] for array in self.moving]
        return one

    def cross_held(self):
        self.over = [swap(one, self.core_bit) for one in self.held]

    def cross_moving(self):
        self.over += [swap(one, self.core_bit) for one in self.moving]

    def sides(self):
        return ([self.held[i], self.moving[i], self.over[i], self.over[i + 2]] for i in range(2))


class Reduction:
    def __init__(self, keep, send, orders, core_bit):
        self.keep, self.orders, self.came = keep, orders, swap(send, core_bit)
        self.later = [[] for _ in orders]
        self.done = 0

    def half(self):
        return self.keep.shape[0] // len(self.orders) >> (self.done + 1)


def merge_kernel(layout, ins, first_out, *refs):
    outs = refs[first_out : first_out + len(layout)]
    at = 0
    for group, out in zip(layout, outs):
        column = 0
        for terms in group:
            total = refs[at][...].astype(F32)
            for ref in refs[at + 1 : at + terms]:
                total = total + ref[...].astype(F32)
            at += terms
            cols = total.shape[-1]
            out[..., column : column + cols] = total.astype(BF16)
            column += cols
    assert at == ins


def merge(reductions, after, values=()):
    specs, arrays, layout, shapes, plans = [], [], [], [], []

    def block(array, count, index):
        shape = (count,) + array.shape[1:]
        return pl.BlockSpec(shape, lambda s: (index,) + (0,) * (len(shape) - 1), pipeline_mode=pl.Buffered(1))

    for r in reductions:
        half = r.half()
        count = max(half, 1)
        size = r.keep.shape[0] // len(r.orders)
        groups = []
        for side in range(len(r.orders)):
            terms = [(one, (side * size + half) // count) for one in (r.keep, r.came)]
            terms += [(one, half // count) for one in r.later[side]]
            for one, index in terms:
                specs.append(block(one, count, index))
                arrays.append(one)
            groups.append(len(terms))
        _, slots, rows, cols = r.keep.shape
        if half:
            layout += [(terms,) for terms in groups]
            shapes += [(half, slots, rows, cols)] * len(groups)
        else:
            layout.append(tuple(groups))
            shapes.append((1, slots, rows, cols * len(groups)))
        plans.append((r, half))
    out = list(pl.pallas_call(
        functools.partial(merge_kernel, layout, len(arrays), len(arrays) + len(values) + len(after)),
        grid=(1,),
        in_specs=specs + [ANY] * (len(values) + len(after)),
        out_specs=[full(*shape) for shape in shapes] + [ANY] * len(values),
        out_shape=[shaped(shape, BF16) for shape in shapes] + [shaped(v.shape, v.dtype) for v in values],
        input_output_aliases={len(arrays) + n: len(shapes) + n for n in range(len(values))},
        compiler_params=pltpu.CompilerParams(vmem_limit_bytes=60 * 2**20),
        cost_estimate=cost(3),
    )(*arrays, *values, *after))
    token, finished = out[0], []
    passed = out[len(shapes) :]
    for r, half in plans:
        if half:
            for side, order in enumerate(r.orders):
                r.later[side].append(swap(out.pop(0), order[r.done]))
            r.done += 1
        else:
            finished.append(out.pop(0)[0])
    return finished, [token], passed


def phase(users, values=(), after=()):
    values = list(values)
    out = list(fence(values + [one for user in users for one in user.moving], after))
    at = len(values)
    for user in users:
        user.moving = out[at : at + len(user.moving)]
        at += len(user.moving)
    return out


def sum_over(value, axes):
    for axis in axes:
        flip = 1
        while flip < lax.axis_size(axis):
            value = value + flipped(value, axis, flip)
            flip *= 2
    return value


def on_device(
    tokens_in,
    segment_ids,
    attn_gain,
    attn_shift,
    mlp_gain,
    mlp_shift,
    qkv_weight,
    qkv_bias,
    out_weight,
    out_bias,
    up_weight,
    up_bias,
    down_weight,
    down_bias,
    out_cotangent,
):
    row_size = lax.axis_size("row")
    col_size = lax.axis_size("col")
    length, width = tokens_in.shape
    rows = qkv_weight.shape[0]
    half_rows = rows // 2
    local_heads = qkv_weight.shape[1] // QKV
    block_cols = local_heads * HEAD
    up_cols = up_weight.shape[1]
    row_id = lax.axis_index("row")
    col_id = lax.axis_index("col")
    half = lax.axis_index("dp") % 2
    me = jnp.stack([row_id * 2 + half, col_id]).astype(jnp.int32)
    row_bits = [2 << i for i in range(row_size.bit_length() - 1)]
    core_bit, far_bits = row_bits[0], row_bits[1:][::-1]
    orders = (far_bits + [1], [1] + far_bits)

    head_weight = jnp.concatenate(
        [qkv_weight.reshape(rows, local_heads, QKV), out_weight.T.reshape(rows, local_heads, HD)], axis=2
    ).reshape(rows, block_cols)
    attn_own = lax.dynamic_slice_in_dim(head_weight, half * half_rows, half_rows, axis=0)
    mlp_own = jnp.concatenate(
        [
            lax.dynamic_slice_in_dim(up_weight, half * half_rows, half_rows, axis=0),
            lax.dynamic_slice_in_dim(down_weight, half * half_rows, half_rows, axis=1).T,
        ],
        axis=1,
    )
    cut = block_cols // 2

    seg_row = lax.dynamic_index_in_dim(segment_ids, row_id * col_size + col_id, axis=0, keepdims=False)
    na, na_t, nm, nm_t, cot_t, keep, ahead, behind, mask = prep_part(
        tokens_in, out_cotangent, [v[None, :] for v in (attn_gain, attn_shift, mlp_gain, mlp_shift)], seg_row,
    )
    blocks_here = (col_id - jnp.arange(col_size)) % col_size
    head_bias = jnp.pad(
        qkv_bias.reshape(col_size, local_heads, QKV), ((0, 0), (0, 0), (0, HEAD - QKV))
    ).reshape(col_size, 1, block_cols)
    head_bias = jnp.take(head_bias, blocks_here, axis=0)
    hidden_bias = jnp.take(up_bias.reshape(col_size, 1, up_cols), blocks_here, axis=0)

    far = len(orders[0])

    def gather_col(own):
        return [own] + [shifted(own, k) for k in range(1, col_size)]

    attn = Gather(jnp.stack(gather_col(attn_own)), orders, core_bit)
    mlp_blocks = gather_col(fence([mlp_own], [attn.held[0]])[0])
    for _ in range(far):
        attn.advance()
        phase([attn], [], [na, mlp_blocks[1]] if attn.done == 1 else mlp_blocks[2:])
    mlp_blocks = fence(mlp_blocks, attn.moving)
    attn.cross_held()
    attn.cross_moving()
    per_call = 2
    starts = list(range(0, col_size, per_call))[::-1]
    mlp_all = Gather(jnp.stack(mlp_blocks), orders, core_bit)
    mlp_all.advance()

    def attention_call(weights, w0, k0, count, slots, slot0, into, after):
        return block_part(
            attention_kernel, w0, k0, count, slots, slot0, into, orders, core_bit, after, me, na, na_t, out_cotangent,
            cot_t, *weights.sides(), [head_bias, keep, ahead, behind, mask], [block_cols, cut], cut,
            [
                pltpu.VMEM((width, block_cols), BF16), pltpu.VMEM((width, cut), BF16),
                pltpu.VMEM((length, block_cols), F32), pltpu.VMEM((length, cut), BF16),
                pltpu.VMEM((width, block_cols), BF16),
            ],
            10,
        )

    def mlp_call(weights, w0, k0, count, slots, slot0, into, after):
        return block_part(
            mlp_kernel, w0, k0, count, slots, slot0, into, orders, core_bit, after, me, nm, nm_t, out_cotangent, cot_t,
            *weights.sides(), [hidden_bias], [up_cols, up_cols], cut, [pltpu.VMEM((width, up_cols), BF16)] * 3, 6,
        )

    per_mlp = up_cols // cut
    attn_calls, into, token = [], [], []
    for n, k0 in enumerate(starts):
        if n == 1:
            phase([mlp_all], [], token)
            while mlp_all.done < far - 1:
                mlp_all.advance()
                phase([mlp_all])
            mlp = [mlp_all.part(slice(at, at + per_call)) for at in starts]
            mlp[0].advance()
            mlp[0].cross_held()
            token = mlp[0].held[:1]
        outs = attention_call(attn, k0, k0, per_call, (1, col_size), k0, into, token)
        attn_calls.append(outs)
        into = list(outs[3:])
        token = [outs[2]]
    sent = phase([mlp[0]], into[1:], token + mlp[0].over)
    mlp[1].advance()
    mlp[0].cross_moving()
    token = sent[-1:]
    attn_sum = Reduction(into[0], sent[0], orders, core_bit)
    begins = list(range(0, col_size + 1, per_call))
    branch, d_norm_attn = attention_tail_part(
        begins, starts, orders, core_bit, token, me, *attn.sides(), [[c[0] for c in attn_calls], [c[1] for c in attn_calls]],
        [], 11,
    )
    totals = {}

    def go_on(reductions, after, values=()):
        reductions = [r for r in reductions if id(r) not in totals]
        ending = [r for r in reductions if not r.half()]
        finished, token, passed = merge(reductions, after, values)
        totals.update(zip((id(r) for r in ending), finished))
        return token, passed

    mlp[1].held = phase(mlp[1:], mlp[1].held, [branch] + mlp[0].over)[:2]
    token, _ = go_on([attn_sum], [branch, mlp[1].moving[0]])
    mlp[1].cross_held()
    mlp[1].cross_moving()
    mlp_calls, mlp_sums = [], []
    for n, k0 in enumerate(starts):
        outs = mlp_call(mlp[n], 0, k0, per_call, (per_mlp, per_mlp * per_call), 0, [], token)
        mlp_calls.append(outs)
        token, sent = go_on([attn_sum] + mlp_sums, [outs[2]] + (mlp[1].over if n == 0 else []), [outs[4]])
        mlp_sums.append(Reduction(outs[3], sent[0], orders, core_bit))
    while id(attn_sum) not in totals:
        token, _ = go_on([attn_sum], token)
    attn_total = totals[id(attn_sum)]
    attn_moves = {0: attn_total[0]}
    for k in range(2, col_size):
        attn_moves[k] = shifted(attn_total[k], -k)
    def settle(parts):
        total = sum((part.astype(F32) for part in parts[1:]), parts[0].astype(F32))
        flip = 2
        while flip < lax.axis_size("dp"):
            total = total + flipped(total, "dp", flip)
            flip *= 2
        mine = total.astype(BF16)
        return mine, swap(mine, 1)

    def whole_block(mine, other):
        first = half == 0
        return jnp.concatenate([jnp.where(first, mine, other), jnp.where(first, other, mine)], axis=0).astype(F32)

    small_ks = tuple((5, k0, col_size) for k0 in starts) + tuple((5 + col_size, k0, col_size) for k0 in starts)
    small_parts = [c[2] for c in mlp_calls] + [c[2] for c in attn_calls]
    mlp_moves = {}
    d_norm_mlp = None
    for n, k0 in enumerate(starts):
        last = n == len(starts) - 1
        sums = [branch] if n == 0 else [branch, d_norm_mlp]
        finals = [
            d_norm_attn, tokens_in, out_cotangent, attn_gain[None, :], mlp_gain[None, :], out_bias[None, :],
            down_bias[None, :],
        ]
        result = mlp_tail_part(
            0, orders, core_bit, token, me, *mlp[n].sides(), mlp_calls[n][0], mlp_calls[n][1], sums,
            finals if last else [], (small_ks, small_parts) if last else None, 9,
        )
        if n == 0:
            token, passed = go_on(mlp_sums, result[:1], [attn_moves[k] for k in range(2, col_size)])
            attn_moves.update(zip(range(2, col_size), passed))
            attn_moves[1] = shifted(attn_total[1], -1)
        else:
            token, passed = go_on(mlp_sums, result[:1], list(result[2:]) + [attn_moves[1]])
            attn_moves[1] = passed[-1]
            attn_mine, attn_other = settle([attn_moves[k] for k in range(col_size)])
        if last:
            block_out, in_grad, _ = result
            smalls = passed[0]
        else:
            branch, d_norm_mlp = result
        while last and len(mlp_moves) < col_size:
            for k1, r in zip(starts, mlp_sums):
                if id(r) in totals and k1 not in mlp_moves:
                    for i in range(per_call):
                        slots = [totals[id(r)][i * per_mlp + j] for j in range(per_mlp)]
                        part = jnp.concatenate([s[:, :cut] for s in slots] + [s[:, cut:] for s in slots], axis=1)
                        if k1 == starts[-1] and k1 + i > 0:
                            smalls = fence([smalls], [part])[0]
                        mlp_moves[k1 + i] = part if k1 + i == 0 else shifted(part, -(k1 + i))
            if len(mlp_moves) < col_size:
                token, passed = go_on(mlp_sums, token, [smalls])
                smalls = passed[0]
    head_row, up_row = 5 + col_size, 5
    smalls = sum_over(smalls, ("row", "dp", "col"))
    smalls, *came = fence([smalls] + [mlp_moves[k] for k in range(1, col_size)])
    mlp_mine, mlp_other = settle([mlp_moves[0]] + came)
    g_heads = whole_block(attn_mine, attn_other).reshape(rows, local_heads, HEAD)
    g_mlp = whole_block(mlp_mine, mlp_other)
    g_up, g_down = g_mlp[:, :up_cols], g_mlp[:, up_cols:]
    return (
        block_out,
        in_grad,
        smalls[1],
        smalls[2],
        smalls[3],
        smalls[4],
        g_heads[:, :, :QKV].reshape(rows, local_heads * QKV),
        smalls[head_row : head_row + col_size].reshape(col_size * local_heads, HEAD)[:, :QKV].reshape(-1),
        g_heads[:, :, QKV:].reshape(rows, local_heads * HD).T,
        smalls[0],
        g_up,
        smalls[up_row : up_row + col_size].reshape(-1),
        g_down.T,
        smalls[0],
    )


def solution(mesh):
    return jax.shard_map(
        on_device,
        mesh=mesh,
        in_specs=(
            P(("dp", "row", "col"), None),
            P("dp", None),
            P(),
            P(),
            P(),
            P(),
            P("row", "col"),
            P(),
            P("col", "row"),
            P(),
            P("row", "col"),
            P(),
            P("col", "row"),
            P(),
            P(("dp", "row", "col"), None),
        ),
        out_specs=(
            P(("dp", "row", "col"), None),
            P(("dp", "row", "col"), None),
            P(),
            P(),
            P(),
            P(),
            P("row", "col"),
            P(),
            P("col", "row"),
            P(),
            P("row", "col"),
            P(),
            P("col", "row"),
            P(),
        ),
        check_vma=False,
    )
```

```python
import copy
import functools
import math

import jax
import jax.numpy as jnp
from jax import lax
from jax.experimental import pallas as pl
from jax.experimental.pallas import tpu as pltpu
from jax.sharding import PartitionSpec as P

HD = 64
ROT = 16
QKV = 3 * HD
HEAD = 4 * HD
EPSILON = 1e-05
ROPE_BASE = 10000.0
NEAR = 128
LONGEST = 256
F32 = jnp.float32
BF16 = jnp.bfloat16


def dot_nn(a, b):
    return lax.dot_general(a, b, (((1,), (0,)), ((), ())), preferred_element_type=F32)


def dot_nt(a, b):
    return lax.dot_general(a, b, (((1,), (1,)), ((), ())), preferred_element_type=F32)


def gathered_order(order, core_bit):
    held = [0]
    for bit in order[:-1]:
        held = held + [j | bit for j in held]
    came = [j | order[-1] for j in held]
    return held, came, [j | core_bit for j in held], [j | core_bit for j in came]


def reduced_order(order):
    kept = [0]
    for bit in order[::-1]:
        kept = kept + [j | bit for j in kept]
    return kept


def assemble(me_ref, w_refs, held, w_scr, at_col):
    for ref, pieces in zip(w_refs, held):
        _, _, rows, cols = ref.shape
        for t, j in enumerate(pieces):
            at = pl.multiple_of((me_ref[0] ^ j) * rows, 16)
            w_scr[pl.ds(at, rows), at_col : at_col + cols] = ref[t, 0]


def hand_out(me_ref, g_scr, at_col, keep_ref, send_ref, first, order, core_bit):
    _, slots, rows, cols = keep_ref.shape
    for t, j in enumerate(reduced_order(order)):
        for ref, piece in ((keep_ref, j), (send_ref, j | core_bit)):
            at = pl.multiple_of((me_ref[0] ^ piece) * rows, 16)
            for slot in range(slots):
                left = at_col + slot * cols
                ref[first + t, slot] = g_scr[pl.ds(at, rows), left : left + cols]


def normalize(x):
    center = x - jnp.mean(x, axis=1, keepdims=True)
    inv_std = lax.rsqrt(jnp.mean(center * center, axis=1, keepdims=True) + EPSILON)
    return center * inv_std, inv_std


def prep_kernel(
    x_ref, cot_ref, ga_ref, sa_ref, gm_ref, sm_ref, segc_ref, segr_ref, freq_ref,
    na_ref, naT_ref, nm_ref, nmT_ref, cotT_ref, keep_ref, ahead_ref, behind_ref, mask_ref,
):
    length = x_ref.shape[0]
    tile = 128

    @pl.loop(0, length // tile)
    def _(t):
        rows = pl.ds(pl.multiple_of(t * tile, tile), tile)
        normed, _ = normalize(x_ref[rows, :].astype(F32))
        na_ref[rows, :] = (normed * ga_ref[...] + sa_ref[...]).astype(BF16)
        nm_ref[rows, :] = (normed * gm_ref[...] + sm_ref[...]).astype(BF16)
        same = segc_ref[rows, :] == segr_ref[...]
        cols = lax.broadcasted_iota(jnp.int32, (tile, length), 1)
        ids = lax.broadcasted_iota(jnp.int32, (tile, length), 0) + t * tile
        mask_ref[rows, :] = jnp.where(same & (cols <= ids), 0.0, -jnp.inf)
        starts = jnp.min(jnp.where(same, cols, length).astype(F32), axis=1, keepdims=True)
        places = ids[:, :1].astype(F32) - starts
        angles = places * freq_ref[...]
        lane = lax.broadcasted_iota(jnp.int32, (tile, 2 * HD), 1) % HD
        cosine, sine = jnp.cos(angles), jnp.sin(angles)
        keep_ref[rows, :] = jnp.where(lane < ROT, cosine, 1.0)
        ahead_ref[rows, :] = jnp.where(lane < ROT // 2, -sine, 0.0)
        behind_ref[rows, :] = jnp.where((lane < ROT) & (lane >= ROT // 2), sine, 0.0)

    naT_ref[...] = na_ref[...].T
    nmT_ref[...] = nm_ref[...].T
    cotT_ref[...] = cot_ref[...].T


def full(*shape):
    return pl.BlockSpec(shape, lambda *_: (0,) * len(shape), pipeline_mode=pl.Buffered(1))


ANY = pl.BlockSpec(memory_space=pl.ANY)
SCALAR = pl.BlockSpec(memory_space=pltpu.SMEM)


def cost(us):
    return pl.CostEstimate(flops=int(us * 1.15e9), bytes_accessed=2**20, transcendentals=0)


def shaped(shape, dtype):
    return jax.ShapeDtypeStruct(shape, dtype)


def prep_part(tokens, cot, gains, seg_row):
    length, width = tokens.shape
    halves = ROT // 2
    step = (lax.iota(jnp.int32, 2 * HD) % HD % halves).astype(F32)
    freq = (ROPE_BASE ** (-(step * (2.0 / ROT))))[None, :]
    table = shaped((length, 2 * HD), F32)
    return pl.pallas_call(
        prep_kernel,
        grid=(1,),
        in_specs=[full(length, width)] * 2 + [full(1, width)] * 4
        + [full(length, 1), full(1, length), full(1, 2 * HD)],
        out_specs=[full(length, width), full(width, length)] * 2 + [full(width, length)]
        + [full(length, 2 * HD)] * 3 + [full(length, length)],
        out_shape=[shaped((length, width), BF16), shaped((width, length), BF16)] * 2
        + [shaped((width, length), BF16)] + [table] * 3 + [shaped((length, length), F32)],
        compiler_params=pltpu.CompilerParams(vmem_limit_bytes=60 * 2**20),
        cost_estimate=cost(6),
    )(tokens, cot, *gains, seg_row[:, None], seg_row[None, :], freq)


def attention_kernel(orders, core_bit, waits, me_ref, na_ref, naT_ref, cot_ref, cotT_ref, *rest):
    left, right, rest = rest[:4], rest[4:8], rest[8:]
    bias_ref, keep_ref, ahead_ref, behind_ref, mask_ref = rest[:5]
    dqkv_ref, mix_ref, dbias_ref, gk_ref, gs_ref, w_scr, wv_scr, qkv_scr, dattn_scr, g_scr = rest[5 + waits :]
    length, width = na_ref.shape
    block_cols = w_scr.shape[1]
    heads = block_cols // HEAD
    kept = gk_ref.shape[0] // 2
    tile = 256
    assemble(me_ref, left, gathered_order(orders[0], core_bit), w_scr, 0)
    assemble(me_ref, right, gathered_order(orders[1], core_bit), w_scr, block_cols // 2)
    for i in range(heads):
        wv_scr[:, i * 2 * HD : (i + 1) * 2 * HD] = w_scr[:, i * HEAD + 2 * HD : (i + 1) * HEAD]

    for t in range(length // tile):
        rows = slice(t * tile, (t + 1) * tile)
        qkv_scr[rows, :] = dot_nn(na_ref[rows, :], w_scr[...]) + bias_ref[0]
        dattn_scr[rows, :] = dot_nn(cot_ref[rows, :], wv_scr[...]).astype(BF16)

    low = lax.broadcasted_iota(jnp.int32, (length, 2 * HD), 1) < HD
    keep, ahead, behind = keep_ref[...], ahead_ref[...], behind_ref[...]
    none = jnp.zeros((length, 2 * HD), BF16)
    spans = [(b * NEAR, (b + 1) * NEAR, max(0, b * NEAR - LONGEST)) for b in range(length // NEAR)]
    q0, k0, v1, go1, qT, goT = [], [], [], [], [], []
    for i in range(heads):
        qk = qkv_scr[:, i * HEAD : i * HEAD + 2 * HD]
        qk = qk * keep + pltpu.roll(qk, 2 * HD - ROT // 2, 1) * ahead + pltpu.roll(qk, ROT // 2, 1) * behind
        q0.append(jnp.where(low, qk * (1.0 / math.sqrt(HD)), 0.0).astype(BF16))
        k0.append(jnp.where(low, pltpu.roll(qk, HD, 1), 0.0).astype(BF16))
        value = pltpu.roll(qkv_scr[:, i * HEAD + 2 * HD : (i + 1) * HEAD], HD, 1)
        v1.append(jnp.where(low, 0.0, value).astype(BF16))
        go = dattn_scr[:, i * 2 * HD : (i + 1) * 2 * HD]
        go1.append(jnp.where(low, none, go))
        qT.append(q0[i].T[:HD])
        goT.append(go.T[HD:])
    parts = [(i, r0, r1, lo) for i in range(heads) for r0, r1, lo in spans]
    s = [dot_nt(q0[i][r0:r1], k0[i][lo:r1]) + mask_ref[r0:r1, lo:r1] for i, r0, r1, lo in parts]
    dp = [dot_nt(go1[i][r0:r1], v1[i][lo:r1]) for i, r0, r1, lo in parts]
    peak = [jnp.max(one, axis=1, keepdims=True) for one in s]
    e = [jnp.exp(one - top) for one, top in zip(s, peak)]
    norm = [1.0 / jnp.sum(one, axis=1, keepdims=True) for one in e]
    p = [one * scale for one, scale in zip(e, norm)]
    p_low = [one.astype(BF16) for one in p]
    mix = [dot_nn(one, v1[i][lo:r1]) for one, (i, r0, r1, lo) in zip(p_low, parts)]
    delta = [
        jnp.sum(one * go1[i][r0:r1].astype(F32), axis=1, keepdims=True) for one, (i, r0, r1, lo) in zip(mix, parts)
    ]
    ds = [(one * (grad - centre)).astype(BF16) for one, grad, centre in zip(p, dp, delta)]
    dq = [dot_nn(one, k0[i][lo:r1]) for one, (i, r0, r1, lo) in zip(ds, parts)]
    dkT = [dot_nn(qT[i][:, r0:r1], one) for one, (i, r0, r1, lo) in zip(ds, parts)]
    dvT = [dot_nn(goT[i][:, r0:r1], one) for one, (i, r0, r1, lo) in zip(p_low, parts)]
    for i in range(heads):
        mine = slice(i * len(spans), (i + 1) * len(spans))
        sums = []
        for group in (dvT[mine], dkT[mine]):
            total = [None] * len(spans)
            for part, (r0, r1, lo) in zip(group, spans):
                for n in range(lo // NEAR, r1 // NEAR):
                    one = part[:, n * NEAR - lo : (n + 1) * NEAR - lo]
                    total[n] = one if total[n] is None else total[n] + one
            sums.append(jnp.concatenate(total, axis=1))
        dvk = jnp.concatenate(sums, axis=0).T
        dqk = jnp.where(low, jnp.concatenate(dq[mine], axis=0) * (1.0 / math.sqrt(HD)), dvk)
        dqk = dqk * keep - pltpu.roll(dqk, 2 * HD - ROT // 2, 1) * ahead - pltpu.roll(dqk, ROT // 2, 1) * behind
        dqkv_ref[0, :, i * HEAD : i * HEAD + 2 * HD] = dqk.astype(BF16)
        dqkv_ref[0, :, i * HEAD + 2 * HD : (i + 1) * HEAD] = jnp.where(low, dvk, 0.0).astype(BF16)
        mix_ref[0, :, i * 2 * HD : (i + 1) * 2 * HD] = jnp.concatenate(mix[mine], axis=0).astype(BF16)

    dbias_ref[0] = jnp.sum(dqkv_ref[0].astype(F32), axis=0, keepdims=True)

    for t in range(width // tile):
        rows = slice(t * tile, (t + 1) * tile)
        g_in = dot_nn(naT_ref[rows, :], dqkv_ref[0])
        g_out = dot_nn(cotT_ref[rows, :], mix_ref[0])
        for i in range(heads):
            at = i * HEAD
            g_scr[rows, at : at + 2 * HD] = g_in[:, at : at + 2 * HD].astype(BF16)
            g_scr[rows, at + 2 * HD : at + HEAD] = (
                g_in[:, at + 2 * HD : at + HEAD] + g_out[:, i * 2 * HD : (i + 1) * 2 * HD]
            ).astype(BF16)

    hand_out(me_ref, g_scr, 0, gk_ref, gs_ref, 0, orders[0], core_bit)
    hand_out(me_ref, g_scr, block_cols // 2, gk_ref, gs_ref, kept, orders[1], core_bit)


def mlp_kernel(orders, core_bit, waits, me_ref, nm_ref, nmT_ref, cot_ref, cotT_ref, *rest):
    left, right, bias_ref, rest = rest[:4], rest[4:8], rest[8], rest[9 + waits :]
    act_ref, dh_ref, dbias_ref, gk_ref, gs_ref, wu_scr, wd_scr, g_scr = rest
    length, width = nm_ref.shape
    up_cols = wu_scr.shape[1]
    kept = gk_ref.shape[0] // 2
    tile = 256
    assemble(me_ref, left, gathered_order(orders[0], core_bit), wu_scr, 0)
    assemble(me_ref, right, gathered_order(orders[1], core_bit), wd_scr, 0)
    dbias_ref[0] = jnp.zeros_like(dbias_ref[0])

    for t in range(length // tile):
        rows = slice(t * tile, (t + 1) * tile)
        for n in range(0, up_cols, tile):
            hidden = dot_nn(nm_ref[rows, :], wu_scr[:, n : n + tile]) + bias_ref[0, :, n : n + tile]
            d_act = dot_nn(cot_ref[rows, :], wd_scr[:, n : n + tile])
            gate = 0.5 * (1.0 + lax.erf(hidden * (1.0 / math.sqrt(2.0))))
            act_ref[0, rows, n : n + tile] = (hidden * gate).astype(BF16)
            slope = gate + hidden * jnp.exp(-0.5 * hidden * hidden) * (1.0 / math.sqrt(2.0 * math.pi))
            dh = (d_act * slope).astype(BF16)
            dh_ref[0, rows, n : n + tile] = dh
            dbias_ref[0, :, n : n + tile] += jnp.sum(dh.astype(F32), axis=0, keepdims=True)

    for side, lhs, rhs in ((0, nmT_ref, dh_ref), (1, cotT_ref, act_ref)):

        for t in range(width // tile):
            rows = slice(t * tile, (t + 1) * tile)
            g_scr[rows, :] = dot_nn(lhs[rows, :], rhs[0]).astype(BF16)

        hand_out(me_ref, g_scr, 0, gk_ref, gs_ref, side * kept, orders[side], core_bit)


def weight_spec(array, block_of):
    count, _, rows, cols = array.shape
    return pl.BlockSpec((count, 1, rows, cols), lambda s: (0, block_of(s), 0, 0))


def block_part(kernel, w0, k0, count, slots, slot0, into, orders, core_bit, after, me, norm, norm_t, cot, cot_t,
               left, right, vectors, mid_cols, g_cols, scratch, us):
    length, width = norm.shape
    rows = left[0].shape[2]
    pieces = width // rows
    cols = vectors[0].shape[-1]
    per_step, total_slots = slots
    g_spec = pl.BlockSpec((pieces, per_step, rows, g_cols), lambda s: (0, slot0 + s, 0, 0))
    after = list(after) + list(into)
    fixed = 5 + len(left + right) + len(vectors) + len(after)
    return pl.pallas_call(
        functools.partial(kernel, orders, core_bit, len(after)),
        grid=(count,),
        in_specs=[SCALAR, full(length, width), full(width, length), full(length, width), full(width, length)]
        + [weight_spec(w, lambda s: w0 + s) for w in left + right]
        + [pl.BlockSpec((1, 1, cols), lambda s: (k0 + s, 0, 0))]
        + [full(*v.shape) for v in vectors[1:]]
        + [ANY] * len(after),
        out_specs=[pl.BlockSpec((1, length, m), lambda s: (s, 0, 0)) for m in mid_cols]
        + [pl.BlockSpec((1, 1, cols), lambda s: (s, 0, 0))] + [g_spec] * 2,
        out_shape=[shaped((count, length, m), BF16) for m in mid_cols]
        + [shaped((count, 1, cols), F32)] + [shaped((pieces, total_slots, rows, g_cols), BF16)] * 2,
        input_output_aliases={fixed - 2: len(mid_cols) + 1, fixed - 1: len(mid_cols) + 2} if into else {},
        scratch_shapes=scratch,
        compiler_params=pltpu.CompilerParams(vmem_limit_bytes=60 * 2**20),
        cost_estimate=cost(us * count),
    )(me, norm, norm_t, cot, cot_t, *left, *right, *vectors, *after)


def pick(refs, begins, scr):
    step = pl.program_id(0)
    for ref, begin, end in zip(refs, begins, begins[1:]):

        @pl.when((step >= begin) & (step < end))
        def _():
            scr[...] = ref[0]


def attention_tail_kernel(orders, core_bit, begins, waits, me_ref, *rest):
    left, right, rest = rest[:4], rest[4:8], rest[8:]
    calls = len(begins) - 1
    dqkv_refs, mix_refs, rest = rest[:calls], rest[calls : 2 * calls], rest[2 * calls :]
    sums_in, rest = rest[: len(rest) - waits - 6], rest[len(rest) - 6 :]
    branch_ref, dna_ref, w_scr, wv_scr, dqkv_scr, mix_scr = rest
    block_cols = w_scr.shape[1]

    @pl.when(pl.program_id(0) == 0)
    def _():
        branch_ref[...] = sums_in[0][...] if sums_in else jnp.zeros_like(branch_ref)
        dna_ref[...] = sums_in[1][...] if len(sums_in) > 1 else jnp.zeros_like(dna_ref)

    pick(dqkv_refs, begins, dqkv_scr)
    pick(mix_refs, begins, mix_scr)
    assemble(me_ref, left, gathered_order(orders[0], core_bit), w_scr, 0)
    assemble(me_ref, right, gathered_order(orders[1], core_bit), w_scr, block_cols // 2)
    for i in range(block_cols // HEAD):
        wv_scr[:, i * 2 * HD : (i + 1) * 2 * HD] = w_scr[:, i * HEAD + 2 * HD : (i + 1) * HEAD]
    tile = 256

    for t in range(branch_ref.shape[0] // tile):
        rows = slice(t * tile, (t + 1) * tile)
        branch_ref[rows, :] += dot_nt(mix_scr[rows, :], wv_scr[...])
        dna_ref[rows, :] += dot_nt(dqkv_scr[rows, :], w_scr[...])


def mlp_tail_kernel(orders, core_bit, sums, small_ks, waits, me_ref, *rest):
    left, right, dh_ref, act_ref, rest = rest[:4], rest[4:8], rest[8], rest[9], rest[10:]
    sums_in, rest = rest[:sums], rest[sums:]
    last = small_ks is not None
    if last:
        dna_ref, x_ref, cot_ref, ga_ref, gm_ref, bo_ref, bd_ref = rest[:7]
        small_refs = rest[7 : 7 + len(small_ks)]
        block_ref, grad_ref, stats_ref, branch_ref, dnm_ref, wu_scr, wd_scr = rest[7 + len(small_ks) + waits :]
    else:
        branch_ref, dnm_ref, wu_scr, wd_scr = rest[waits:]
    length = branch_ref.shape[0]
    step = pl.program_id(0)

    @pl.when(step == 0)
    def _():
        branch_ref[...] = sums_in[0][...] if sums else jnp.zeros_like(branch_ref)
        dnm_ref[...] = sums_in[1][...] if sums > 1 else jnp.zeros_like(dnm_ref)

    assemble(me_ref, left, gathered_order(orders[0], core_bit), wu_scr, 0)
    assemble(me_ref, right, gathered_order(orders[1], core_bit), wd_scr, 0)
    tile = 256

    for t in range(length // tile):
        rows = slice(t * tile, (t + 1) * tile)
        branch_ref[rows, :] += dot_nt(act_ref[0, rows, :], wd_scr[...])
        dnm_ref[rows, :] += dot_nt(dh_ref[0, rows, :], wu_scr[...])

    if not last:
        return

    @pl.when(step == pl.num_programs(0) - 1)
    def _():
        stats_ref[...] = jnp.zeros_like(stats_ref)
        small = 128

        @pl.loop(0, length // small)
        def _(t):
            rows = pl.ds(pl.multiple_of(t * small, small), small)
            x = x_ref[rows, :].astype(F32)
            cot = cot_ref[rows, :].astype(F32)
            normed, inv_std = normalize(x)
            block_ref[rows, :] = (x + branch_ref[rows, :] + bo_ref[...] + bd_ref[...]).astype(BF16)
            dna, dnm = dna_ref[rows, :], dnm_ref[rows, :]
            d_normed = dna * ga_ref[...] + dnm * gm_ref[...]
            pulled = (
                d_normed
                - jnp.mean(d_normed, axis=1, keepdims=True)
                - normed * jnp.mean(d_normed * normed, axis=1, keepdims=True)
            )
            grad_ref[rows, :] = (cot + inv_std * pulled).astype(BF16)
            for at, term in enumerate((cot, dna * normed, dna, dnm * normed, dnm)):
                stats_ref[at : at + 1, :] += jnp.sum(term, axis=0, keepdims=True)

        for ref, (first, k0, blocks) in zip(small_refs, small_ks):
            for i in range(ref.shape[0]):
                block = lax.rem(me_ref[1] + (blocks - k0 - i), blocks)
                stats_ref[pl.ds(first + block, 1), :] = ref[i]


def attention_tail_part(begins, starts, orders, core_bit, after, me, left, right, mids, sums, us):
    steps = left[0].shape[1]
    pieces = 2 * sum(w.shape[0] for w in left) // 2
    width = pieces * left[0].shape[2]
    length = mids[0][0].shape[1]

    def mid_spec(array, n):
        begin, end = begins[n], begins[n + 1]
        return pl.BlockSpec(
            (1,) + array.shape[1:], lambda s: (jnp.clip(s - begin, 0, end - begin - 1), 0, 0)
        )

    def block_of(step):
        block = step
        for begin, start in zip(begins, starts):
            block = jnp.where(step >= begin, start + step - begin, block)
        return block

    block_cols, half_cols = mids[0][0].shape[2], mids[1][0].shape[2]
    outs = [shaped((length, width), F32)] * 2
    return pl.pallas_call(
        functools.partial(attention_tail_kernel, orders, core_bit, begins, len(after)),
        grid=(steps,),
        in_specs=[SCALAR] + [weight_spec(w, lambda s: block_of(s)) for w in left + right]
        + [mid_spec(array, n) for group in mids for n, array in enumerate(group)]
        + [full(*e.shape) for e in sums] + [ANY] * len(after),
        out_specs=[full(*o.shape) for o in outs],
        out_shape=outs,
        scratch_shapes=[pltpu.VMEM((width, block_cols), BF16), pltpu.VMEM((width, half_cols), BF16)]
        + [pltpu.VMEM(group[0].shape[1:], BF16) for group in mids],
        compiler_params=pltpu.CompilerParams(vmem_limit_bytes=60 * 2**20),
        cost_estimate=cost(us),
    )(me, *left, *right, *[array for group in mids for array in group], *sums, *after)


def mlp_tail_part(w0, orders, core_bit, after, me, left, right, act, dh, sums, finals, smalls, us):
    count, length, cols = dh.shape
    width = sum(w.shape[0] for w in left) * left[0].shape[2]
    mid_spec = pl.BlockSpec((1, length, cols), lambda s: (s, 0, 0))
    total = shaped((length, width), F32)
    scratch = [pltpu.VMEM((width, cols), BF16)] * 2
    outs, small_ks = [total] * 2, None
    if finals:
        small_ks, arrays = smalls
        blocks = small_ks[0][2]
        outs = [shaped((length, width), BF16)] * 2 + [shaped((-(-(5 + 2 * blocks) // 8) * 8, width), F32)]
        scratch = [pltpu.VMEM((length, width), F32)] * 2 + scratch
        finals = list(finals) + list(arrays)
    extra = list(sums) + list(finals)
    return pl.pallas_call(
        functools.partial(mlp_tail_kernel, orders, core_bit, len(sums), small_ks, len(after)),
        grid=(count,),
        in_specs=[SCALAR] + [weight_spec(w, lambda s: w0 + s) for w in left + right] + [mid_spec] * 2
        + [full(*e.shape) for e in extra] + [ANY] * len(after),
        out_specs=[full(*o.shape) for o in outs],
        out_shape=outs,
        scratch_shapes=scratch,
        compiler_params=pltpu.CompilerParams(vmem_limit_bytes=60 * 2**20),
        cost_estimate=cost(us),
    )(me, *left, *right, dh, act, *extra, *after)


def fence_kernel(*_):
    pass


def fence(values, after=()):
    count = len(values)
    return pl.pallas_call(
        fence_kernel,
        in_specs=[ANY] * (count + len(after)),
        out_specs=[ANY] * count,
        out_shape=[shaped(value.shape, value.dtype) for value in values],
        input_output_aliases={n: n for n in range(count)},
        cost_estimate=cost(1),
    )(*values, *after)


def swap(value, bit):
    axis, flip = ("dp", 1) if bit == 1 else ("row", bit // 2)
    return flipped(value, axis, flip)


def flipped(value, axis, flip):
    return lax.ppermute(value, axis, [(i, i ^ flip) for i in range(lax.axis_size(axis))])


def shifted(value, by):
    size = lax.axis_size("col")
    return lax.ppermute(value, "col", [(i, (i + by) % size) for i in range(size)])


class Gather:
    def __init__(self, blocks, orders, core_bit):
        cut = blocks.shape[2] // 2
        self.orders, self.core_bit, self.done = orders, core_bit, 0
        self.block = blocks[0]
        self.held = [blocks[None, :, :, :cut], blocks[None, :, :, cut:]]

    def advance(self):
        if self.done > 0:
            self.held = [jnp.concatenate(pair, axis=0) for pair in zip(self.held, self.moving)]
        self.moving = [swap(one, order[self.done]) for one, order in zip(self.held, self.orders)]
        self.done += 1

    def part(self, blocks):
        one = copy.copy(self)
        one.held = [array[:, blocks] for array in self.held]
        one.moving = [array[:, blocks] for array in self.moving]
        return one

    def cross_held(self):
        self.over = [swap(one, self.core_bit) for one in self.held]

    def cross_moving(self):
        self.over += [swap(one, self.core_bit) for one in self.moving]

    def sides(self):
        return ([self.held[i], self.moving[i], self.over[i], self.over[i + 2]] for i in range(2))


class Reduction:
    def __init__(self, keep, send, orders, core_bit):
        self.keep, self.orders, self.came = keep, orders, swap(send, core_bit)
        self.later = [[] for _ in orders]
        self.done = 0

    def half(self):
        return self.keep.shape[0] // len(self.orders) >> (self.done + 1)


def merge_kernel(layout, ins, first_out, *refs):
    outs = refs[first_out : first_out + len(layout)]
    at = 0
    for group, out in zip(layout, outs):
        column = 0
        for terms in group:
            total = refs[at][...].astype(F32)
            for ref in refs[at + 1 : at + terms]:
                total = total + ref[...].astype(F32)
            at += terms
            cols = total.shape[-1]
            out[..., column : column + cols] = total.astype(BF16)
            column += cols
    assert at == ins


def merge(reductions, after, values=()):
    specs, arrays, layout, shapes, plans = [], [], [], [], []

    def block(array, count, index):
        shape = (count,) + array.shape[1:]
        return pl.BlockSpec(shape, lambda s: (index,) + (0,) * (len(shape) - 1), pipeline_mode=pl.Buffered(1))

    for r in reductions:
        half = r.half()
        count = max(half, 1)
        size = r.keep.shape[0] // len(r.orders)
        groups = []
        for side in range(len(r.orders)):
            terms = [(one, (side * size + half) // count) for one in (r.keep, r.came)]
            terms += [(one, half // count) for one in r.later[side]]
            for one, index in terms:
                specs.append(block(one, count, index))
                arrays.append(one)
            groups.append(len(terms))
        _, slots, rows, cols = r.keep.shape
        if half:
            layout += [(terms,) for terms in groups]
            shapes += [(half, slots, rows, cols)] * len(groups)
        else:
            layout.append(tuple(groups))
            shapes.append((1, slots, rows, cols * len(groups)))
        plans.append((r, half))
    out = list(pl.pallas_call(
        functools.partial(merge_kernel, layout, len(arrays), len(arrays) + len(values) + len(after)),
        grid=(1,),
        in_specs=specs + [ANY] * (len(values) + len(after)),
        out_specs=[full(*shape) for shape in shapes] + [ANY] * len(values),
        out_shape=[shaped(shape, BF16) for shape in shapes] + [shaped(v.shape, v.dtype) for v in values],
        input_output_aliases={len(arrays) + n: len(shapes) + n for n in range(len(values))},
        compiler_params=pltpu.CompilerParams(vmem_limit_bytes=60 * 2**20),
        cost_estimate=cost(3),
    )(*arrays, *values, *after))
    token, finished = out[0], []
    passed = out[len(shapes) :]
    for r, half in plans:
        if half:
            for side, order in enumerate(r.orders):
                r.later[side].append(swap(out.pop(0), order[r.done]))
            r.done += 1
        else:
            finished.append(out.pop(0)[0])
    return finished, [token], passed


def phase(users, values=(), after=()):
    values = list(values)
    out = list(fence(values + [one for user in users for one in user.moving], after))
    at = len(values)
    for user in users:
        user.moving = out[at : at + len(user.moving)]
        at += len(user.moving)
    return out


def sum_over(value, axes):
    for axis in axes:
        flip = 1
        while flip < lax.axis_size(axis):
            value = value + flipped(value, axis, flip)
            flip *= 2
    return value


def on_device(
    tokens_in,
    segment_ids,
    attn_gain,
    attn_shift,
    mlp_gain,
    mlp_shift,
    qkv_weight,
    qkv_bias,
    out_weight,
    out_bias,
    up_weight,
    up_bias,
    down_weight,
    down_bias,
    out_cotangent,
):
    row_size = lax.axis_size("row")
    col_size = lax.axis_size("col")
    length, width = tokens_in.shape
    rows = qkv_weight.shape[0]
    half_rows = rows // 2
    local_heads = qkv_weight.shape[1] // QKV
    block_cols = local_heads * HEAD
    up_cols = up_weight.shape[1]
    row_id = lax.axis_index("row")
    col_id = lax.axis_index("col")
    half = lax.axis_index("dp") % 2
    me = jnp.stack([row_id * 2 + half, col_id]).astype(jnp.int32)
    row_bits = [2 << i for i in range(row_size.bit_length() - 1)]
    core_bit, far_bits = row_bits[0], row_bits[1:][::-1]
    orders = (far_bits + [1], [1] + far_bits)

    head_weight = jnp.concatenate(
        [qkv_weight.reshape(rows, local_heads, QKV), out_weight.T.reshape(rows, local_heads, HD)], axis=2
    ).reshape(rows, block_cols)
    attn_own = lax.dynamic_slice_in_dim(head_weight, half * half_rows, half_rows, axis=0)
    mlp_own = jnp.concatenate(
        [
            lax.dynamic_slice_in_dim(up_weight, half * half_rows, half_rows, axis=0),
            lax.dynamic_slice_in_dim(down_weight, half * half_rows, half_rows, axis=1).T,
        ],
        axis=1,
    )
    cut = block_cols // 2

    seg_row = lax.dynamic_index_in_dim(segment_ids, row_id * col_size + col_id, axis=0, keepdims=False)
    na, na_t, nm, nm_t, cot_t, keep, ahead, behind, mask = prep_part(
        tokens_in, out_cotangent, [v[None, :] for v in (attn_gain, attn_shift, mlp_gain, mlp_shift)], seg_row,
    )
    blocks_here = (col_id - jnp.arange(col_size)) % col_size
    head_bias = jnp.pad(
        qkv_bias.reshape(col_size, local_heads, QKV), ((0, 0), (0, 0), (0, HEAD - QKV))
    ).reshape(col_size, 1, block_cols)
    head_bias = jnp.take(head_bias, blocks_here, axis=0)
    hidden_bias = jnp.take(up_bias.reshape(col_size, 1, up_cols), blocks_here, axis=0)

    far = len(orders[0])

    def gather_col(own):
        return [own] + [shifted(own, k) for k in range(1, col_size)]

    attn = Gather(jnp.stack(gather_col(attn_own)), orders, core_bit)
    mlp_blocks = gather_col(fence([mlp_own], [attn.held[0]])[0])
    for _ in range(far):
        attn.advance()
        phase([attn], [], [na, mlp_blocks[1]] if attn.done == 1 else mlp_blocks[2:])
    mlp_blocks = fence(mlp_blocks, attn.moving)
    attn.cross_held()
    attn.cross_moving()
    per_call = 2
    starts = list(range(0, col_size, per_call))[::-1]
    mlp_all = Gather(jnp.stack(mlp_blocks), orders, core_bit)
    mlp_all.advance()

    def attention_call(weights, w0, k0, count, slots, slot0, into, after):
        return block_part(
            attention_kernel, w0, k0, count, slots, slot0, into, orders, core_bit, after, me, na, na_t, out_cotangent,
            cot_t, *weights.sides(), [head_bias, keep, ahead, behind, mask], [block_cols, cut], cut,
            [
                pltpu.VMEM((width, block_cols), BF16), pltpu.VMEM((width, cut), BF16),
                pltpu.VMEM((length, block_cols), F32), pltpu.VMEM((length, cut), BF16),
                pltpu.VMEM((width, block_cols), BF16),
            ],
            10,
        )

    def mlp_call(weights, w0, k0, count, slots, slot0, into, after):
        return block_part(
            mlp_kernel, w0, k0, count, slots, slot0, into, orders, core_bit, after, me, nm, nm_t, out_cotangent, cot_t,
            *weights.sides(), [hidden_bias], [up_cols, up_cols], cut, [pltpu.VMEM((width, up_cols), BF16)] * 3, 6,
        )

    per_mlp = up_cols // cut
    attn_calls, into, token = [], [], []
    for n, k0 in enumerate(starts):
        if n == 1:
            phase([mlp_all], [], token)
            while mlp_all.done < far - 1:
                mlp_all.advance()
                phase([mlp_all])
            mlp = [mlp_all.part(slice(at, at + per_call)) for at in starts]
            mlp[0].advance()
            mlp[0].cross_held()
            token = mlp[0].held[:1]
        outs = attention_call(attn, k0, k0, per_call, (1, col_size), k0, into, token)
        attn_calls.append(outs)
        into = list(outs[3:])
        token = [outs[2]]
    sent = phase([mlp[0]], into[1:], token + mlp[0].over)
    mlp[1].advance()
    mlp[0].cross_moving()
    token = sent[-1:]
    attn_sum = Reduction(into[0], sent[0], orders, core_bit)
    begins = list(range(0, col_size + 1, per_call))
    branch, d_norm_attn = attention_tail_part(
        begins, starts, orders, core_bit, token, me, *attn.sides(), [[c[0] for c in attn_calls], [c[1] for c in attn_calls]],
        [], 11,
    )
    totals = {}

    def go_on(reductions, after, values=()):
        reductions = [r for r in reductions if id(r) not in totals]
        ending = [r for r in reductions if not r.half()]
        finished, token, passed = merge(reductions, after, values)
        totals.update(zip((id(r) for r in ending), finished))
        return token, passed

    mlp[1].held = phase(mlp[1:], mlp[1].held, [branch] + mlp[0].over)[:2]
    token, _ = go_on([attn_sum], [branch, mlp[1].moving[0]])
    mlp[1].cross_held()
    mlp[1].cross_moving()
    mlp_calls, mlp_sums = [], []
    for n, k0 in enumerate(starts):
        outs = mlp_call(mlp[n], 0, k0, per_call, (per_mlp, per_mlp * per_call), 0, [], token)
        mlp_calls.append(outs)
        token, sent = go_on([attn_sum] + mlp_sums, [outs[2]] + (mlp[1].over if n == 0 else []), [outs[4]])
        mlp_sums.append(Reduction(outs[3], sent[0], orders, core_bit))
    while id(attn_sum) not in totals:
        token, _ = go_on([attn_sum], token)
    attn_total = totals[id(attn_sum)]
    attn_moves = {0: attn_total[0]}
    for k in range(2, col_size):
        attn_moves[k] = shifted(attn_total[k], -k)
    def settle(parts):
        total = sum((part.astype(F32) for part in parts[1:]), parts[0].astype(F32))
        flip = 2
        while flip < lax.axis_size("dp"):
            total = total + flipped(total, "dp", flip)
            flip *= 2
        mine = total.astype(BF16)
        return mine, swap(mine, 1)

    def whole_block(mine, other):
        first = half == 0
        return jnp.concatenate([jnp.where(first, mine, other), jnp.where(first, other, mine)], axis=0).astype(F32)

    small_ks = tuple((5, k0, col_size) for k0 in starts) + tuple((5 + col_size, k0, col_size) for k0 in starts)
    small_parts = [c[2] for c in mlp_calls] + [c[2] for c in attn_calls]
    mlp_moves = {}
    d_norm_mlp = None
    for n, k0 in enumerate(starts):
        last = n == len(starts) - 1
        sums = [branch] if n == 0 else [branch, d_norm_mlp]
        finals = [
            d_norm_attn, tokens_in, out_cotangent, attn_gain[None, :], mlp_gain[None, :], out_bias[None, :],
            down_bias[None, :],
        ]
        result = mlp_tail_part(
            0, orders, core_bit, token, me, *mlp[n].sides(), mlp_calls[n][0], mlp_calls[n][1], sums,
            finals if last else [], (small_ks, small_parts) if last else None, 9,
        )
        if n == 0:
            token, passed = go_on(mlp_sums, result[:1], [attn_moves[k] for k in range(2, col_size)])
            attn_moves.update(zip(range(2, col_size), passed))
            attn_moves[1] = shifted(attn_total[1], -1)
        else:
            token, passed = go_on(mlp_sums, result[:1], list(result[2:]) + [attn_moves[1]])
            attn_moves[1] = passed[-1]
            attn_mine, attn_other = settle([attn_moves[k] for k in range(col_size)])
        if last:
            block_out, in_grad, _ = result
            smalls = passed[0]
        else:
            branch, d_norm_mlp = result
        while last and len(mlp_moves) < col_size:
            for k1, r in zip(starts, mlp_sums):
                if id(r) in totals and k1 not in mlp_moves:
                    for i in range(per_call):
                        slots = [totals[id(r)][i * per_mlp + j] for j in range(per_mlp)]
                        part = jnp.concatenate([s[:, :cut] for s in slots] + [s[:, cut:] for s in slots], axis=1)
                        mlp_moves[k1 + i] = part if k1 + i == 0 else shifted(part, -(k1 + i))
            if len(mlp_moves) < col_size:
                smalls = sum_over(smalls, ("row", "dp"))
                late = [mlp_moves[col_size - 1]] if col_size - 1 in mlp_moves else []
                token, passed = go_on(mlp_sums, token, [smalls] + late)
                smalls = passed[0]
                if late:
                    mlp_moves[col_size - 1] = passed[1]
    head_row, up_row = 5 + col_size, 5
    col_flips = [1 << n for n in range(col_size.bit_length() - 1)]
    for flip in col_flips[:-1]:
        smalls = smalls + flipped(smalls, "col", flip)
    smalls, *came = fence([smalls] + [mlp_moves[k] for k in range(1, col_size)])
    mlp_mine, mlp_other = settle([mlp_moves[0]] + came)
    smalls = fence([smalls], [mlp_mine])[0]
    smalls = smalls + flipped(smalls, "col", col_flips[-1])
    g_heads = whole_block(attn_mine, attn_other).reshape(rows, local_heads, HEAD)
    g_mlp = whole_block(mlp_mine, mlp_other)
    g_up, g_down = g_mlp[:, :up_cols], g_mlp[:, up_cols:]
    return (
        block_out,
        in_grad,
        smalls[1],
        smalls[2],
        smalls[3],
        smalls[4],
        g_heads[:, :, :QKV].reshape(rows, local_heads * QKV),
        smalls[head_row : head_row + col_size].reshape(col_size * local_heads, HEAD)[:, :QKV].reshape(-1),
        g_heads[:, :, QKV:].reshape(rows, local_heads * HD).T,
        smalls[0],
        g_up,
        smalls[up_row : up_row + col_size].reshape(-1),
        g_down.T,
        smalls[0],
    )


def solution(mesh):
    return jax.shard_map(
        on_device,
        mesh=mesh,
        in_specs=(
            P(("dp", "row", "col"), None),
            P("dp", None),
            P(),
            P(),
            P(),
            P(),
            P("row", "col"),
            P(),
            P("col", "row"),
            P(),
            P("row", "col"),
            P(),
            P("col", "row"),
            P(),
            P(("dp", "row", "col"), None),
        ),
        out_specs=(
            P(("dp", "row", "col"), None),
            P(("dp", "row", "col"), None),
            P(),
            P(),
            P(),
            P(),
            P("row", "col"),
            P(),
            P("col", "row"),
            P(),
            P("row", "col"),
            P(),
            P("col", "row"),
            P(),
        ),
        check_vma=False,
    )
```

```python
import copy
import functools
import math

import jax
import jax.numpy as jnp
from jax import lax
from jax.experimental import pallas as pl
from jax.experimental.pallas import tpu as pltpu
from jax.sharding import PartitionSpec as P

HD = 64
ROT = 16
QKV = 3 * HD
HEAD = 4 * HD
EPSILON = 1e-05
ROPE_BASE = 10000.0
NEAR = 128
LONGEST = 256
F32 = jnp.float32
BF16 = jnp.bfloat16


def dot_nn(a, b):
    return lax.dot_general(a, b, (((1,), (0,)), ((), ())), preferred_element_type=F32)


def dot_nt(a, b):
    return lax.dot_general(a, b, (((1,), (1,)), ((), ())), preferred_element_type=F32)


def gathered_order(order, core_bit):
    held = [0]
    for bit in order[:-1]:
        held = held + [j | bit for j in held]
    came = [j | order[-1] for j in held]
    return held, came, [j | core_bit for j in held], [j | core_bit for j in came]


def reduced_order(order):
    kept = [0]
    for bit in order[::-1]:
        kept = kept + [j | bit for j in kept]
    return kept


def assemble(me_ref, w_refs, held, w_scr, at_col):
    for ref, pieces in zip(w_refs, held):
        _, _, rows, cols = ref.shape
        for t, j in enumerate(pieces):
            at = pl.multiple_of((me_ref[0] ^ j) * rows, 16)
            w_scr[pl.ds(at, rows), at_col : at_col + cols] = ref[t, 0]


def hand_out(me_ref, g_scr, at_col, keep_ref, send_ref, first, order, core_bit):
    _, slots, rows, cols = keep_ref.shape
    for t, j in enumerate(reduced_order(order)):
        for ref, piece in ((keep_ref, j), (send_ref, j | core_bit)):
            at = pl.multiple_of((me_ref[0] ^ piece) * rows, 16)
            for slot in range(slots):
                left = at_col + slot * cols
                ref[first + t, slot] = g_scr[pl.ds(at, rows), left : left + cols]


def normalize(x):
    center = x - jnp.mean(x, axis=1, keepdims=True)
    inv_std = lax.rsqrt(jnp.mean(center * center, axis=1, keepdims=True) + EPSILON)
    return center * inv_std, inv_std


def prep_kernel(
    x_ref, cot_ref, ga_ref, sa_ref, gm_ref, sm_ref, segc_ref, segr_ref, freq_ref,
    na_ref, naT_ref, nm_ref, nmT_ref, cotT_ref, keep_ref, ahead_ref, behind_ref, mask_ref,
):
    length = x_ref.shape[0]
    tile = 128

    @pl.loop(0, length // tile)
    def _(t):
        rows = pl.ds(pl.multiple_of(t * tile, tile), tile)
        normed, _ = normalize(x_ref[rows, :].astype(F32))
        na_ref[rows, :] = (normed * ga_ref[...] + sa_ref[...]).astype(BF16)
        nm_ref[rows, :] = (normed * gm_ref[...] + sm_ref[...]).astype(BF16)
        same = segc_ref[rows, :] == segr_ref[...]
        cols = lax.broadcasted_iota(jnp.int32, (tile, length), 1)
        ids = lax.broadcasted_iota(jnp.int32, (tile, length), 0) + t * tile
        mask_ref[rows, :] = jnp.where(same & (cols <= ids), 0.0, -jnp.inf)
        starts = jnp.min(jnp.where(same, cols, length).astype(F32), axis=1, keepdims=True)
        places = ids[:, :1].astype(F32) - starts
        angles = places * freq_ref[...]
        lane = lax.broadcasted_iota(jnp.int32, (tile, 2 * HD), 1) % HD
        cosine, sine = jnp.cos(angles), jnp.sin(angles)
        keep_ref[rows, :] = jnp.where(lane < ROT, cosine, 1.0)
        ahead_ref[rows, :] = jnp.where(lane < ROT // 2, -sine, 0.0)
        behind_ref[rows, :] = jnp.where((lane < ROT) & (lane >= ROT // 2), sine, 0.0)

    naT_ref[...] = na_ref[...].T
    nmT_ref[...] = nm_ref[...].T
    cotT_ref[...] = cot_ref[...].T


def full(*shape):
    return pl.BlockSpec(shape, lambda *_: (0,) * len(shape), pipeline_mode=pl.Buffered(1))


ANY = pl.BlockSpec(memory_space=pl.ANY)
SCALAR = pl.BlockSpec(memory_space=pltpu.SMEM)


def cost(us):
    return pl.CostEstimate(flops=int(us * 1.15e9), bytes_accessed=2**20, transcendentals=0)


def shaped(shape, dtype):
    return jax.ShapeDtypeStruct(shape, dtype)


def prep_part(tokens, cot, gains, seg_row):
    length, width = tokens.shape
    halves = ROT // 2
    step = (lax.iota(jnp.int32, 2 * HD) % HD % halves).astype(F32)
    freq = (ROPE_BASE ** (-(step * (2.0 / ROT))))[None, :]
    table = shaped((length, 2 * HD), F32)
    return pl.pallas_call(
        prep_kernel,
        grid=(1,),
        in_specs=[full(length, width)] * 2 + [full(1, width)] * 4
        + [full(length, 1), full(1, length), full(1, 2 * HD)],
        out_specs=[full(length, width), full(width, length)] * 2 + [full(width, length)]
        + [full(length, 2 * HD)] * 3 + [full(length, length)],
        out_shape=[shaped((length, width), BF16), shaped((width, length), BF16)] * 2
        + [shaped((width, length), BF16)] + [table] * 3 + [shaped((length, length), F32)],
        compiler_params=pltpu.CompilerParams(vmem_limit_bytes=60 * 2**20),
        cost_estimate=cost(6),
    )(tokens, cot, *gains, seg_row[:, None], seg_row[None, :], freq)


def attention_kernel(orders, core_bit, waits, me_ref, na_ref, naT_ref, cot_ref, cotT_ref, *rest):
    left, right, rest = rest[:4], rest[4:8], rest[8:]
    bias_ref, keep_ref, ahead_ref, behind_ref, mask_ref = rest[:5]
    dqkv_ref, mix_ref, dbias_ref, gk_ref, gs_ref, w_scr, wv_scr, qkv_scr, dattn_scr, g_scr = rest[5 + waits :]
    length, width = na_ref.shape
    block_cols = w_scr.shape[1]
    heads = block_cols // HEAD
    kept = gk_ref.shape[0] // 2
    tile = 256
    assemble(me_ref, left, gathered_order(orders[0], core_bit), w_scr, 0)
    assemble(me_ref, right, gathered_order(orders[1], core_bit), w_scr, block_cols // 2)
    for i in range(heads):
        wv_scr[:, i * 2 * HD : (i + 1) * 2 * HD] = w_scr[:, i * HEAD + 2 * HD : (i + 1) * HEAD]

    for t in range(length // tile):
        rows = slice(t * tile, (t + 1) * tile)
        qkv_scr[rows, :] = dot_nn(na_ref[rows, :], w_scr[...]) + bias_ref[0]
        dattn_scr[rows, :] = dot_nn(cot_ref[rows, :], wv_scr[...]).astype(BF16)

    low = lax.broadcasted_iota(jnp.int32, (length, 2 * HD), 1) < HD
    keep, ahead, behind = keep_ref[...], ahead_ref[...], behind_ref[...]
    none = jnp.zeros((length, 2 * HD), BF16)
    spans = [(b * NEAR, (b + 1) * NEAR, max(0, b * NEAR - LONGEST)) for b in range(length // NEAR)]
    q0, k0, v1, go1, qT, goT = [], [], [], [], [], []
    for i in range(heads):
        qk = qkv_scr[:, i * HEAD : i * HEAD + 2 * HD]
        qk = qk * keep + pltpu.roll(qk, 2 * HD - ROT // 2, 1) * ahead + pltpu.roll(qk, ROT // 2, 1) * behind
        q0.append(jnp.where(low, qk * (1.0 / math.sqrt(HD)), 0.0).astype(BF16))
        k0.append(jnp.where(low, pltpu.roll(qk, HD, 1), 0.0).astype(BF16))
        value = pltpu.roll(qkv_scr[:, i * HEAD + 2 * HD : (i + 1) * HEAD], HD, 1)
        v1.append(jnp.where(low, 0.0, value).astype(BF16))
        go = dattn_scr[:, i * 2 * HD : (i + 1) * 2 * HD]
        go1.append(jnp.where(low, none, go))
        qT.append(q0[i].T[:HD])
        goT.append(go.T[HD:])
    parts = [(i, r0, r1, lo) for i in range(heads) for r0, r1, lo in spans]
    s = [dot_nt(q0[i][r0:r1], k0[i][lo:r1]) + mask_ref[r0:r1, lo:r1] for i, r0, r1, lo in parts]
    dp = [dot_nt(go1[i][r0:r1], v1[i][lo:r1]) for i, r0, r1, lo in parts]
    peak = [jnp.max(one, axis=1, keepdims=True) for one in s]
    e = [jnp.exp(one - top) for one, top in zip(s, peak)]
    norm = [1.0 / jnp.sum(one, axis=1, keepdims=True) for one in e]
    p = [one * scale for one, scale in zip(e, norm)]
    p_low = [one.astype(BF16) for one in p]
    mix = [dot_nn(one, v1[i][lo:r1]) for one, (i, r0, r1, lo) in zip(p_low, parts)]
    delta = [
        jnp.sum(one * go1[i][r0:r1].astype(F32), axis=1, keepdims=True) for one, (i, r0, r1, lo) in zip(mix, parts)
    ]
    ds = [(one * (grad - centre)).astype(BF16) for one, grad, centre in zip(p, dp, delta)]
    dq = [dot_nn(one, k0[i][lo:r1]) for one, (i, r0, r1, lo) in zip(ds, parts)]
    dkT = [dot_nn(qT[i][:, r0:r1], one) for one, (i, r0, r1, lo) in zip(ds, parts)]
    dvT = [dot_nn(goT[i][:, r0:r1], one) for one, (i, r0, r1, lo) in zip(p_low, parts)]
    for i in range(heads):
        mine = slice(i * len(spans), (i + 1) * len(spans))
        sums = []
        for group in (dvT[mine], dkT[mine]):
            total = [None] * len(spans)
            for part, (r0, r1, lo) in zip(group, spans):
                for n in range(lo // NEAR, r1 // NEAR):
                    one = part[:, n * NEAR - lo : (n + 1) * NEAR - lo]
                    total[n] = one if total[n] is None else total[n] + one
            sums.append(jnp.concatenate(total, axis=1))
        dvk = jnp.concatenate(sums, axis=0).T
        dqk = jnp.where(low, jnp.concatenate(dq[mine], axis=0) * (1.0 / math.sqrt(HD)), dvk)
        dqk = dqk * keep - pltpu.roll(dqk, 2 * HD - ROT // 2, 1) * ahead - pltpu.roll(dqk, ROT // 2, 1) * behind
        dqkv_ref[0, :, i * HEAD : i * HEAD + 2 * HD] = dqk.astype(BF16)
        dqkv_ref[0, :, i * HEAD + 2 * HD : (i + 1) * HEAD] = jnp.where(low, dvk, 0.0).astype(BF16)
        mix_ref[0, :, i * 2 * HD : (i + 1) * 2 * HD] = jnp.concatenate(mix[mine], axis=0).astype(BF16)

    dbias_ref[0] = jnp.sum(dqkv_ref[0].astype(F32), axis=0, keepdims=True)

    for t in range(width // tile):
        rows = slice(t * tile, (t + 1) * tile)
        g_in = dot_nn(naT_ref[rows, :], dqkv_ref[0])
        g_out = dot_nn(cotT_ref[rows, :], mix_ref[0])
        for i in range(heads):
            at = i * HEAD
            g_scr[rows, at : at + 2 * HD] = g_in[:, at : at + 2 * HD].astype(BF16)
            g_scr[rows, at + 2 * HD : at + HEAD] = (
                g_in[:, at + 2 * HD : at + HEAD] + g_out[:, i * 2 * HD : (i + 1) * 2 * HD]
            ).astype(BF16)

    hand_out(me_ref, g_scr, 0, gk_ref, gs_ref, 0, orders[0], core_bit)
    hand_out(me_ref, g_scr, block_cols // 2, gk_ref, gs_ref, kept, orders[1], core_bit)


def mlp_kernel(orders, core_bit, waits, me_ref, nm_ref, nmT_ref, cot_ref, cotT_ref, *rest):
    left, right, bias_ref, rest = rest[:4], rest[4:8], rest[8], rest[9 + waits :]
    act_ref, dh_ref, dbias_ref, gk_ref, gs_ref, wu_scr, wd_scr, g_scr = rest
    length, width = nm_ref.shape
    up_cols = wu_scr.shape[1]
    kept = gk_ref.shape[0] // 2
    tile = 256
    assemble(me_ref, left, gathered_order(orders[0], core_bit), wu_scr, 0)
    assemble(me_ref, right, gathered_order(orders[1], core_bit), wd_scr, 0)
    dbias_ref[0] = jnp.zeros_like(dbias_ref[0])

    for t in range(length // tile):
        rows = slice(t * tile, (t + 1) * tile)
        for n in range(0, up_cols, tile):
            hidden = dot_nn(nm_ref[rows, :], wu_scr[:, n : n + tile]) + bias_ref[0, :, n : n + tile]
            d_act = dot_nn(cot_ref[rows, :], wd_scr[:, n : n + tile])
            gate = 0.5 * (1.0 + lax.erf(hidden * (1.0 / math.sqrt(2.0))))
            act_ref[0, rows, n : n + tile] = (hidden * gate).astype(BF16)
            slope = gate + hidden * jnp.exp(-0.5 * hidden * hidden) * (1.0 / math.sqrt(2.0 * math.pi))
            dh = (d_act * slope).astype(BF16)
            dh_ref[0, rows, n : n + tile] = dh
            dbias_ref[0, :, n : n + tile] += jnp.sum(dh.astype(F32), axis=0, keepdims=True)

    for side, lhs, rhs in ((0, nmT_ref, dh_ref), (1, cotT_ref, act_ref)):

        for t in range(width // tile):
            rows = slice(t * tile, (t + 1) * tile)
            g_scr[rows, :] = dot_nn(lhs[rows, :], rhs[0]).astype(BF16)

        hand_out(me_ref, g_scr, 0, gk_ref, gs_ref, side * kept, orders[side], core_bit)


def weight_spec(array, block_of):
    count, _, rows, cols = array.shape
    return pl.BlockSpec((count, 1, rows, cols), lambda s: (0, block_of(s), 0, 0))


def block_part(kernel, w0, k0, count, slots, slot0, into, orders, core_bit, after, me, norm, norm_t, cot, cot_t,
               left, right, vectors, mid_cols, g_cols, scratch, us):
    length, width = norm.shape
    rows = left[0].shape[2]
    pieces = width // rows
    cols = vectors[0].shape[-1]
    per_step, total_slots = slots
    g_spec = pl.BlockSpec((pieces, per_step, rows, g_cols), lambda s: (0, slot0 + s, 0, 0))
    after = list(after) + list(into)
    fixed = 5 + len(left + right) + len(vectors) + len(after)
    return pl.pallas_call(
        functools.partial(kernel, orders, core_bit, len(after)),
        grid=(count,),
        in_specs=[SCALAR, full(length, width), full(width, length), full(length, width), full(width, length)]
        + [weight_spec(w, lambda s: w0 + s) for w in left + right]
        + [pl.BlockSpec((1, 1, cols), lambda s: (k0 + s, 0, 0))]
        + [full(*v.shape) for v in vectors[1:]]
        + [ANY] * len(after),
        out_specs=[pl.BlockSpec((1, length, m), lambda s: (s, 0, 0)) for m in mid_cols]
        + [pl.BlockSpec((1, 1, cols), lambda s: (s, 0, 0))] + [g_spec] * 2,
        out_shape=[shaped((count, length, m), BF16) for m in mid_cols]
        + [shaped((count, 1, cols), F32)] + [shaped((pieces, total_slots, rows, g_cols), BF16)] * 2,
        input_output_aliases={fixed - 2: len(mid_cols) + 1, fixed - 1: len(mid_cols) + 2} if into else {},
        scratch_shapes=scratch,
        compiler_params=pltpu.CompilerParams(vmem_limit_bytes=60 * 2**20),
        cost_estimate=cost(us * count),
    )(me, norm, norm_t, cot, cot_t, *left, *right, *vectors, *after)


def pick(refs, begins, scr):
    step = pl.program_id(0)
    for ref, begin, end in zip(refs, begins, begins[1:]):

        @pl.when((step >= begin) & (step < end))
        def _():
            scr[...] = ref[0]


def attention_tail_kernel(orders, core_bit, begins, waits, me_ref, *rest):
    left, right, rest = rest[:4], rest[4:8], rest[8:]
    calls = len(begins) - 1
    dqkv_refs, mix_refs, rest = rest[:calls], rest[calls : 2 * calls], rest[2 * calls :]
    sums_in, rest = rest[: len(rest) - waits - 6], rest[len(rest) - 6 :]
    branch_ref, dna_ref, w_scr, wv_scr, dqkv_scr, mix_scr = rest
    block_cols = w_scr.shape[1]

    @pl.when(pl.program_id(0) == 0)
    def _():
        branch_ref[...] = sums_in[0][...] if sums_in else jnp.zeros_like(branch_ref)
        dna_ref[...] = sums_in[1][...] if len(sums_in) > 1 else jnp.zeros_like(dna_ref)

    pick(dqkv_refs, begins, dqkv_scr)
    pick(mix_refs, begins, mix_scr)
    assemble(me_ref, left, gathered_order(orders[0], core_bit), w_scr, 0)
    assemble(me_ref, right, gathered_order(orders[1], core_bit), w_scr, block_cols // 2)
    for i in range(block_cols // HEAD):
        wv_scr[:, i * 2 * HD : (i + 1) * 2 * HD] = w_scr[:, i * HEAD + 2 * HD : (i + 1) * HEAD]
    tile = 256

    for t in range(branch_ref.shape[0] // tile):
        rows = slice(t * tile, (t + 1) * tile)
        branch_ref[rows, :] += dot_nt(mix_scr[rows, :], wv_scr[...])
        dna_ref[rows, :] += dot_nt(dqkv_scr[rows, :], w_scr[...])


def mlp_tail_kernel(orders, core_bit, sums, small_ks, waits, me_ref, *rest):
    left, right, dh_ref, act_ref, rest = rest[:4], rest[4:8], rest[8], rest[9], rest[10:]
    sums_in, rest = rest[:sums], rest[sums:]
    last = small_ks is not None
    if last:
        dna_ref, x_ref, cot_ref, ga_ref, gm_ref, bo_ref, bd_ref = rest[:7]
        small_refs = rest[7 : 7 + len(small_ks)]
        block_ref, grad_ref, stats_ref, branch_ref, dnm_ref, wu_scr, wd_scr = rest[7 + len(small_ks) + waits :]
    else:
        branch_ref, dnm_ref, wu_scr, wd_scr = rest[waits:]
    length = branch_ref.shape[0]
    step = pl.program_id(0)

    @pl.when(step == 0)
    def _():
        branch_ref[...] = sums_in[0][...] if sums else jnp.zeros_like(branch_ref)
        dnm_ref[...] = sums_in[1][...] if sums > 1 else jnp.zeros_like(dnm_ref)

    assemble(me_ref, left, gathered_order(orders[0], core_bit), wu_scr, 0)
    assemble(me_ref, right, gathered_order(orders[1], core_bit), wd_scr, 0)
    tile = 256

    for t in range(length // tile):
        rows = slice(t * tile, (t + 1) * tile)
        branch_ref[rows, :] += dot_nt(act_ref[0, rows, :], wd_scr[...])
        dnm_ref[rows, :] += dot_nt(dh_ref[0, rows, :], wu_scr[...])

    if not last:
        return

    @pl.when(step == pl.num_programs(0) - 1)
    def _():
        stats_ref[...] = jnp.zeros_like(stats_ref)
        small = 128

        @pl.loop(0, length // small)
        def _(t):
            rows = pl.ds(pl.multiple_of(t * small, small), small)
            x = x_ref[rows, :].astype(F32)
            cot = cot_ref[rows, :].astype(F32)
            normed, inv_std = normalize(x)
            block_ref[rows, :] = (x + branch_ref[rows, :] + bo_ref[...] + bd_ref[...]).astype(BF16)
            dna, dnm = dna_ref[rows, :], dnm_ref[rows, :]
            d_normed = dna * ga_ref[...] + dnm * gm_ref[...]
            pulled = (
                d_normed
                - jnp.mean(d_normed, axis=1, keepdims=True)
                - normed * jnp.mean(d_normed * normed, axis=1, keepdims=True)
            )
            grad_ref[rows, :] = (cot + inv_std * pulled).astype(BF16)
            for at, term in enumerate((cot, dna * normed, dna, dnm * normed, dnm)):
                stats_ref[at : at + 1, :] += jnp.sum(term, axis=0, keepdims=True)

        for ref, (first, k0, blocks) in zip(small_refs, small_ks):
            for i in range(ref.shape[0]):
                block = lax.rem(me_ref[1] + (blocks - k0 - i), blocks)
                stats_ref[pl.ds(first + block, 1), :] = ref[i]


def attention_tail_part(begins, starts, orders, core_bit, after, me, left, right, mids, sums, us):
    steps = left[0].shape[1]
    pieces = 2 * sum(w.shape[0] for w in left) // 2
    width = pieces * left[0].shape[2]
    length = mids[0][0].shape[1]

    def mid_spec(array, n):
        begin, end = begins[n], begins[n + 1]
        return pl.BlockSpec(
            (1,) + array.shape[1:], lambda s: (jnp.clip(s - begin, 0, end - begin - 1), 0, 0)
        )

    def block_of(step):
        block = step
        for begin, start in zip(begins, starts):
            block = jnp.where(step >= begin, start + step - begin, block)
        return block

    block_cols, half_cols = mids[0][0].shape[2], mids[1][0].shape[2]
    outs = [shaped((length, width), F32)] * 2
    return pl.pallas_call(
        functools.partial(attention_tail_kernel, orders, core_bit, begins, len(after)),
        grid=(steps,),
        in_specs=[SCALAR] + [weight_spec(w, lambda s: block_of(s)) for w in left + right]
        + [mid_spec(array, n) for group in mids for n, array in enumerate(group)]
        + [full(*e.shape) for e in sums] + [ANY] * len(after),
        out_specs=[full(*o.shape) for o in outs],
        out_shape=outs,
        scratch_shapes=[pltpu.VMEM((width, block_cols), BF16), pltpu.VMEM((width, half_cols), BF16)]
        + [pltpu.VMEM(group[0].shape[1:], BF16) for group in mids],
        compiler_params=pltpu.CompilerParams(vmem_limit_bytes=60 * 2**20),
        cost_estimate=cost(us),
    )(me, *left, *right, *[array for group in mids for array in group], *sums, *after)


def mlp_tail_part(w0, orders, core_bit, after, me, left, right, act, dh, sums, finals, smalls, us):
    count, length, cols = dh.shape
    width = sum(w.shape[0] for w in left) * left[0].shape[2]
    mid_spec = pl.BlockSpec((1, length, cols), lambda s: (s, 0, 0))
    total = shaped((length, width), F32)
    scratch = [pltpu.VMEM((width, cols), BF16)] * 2
    outs, small_ks = [total] * 2, None
    if finals:
        small_ks, arrays = smalls
        blocks = small_ks[0][2]
        outs = [shaped((length, width), BF16)] * 2 + [shaped((-(-(5 + 2 * blocks) // 8) * 8, width), F32)]
        scratch = [pltpu.VMEM((length, width), F32)] * 2 + scratch
        finals = list(finals) + list(arrays)
    extra = list(sums) + list(finals)
    return pl.pallas_call(
        functools.partial(mlp_tail_kernel, orders, core_bit, len(sums), small_ks, len(after)),
        grid=(count,),
        in_specs=[SCALAR] + [weight_spec(w, lambda s: w0 + s) for w in left + right] + [mid_spec] * 2
        + [full(*e.shape) for e in extra] + [ANY] * len(after),
        out_specs=[full(*o.shape) for o in outs],
        out_shape=outs,
        scratch_shapes=scratch,
        compiler_params=pltpu.CompilerParams(vmem_limit_bytes=60 * 2**20),
        cost_estimate=cost(us),
    )(me, *left, *right, dh, act, *extra, *after)


def fence_kernel(*_):
    pass


def fence(values, after=()):
    count = len(values)
    return pl.pallas_call(
        fence_kernel,
        in_specs=[ANY] * (count + len(after)),
        out_specs=[ANY] * count,
        out_shape=[shaped(value.shape, value.dtype) for value in values],
        input_output_aliases={n: n for n in range(count)},
        cost_estimate=cost(1),
    )(*values, *after)


def swap(value, bit):
    axis, flip = ("dp", 1) if bit == 1 else ("row", bit // 2)
    return flipped(value, axis, flip)


def flipped(value, axis, flip):
    return lax.ppermute(value, axis, [(i, i ^ flip) for i in range(lax.axis_size(axis))])


def shifted(value, by):
    size = lax.axis_size("col")
    return lax.ppermute(value, "col", [(i, (i + by) % size) for i in range(size)])


class Gather:
    def __init__(self, blocks, orders, core_bit):
        cut = blocks.shape[2] // 2
        self.orders, self.core_bit, self.done = orders, core_bit, 0
        self.block = blocks[0]
        self.held = [blocks[None, :, :, :cut], blocks[None, :, :, cut:]]

    def advance(self):
        if self.done > 0:
            self.held = [jnp.concatenate(pair, axis=0) for pair in zip(self.held, self.moving)]
        self.moving = [swap(one, order[self.done]) for one, order in zip(self.held, self.orders)]
        self.done += 1

    def part(self, blocks):
        one = copy.copy(self)
        one.held = [array[:, blocks] for array in self.held]
        one.moving = [array[:, blocks] for array in self.moving]
        return one

    def cross_held(self):
        self.over = [swap(one, self.core_bit) for one in self.held]

    def cross_moving(self):
        self.over += [swap(one, self.core_bit) for one in self.moving]

    def sides(self):
        return ([self.held[i], self.moving[i], self.over[i], self.over[i + 2]] for i in range(2))


class Reduction:
    def __init__(self, keep, send, orders, core_bit):
        self.keep, self.orders, self.came = keep, orders, swap(send, core_bit)
        self.later = [[] for _ in orders]
        self.done = 0

    def half(self):
        return self.keep.shape[0] // len(self.orders) >> (self.done + 1)


def merge_kernel(layout, ins, first_out, *refs):
    outs = refs[first_out : first_out + len(layout)]
    at = 0
    for group, out in zip(layout, outs):
        column = 0
        for terms in group:
            total = refs[at][...].astype(F32)
            for ref in refs[at + 1 : at + terms]:
                total = total + ref[...].astype(F32)
            at += terms
            cols = total.shape[-1]
            out[..., column : column + cols] = total.astype(BF16)
            column += cols
    assert at == ins


def merge(reductions, after, values=()):
    specs, arrays, layout, shapes, plans = [], [], [], [], []

    def block(array, count, index):
        shape = (count,) + array.shape[1:]
        return pl.BlockSpec(shape, lambda s: (index,) + (0,) * (len(shape) - 1), pipeline_mode=pl.Buffered(1))

    for r in reductions:
        half = r.half()
        count = max(half, 1)
        size = r.keep.shape[0] // len(r.orders)
        groups = []
        for side in range(len(r.orders)):
            terms = [(one, (side * size + half) // count) for one in (r.keep, r.came)]
            terms += [(one, half // count) for one in r.later[side]]
            for one, index in terms:
                specs.append(block(one, count, index))
                arrays.append(one)
            groups.append(len(terms))
        _, slots, rows, cols = r.keep.shape
        if half:
            layout += [(terms,) for terms in groups]
            shapes += [(half, slots, rows, cols)] * len(groups)
        else:
            layout.append(tuple(groups))
            shapes.append((1, slots, rows, cols * len(groups)))
        plans.append((r, half))
    out = list(pl.pallas_call(
        functools.partial(merge_kernel, layout, len(arrays), len(arrays) + len(values) + len(after)),
        grid=(1,),
        in_specs=specs + [ANY] * (len(values) + len(after)),
        out_specs=[full(*shape) for shape in shapes] + [ANY] * len(values),
        out_shape=[shaped(shape, BF16) for shape in shapes] + [shaped(v.shape, v.dtype) for v in values],
        input_output_aliases={len(arrays) + n: len(shapes) + n for n in range(len(values))},
        compiler_params=pltpu.CompilerParams(vmem_limit_bytes=60 * 2**20),
        cost_estimate=cost(3),
    )(*arrays, *values, *after))
    token, finished = out[0], []
    passed = out[len(shapes) :]
    for r, half in plans:
        if half:
            for side, order in enumerate(r.orders):
                r.later[side].append(swap(out.pop(0), order[r.done]))
            r.done += 1
        else:
            finished.append(out.pop(0)[0])
    return finished, [token], passed


def phase(users, values=(), after=()):
    values = list(values)
    out = list(fence(values + [one for user in users for one in user.moving], after))
    at = len(values)
    for user in users:
        user.moving = out[at : at + len(user.moving)]
        at += len(user.moving)
    return out


def sum_over(value, axes):
    for axis in axes:
        flip = 1
        while flip < lax.axis_size(axis):
            value = value + flipped(value, axis, flip)
            flip *= 2
    return value


def on_device(
    tokens_in,
    segment_ids,
    attn_gain,
    attn_shift,
    mlp_gain,
    mlp_shift,
    qkv_weight,
    qkv_bias,
    out_weight,
    out_bias,
    up_weight,
    up_bias,
    down_weight,
    down_bias,
    out_cotangent,
):
    row_size = lax.axis_size("row")
    col_size = lax.axis_size("col")
    length, width = tokens_in.shape
    rows = qkv_weight.shape[0]
    half_rows = rows // 2
    local_heads = qkv_weight.shape[1] // QKV
    block_cols = local_heads * HEAD
    up_cols = up_weight.shape[1]
    row_id = lax.axis_index("row")
    col_id = lax.axis_index("col")
    half = lax.axis_index("dp") % 2
    me = jnp.stack([row_id * 2 + half, col_id]).astype(jnp.int32)
    row_bits = [2 << i for i in range(row_size.bit_length() - 1)]
    core_bit, far_bits = row_bits[0], row_bits[1:][::-1]
    orders = (far_bits + [1], [1] + far_bits)

    head_weight = jnp.concatenate(
        [qkv_weight.reshape(rows, local_heads, QKV), out_weight.T.reshape(rows, local_heads, HD)], axis=2
    ).reshape(rows, block_cols)
    attn_own = lax.dynamic_slice_in_dim(head_weight, half * half_rows, half_rows, axis=0)
    mlp_own = jnp.concatenate(
        [
            lax.dynamic_slice_in_dim(up_weight, half * half_rows, half_rows, axis=0),
            lax.dynamic_slice_in_dim(down_weight, half * half_rows, half_rows, axis=1).T,
        ],
        axis=1,
    )
    cut = block_cols // 2

    seg_row = lax.dynamic_index_in_dim(segment_ids, row_id * col_size + col_id, axis=0, keepdims=False)
    na, na_t, nm, nm_t, cot_t, keep, ahead, behind, mask = prep_part(
        tokens_in, out_cotangent, [v[None, :] for v in (attn_gain, attn_shift, mlp_gain, mlp_shift)], seg_row,
    )
    blocks_here = (col_id - jnp.arange(col_size)) % col_size
    head_bias = jnp.pad(
        qkv_bias.reshape(col_size, local_heads, QKV), ((0, 0), (0, 0), (0, HEAD - QKV))
    ).reshape(col_size, 1, block_cols)
    head_bias = jnp.take(head_bias, blocks_here, axis=0)
    hidden_bias = jnp.take(up_bias.reshape(col_size, 1, up_cols), blocks_here, axis=0)

    far = len(orders[0])

    def gather_col(own):
        return [own] + [shifted(own, k) for k in range(1, col_size)]

    attn = Gather(jnp.stack(gather_col(attn_own)), orders, core_bit)
    mlp_blocks = gather_col(fence([mlp_own], [attn.held[0]])[0])
    for _ in range(far):
        attn.advance()
        phase([attn], [], [na, mlp_blocks[1]] if attn.done == 1 else mlp_blocks[2:])
    mlp_blocks = fence(mlp_blocks, attn.moving)
    attn.cross_held()
    attn.cross_moving()
    per_call = 2
    starts = list(range(0, col_size, per_call))[::-1]
    mlp_all = Gather(jnp.stack(mlp_blocks), orders, core_bit)
    mlp_all.advance()

    def attention_call(weights, w0, k0, count, slots, slot0, into, after):
        return block_part(
            attention_kernel, w0, k0, count, slots, slot0, into, orders, core_bit, after, me, na, na_t, out_cotangent,
            cot_t, *weights.sides(), [head_bias, keep, ahead, behind, mask], [block_cols, cut], cut,
            [
                pltpu.VMEM((width, block_cols), BF16), pltpu.VMEM((width, cut), BF16),
                pltpu.VMEM((length, block_cols), F32), pltpu.VMEM((length, cut), BF16),
                pltpu.VMEM((width, block_cols), BF16),
            ],
            10,
        )

    def mlp_call(weights, w0, k0, count, slots, slot0, into, after):
        return block_part(
            mlp_kernel, w0, k0, count, slots, slot0, into, orders, core_bit, after, me, nm, nm_t, out_cotangent, cot_t,
            *weights.sides(), [hidden_bias], [up_cols, up_cols], cut, [pltpu.VMEM((width, up_cols), BF16)] * 3, 6,
        )

    per_mlp = up_cols // cut
    attn_calls, into, token = [], [], []
    for n, k0 in enumerate(starts):
        if n == 1:
            phase([mlp_all], [], token)
            while mlp_all.done < far - 1:
                mlp_all.advance()
                phase([mlp_all])
            mlp = [mlp_all.part(slice(at, at + per_call)) for at in starts]
            mlp[0].advance()
            mlp[0].cross_held()
            token = mlp[0].held[:1]
        outs = attention_call(attn, k0, k0, per_call, (1, col_size), k0, into, token)
        attn_calls.append(outs)
        into = list(outs[3:])
        token = [outs[2]]
    sent = phase([mlp[0]], into[1:], token + mlp[0].over)
    mlp[1].advance()
    mlp[0].cross_moving()
    token = sent[-1:]
    attn_sum = Reduction(into[0], sent[0], orders, core_bit)
    begins = list(range(0, col_size + 1, per_call))
    branch, d_norm_attn = attention_tail_part(
        begins, starts, orders, core_bit, token, me, *attn.sides(), [[c[0] for c in attn_calls], [c[1] for c in attn_calls]],
        [], 11,
    )
    totals = {}

    def go_on(reductions, after, values=()):
        reductions = [r for r in reductions if id(r) not in totals]
        ending = [r for r in reductions if not r.half()]
        finished, token, passed = merge(reductions, after, values)
        totals.update(zip((id(r) for r in ending), finished))
        return token, passed

    mlp[1].held = phase(mlp[1:], mlp[1].held, [branch] + mlp[0].over)[:2]
    token, _ = go_on([attn_sum], [branch, mlp[1].moving[0]])
    mlp[1].cross_held()
    mlp[1].cross_moving()
    mlp_calls, mlp_sums = [], []
    for n, k0 in enumerate(starts):
        outs = mlp_call(mlp[n], 0, k0, per_call, (per_mlp, per_mlp * per_call), 0, [], token)
        mlp_calls.append(outs)
        token, sent = go_on([attn_sum] + mlp_sums, [outs[2]] + (mlp[1].over if n == 0 else []), [outs[4]])
        mlp_sums.append(Reduction(outs[3], sent[0], orders, core_bit))
    while id(attn_sum) not in totals:
        token, _ = go_on([attn_sum], token)
    attn_total = totals[id(attn_sum)]
    attn_moves = {0: attn_total[0]}
    for k in range(2, col_size):
        attn_moves[k] = shifted(attn_total[k], -k)
    def settle(parts):
        total = sum((part.astype(F32) for part in parts[1:]), parts[0].astype(F32))
        flip = 2
        while flip < lax.axis_size("dp"):
            total = total + flipped(total, "dp", flip)
            flip *= 2
        mine = total.astype(BF16)
        return mine, swap(mine, 1)

    def whole_block(mine, other):
        first = half == 0
        return jnp.concatenate([jnp.where(first, mine, other), jnp.where(first, other, mine)], axis=0).astype(F32)

    small_ks = tuple((5, k0, col_size) for k0 in starts) + tuple((5 + col_size, k0, col_size) for k0 in starts)
    small_parts = [c[2] for c in mlp_calls] + [c[2] for c in attn_calls]
    mlp_moves = {}
    d_norm_mlp = None
    for n, k0 in enumerate(starts):
        last = n == len(starts) - 1
        sums = [branch] if n == 0 else [branch, d_norm_mlp]
        finals = [
            d_norm_attn, tokens_in, out_cotangent, attn_gain[None, :], mlp_gain[None, :], out_bias[None, :],
            down_bias[None, :],
        ]
        result = mlp_tail_part(
            0, orders, core_bit, token, me, *mlp[n].sides(), mlp_calls[n][0], mlp_calls[n][1], sums,
            finals if last else [], (small_ks, small_parts) if last else None, 9,
        )
        if n == 0:
            token, passed = go_on(mlp_sums, result[:1], [attn_moves[k] for k in range(2, col_size)])
            attn_moves.update(zip(range(2, col_size), passed))
            attn_moves[1] = shifted(attn_total[1], -1)
        else:
            token, passed = go_on(mlp_sums, result[:1], list(result[2:]) + [attn_moves[1]])
            attn_moves[1] = passed[-1]
            attn_mine, attn_other = settle([attn_moves[k] for k in range(col_size)])
        if last:
            block_out, in_grad, _ = result
            smalls = passed[0]
        else:
            branch, d_norm_mlp = result
        while last and len(mlp_moves) < col_size:
            for k1, r in zip(starts, mlp_sums):
                if id(r) in totals and k1 not in mlp_moves:
                    for i in range(per_call):
                        slots = [totals[id(r)][i * per_mlp + j] for j in range(per_mlp)]
                        part = jnp.concatenate([s[:, :cut] for s in slots] + [s[:, cut:] for s in slots], axis=1)
                        mlp_moves[k1 + i] = part if k1 + i == 0 else shifted(part, -(k1 + i))
            if len(mlp_moves) < col_size:
                smalls = sum_over(smalls, ("row",))
                late = [mlp_moves[col_size - 1]] if col_size - 1 in mlp_moves else []
                token, passed = go_on(mlp_sums, token, [smalls] + late)
                smalls = passed[0]
                if late:
                    mlp_moves[col_size - 1] = passed[1]
    head_row, up_row = 5 + col_size, 5
    col_flips = [1 << n for n in range(col_size.bit_length() - 1)]
    smalls = sum_over(smalls, ("dp",))
    for flip in col_flips[:-1]:
        smalls = smalls + flipped(smalls, "col", flip)
    smalls, *came = fence([smalls] + [mlp_moves[k] for k in range(1, col_size)])
    mlp_mine, mlp_other = settle([mlp_moves[0]] + came)
    smalls = fence([smalls], [mlp_mine])[0]
    smalls = smalls + flipped(smalls, "col", col_flips[-1])
    g_heads = whole_block(attn_mine, attn_other).reshape(rows, local_heads, HEAD)
    g_mlp = whole_block(mlp_mine, mlp_other)
    g_up, g_down = g_mlp[:, :up_cols], g_mlp[:, up_cols:]
    return (
        block_out,
        in_grad,
        smalls[1],
        smalls[2],
        smalls[3],
        smalls[4],
        g_heads[:, :, :QKV].reshape(rows, local_heads * QKV),
        smalls[head_row : head_row + col_size].reshape(col_size * local_heads, HEAD)[:, :QKV].reshape(-1),
        g_heads[:, :, QKV:].reshape(rows, local_heads * HD).T,
        smalls[0],
        g_up,
        smalls[up_row : up_row + col_size].reshape(-1),
        g_down.T,
        smalls[0],
    )


def solution(mesh):
    return jax.shard_map(
        on_device,
        mesh=mesh,
        in_specs=(
            P(("dp", "row", "col"), None),
            P("dp", None),
            P(),
            P(),
            P(),
            P(),
            P("row", "col"),
            P(),
            P("col", "row"),
            P(),
            P("row", "col"),
            P(),
            P("col", "row"),
            P(),
            P(("dp", "row", "col"), None),
        ),
        out_specs=(
            P(("dp", "row", "col"), None),
            P(("dp", "row", "col"), None),
            P(),
            P(),
            P(),
            P(),
            P("row", "col"),
            P(),
            P("col", "row"),
            P(),
            P("row", "col"),
            P(),
            P("col", "row"),
            P(),
        ),
        check_vma=False,
    )
```
